32 devices in a mesh: dp: 4 (over z), seq: 4 (over x, core), expert: 2 (over y).
Axes of the slice: x: 2, y: 2, z: 4, core: 2. Of those that a mesh axis runs over, the one named last changes fastest.
Arguments:
- layer_input: bfloat16 [2, 4, 2, 256, 768], P(None, 'dp', 'expert', 'seq'), may hold values from -6 to 6
- memory: bfloat16 [2, 4, 2, 256, 768], P(None, 'dp', 'expert', 'seq'), may hold values from -6 to 6
- cotangent: bfloat16 [2, 4, 2, 256, 768], P(None, 'dp', 'expert', 'seq'), may hold values from -6 to 6
- routes: int32 [2, 4, 2, 256, 1], P(None, 'dp', 'expert', 'seq'), may hold values from 0 to 1
- doc_lengths: int32 [2, 4, 2, 3], P(None, 'dp', 'expert'), may hold values from 1 to 254, as said below
- rel_buckets: int32 [256], replicated, may hold values from 0 to 31, as said below
- gains: float32 [3, 768], replicated, may hold values from 0.5 to 1.5
- bias_table: float32 [32, 12], replicated, may hold values from -3 to 3
- router: bfloat16 [768, 2], replicated, may hold values from -0.15625 to 0.15625
- attn_in: bfloat16 [4608, 768], P(('dp', 'seq', 'expert')), may hold values from -0.21875 to 0.21875
- attn_out: bfloat16 [1536, 768], P(('dp', 'seq', 'expert')), may hold values from -0.875 to 0.875
- expert_in: bfloat16 [2, 768, 3072], P('expert', ('dp', 'seq')), may hold values from -0.21875 to 0.21875
- expert_out: bfloat16 [2, 3072, 768], P('expert', ('dp', 'seq')), may hold values from -0.375 to 0.375
Outputs:
- layer_output: bfloat16 [2, 4, 2, 256, 768], P(None, 'dp', 'expert', 'seq')
- grad_input: float32 [2, 4, 2, 256, 768], P(None, 'dp', 'expert', 'seq')
- grad_memory: float32 [2, 4, 2, 256, 768], P(None, 'dp', 'expert', 'seq')
- grad_gains: float32 [3, 768], replicated
- grad_bias: float32 [32, 12], replicated
- grad_router: float32 [768, 2], replicated
- grad_attn_in: float32 [4608, 768], P(('dp', 'seq', 'expert'))
- grad_attn_out: float32 [1536, 768], P(('dp', 'seq', 'expert'))
- grad_expert_in: float32 [2, 768, 3072], P('expert', ('dp', 'seq'))
- grad_expert_out: float32 [2, 3072, 768], P('expert', ('dp', 'seq'))
The draws below stay inside these ranges and needn't reach their ends.
Inputs may be any that keep to these rules, and one draw needn't show every extreme that they name: `doc_lengths`: each pack holds 3 documents laid end to end, their lengths summing to 256; one of them, at a place drawn from the seed, is longer than 192, the others are shorter than 32. `rel_buckets`: the bucket never falls as the distance grows; distance 0 has bucket 0 and distance 256 - 1 has bucket 32 - 1.
All inputs are finite; a program needn't handle non-finite values.
Results may differ from the reference program's by a relative error of at most 0.022.
Values may be sent and summed in bfloat16 or wider, within the bound.
A program may use at most 256 MiB of HBM per device.

```python
import jax
import jax.numpy as jnp
from jax import lax

D = 768
HEADS = 12
HEAD = 64
FF = 3072
BUCKETS = 32
TOK_DEV = 64
MB = 2
DOCS = 3
EXPERTS = 2
GROUP = 256
CAP = 40
N_DP = 4
N_SEQ = 4
N_EXPERT = 2


def draw_doc_lengths(key, part):
    key = jax.random.fold_in(key, 11)
    keys = jax.random.split(key, 3)
    shape = (MB, N_DP, N_EXPERT)
    first = jax.random.randint(keys[0], shape, 1, TOK_DEV // 2)
    last = jax.random.randint(keys[1], shape, 1, TOK_DEV // 2)
    first = first.at[0, 0, 0].set(1)
    last = last.at[0, 0, 0].set(1)
    longest = GROUP - first - last
    stacked = jnp.stack([first, longest, last], axis=-1)
    place = jax.random.randint(keys[2], shape, 0, 3)
    index = (jnp.arange(3, dtype=jnp.int32) - place[..., None]) % 3
    return jnp.take_along_axis(stacked, index, axis=-1).astype(jnp.int32)


def draw_rel_buckets(key, part):
    key = jax.random.fold_in(key, 23)
    distance = jnp.arange(GROUP, dtype=jnp.int32)
    coin = jax.random.randint(key, (GROUP,), 0, 16)
    step = jnp.where(distance < BUCKETS // 2, 1, (coin == 0).astype(jnp.int32))
    step = jnp.where(distance == 0, 0, step)
    bucket = jnp.minimum(jnp.cumsum(step), BUCKETS - 2)
    return jnp.where(distance == GROUP - 1, BUCKETS - 1, bucket).astype(jnp.int32)


def block_levels(rng, dims, pieces, least, largest):
    def one(axis_at, shards_of):
        heights = jax.random.uniform(jax.random.fold_in(jax.random.fold_in(rng, 6), axis_at), (shards_of,), jnp.float32, least / len(pieces), largest / len(pieces))
        return jnp.repeat(jnp.exp(heights), dims[axis_at] // shards_of).reshape((-1,) + (1,) * (len(dims) - axis_at - 1))

    level = one(*pieces[0])
    for cut in pieces[1:]:
        level = level * one(*cut)
    return level


def picks_of(stream_key, rows, number_of, top, lift):
    sequence = jax.random.permutation(jax.random.fold_in(stream_key, 1), number_of)
    favour = sequence
    for power in range(3):
        favour = favour * favour // number_of
    favour = favour * lift // number_of
    lots = jax.random.randint(jax.random.fold_in(stream_key, 2), (rows, number_of), 0, 4096) + favour
    fixed_rows = jax.random.permutation(jax.random.fold_in(stream_key, 3), rows)[jnp.arange(number_of) % rows]
    lots = jnp.where(jnp.arange(rows)[:, None] == fixed_rows[None, :], 1 << 14, lots)
    score = lots * number_of + jnp.arange(number_of)
    return lax.top_k(score.astype(jnp.int32), top)[1].astype(jnp.int32)


def bell_draw(rng, extent, spread, limit, cuts=(), kind=jnp.bfloat16):
    array = spread * jax.random.normal(rng, extent, jnp.float32)
    if cuts:
        array = array * block_levels(rng, extent, cuts, -0.22, 0.18)
    return jnp.clip(array, -limit, limit).astype(kind)


def setup_inputs(seed: int = 0) -> dict:
    arg_keys = jax.random.split(jax.random.key(seed), 14)
    return {
        "layer_input": bell_draw(arg_keys[0], (MB, N_DP, N_EXPERT, GROUP, D), 1.0, 6.0, ((1, 4), (2, 2), (3, 4))),
        "memory": bell_draw(arg_keys[1], (MB, N_DP, N_EXPERT, GROUP, D), 1.0, 6.0, ((1, 4), (2, 2), (3, 4))),
        "cotangent": bell_draw(arg_keys[2], (MB, N_DP, N_EXPERT, GROUP, D), 1.0, 6.0, ((1, 4), (2, 2), (3, 4))),
        "routes": picks_of(arg_keys[3], MB * N_DP * N_EXPERT * GROUP, EXPERTS, 1, 4096).reshape((MB, N_DP, N_EXPERT, GROUP, 1)),
        "doc_lengths": draw_doc_lengths(jax.random.fold_in(arg_keys[13], 71), 0),
        "rel_buckets": draw_rel_buckets(jax.random.fold_in(arg_keys[13], 71), 0),
        "gains": jnp.clip(1.0 + 0.1 * jax.random.normal(arg_keys[6], (3, D), jnp.float32), 0.5, 1.5),
        "bias_table": bell_draw(arg_keys[7], (BUCKETS, HEADS), 0.5, 3.0, (), jnp.float32),
        "router": bell_draw(arg_keys[8], (D, EXPERTS), (2 * D) ** -0.5, 0.15625),
        "attn_in": bell_draw(arg_keys[9], (6 * D, D), D ** -0.5, 0.21875, ((0, 32),)),
        "attn_out": bell_draw(arg_keys[10], (2 * D, D), (D // 16) ** -0.5, 0.875, ((0, 32),)),
        "expert_in": bell_draw(arg_keys[11], (EXPERTS, D, FF), D ** -0.5, 0.21875, ((0, 2), (1, 16))),
        "expert_out": bell_draw(arg_keys[12], (EXPERTS, FF, D), (max(1, FF // (3 * EXPERTS * EXPERTS))) ** -0.5, 0.375, ((0, 2), (1, 16))),
    }


EPS = 1e-06
NEG = -1e+30
HIGHEST = lax.Precision.HIGHEST

@jax.custom_vjp
def low(v):
    return lax.optimization_barrier(v.astype(jnp.bfloat16)).astype(jnp.float32)

@jax.custom_vjp
def low_back(v):
    return v

def low_keep(v):
    return (low(v), None)

def low_pass(kept, grad):
    return (grad,)

def back_keep(v):
    return (v, None)

def back_low(kept, grad):
    return (low(grad),)
low.defvjp(low_keep, low_pass)
low_back.defvjp(back_keep, back_low)

def product(left, right):
    return jnp.dot(left, right, precision=HIGHEST)

def norm_apply(value, gain):
    return value * lax.rsqrt(lax.optimization_barrier(jnp.mean(value * value, axis=-1, keepdims=True)) + EPS) * gain

def attention(query, keys, values, allowed, bias):
    count = query.shape[0]
    query3 = query.reshape(count, HEADS, HEAD)
    keys3 = keys.reshape(-1, HEADS, HEAD)
    values3 = values.reshape(-1, HEADS, HEAD)
    scores = jnp.einsum('qhd,khd->hqk', query3, keys3, precision=HIGHEST) * HEAD ** (-0.5) + bias
    scores = low_back(scores)
    chances = jax.nn.softmax(jnp.where(allowed[None], scores, NEG), axis=-1)
    mixed = jnp.einsum('hqk,khd->qhd', low(chances), values3, precision=HIGHEST)
    return low_back(low(mixed.reshape(count, HEADS * HEAD)))

def slot_table(route_block):
    hot = (route_block[:, None] == jnp.arange(EXPERTS, dtype=jnp.int32)).astype(jnp.int32)
    slot = lax.optimization_barrier(jnp.sum((jnp.cumsum(hot, axis=0) - hot) * hot, axis=1))
    target = jnp.where(slot < CAP, route_block * CAP + slot, -1)
    return (target[:, None] == jnp.arange(EXPERTS * CAP, dtype=jnp.int32)).astype(jnp.float32)

def pack_layer(x_pack, mem_pack, route_pack, length_pack, rel_buckets, gains, bias_table, router, attn_in, attn_out, expert_in, expert_out):
    position = jnp.arange(GROUP, dtype=jnp.int32)
    ends = jnp.cumsum(length_pack)
    owner_doc = lax.optimization_barrier(jnp.sum((position[:, None] >= ends[None, :]).astype(jnp.int32), axis=1))
    same = owner_doc[:, None] == owner_doc[None, :]
    causal = same & (position[None, :] <= position[:, None])
    distance = jnp.maximum(position[:, None] - position[None, :], 0)
    bias = jnp.transpose(bias_table[rel_buckets[distance]], (2, 0, 1))
    w_in = attn_in.reshape(6, D, D)
    w_out = attn_out.reshape(2, D, D)
    normed1 = low(norm_apply(x_pack, gains[0]))
    query = low_back(low(product(normed1, w_in[0])))
    keys = low_back(low(product(normed1, w_in[1])))
    values = low_back(low(product(normed1, w_in[2])))
    mem_keys = low_back(low(product(mem_pack, w_in[4])))
    mem_values = low_back(low(product(mem_pack, w_in[5])))
    hidden1 = x_pack + low_back(product(attention(query, keys, values, causal, bias), w_out[0]))
    normed2 = low(norm_apply(hidden1, gains[1]))
    cross_query = low_back(low(product(normed2, w_in[3])))
    hidden2 = hidden1 + low_back(product(attention(cross_query, mem_keys, mem_values, same, 0.0), w_out[1]))
    normed3 = low(norm_apply(hidden2, gains[2]))
    routing = jax.nn.softmax(product(normed3, router), axis=-1)
    hot = route_pack[:, None] == jnp.arange(EXPERTS, dtype=jnp.int32)
    gate = lax.optimization_barrier(jnp.sum(jnp.where(hot, routing, 0.0), axis=1))
    dispatch = jax.vmap(slot_table)(route_pack.reshape(N_SEQ, TOK_DEV))
    buffer = jnp.einsum('btc,btd->bcd', dispatch, normed3.reshape(N_SEQ, TOK_DEV, D), precision=HIGHEST)
    buffer = low_back(buffer.reshape(N_SEQ, EXPERTS, CAP, D))
    inner = low_back(jnp.einsum('becd,edf->becf', buffer, expert_in, precision=HIGHEST))
    hidden = low(jax.nn.gelu(inner, approximate=True))
    result = low_back(low(jnp.einsum('becf,efd->becd', hidden, expert_out, precision=HIGHEST)))
    back = jnp.einsum('btc,bcd->btd', dispatch, result.reshape(N_SEQ, EXPERTS * CAP, D), precision=HIGHEST)
    return hidden2 + gate[:, None] * back.reshape(GROUP, D)

def reference(layer_input, memory, cotangent, routes, doc_lengths, rel_buckets, gains, bias_table, router, attn_in, attn_out, expert_in, expert_out):
    packs = MB * N_DP * N_EXPERT
    x_all = layer_input.astype(jnp.float32).reshape(packs, GROUP, D)
    mem_all = memory.astype(jnp.float32).reshape(packs, GROUP, D)
    route_all = routes.reshape(packs, GROUP).astype(jnp.int32)
    length_all = doc_lengths.reshape(packs, DOCS).astype(jnp.int32)

    def forward(x_all, mem_all, gains, bias_table, router, attn_in, attn_out, expert_in, expert_out):

        def one(items):
            x_pack, mem_pack, route_pack, length_pack = items
            return pack_layer(x_pack, mem_pack, route_pack, length_pack, rel_buckets, gains, bias_table, router, attn_in, attn_out, expert_in, expert_out)
        return lax.map(jax.checkpoint(one), (x_all, mem_all, route_all, length_all))
    result, pull = jax.vjp(forward, x_all, mem_all, gains, bias_table, router.astype(jnp.float32), attn_in.astype(jnp.float32), attn_out.astype(jnp.float32), expert_in.astype(jnp.float32), expert_out.astype(jnp.float32))
    grads = pull(cotangent.astype(jnp.float32).reshape(packs, GROUP, D))
    shape = (MB, N_DP, N_EXPERT, GROUP, D)
    return (result.reshape(shape).astype(jnp.bfloat16), grads[0].reshape(shape), grads[1].reshape(shape), grads[2], grads[3], grads[4], grads[5], grads[6], grads[7], grads[8])
```

```python
import functools

import jax
import jax.numpy as jnp
from jax import lax
from jax.experimental import pallas as pl
from jax.experimental.pallas import tpu as pltpu
from jax.sharding import PartitionSpec as P

HEADS = 12
HEAD = 64

EPS = 1e-06
NEG = -1e30
HIGHEST = lax.Precision.HIGHEST
MESH = pl.DeviceIdType.MESH
BF = jnp.bfloat16
F32 = jnp.float32


class Place:
    def __init__(self):
        self.nz, self.ns, self.ny = (lax.axis_size(a) for a in ("dp", "seq", "expert"))
        self.nx = self.ns // 2
        self.z, self.s, self.y = (lax.axis_index(a) for a in ("dp", "seq", "expert"))
        self.x, self.c = self.s // 2, lax.rem(self.s, 2)

    def device(self, z=None, x=None, c=None, y=None):
        z = self.z if z is None else z
        x = self.x if x is None else x
        c = self.c if c is None else c
        y = self.y if y is None else y
        return (z, x * 2 + c, y)

    def other_x(self):
        return [lax.rem(self.x + k, self.nx) for k in range(1, self.nx)]

    def other_y(self):
        return [lax.rem(self.y + k, self.ny) for k in range(1, self.ny)]

    def by_distance(self, k):
        order = [sorted(range(self.nz), key=lambda d: (abs(d - z), d)) for z in range(self.nz)]
        out = jnp.int32(0)
        for z in range(self.nz):
            out = jnp.where(self.z == z, jnp.int32(order[z][k]), out)
        return out

    def greet(self):
        barrier = pltpu.get_barrier_semaphore()
        for x in self.other_x():
            pl.semaphore_signal(barrier, inc=1, device_id=self.device(x=x), device_id_type=MESH)
        for y in self.other_y():
            pl.semaphore_signal(barrier, inc=1, device_id=self.device(y=y), device_id_type=MESH)
        pl.semaphore_signal(barrier, inc=1, device_id=self.device(c=1 - self.c), device_id_type=MESH)

        @pl.when(self.z > 0)
        def _():
            pl.semaphore_signal(barrier, inc=1, device_id=self.device(z=self.z - 1), device_id_type=MESH)

        @pl.when(self.z < self.nz - 1)
        def _():
            pl.semaphore_signal(barrier, inc=1, device_id=self.device(z=self.z + 1), device_id_type=MESH)

        beside = jnp.where(self.z > 0, 1, 0) + jnp.where(self.z < self.nz - 1, 1, 0)
        pl.semaphore_wait(barrier, self.nx - 1 + self.ny - 1 + 1 + beside)


def spread_kernel(x_ref, m_ref, ain, aout, ein, eout, xo, mo, aino, aouto, eino, eouto,
                  act_send, act_recv, line_send, side_send, core_send, ici_recv, core_recv, own_sem):
    at = Place()
    nz, nx, ny = at.nz, at.nx, at.ny
    tok = x_ref.shape[1]
    shards = (ain, aout, ein, eout)
    fulls = (aino, aouto, eino, eouto)
    acts = ((x_ref, xo), (m_ref, mo))
    dense, expert = (0, 1), (2, 3)

    def spot(a, z, x, c, y):
        s = x * 2 + c
        rows = shards[a].shape[0]
        index = (z * at.ns + s) * ny + y if a in dense else z * at.ns + s
        return fulls[a].at[pl.ds(pl.multiple_of(index * rows, 16), rows)]

    waits = []

    def send(src, dst, ssem, rsem, **where):
        copy = pltpu.make_async_remote_copy(
            src_ref=src, dst_ref=dst, send_sem=ssem, recv_sem=rsem,
            device_id=at.device(**where), device_id_type=MESH,
        )
        copy.start()
        waits.append(copy.wait_send)

    def arrive(ref, sem):
        pltpu.make_async_copy(ref, ref, sem).wait()

    at.greet()
    for i, (src, full) in enumerate(acts):
        dst = full.at[:, pl.ds(pl.multiple_of(at.s * tok, 16), tok)]
        for k, x in enumerate(at.other_x()):
            send(src, dst, act_send.at[i, k], act_recv.at[i, at.x, at.c], x=x)
        send(src, dst, act_send.at[i, nx - 1 + at.x], act_recv.at[i, at.x, at.c], c=1 - at.c)
        own = pltpu.make_async_copy(src, dst, own_sem.at[4 + i])
        own.start()
        waits.append(own.wait)

    def along_line(a, z, src):
        dst = spot(a, z, at.x, at.c, at.y)
        sem = ici_recv.at[a, z, at.x, at.y]

        def one(side, to):
            return pltpu.make_async_remote_copy(
                src_ref=src, dst_ref=dst, send_sem=line_send.at[a, z, side], recv_sem=sem,
                device_id=at.device(z=to), device_id_type=MESH,
            )

        left = (z >= at.z) & (at.z > 0)
        right = (z <= at.z) & (at.z < nz - 1)

        @pl.when(left)
        def _():
            one(0, at.z - 1).start()

        @pl.when(right)
        def _():
            one(1, at.z + 1).start()

        def wait():
            @pl.when(left)
            def _():
                one(0, at.z - 1).wait_send()

            @pl.when(right)
            def _():
                one(1, at.z + 1).wait_send()

        waits.append(wait)

    def to_sides(a, z, src):
        dst = spot(a, z, at.x, at.c, at.y)
        for k, x in enumerate(at.other_x()):
            send(src, dst, side_send.at[a, z, k], ici_recv.at[a, z, at.x, at.y], x=x)
        if a in dense:
            for k, y in enumerate(at.other_y()):
                send(src, dst, side_send.at[a, z, nx - 1 + k], ici_recv.at[a, z, at.x, at.y], y=y)

    def to_core(a, z, x, y, src):
        send(src, spot(a, z, x, at.c, y), core_send.at[a, z, x, y], core_recv.at[a, z, x, y], c=1 - at.c)

    zs = [at.by_distance(k) for k in range(nz)]
    for group in (dense, expert):
        for a in group:
            along_line(a, at.z, shards[a])
    for k in range(nz):
        for a in dense:
            here = spot(a, zs[k], at.x, at.c, at.y)
            if k:
                arrive(here, ici_recv.at[a, zs[k], at.x, at.y])
                along_line(a, zs[k], here)
            else:
                own = pltpu.make_async_copy(shards[a], here, own_sem.at[a])
                own.start()
                waits.append(own.wait)
            to_sides(a, zs[k], here if k else shards[a])
            to_core(a, zs[k], at.x, at.y, here if k else shards[a])
        if k == 0:
            for i, (src, full) in enumerate(acts):
                for j, x in enumerate(at.other_x()):
                    dst = full.at[:, pl.ds(pl.multiple_of((x * 2 + at.c) * tok, 16), tok)]
                    arrive(dst, act_recv.at[i, x, at.c])
                    send(dst, dst, act_send.at[i, nx - 1 + x], act_recv.at[i, x, at.c], c=1 - at.c)
    for k in range(nz):
        for a in expert:
            here = spot(a, zs[k], at.x, at.c, at.y)
            if k:
                arrive(here, ici_recv.at[a, zs[k], at.x, at.y])
                along_line(a, zs[k], here)
            else:
                own = pltpu.make_async_copy(shards[a], here, own_sem.at[a])
                own.start()
                waits.append(own.wait)
            to_sides(a, zs[k], here if k else shards[a])
            to_core(a, zs[k], at.x, at.y, here if k else shards[a])
        for a in dense:
            for x in at.other_x():
                here = spot(a, zs[k], x, at.c, at.y)
                arrive(here, ici_recv.at[a, zs[k], x, at.y])
                for j, y in enumerate(at.other_y()):
                    send(here, here, side_send.at[a, zs[k], nx - 1 + ny - 1 + j + (ny - 1) * x],
                         ici_recv.at[a, zs[k], x, at.y], y=y)
                to_core(a, zs[k], x, at.y, here)
    for k in range(nz):
        for a in dense:
            for y in at.other_y():
                for x in range(nx):
                    here = spot(a, zs[k], x, at.c, y)
                    arrive(here, ici_recv.at[a, zs[k], x, y])
                    to_core(a, zs[k], x, y, here)
        for a in expert:
            for x in at.other_x():
                here = spot(a, zs[k], x, at.c, at.y)
                arrive(here, ici_recv.at[a, zs[k], x, at.y])
                to_core(a, zs[k], x, at.y, here)
    for a in range(4):
        for z in range(nz):
            for x in range(nx):
                for y in range(ny) if a in dense else [at.y]:
                    arrive(spot(a, z, x, 1 - at.c, y), core_recv.at[a, z, x, y])
    for i, (src, full) in enumerate(acts):
        for x in range(nx):
            dst = full.at[:, pl.ds(pl.multiple_of((x * 2 + 1 - at.c) * tok, 16), tok)]
            arrive(dst, act_recv.at[i, x, 1 - at.c])
    for wait in waits:
        wait()


def in_tiles(*arrays):
    return all(a.shape[-2] % 16 == 0 for a in arrays)


def spread(x, m, ain, aout, ein, eout):
    if not in_tiles(x, m, ain, aout, ein, eout):
        everywhere, peers = ("dp", "seq", "expert"), ("dp", "seq")
        return (
            *[lax.all_gather(a, "seq", axis=1, tiled=True) for a in (x, m)],
            *[lax.all_gather(a, everywhere, axis=0, tiled=True) for a in (ain, aout)],
            *[lax.all_gather(a, peers, axis=0, tiled=True) for a in (ein, eout)],
        )
    nz, ns, ny = (lax.axis_size(a) for a in ("dp", "seq", "expert"))
    nx = ns // 2
    tall = nz * ns
    any_ = pl.BlockSpec(memory_space=pl.ANY)
    dma = pltpu.SemaphoreType.DMA
    return pl.pallas_call(
        spread_kernel,
        out_shape=[
            jax.ShapeDtypeStruct((x.shape[0], ns * x.shape[1], x.shape[2]), BF),
            jax.ShapeDtypeStruct((x.shape[0], ns * x.shape[1], x.shape[2]), BF),
            jax.ShapeDtypeStruct((tall * ny * ain.shape[0], ain.shape[1]), BF),
            jax.ShapeDtypeStruct((tall * ny * aout.shape[0], aout.shape[1]), BF),
            jax.ShapeDtypeStruct((tall * ein.shape[0], ein.shape[1]), BF),
            jax.ShapeDtypeStruct((tall * eout.shape[0], eout.shape[1]), BF),
        ],
        in_specs=[any_] * 6,
        out_specs=[any_] * 6,
        scratch_shapes=[
            dma((2, 2 * nx)),
            dma((2, nx, 2)),
            dma((4, nz, 2)),
            dma((4, nz, nx - 1 + (ny - 1) * (1 + nx))),
            dma((4, nz, nx, ny)),
            dma((4, nz, nx, ny)),
            dma((4, nz, nx, ny)),
            dma((6,)),
        ],
        compiler_params=pltpu.CompilerParams(collective_id=0, has_side_effects=True),
        name="spread",
    )(x, m, ain, aout, ein, eout)


def add_into(total, other):
    lead = total.shape[:-2]
    count = 1
    for n in lead:
        count *= n
    rows = total.shape[-2]
    step = 48 if total.shape[-1] <= 1024 else 16

    def body(i, carry):
        index = []
        rest = i // (rows // step)
        for n in reversed(lead):
            index.insert(0, lax.rem(rest, n))
            rest = rest // n
        r = pl.ds(pl.multiple_of(lax.rem(i, rows // step) * step, 16), step)
        at = (*index, r)
        total[at] = (total[at].astype(F32) + other[at].astype(F32)).astype(total.dtype)
        return carry

    lax.fori_loop(0, count * (rows // step), body, 0)


def collect_kernel(g0, g1, g2, g3, o0, o1, o2, o3, c0, c1, c2, c3, y0, y1, x0, x1, x2, x3, z0, z1, z2, z3,
                   core_send, core_recv, y_send, y_recv, x_send, x_recv, z_send, z_recv):
    at = Place()
    nz, nx, ny = at.nz, at.nx, at.ny
    grads, outs = (g0, g1, g2, g3), (o0, o1, o2, o3)
    cores, ys, xs, zs_ = (c0, c1, c2, c3), (y0, y1), (x0, x1, x2, x3), (z0, z1, z2, z3)
    dense, expert = (0, 1), (2, 3)
    waits = []

    def copy(src, dst, ssem, rsem, **where):
        return pltpu.make_async_remote_copy(
            src_ref=src, dst_ref=dst, send_sem=ssem, recv_sem=rsem,
            device_id=at.device(**where), device_id_type=MESH,
        )

    def send(*args, **where):
        one = copy(*args, **where)
        one.start()
        waits.append(one.wait_send)

    def arrive(ref, sem):
        pltpu.make_async_copy(ref, ref, sem).wait()

    at.greet()
    order = [at.by_distance(nz - 1 - k) for k in range(nz)]

    def core_part(a, k, c):
        return grads[a].at[order[k], :, c]

    for k in range(nz):
        for a in range(4):
            send(core_part(a, k, 1 - at.c), cores[a].at[k], core_send.at[a, k], core_recv.at[a, k], c=1 - at.c)

    def stage_core(k):
        for a in expert + dense:
            arrive(cores[a].at[k], core_recv.at[a, k])
            add_into(cores[a].at[k], core_part(a, k, at.c))
            if a in expert:
                for j, x in enumerate(at.other_x()):
                    send(cores[a].at[k, x], xs[a].at[k, nx - 2 - j], x_send.at[a, k, j], x_recv.at[a, k, nx - 2 - j], x=x)
            else:
                for j, y in enumerate(at.other_y()):
                    send(cores[a].at[k, :, y], ys[a].at[k, ny - 2 - j], y_send.at[a, k, j], y_recv.at[a, k, ny - 2 - j], y=y)

    def stage_y(k):
        for a in dense:
            for j in range(ny - 1):
                arrive(ys[a].at[k, j], y_recv.at[a, k, j])
                add_into(ys[a].at[k, 0], ys[a].at[k, j] if j else cores[a].at[k, :, at.y])
            for j, x in enumerate(at.other_x()):
                send(ys[a].at[k, 0, x], xs[a].at[k, nx - 2 - j], x_send.at[a, k, j], x_recv.at[a, k, nx - 2 - j], x=x)

    def stage_x(k):
        for a in expert + dense:
            for j in range(nx - 1):
                arrive(xs[a].at[k, j], x_recv.at[a, k, j])
                own = cores[a].at[k, at.x] if a in expert else ys[a].at[k, 0, at.x]
                add_into(xs[a].at[k, 0], xs[a].at[k, j] if j else own)

    def stage_z(k):
        d = order[k]
        for a in expert + dense:
            total = xs[a].at[k, 0]
            for side, here in enumerate((at.z > 0, at.z < nz - 1)):
                feeds = here & ((d >= at.z) if side == 0 else (d <= at.z))

                @pl.when(feeds)
                def _(a=a, side=side, total=total):
                    arrive(zs_[a].at[side, d], z_recv.at[a, side, d])
                    add_into(total, zs_[a].at[side, d])

            if k == nz - 1:
                outs[a][...] = total[...].astype(F32)
                continue

            def hop(side, a=a, total=total):
                return copy(total, zs_[a].at[1 - side, d], z_send.at[a, d], z_recv.at[a, 1 - side, d],
                            z=at.z - 1 if side == 0 else at.z + 1)

            @pl.when(d < at.z)
            def _():
                hop(0).start()

            @pl.when(d > at.z)
            def _():
                hop(1).start()

            def wait(hop=hop):
                @pl.when(d < at.z)
                def _():
                    hop(0).wait_send()

                @pl.when(d > at.z)
                def _():
                    hop(1).wait_send()

            waits.append(wait)

    for t in range(nz + 2):
        if 0 <= t < nz:
            stage_core(t)
        if 0 <= t - 1 < nz:
            stage_y(t - 1)
        if 0 <= t - 2 < nz:
            stage_x(t - 2)
            stage_z(t - 2)
    for wait in waits:
        wait()


def collect(gin, gout, gein, geout):
    nz, ns, ny = (lax.axis_size(a) for a in ("dp", "seq", "expert"))
    nx = ns // 2
    width = gin.shape[-1]
    parts = (
        gin.reshape(nz, nx, 2, ny, -1, width),
        gout.reshape(nz, nx, 2, ny, -1, width),
        gein.reshape(nz, nx, 2, -1, gein.shape[-1]),
        geout.reshape(nz, nx, 2, -1, width),
    )
    ends = [p.shape[-2:] for p in parts]
    if not in_tiles(*parts):
        everywhere, peers = ("dp", "seq", "expert"), ("dp", "seq")
        return [
            lax.psum_scatter(a, over, scatter_dimension=0, tiled=True).astype(F32)
            for a, over in ((gin, everywhere), (gout, everywhere), (gein, peers), (geout, peers))
        ]
    vmem = pl.BlockSpec(memory_space=pltpu.VMEM)
    dma = pltpu.SemaphoreType.DMA
    return pl.pallas_call(
        collect_kernel,
        out_shape=[jax.ShapeDtypeStruct(e, F32) for e in ends],
        in_specs=[vmem] * 4,
        out_specs=[vmem] * 4,
        scratch_shapes=[
            *[pltpu.VMEM((nz, nx, ny, *e), BF) for e in ends[:2]],
            *[pltpu.VMEM((nz, nx, *e), BF) for e in ends[2:]],
            *[pltpu.VMEM((nz, ny - 1, nx, *e), BF) for e in ends[:2]],
            *[pltpu.VMEM((nz, nx - 1, *e), BF) for e in ends],
            *[pltpu.VMEM((2, nz, *e), BF) for e in ends],
            dma((4, nz)),
            dma((4, nz)),
            dma((2, nz, ny - 1)),
            dma((2, nz, ny - 1)),
            dma((4, nz, nx - 1)),
            dma((4, nz, nx - 1)),
            dma((4, nz)),
            dma((4, 2, nz)),
        ],
        compiler_params=pltpu.CompilerParams(
            collective_id=1, has_side_effects=True, vmem_limit_bytes=60 * 2**20
        ),
        name="collect",
    )(*parts)


def norm_apply(value, gain):
    return value * lax.rsqrt(jnp.mean(value * value, axis=-1, keepdims=True) + EPS) * gain


def norm_back(value, gain, grad):
    r = lax.rsqrt(jnp.mean(value * value, axis=-1, keepdims=True) + EPS)
    scaled = grad * gain
    back = r * scaled - value * (r * r * r) * jnp.mean(scaled * value, axis=-1, keepdims=True)
    return back, jnp.sum(grad * value * r, axis=0)


def gelu_tanh(value):
    return jax.nn.gelu(value, approximate=True)


def times(left, right):
    return jnp.dot(left, right, preferred_element_type=F32)


def times_right(left, right):
    return jnp.einsum("te,de->td", left, right, preferred_element_type=F32)


def times_left(left, right):
    return jnp.einsum("td,te->de", left, right, preferred_element_type=F32)


def split(a, packs):
    return a.reshape(packs, -1, HEADS, HEAD)


def attend(query, keys, values, allowed, bias, packs):
    scores = jnp.einsum("pqhd,pkhd->phqk", split(query, packs), split(keys, packs), preferred_element_type=F32)
    masked = jnp.where(allowed[:, None], scores * HEAD**-0.5 + bias, NEG)
    raised = jnp.exp(masked - jnp.max(masked, axis=3, keepdims=True))
    chances = raised / jnp.sum(raised, axis=3, keepdims=True)
    mixed = jnp.einsum("phqk,pkhd->pqhd", chances.astype(BF), split(values, packs), preferred_element_type=F32)
    return mixed.reshape(query.shape).astype(BF), chances


def attend_back(query, keys, values, chances, grad, packs):
    scale = HEAD**-0.5
    g4 = split(grad, packs)
    grad_chances = jnp.einsum("pqhd,pkhd->phqk", g4, split(values, packs), preferred_element_type=F32)
    spread_ = jnp.sum(chances * grad_chances, axis=3, keepdims=True)
    grad_scores = (chances * (grad_chances - spread_)).astype(BF)
    grad_query = jnp.einsum("phqk,pkhd->pqhd", grad_scores, split(keys, packs), preferred_element_type=F32) * scale
    grad_keys = jnp.einsum("phqk,pqhd->pkhd", grad_scores, split(query, packs), preferred_element_type=F32) * scale
    grad_values = jnp.einsum("phqk,pqhd->pkhd", chances.astype(BF), g4, preferred_element_type=F32)
    return (
        grad_query.reshape(query.shape).astype(BF),
        grad_keys.reshape(keys.shape).astype(BF),
        grad_values.reshape(keys.shape).astype(BF),
        grad_scores,
    )


def per_device(layer_input, memory, cotangent, routes, doc_lengths, rel_buckets, gains, bias_table, router,
               attn_in, attn_out, expert_in, expert_out):
    packs, rows, width = layer_input.shape[0], layer_input.shape[3], layer_input.shape[4]
    seqs = lax.axis_size("seq")
    group = rows * seqs
    experts = router.shape[1]
    capacity = (5 * rows + 4 * experts - 1) // (4 * experts)
    buckets = bias_table.shape[0]
    rank = lax.axis_index("seq")

    x_all, m_all, w_in, w_out, e_in, e_out = spread(
        layer_input[:, 0, 0], memory[:, 0, 0], attn_in, attn_out, expert_in[0], expert_out[0]
    )
    w_in = w_in.reshape(6, width, width)
    w_out = w_out.reshape(2, width, width)
    x_all = x_all.reshape(packs * group, width)
    m_all = m_all.reshape(packs * group, width)
    x_rows = layer_input.reshape(packs * rows, width).astype(F32)

    query_pos = rank * rows + jnp.arange(rows, dtype=jnp.int32)
    key_pos = jnp.arange(group, dtype=jnp.int32)
    ends = jnp.cumsum(doc_lengths[:, 0, 0], axis=1)
    query_doc = jnp.sum((query_pos[None, :, None] >= ends[:, None, :]).astype(jnp.int32), axis=2)
    key_doc = jnp.sum((key_pos[None, :, None] >= ends[:, None, :]).astype(jnp.int32), axis=2)
    same = query_doc[:, :, None] == key_doc[:, None, :]
    causal = same & (key_pos[None, None, :] <= query_pos[None, :, None])
    bucket_hot = (rel_buckets[:, None] == jnp.arange(buckets, dtype=jnp.int32)).astype(F32)
    line_at = jnp.arange(group + rows, dtype=jnp.int32) - (group - 1) + rank * rows
    line_hot = (jnp.take(rel_buckets, jnp.clip(line_at, 0, group - 1))[None, :] == jnp.arange(buckets)[:, None]).astype(F32)
    line = jnp.einsum("bh,bj->hj", bias_table, line_hot, precision=HIGHEST)
    line = line[:, ::-1]
    wide = group + rows
    tiled = jnp.broadcast_to(line[:, None, :], (HEADS, rows, wide)).reshape(HEADS, rows * wide)
    skew = tiled[:, rows : rows + rows * (wide - 1)].reshape(HEADS, rows, wide - 1)[:, :, :group]

    normed1_all = norm_apply(x_all.astype(F32), gains[0]).astype(BF)
    normed1 = norm_apply(x_rows, gains[0]).astype(BF)
    query = times(normed1, w_in[0]).astype(BF)
    keys = times(normed1_all, w_in[1]).astype(BF)
    values = times(normed1_all, w_in[2]).astype(BF)
    mem_keys = times(m_all, w_in[4]).astype(BF)
    mem_values = times(m_all, w_in[5]).astype(BF)
    mixed, chances_self = attend(query, keys, values, causal, skew[None], packs)
    hidden1 = x_rows + times(mixed, w_out[0])
    normed2 = norm_apply(hidden1, gains[1]).astype(BF)
    cross_query = times(normed2, w_in[3]).astype(BF)
    cross_mixed, chances_cross = attend(cross_query, mem_keys, mem_values, same, 0.0, packs)
    hidden2 = hidden1 + times(cross_mixed, w_out[1])
    normed3 = norm_apply(hidden2, gains[2]).astype(BF)

    routing = jax.nn.softmax(times(normed3, router), axis=1)
    route = routes[:, 0, 0, :, 0]
    route_hot = (route[:, :, None] == jnp.arange(experts, dtype=jnp.int32)).astype(jnp.int32)
    slot = jnp.sum((jnp.cumsum(route_hot, axis=1) - route_hot) * route_hot, axis=2)
    hot = route_hot.reshape(packs * rows, experts).astype(F32)
    gate = jnp.sum(routing * hot, axis=1)
    target = jnp.where(slot < capacity, (route * packs + jnp.arange(packs)[:, None]) * capacity + slot, -1).reshape(-1)
    dispatch = (target[:, None] == jnp.arange(experts * packs * capacity, dtype=jnp.int32)).astype(BF)

    def swap(a):
        shape = (experts, packs * capacity, width)
        return lax.all_to_all(a.reshape(shape), "expert", split_axis=0, concat_axis=0, tiled=True).reshape(-1, width)

    received = swap(times_left(dispatch, normed3).astype(BF))
    inner = times(received, e_in)
    hidden, pull = jax.vjp(gelu_tanh, inner)
    hidden = hidden.astype(BF)
    result = times(hidden, e_out).astype(BF)
    combined = times(dispatch, swap(result))
    out_rows = (hidden2 + gate[:, None] * combined).astype(BF)
    grad_top = cotangent.reshape(packs * rows, width).astype(F32)
    grad_gate = jnp.sum(grad_top * combined, axis=1)
    grad_result = swap(times_left(dispatch, (gate[:, None] * grad_top).astype(BF)).astype(BF))
    grad_hidden = times_right(grad_result, e_out)
    grad_eout = times_left(hidden, grad_result).astype(BF)
    grad_inner = pull(grad_hidden)[0].astype(BF)
    grad_ein = times_left(received, grad_inner).astype(BF)
    grad_send = swap(times_right(grad_inner, e_in).astype(BF))
    grad_logits = grad_gate[:, None] * routing * (hot - gate[:, None])
    grad_router = jnp.einsum("td,te->de", normed3.astype(F32), grad_logits, precision=HIGHEST)
    grad_normed3 = times(dispatch, grad_send) + jnp.einsum(
        "te,de->td", grad_logits, router.astype(F32), precision=HIGHEST
    )
    back3, gain3 = norm_back(hidden2, gains[2], grad_normed3)
    grad_h2 = grad_top + back3
    grad_h2_low = grad_h2.astype(BF)
    grad_wco = times_left(cross_mixed, grad_h2_low)
    grad_cross = times_right(grad_h2_low, w_out[1]).astype(BF)
    grad_cq, grad_ck, grad_cv, _ = attend_back(cross_query, mem_keys, mem_values, chances_cross, grad_cross, packs)
    back2, gain2 = norm_back(hidden1, gains[1], times_right(grad_cq, w_in[3]))
    grad_h1 = grad_h2 + back2
    grad_h1_low = grad_h1.astype(BF)
    grad_wso = times_left(mixed, grad_h1_low)
    grad_mixed = times_right(grad_h1_low, w_out[0]).astype(BF)
    grad_q, grad_k, grad_v, grad_scores = attend_back(query, keys, values, chances_self, grad_mixed, packs)

    total = jnp.sum(grad_scores.astype(F32), axis=0)[:, ::-1]
    padded = jnp.pad(total, ((0, 0), (0, 0), (0, wide - group))).reshape(HEADS, rows * wide)
    diagonal = padded[:, : rows * (wide - 1)].reshape(HEADS, rows, wide - 1).sum(axis=1)
    at = jnp.clip(rank * rows + (rows - 1) - jnp.arange(wide - 1, dtype=jnp.int32), 0, group - 1)
    diagonal_hot = (jnp.take(rel_buckets, at)[:, None] == jnp.arange(buckets)).astype(F32)
    grad_table = jnp.einsum("jb,hj->bh", diagonal_hot, diagonal, precision=HIGHEST)

    def to_owner(a):
        return lax.psum_scatter(a.reshape(packs, group, width), "seq", scatter_dimension=1, tiled=True)

    grad_memory = to_owner((times_right(grad_ck, w_in[4]) + times_right(grad_cv, w_in[5])).astype(BF))
    part1 = to_owner((times_right(grad_k, w_in[1]) + times_right(grad_v, w_in[2])).astype(BF))
    grad_normed1 = times_right(grad_q, w_in[0]) + part1.reshape(packs * rows, width).astype(F32)
    back1, gain1 = norm_back(x_rows, gains[0], grad_normed1)
    grad_x = grad_h1 + back1
    grad_in = jnp.concatenate(
        [
            times_left(normed1, grad_q),
            times_left(normed1_all, grad_k),
            times_left(normed1_all, grad_v),
            times_left(normed2, grad_cq),
            times_left(m_all, grad_ck),
            times_left(m_all, grad_cv),
        ]
    ).astype(BF)
    grad_out = jnp.concatenate([grad_wso, grad_wco]).astype(BF)
    shards = collect(grad_in, grad_out, grad_ein, grad_eout)
    small = lax.psum((jnp.stack([gain1, gain2, gain3]), grad_table, grad_router), ("dp", "seq", "expert"))
    shape = (packs, 1, 1, rows, width)
    return (
        out_rows.reshape(shape),
        grad_x.reshape(shape),
        grad_memory.astype(F32).reshape(shape),
        *small,
        shards[0],
        shards[1],
        shards[2][None],
        shards[3][None],
    )


def solution(mesh):
    tokens = P(None, "dp", "expert", "seq", None)
    dense = P(("dp", "seq", "expert"), None)
    expert = P("expert", ("dp", "seq"), None)
    return jax.shard_map(
        per_device,
        mesh=mesh,
        in_specs=(tokens, tokens, tokens, tokens, P(None, "dp", "expert", None), P(), P(), P(), P(),
                  dense, dense, expert, expert),
        out_specs=(tokens, tokens, tokens, P(), P(), P(), dense, dense, expert, expert),
        check_vma=False,
    )
```

```python
import functools

import jax
import jax.numpy as jnp
from jax import lax
from jax.experimental import pallas as pl
from jax.experimental.pallas import tpu as pltpu
from jax.sharding import PartitionSpec as P

HEADS = 12
HEAD = 64

EPS = 1e-06
NEG = -1e30
HIGHEST = lax.Precision.HIGHEST
MESH = pl.DeviceIdType.MESH
BF = jnp.bfloat16
F32 = jnp.float32


class Place:
    def __init__(self):
        self.nz, self.ns, self.ny = (lax.axis_size(a) for a in ("dp", "seq", "expert"))
        self.nx = self.ns // 2
        self.z, self.s, self.y = (lax.axis_index(a) for a in ("dp", "seq", "expert"))
        self.x, self.c = self.s // 2, lax.rem(self.s, 2)

    def device(self, z=None, x=None, c=None, y=None):
        z = self.z if z is None else z
        x = self.x if x is None else x
        c = self.c if c is None else c
        y = self.y if y is None else y
        return (z, x * 2 + c, y)

    def other_x(self):
        return [lax.rem(self.x + k, self.nx) for k in range(1, self.nx)]

    def other_y(self):
        return [lax.rem(self.y + k, self.ny) for k in range(1, self.ny)]

    def by_distance(self, k):
        order = [sorted(range(self.nz), key=lambda d: (abs(d - z), d)) for z in range(self.nz)]
        return self.pick([row[k] for row in order])

    def pick(self, values):
        out = jnp.int32(values[0])
        for z in range(1, self.nz):
            out = jnp.where(self.z == z, jnp.int32(values[z]), out)
        return out

    def greet(self):
        barrier = pltpu.get_barrier_semaphore()
        for x in self.other_x():
            pl.semaphore_signal(barrier, inc=1, device_id=self.device(x=x), device_id_type=MESH)
        for y in self.other_y():
            pl.semaphore_signal(barrier, inc=1, device_id=self.device(y=y), device_id_type=MESH)
        pl.semaphore_signal(barrier, inc=1, device_id=self.device(c=1 - self.c), device_id_type=MESH)

        for k in range(1, self.nz):
            z = lax.rem(self.z + k, self.nz)
            pl.semaphore_signal(barrier, inc=1, device_id=self.device(z=z), device_id_type=MESH)
        pl.semaphore_wait(barrier, self.nx - 1 + self.ny - 1 + 1 + self.nz - 1)


def rms_rows(src, gain, dst, rows, step=64):
    @pl.loop(0, rows // step)
    def _(i):
        at = pl.ds(pl.multiple_of(i * step, step), step)
        value = src[at, :].astype(F32)
        r = lax.rsqrt(jnp.mean(value * value, axis=-1, keepdims=True) + EPS)
        dst[at, :] = (value * r * gain).astype(BF)


def project(left, weight, base, dst):
    width = dst.shape[-1]
    step = 256 if width % 256 == 0 else width

    @pl.loop(0, width // step)
    def _(j):
        at = pl.ds(pl.multiple_of(j * step, step), step)
        out = jnp.dot(left[...], weight[pl.ds(base, width), at], preferred_element_type=F32)
        dst[:, at] = out.astype(dst.dtype)


def prepare_bias(rel, table, bias, rank, rows, group):
    buckets, heads = table.shape
    wide = group + 128
    lane = lax.broadcasted_iota(jnp.int32, (group, wide), 1)
    shift = jnp.where(lane < group, lane, lane - wide)
    distance = jnp.clip(rank * rows - shift, 0, group - 1)
    hot = (lax.broadcasted_iota(jnp.int32, (group, wide), 0) == distance).astype(F32).astype(BF)
    which = jnp.dot(jnp.broadcast_to(rel[...].astype(F32), (8, group)).astype(BF), hot, preferred_element_type=F32)
    picks = (lax.broadcasted_iota(jnp.int32, (buckets, wide), 0) == which[0:1].astype(jnp.int32)).astype(F32)
    line = lax.dot_general(table[...], picks, (((0,), (0,)), ((), ())), precision=HIGHEST, preferred_element_type=F32)
    for h in range(heads):
        band = pltpu.roll(jnp.broadcast_to(line[h : h + 1], (rows, wide)), 0, 1, stride=1, stride_axis=0)
        bias[h // 2, pl.ds((h % 2) * rows, rows), :] = band[:, :group]


def prepare_masks(lengths, same, causal, rank, rows, group):
    key = lax.broadcasted_iota(jnp.int32, (rows, group), 1)
    query = rank * rows + lax.broadcasted_iota(jnp.int32, (rows, group), 0)
    for p in range(same.shape[0]):
        end = jnp.int32(0)
        kd = jnp.zeros((rows, group), jnp.int32)
        qd = jnp.zeros((rows, group), jnp.int32)
        for n in range(lengths.shape[1]):
            end = end + lengths[p, n]
            kd = kd + jnp.where(key >= end, 1, 0)
            qd = qd + jnp.where(query >= end, 1, 0)
        same[p] = jnp.where(kd == qd, 0.0, NEG)
        causal[p] = jnp.where((kd == qd) & (key <= query), 0.0, NEG)


def two_heads(pair):
    first = lax.broadcasted_iota(jnp.int32, pair.shape, 1) < HEAD
    zero = jnp.zeros_like(pair)
    return jnp.concatenate([jnp.where(first, pair, zero), jnp.where(first, zero, pair)], axis=0)


def one_pair(stacked):
    rows = stacked.shape[0] // 2
    first = lax.broadcasted_iota(jnp.int32, (rows, stacked.shape[1]), 1) < HEAD
    return jnp.where(first, stacked[:rows], stacked[rows:])


def attend_pairs(query, keys, values, bias, mask, chances, mixed):
    packs, pairs, double, group = chances.shape
    rows = double // 2

    def body(i, carry):
        p, j = i // pairs, lax.rem(i, pairs)
        mine = pl.ds(pl.multiple_of(p * rows, rows), rows)
        theirs = pl.ds(pl.multiple_of(p * group, group), group)
        lanes = pl.ds(pl.multiple_of(j * 128, 128), 128)
        scores = lax.dot_general(
            two_heads(query[mine, lanes]), keys[theirs, lanes], (((1,), (1,)), ((), ())), preferred_element_type=F32
        )
        scores = scores * HEAD**-0.5
        if bias is not None:
            scores = scores + bias[j]
        scores = (scores.reshape(2, rows, group) + mask[p][None]).reshape(double, group)
        raised = jnp.exp(scores - jnp.max(scores, axis=1, keepdims=True))
        weights = (raised * (1.0 / jnp.sum(raised, axis=1, keepdims=True))).astype(BF)
        chances[p, j] = weights
        out = jnp.dot(weights, values[theirs, lanes], preferred_element_type=F32)
        mixed[mine, lanes] = one_pair(out).astype(BF)
        return carry

    lax.fori_loop(0, packs * pairs, body, 0, unroll=2)


def add_product(total, left, weight, base):
    width = total.shape[-1]
    step = 256 if width % 256 == 0 else width

    @pl.loop(0, width // step)
    def _(j):
        at = pl.ds(pl.multiple_of(j * step, step), step)
        total[:, at] += jnp.dot(left[...], weight[pl.ds(base, width), at], preferred_element_type=F32)


def forward_kernel(lengths, rel, gains, table, x_ref, m_ref, ain, aout, ein, eout,
                   ain_out, aout_out, eino, eouto, xo, mo, n1_all, q, k_, v, kc, vc, pr_self, pr_cross, mixed, n2,
                   qc, cross_mixed, h1, h2, n3, n1,
                   aino, aouto, bias, same, causal,
                   act_send, act_recv, line_send, side_send, core_send, ici_recv, core_recv, own_sem):
    at = Place()
    width = x_ref.shape[-1]
    packs = x_ref.shape[0]
    group = xo.shape[1]
    nz, nx, ny = at.nz, at.nx, at.ny
    tok = x_ref.shape[1]
    shards = (ain, aout, ein, eout)
    fulls = (aino, aouto, eino, eouto)
    acts = ((x_ref, xo), (m_ref, mo))
    dense, expert = (0, 1), (2, 3)

    def spot(a, z, x, c, y):
        s = x * 2 + c
        rows = shards[a].shape[0]
        index = (z * at.ns + s) * ny + y if a in dense else z * at.ns + s
        return fulls[a].at[pl.ds(pl.multiple_of(index * rows, 16), rows)]

    waits, own_acts, own_dense = [], [], []

    def send(src, dst, ssem, rsem, **where):
        copy = pltpu.make_async_remote_copy(
            src_ref=src, dst_ref=dst, send_sem=ssem, recv_sem=rsem,
            device_id=at.device(**where), device_id_type=MESH,
        )
        copy.start()
        waits.append(copy.wait_send)

    def arrive(ref, sem):
        pltpu.make_async_copy(ref, ref, sem).wait()

    at.greet()
    for i, (src, full) in enumerate(acts):
        dst = full.at[:, pl.ds(pl.multiple_of(at.s * tok, 16), tok)]
        for k, x in enumerate(at.other_x()):
            send(src, dst, act_send.at[i, k], act_recv.at[i, at.x, at.c], x=x)
        send(src, dst, act_send.at[i, nx - 1 + at.x], act_recv.at[i, at.x, at.c], c=1 - at.c)
        own = pltpu.make_async_copy(src, dst, own_sem.at[4 + i])
        own.start()
        own_acts.append(own.wait)

    def along_line(a, z, src):
        dst = spot(a, z, at.x, at.c, at.y)
        sem = ici_recv.at[a, z, at.x, at.y]

        def one(side, to):
            return pltpu.make_async_remote_copy(
                src_ref=src, dst_ref=dst, send_sem=line_send.at[a, z, side], recv_sem=sem,
                device_id=at.device(z=to), device_id_type=MESH,
            )

        left = (z >= at.z) & (at.z > 0)
        right = (z <= at.z) & (at.z < nz - 1)

        @pl.when(left)
        def _():
            one(0, at.z - 1).start()

        @pl.when(right)
        def _():
            one(1, at.z + 1).start()

        def wait():
            @pl.when(left)
            def _():
                one(0, at.z - 1).wait_send()

            @pl.when(right)
            def _():
                one(1, at.z + 1).wait_send()

        waits.append(wait)

    def to_sides(a, z, src):
        dst = spot(a, z, at.x, at.c, at.y)
        for k, x in enumerate(at.other_x()):
            send(src, dst, side_send.at[a, z, k], ici_recv.at[a, z, at.x, at.y], x=x)
        if a in dense:
            for k, y in enumerate(at.other_y()):
                send(src, dst, side_send.at[a, z, nx - 1 + k], ici_recv.at[a, z, at.x, at.y], y=y)

    def to_core(a, z, x, y, src):
        send(src, spot(a, z, x, at.c, y), core_send.at[a, z, x, y], core_recv.at[a, z, x, y], c=1 - at.c)

    zs = [at.by_distance(k) for k in range(nz)]
    for kind in (dense, expert):
        for a in kind:
            along_line(a, at.z, shards[a])
    for k in range(nz):
        for a in dense:
            here = spot(a, zs[k], at.x, at.c, at.y)
            if k:
                arrive(here, ici_recv.at[a, zs[k], at.x, at.y])
                along_line(a, zs[k], here)
            else:
                own = pltpu.make_async_copy(shards[a], here, own_sem.at[a])
                own.start()
                own_dense.append(own.wait)
            to_sides(a, zs[k], here if k else shards[a])
            to_core(a, zs[k], at.x, at.y, here if k else shards[a])
        if k == 0:
            for i, (src, full) in enumerate(acts):
                for j, x in enumerate(at.other_x()):
                    dst = full.at[:, pl.ds(pl.multiple_of((x * 2 + at.c) * tok, 16), tok)]
                    arrive(dst, act_recv.at[i, x, at.c])
                    send(dst, dst, act_send.at[i, nx - 1 + x], act_recv.at[i, x, at.c], c=1 - at.c)
    for k in range(nz):
        for a in expert:
            here = spot(a, zs[k], at.x, at.c, at.y)
            if k:
                arrive(here, ici_recv.at[a, zs[k], at.x, at.y])
                along_line(a, zs[k], here)
            else:
                own = pltpu.make_async_copy(shards[a], here, own_sem.at[a])
                own.start()
                waits.append(own.wait)
            to_sides(a, zs[k], here if k else shards[a])
            to_core(a, zs[k], at.x, at.y, here if k else shards[a])
        for a in dense:
            for x in at.other_x():
                here = spot(a, zs[k], x, at.c, at.y)
                arrive(here, ici_recv.at[a, zs[k], x, at.y])
                for j, y in enumerate(at.other_y()):
                    send(here, here, side_send.at[a, zs[k], nx - 1 + ny - 1 + j + (ny - 1) * x],
                         ici_recv.at[a, zs[k], x, at.y], y=y)
                to_core(a, zs[k], x, at.y, here)
    prepare_bias(rel, table, bias, at.s, tok, group)
    prepare_masks(lengths, same, causal, at.s, tok, group)
    for i, (src, full) in enumerate(acts):
        for x in range(nx):
            dst = full.at[:, pl.ds(pl.multiple_of((x * 2 + 1 - at.c) * tok, 16), tok)]
            arrive(dst, act_recv.at[i, x, 1 - at.c])
    own_acts[0]()
    own_acts[1]()
    for p in range(packs):
        rms_rows(xo.at[p], gains[0:1], n1_all.at[pl.ds(p * group, group)], group)
        h1[pl.ds(p * tok, tok), :] = x_ref[p].astype(F32)
        n1[pl.ds(p * tok, tok), :] = n1_all[pl.ds(pl.multiple_of(p * group + at.s * tok, tok), tok), :]
    for k in range(nz):
        for a in dense:
            for y in at.other_y():
                for x in range(nx):
                    here = spot(a, zs[k], x, at.c, y)
                    arrive(here, ici_recv.at[a, zs[k], x, y])
                    to_core(a, zs[k], x, y, here)
    for a in dense:
        for z in range(nz):
            for x in range(nx):
                for y in range(ny):
                    arrive(spot(a, z, x, 1 - at.c, y), core_recv.at[a, z, x, y])
    for wait in own_dense:
        wait()
    keep = [pltpu.make_async_copy(aino, ain_out, own_sem.at[6]), pltpu.make_async_copy(aouto, aout_out, own_sem.at[7])]
    for copy in keep:
        copy.start()

    project(n1, aino, 0, q)
    project(n1_all, aino, width, k_)
    project(n1_all, aino, 2 * width, v)
    for p in range(packs):
        project(mo.at[p], aino, 4 * width, kc.at[pl.ds(p * group, group)])
        project(mo.at[p], aino, 5 * width, vc.at[pl.ds(p * group, group)])
    attend_pairs(q, k_, v, bias, causal, pr_self, mixed)
    add_product(h1, mixed, aouto, 0)
    rms_rows(h1, gains[1:2], n2, packs * tok)
    project(n2, aino, 3 * width, qc)
    attend_pairs(qc, kc, vc, None, same, pr_cross, cross_mixed)
    h2[...] = h1[...]
    add_product(h2, cross_mixed, aouto, width)
    rms_rows(h2, gains[2:3], n3, packs * tok)

    for k in range(nz):
        for a in expert:
            for x in at.other_x():
                here = spot(a, zs[k], x, at.c, at.y)
                arrive(here, ici_recv.at[a, zs[k], x, at.y])
                to_core(a, zs[k], x, at.y, here)
    for a in expert:
        for z in range(nz):
            for x in range(nx):
                arrive(spot(a, z, x, 1 - at.c, at.y), core_recv.at[a, z, x, at.y])
    for copy in keep:
        copy.wait()
    for wait in waits:
        wait()


def in_tiles(*arrays):
    return all(a.shape[-2] % 16 == 0 for a in arrays)


def forward(lengths, rel, gains, table, x, m, ain, aout, ein, eout):
    nz, ns, ny = (lax.axis_size(a) for a in ("dp", "seq", "expert"))
    nx = ns // 2
    tall = nz * ns
    packs, tok, width = x.shape
    group = ns * tok
    pairs = width // 128
    any_ = pl.BlockSpec(memory_space=pl.ANY)
    vmem = pl.BlockSpec(memory_space=pltpu.VMEM)
    smem = pl.BlockSpec(memory_space=pltpu.SMEM)
    dma = pltpu.SemaphoreType.DMA
    full = [(tall * ny * ain.shape[0], width), (tall * ny * aout.shape[0], width)]
    low = lambda *shape: jax.ShapeDtypeStruct(shape, BF)
    every, mine = low(packs * group, width), low(packs * tok, width)
    chances = low(packs, pairs, 2 * tok, group)
    wide = jax.ShapeDtypeStruct((packs * tok, width), F32)
    return pl.pallas_call(
        forward_kernel,
        out_shape=[
            low(*full[0]),
            low(*full[1]),
            low(tall * ein.shape[0], ein.shape[1]),
            low(tall * eout.shape[0], width),
            low(packs, group, width),
            low(packs, group, width),
            every, mine, every, every, every, every, chances, chances, mine, mine, mine, mine, wide, wide, mine, mine,
        ],
        in_specs=[smem, *[vmem] * 5, *[any_] * 4],
        out_specs=[*[any_] * 4, *[vmem] * 18],
        scratch_shapes=[
            pltpu.VMEM(full[0], BF),
            pltpu.VMEM(full[1], BF),
            pltpu.VMEM((pairs, 2 * tok, group), F32),
            pltpu.VMEM((packs, tok, group), F32),
            pltpu.VMEM((packs, tok, group), F32),
            dma((2, 2 * nx)),
            dma((2, nx, 2)),
            dma((4, nz, 2)),
            dma((4, nz, nx - 1 + (ny - 1) * (1 + nx))),
            dma((4, nz, nx, ny)),
            dma((4, nz, nx, ny)),
            dma((4, nz, nx, ny)),
            dma((8,)),
        ],
        compiler_params=pltpu.CompilerParams(
            collective_id=0, has_side_effects=True, vmem_limit_bytes=60 * 2**20
        ),
        name="forward",
    )(lengths, rel.reshape(1, -1), gains, table, x, m, ain, aout, ein, eout)


def add_into(total, other):
    lead = total.shape[:-2]
    count = 1
    for n in lead:
        count *= n
    rows = total.shape[-2]
    step = next(n for n in ((48, 32, 16) if total.shape[-1] <= 1024 else (16,)) if rows % n == 0)

    def body(i, carry):
        index = []
        rest = i // (rows // step)
        for n in reversed(lead):
            index.insert(0, lax.rem(rest, n))
            rest = rest // n
        r = pl.ds(pl.multiple_of(lax.rem(i, rows // step) * step, 16), step)
        at = (*index, r)
        total[at] = (total[at].astype(F32) + other[at].astype(F32)).astype(total.dtype)
        return carry

    lax.fori_loop(0, count * (rows // step), body, 0)


def product_t(left, weight, base, dst, add=False):
    width = weight.shape[-1]
    step = 256 if width % 256 == 0 else width
    shape = dst.shape[:-1]

    @pl.loop(0, width // step)
    def _(j):
        at = pl.ds(pl.multiple_of(j * step, step), step)
        rows = weight[pl.ds(pl.multiple_of(base + j * step, step), step), :]
        out = lax.dot_general(left[...], rows, (((1,), (1,)), ((), ())), preferred_element_type=F32)
        out = out.reshape(*shape, step)
        where = (*[slice(None)] * len(shape), at)
        if add:
            out = out + dst[where].astype(F32)
        dst[where] = out.astype(dst.dtype)


def two_products_t(left1, base1, left2, base2, weight, dst):
    width = weight.shape[-1]
    step = 256 if width % 256 == 0 else width
    shape = dst.shape[:-1]

    @pl.loop(0, width // step)
    def _(j):
        at = pl.ds(pl.multiple_of(j * step, step), step)
        out = 0.0
        for left, base in ((left1, base1), (left2, base2)):
            rows = weight[pl.ds(pl.multiple_of(base + j * step, step), step), :]
            out = out + lax.dot_general(left[...], rows, (((1,), (1,)), ((), ())), preferred_element_type=F32)
        dst[(*[slice(None)] * len(shape), at)] = out.reshape(*shape, step).astype(dst.dtype)


def outer_product(left, right, dst, base):
    width = dst.shape[-1]
    step = 256 if width % 256 == 0 else width

    @pl.loop(0, width // step)
    def _(j):
        at = pl.ds(pl.multiple_of(j * step, step), step)
        out = lax.dot_general(left[:, at], right[...], (((0,), (0,)), ((), ())), preferred_element_type=F32)
        dst[pl.ds(pl.multiple_of(base + j * step, step), step), :] = out.astype(dst.dtype)


def norm_back_rows(value, gain, grad, total, gain_grad, step=64):
    gain_grad[...] = jnp.zeros_like(gain_grad)

    @pl.loop(0, value.shape[0] // step)
    def _(i):
        at = pl.ds(pl.multiple_of(i * step, step), step)
        v, g = value[at, :].astype(F32), grad[at, :]
        r = lax.rsqrt(jnp.mean(v * v, axis=-1, keepdims=True) + EPS)
        scaled = g * gain
        total[at, :] += r * scaled - v * (r * r * r) * jnp.mean(scaled * v, axis=-1, keepdims=True)
        gain_grad[...] += jnp.sum(g * v * r, axis=0, keepdims=True)


def attend_pairs_back(query, keys, values, chances, grad, grad_q, grad_k, grad_v, diagonal):
    packs, pairs, double, group = chances.shape
    rows = double // 2
    scale = HEAD**-0.5

    def body(i, carry):
        p, j = i // pairs, lax.rem(i, pairs)
        mine = pl.ds(pl.multiple_of(p * rows, rows), rows)
        theirs = pl.ds(pl.multiple_of(p * group, group), group)
        lanes = pl.ds(pl.multiple_of(j * 128, 128), 128)
        ga = two_heads(grad[mine, lanes])
        low = chances[p, j]
        wide = low.astype(F32)
        gp = lax.dot_general(ga, values[theirs, lanes], (((1,), (1,)), ((), ())), preferred_element_type=F32)
        gs = (wide * (gp - jnp.sum(wide * gp, axis=1, keepdims=True))).astype(BF)
        gq = jnp.dot(gs, keys[theirs, lanes], preferred_element_type=F32)
        grad_q[mine, lanes] = (one_pair(gq) * scale).astype(BF)
        gk = lax.dot_general(gs, two_heads(query[mine, lanes]), (((0,), (0,)), ((), ())), preferred_element_type=F32)
        grad_k[theirs, lanes] = (gk * scale).astype(BF)
        gv = lax.dot_general(low, ga, (((0,), (0,)), ((), ())), preferred_element_type=F32)
        grad_v[theirs, lanes] = gv.astype(BF)
        if diagonal is not None:
            a = lax.broadcasted_iota(jnp.int32, (rows, rows), 0)
            b = lax.broadcasted_iota(jnp.int32, (rows, rows), 1)
            flip = (a + b == rows - 1).astype(F32).astype(BF)
            for half in range(2):
                turned = jnp.dot(flip, gs[half * rows : (half + 1) * rows], preferred_element_type=F32)
                turned = jnp.concatenate([turned, jnp.zeros((rows, 128), F32)], axis=1)
                band = pltpu.roll(turned, 0, 1, stride=1, stride_axis=0)
                diagonal[pl.ds(2 * j + half, 1), :] += jnp.sum(band, axis=0, keepdims=True)
        return carry

    lax.fori_loop(0, packs * pairs, body, 0, unroll=2)


def table_grad(rel, diagonal, rank, rows, group, buckets):
    wide = group + 128
    lane = lax.broadcasted_iota(jnp.int32, (group, wide), 1)
    distance = jnp.clip(rank * rows + rows - 1 - lane, 0, group - 1)
    hot = (lax.broadcasted_iota(jnp.int32, (group, wide), 0) == distance).astype(F32).astype(BF)
    which = jnp.dot(jnp.broadcast_to(rel[...].astype(F32), (8, group)).astype(BF), hot, preferred_element_type=F32)
    picks = (lax.broadcasted_iota(jnp.int32, (buckets, wide), 0) == which[0:1].astype(jnp.int32)).astype(F32)
    return lax.dot_general(picks, diagonal[...], (((1,), (1,)), ((), ())), precision=HIGHEST, preferred_element_type=F32)


def backward_kernel(rel, gains, x_rows, win_hbm, wout_hbm, gein_hbm, geout_hbm, m_all, n1_all, n1, q, k_, v, kc, vc,
                    pr_self, pr_cross, mixed, n2, qc, cross_mixed, h1, gh2, gain3, grouter,
                    o0, o1, o2, o3, grad_x, grad_mem, sum_wide, sum_table,
                    win, wout, gin, gout, own2, own3, c0, c1, c2, c3, y0, y1, x0, x1, x2, x3, z0, z1, z2, z3,
                    gb, ga, gq, gk, gv, gn, diagonal, gain_row, act_part, act_core, act_x, wide_sum, table_sum,
                    wide_in, table_in,
                    load_sem, core_send, core_recv, y_send, y_recv, x_send, x_recv, z_send, z_recv,
                    act_send, act_recv, small_send, small_recv):
    at = Place()
    nz, nx, ny = at.nz, at.nx, at.ny
    packs, group = act_part.shape[1], m_all.shape[0] // act_part.shape[1]
    tok, width = act_part.shape[4], m_all.shape[1]
    buckets = table_sum.shape[1]
    outs = (o0, o1, o2, o3)
    cores, ys, xs, zs_ = (c0, c1, c2, c3), (y0, y1), (x0, x1, x2, x3), (z0, z1, z2, z3)
    dense, expert = (0, 1), (2, 3)
    waits = []

    def copy(src, dst, ssem, rsem, **where):
        return pltpu.make_async_remote_copy(
            src_ref=src, dst_ref=dst, send_sem=ssem, recv_sem=rsem,
            device_id=at.device(**where), device_id_type=MESH,
        )

    def send(*args, **where):
        one = copy(*args, **where)
        one.start()
        waits.append(one.wait_send)

    def arrive(ref, sem):
        pltpu.make_async_copy(ref, ref, sem).wait()

    at.greet()

    far = [[d for d in sorted(range(nz), key=lambda d: (-abs(d - z), d))] for z in range(nz)]
    order_e = [at.pick([far[z][k] for z in range(nz)]) for k in range(nz)]
    halves = [[d for d in row if d >= nz // 2] + [d for d in row if d < nz // 2] for row in far]
    order_d = [at.pick([halves[z][k] for z in range(nz)]) for k in range(nz)]

    loads = [
        pltpu.make_async_copy(gein_hbm.at[:, :, at.c], own2, load_sem.at[0]),
        pltpu.make_async_copy(geout_hbm.at[:, :, at.c], own3, load_sem.at[1]),
        pltpu.make_async_copy(wout_hbm, wout, load_sem.at[2]),
        pltpu.make_async_copy(win_hbm, win, load_sem.at[3]),
    ]
    for k in range(nz):
        for a, src in ((2, gein_hbm), (3, geout_hbm)):
            send(src.at[order_e[k], :, 1 - at.c], cores[a].at[k], core_send.at[a, k, 0], core_recv.at[a, k, 0], c=1 - at.c)
        if k == 0:
            for load in loads:
                load.start()


    def core_expert(k):
        for a, own in ((2, own2), (3, own3)):
            arrive(cores[a].at[k], core_recv.at[a, k, 0])
            add_into(cores[a].at[k], own.at[order_e[k]])
            for j, x in enumerate(at.other_x()):
                send(cores[a].at[k, x], xs[a].at[k, nx - 2 - j], x_send.at[a, k, j], x_recv.at[a, k, nx - 2 - j], x=x)

    def dense_rows(a, d, x, c):
        rows = cores[a].shape[2]
        return (gin, gout)[a].at[pl.ds(pl.multiple_of(((d * nx + x) * 2 + c) * rows, 16), rows)]

    def start_dense(k):
        for a in dense:
            for x in range(nx):
                send(dense_rows(a, order_d[k], x, 1 - at.c), cores[a].at[k, x], core_send.at[a, k, x],
                     core_recv.at[a, k, x], c=1 - at.c)

    def core_dense(k):
        for a in dense:
            rows = ys[a].shape[3]
            for x in range(nx):
                arrive(cores[a].at[k, x], core_recv.at[a, k, x])
                add_into(cores[a].at[k, x], dense_rows(a, order_d[k], x, at.c))
            for j, y in enumerate(at.other_y()):
                send(cores[a].at[k, :, pl.ds(pl.multiple_of(y * rows, 16), rows)], ys[a].at[k, ny - 2 - j],
                     y_send.at[a, k, j], y_recv.at[a, k, ny - 2 - j], y=y)

    def y_dense(k):
        for a in dense:
            rows = ys[a].shape[3]
            for j in range(ny - 1):
                arrive(ys[a].at[k, j], y_recv.at[a, k, j])
                own = cores[a].at[k, :, pl.ds(pl.multiple_of(at.y * rows, 16), rows)]
                add_into(ys[a].at[k, 0], ys[a].at[k, j] if j else own)
            for j, x in enumerate(at.other_x()):
                send(ys[a].at[k, 0, x], xs[a].at[k, nx - 2 - j], x_send.at[a, k, j], x_recv.at[a, k, nx - 2 - j], x=x)

    def x_and_line(kind, k):
        d = (order_e if kind is expert else order_d)[k]
        for a in kind:
            total = xs[a].at[k, 0]
            for j in range(nx - 1):
                arrive(xs[a].at[k, j], x_recv.at[a, k, j])
                own = cores[a].at[k, at.x] if a in expert else ys[a].at[k, 0, at.x]
                add_into(total, xs[a].at[k, j] if j else own)
            for side in range(2):
                feeds = (at.z > 0) & (d >= at.z) if side == 0 else (at.z < nz - 1) & (d <= at.z)
                slot = d if side == 0 else jnp.where(d == at.z, nz, d)

                @pl.when(feeds)
                def _(a=a, slot=slot, total=total):
                    arrive(zs_[a].at[slot], z_recv.at[a, slot])
                    add_into(total, zs_[a].at[slot])

            def hop(to, a=a, total=total):
                slot = d if to > 0 else jnp.where(d == at.z - 1, nz, d)
                return copy(total, zs_[a].at[slot], z_send.at[a, k], z_recv.at[a, slot], z=at.z + to)

            @pl.when(d < at.z)
            def _():
                hop(-1).start()

            @pl.when(d > at.z)
            def _():
                hop(1).start()

            @pl.when(d == at.z)
            def _(a=a, total=total):
                outs[a][...] = total[...].astype(F32)

            def wait(hop=hop):
                @pl.when(d < at.z)
                def _():
                    hop(-1).wait_send()

                @pl.when(d > at.z)
                def _():
                    hop(1).wait_send()

            waits.append(wait)

    def start_act(w):
        send(act_part.at[w, :, :, 1 - at.c], act_core.at[w], act_send.at[w, 0], act_recv.at[w, 0], c=1 - at.c)

    def core_act(w):
        arrive(act_core.at[w], act_recv.at[w, 0])
        add_into(act_core.at[w], act_part.at[w, :, :, at.c])
        for j, x in enumerate(at.other_x()):
            send(act_core.at[w, :, x], act_x.at[w, nx - 2 - j], act_send.at[w, 1 + j], act_recv.at[w, nx - 1 - j], x=x)

    def x_act(w):
        for j in range(nx - 1):
            arrive(act_x.at[w, j], act_recv.at[w, 1 + j])
        for p in range(packs):
            out = act_core[w, p, at.x].astype(F32)
            for j in range(nx - 1):
                out = out + act_x[w, j, p].astype(F32)
            if w == 0:
                grad_mem[pl.ds(p * tok, tok), :] = out
            else:
                gn[pl.ds(p * tok, tok), :] += out

    pair_sums = ((wide_sum, wide_in), (table_sum, table_in))
    stages = [("c", [1 - at.c]), ("y", at.other_y()), ("x", at.other_x())]

    def start_small(t):
        axis, peers = stages[t]
        for i, (total, inbox) in enumerate(pair_sums):
            for j, peer in enumerate(peers):
                back = len(peers) - 1 - j
                base = [0, 1, ny][t]
                send(total.at[t], inbox.at[base + back], small_send.at[i, base + j], small_recv.at[i, base + back], **{axis: peer})

    def end_small(t):
        axis, peers = stages[t]
        base = [0, 1, ny][t]
        for i, (total, inbox) in enumerate(pair_sums):
            out = total[t]
            for j in range(len(peers)):
                arrive(inbox.at[base + j], small_recv.at[i, base + j])
                out = out + inbox[base + j]
            total[t + 1] = out

    tail = ny + nx - 1

    def start_line():
        for i, (total, inbox) in enumerate(pair_sums):
            for j in range(1, nz):
                z = lax.rem(at.z + j, nz)
                send(total.at[3], inbox.at[tail + at.z], small_send.at[i, tail + j], small_recv.at[i, tail + at.z], z=z)

    def end_line():
        for i, (total, inbox) in enumerate(pair_sums):
            for j in range(1, nz):
                z = lax.rem(at.z + j, nz)
                arrive(inbox.at[tail + z], small_recv.at[i, tail + z])
            out = None
            for z in range(nz):
                term = jnp.where(at.z == z, total[3], inbox[tail + z])
                out = term if out is None else out + term
            (sum_wide, sum_table)[i][...] = out

    diagonal[...] = jnp.zeros_like(diagonal)
    for i, (_, inbox) in enumerate(pair_sums):
        inbox[pl.ds(tail + at.z, 1)] = jnp.zeros_like(inbox[pl.ds(0, 1)])
    wide_sum[0] = jnp.zeros_like(wide_sum[0])
    wide_sum[0, 2:3, :] = gain3[...]
    wide_sum[0, pl.ds(3, grouter.shape[0]), :] = grouter[...]
    gb[...] = gh2[...].astype(BF)
    loads[0].wait()
    loads[1].wait()
    core_expert(0)
    loads[2].wait()
    product_t(gb, wout, width, ga)
    outer_product(cross_mixed, gb, gout, width)
    core_expert(1)
    attend_pairs_back(qc, kc, vc, pr_cross, ga, gq, gk, gv, None)
    core_expert(2)
    loads[3].wait()
    outer_product(n2, gq, gin, 3 * width)
    outer_product(m_all, gk, gin, 4 * width)
    outer_product(m_all, gv, gin, 5 * width)
    core_expert(3)
    for k in range(nz // 2):
        start_dense(k)
    two_products_t(gk, 4 * width, gv, 5 * width, win, act_part.at[0])
    start_act(0)
    x_and_line(expert, 0)
    product_t(gq, win, 3 * width, gn)
    grad_x[...] = gh2[...]
    norm_back_rows(h1, gains[1:2], gn, grad_x, gain_row)
    wide_sum[0, 1:2, :] = gain_row[...]
    gb[...] = grad_x[...].astype(BF)
    product_t(gb, wout, 0, ga)
    core_dense(0)
    outer_product(mixed, gb, gout, 0)
    core_act(0)
    core_dense(1)
    x_and_line(expert, 1)
    attend_pairs_back(q, k_, v, pr_self, ga, gq, gk, gv, diagonal)
    outer_product(n1, gq, gin, 0)
    outer_product(n1_all, gk, gin, width)
    outer_product(n1_all, gv, gin, 2 * width)
    for k in range(nz // 2, nz):
        start_dense(k)
    two_products_t(gk, width, gv, 2 * width, win, act_part.at[1])
    start_act(1)
    y_dense(0)
    x_and_line(expert, 2)
    core_act(1)
    y_dense(1)
    for k in range(nz // 2, nz):
        core_dense(k)
    product_t(gq, win, 0, gn)
    table_sum[0] = table_grad(rel, diagonal, at.s, tok, group, buckets)
    x_and_line(expert, 3)
    x_act(0)
    x_and_line(dense, 0)
    x_act(1)
    norm_back_rows(x_rows, gains[0:1], gn, grad_x, gain_row)
    wide_sum[0, 0:1, :] = gain_row[...]
    start_small(0)
    y_dense(2)
    end_small(0)
    start_small(1)
    x_and_line(dense, 1)
    end_small(1)
    start_small(2)
    y_dense(3)
    end_small(2)
    start_line()
    x_and_line(dense, 2)
    end_line()
    x_and_line(dense, 3)
    for wait in waits:
        wait()


def backward(rel, gains, x_rows, w_in, w_out, gein, geout, acts, heads, buckets):
    nz, ns, ny = (lax.axis_size(a) for a in ("dp", "seq", "expert"))
    nx = ns // 2
    width = gains.shape[1]
    m_all, q, pr = acts[0], acts[3], acts[8]
    packs, group = pr.shape[0], pr.shape[3]
    tok = group // ns
    extra = -(-(3 + acts[-1].shape[0]) // 8) * 8
    ends = [
        (w_in.shape[0] // (nz * ns * ny), width),
        (w_out.shape[0] // (nz * ns * ny), width),
        (gein.shape[0] // (nz * ns), gein.shape[1]),
        (geout.shape[0] // (nz * ns), width),
    ]
    any_ = pl.BlockSpec(memory_space=pl.ANY)
    vmem = pl.BlockSpec(memory_space=pltpu.VMEM)
    dma = pltpu.SemaphoreType.DMA
    low = lambda *shape: pltpu.VMEM(shape, BF)
    wide = lambda *shape: pltpu.VMEM(shape, F32)
    small = 1 + ny - 1 + nx - 1 + nz
    return pl.pallas_call(
        backward_kernel,
        out_shape=[
            *[jax.ShapeDtypeStruct(e, F32) for e in ends],
            jax.ShapeDtypeStruct((packs * tok, width), F32),
            jax.ShapeDtypeStruct((packs * tok, width), F32),
            jax.ShapeDtypeStruct((extra, width), F32),
            jax.ShapeDtypeStruct((buckets, 128), F32),
        ],
        in_specs=[*[vmem] * 3, *[any_] * 4, *[vmem] * len(acts)],
        out_specs=[vmem] * 8,
        scratch_shapes=[
            low(*w_in.shape),
            low(*w_out.shape),
            low(*w_in.shape),
            low(*w_out.shape),
            *[low(nz, nx, *e) for e in ends[2:]],
            *[low(nz, nx, ny * e[0], e[1]) for e in ends[:2]],
            *[low(nz, nx, *e) for e in ends[2:]],
            *[low(nz, ny - 1, nx, *e) for e in ends[:2]],
            *[low(nz, nx - 1, *e) for e in ends],
            *[low(nz + 1, *e) for e in ends],
            low(packs * tok, width),
            low(packs * tok, width),
            low(packs * tok, width),
            low(packs * group, width),
            low(packs * group, width),
            wide(packs * tok, width),
            wide(128, group + 128),
            wide(1, width),
            low(2, packs, nx, 2, tok, width),
            low(2, packs, nx, tok, width),
            low(2, nx - 1, packs, tok, width),
            wide(4, extra, width),
            wide(4, buckets, 128),
            wide(small, extra, width),
            wide(small, buckets, 128),
            dma((4,)),
            dma((4, nz, nx)),
            dma((4, nz, nx)),
            dma((2, nz, ny - 1)),
            dma((2, nz, ny - 1)),
            dma((4, nz, nx - 1)),
            dma((4, nz, nx - 1)),
            dma((4, nz)),
            dma((4, nz + 1)),
            dma((2, nx)),
            dma((2, nx)),
            dma((2, small)),
            dma((2, small)),
        ],
        compiler_params=pltpu.CompilerParams(
            collective_id=1, has_side_effects=True, vmem_limit_bytes=62 * 2**20
        ),
        name="backward",
    )(
        rel.reshape(1, -1), gains, x_rows, w_in, w_out,
        gein.reshape(nz, nx, 2, *ends[2]), geout.reshape(nz, nx, 2, *ends[3]), *acts,
    )


def norm_apply(value, gain):
    return value * lax.rsqrt(jnp.mean(value * value, axis=-1, keepdims=True) + EPS) * gain


def norm_back(value, gain, grad):
    r = lax.rsqrt(jnp.mean(value * value, axis=-1, keepdims=True) + EPS)
    scaled = grad * gain
    back = r * scaled - value * (r * r * r) * jnp.mean(scaled * value, axis=-1, keepdims=True)
    return back, jnp.sum(grad * value * r, axis=0)


def gelu_tanh(value):
    return jax.nn.gelu(value, approximate=True)


def times(left, right):
    return jnp.dot(left, right, preferred_element_type=F32)


def times_right(left, right):
    return jnp.einsum("te,de->td", left, right, preferred_element_type=F32)


def times_left(left, right):
    return jnp.einsum("td,te->de", left, right, preferred_element_type=F32)


def split(a, packs):
    return a.reshape(packs, -1, HEADS, HEAD)


def attend(query, keys, values, allowed, bias, packs):
    scores = jnp.einsum("pqhd,pkhd->phqk", split(query, packs), split(keys, packs), preferred_element_type=F32)
    masked = jnp.where(allowed[:, None], scores * HEAD**-0.5 + bias, NEG)
    raised = jnp.exp(masked - jnp.max(masked, axis=3, keepdims=True))
    chances = raised / jnp.sum(raised, axis=3, keepdims=True)
    mixed = jnp.einsum("phqk,pkhd->pqhd", chances.astype(BF), split(values, packs), preferred_element_type=F32)
    return mixed.reshape(query.shape).astype(BF), chances


def attend_back(query, keys, values, chances, grad, packs):
    scale = HEAD**-0.5
    g4 = split(grad, packs)
    grad_chances = jnp.einsum("pqhd,pkhd->phqk", g4, split(values, packs), preferred_element_type=F32)
    spread_ = jnp.sum(chances * grad_chances, axis=3, keepdims=True)
    grad_scores = (chances * (grad_chances - spread_)).astype(BF)
    grad_query = jnp.einsum("phqk,pkhd->pqhd", grad_scores, split(keys, packs), preferred_element_type=F32) * scale
    grad_keys = jnp.einsum("phqk,pqhd->pkhd", grad_scores, split(query, packs), preferred_element_type=F32) * scale
    grad_values = jnp.einsum("phqk,pqhd->pkhd", chances.astype(BF), g4, preferred_element_type=F32)
    return (
        grad_query.reshape(query.shape).astype(BF),
        grad_keys.reshape(keys.shape).astype(BF),
        grad_values.reshape(keys.shape).astype(BF),
        grad_scores,
    )


def per_device(layer_input, memory, cotangent, routes, doc_lengths, rel_buckets, gains, bias_table, router,
               attn_in, attn_out, expert_in, expert_out):
    packs, rows, width = layer_input.shape[0], layer_input.shape[3], layer_input.shape[4]
    seqs = lax.axis_size("seq")
    group = rows * seqs
    experts = router.shape[1]
    capacity = (5 * rows + 4 * experts - 1) // (4 * experts)
    buckets = bias_table.shape[0]
    rank = lax.axis_index("seq")

    x_in, m_in, e_in, e_out = layer_input[:, 0, 0], memory[:, 0, 0], expert_in[0], expert_out[0]
    fits = in_tiles(x_in, attn_in, attn_out, e_in, e_out)
    x_rows = x_in.reshape(packs * rows, width).astype(F32)
    if fits:
        (
            w_in, w_out, e_in, e_out, x_all, m_all, normed1_all, query, keys, values, mem_keys, mem_values,
            chances_self, chances_cross, mixed, normed2, cross_query, cross_mixed, hidden1, hidden2, normed3, normed1,
        ) = forward(
            doc_lengths[:, 0, 0], rel_buckets, gains, bias_table, x_in, m_in, attn_in, attn_out, e_in, e_out
        )
        pairs_self, pairs_cross = chances_self, chances_cross
        chances_self, chances_cross = (a.reshape(packs, HEADS, rows, group) for a in (chances_self, chances_cross))
    else:
        everywhere, peers = ("dp", "seq", "expert"), ("dp", "seq")
        x_all, m_all = (lax.all_gather(a, "seq", axis=1, tiled=True) for a in (x_in, m_in))
        w_in, w_out = (lax.all_gather(a, everywhere, axis=0, tiled=True) for a in (attn_in, attn_out))
        e_in, e_out = (lax.all_gather(a, peers, axis=0, tiled=True) for a in (e_in, e_out))
    w_in = w_in.reshape(6, width, width)
    w_out = w_out.reshape(2, width, width)
    x_all = x_all.reshape(packs * group, width)
    m_all = m_all.reshape(packs * group, width)
    wide = group + rows
    if not fits:
        query_pos = rank * rows + jnp.arange(rows, dtype=jnp.int32)
        key_pos = jnp.arange(group, dtype=jnp.int32)
        ends = jnp.cumsum(doc_lengths[:, 0, 0], axis=1)
        query_doc = jnp.sum((query_pos[None, :, None] >= ends[:, None, :]).astype(jnp.int32), axis=2)
        key_doc = jnp.sum((key_pos[None, :, None] >= ends[:, None, :]).astype(jnp.int32), axis=2)
        same = query_doc[:, :, None] == key_doc[:, None, :]
        causal = same & (key_pos[None, None, :] <= query_pos[None, :, None])
        bucket_hot = (rel_buckets[:, None] == jnp.arange(buckets, dtype=jnp.int32)).astype(F32)
        line_at = jnp.arange(group + rows, dtype=jnp.int32) - (group - 1) + rank * rows
        line_hot = (jnp.take(rel_buckets, jnp.clip(line_at, 0, group - 1))[None, :] == jnp.arange(buckets)[:, None]).astype(F32)
        line = jnp.einsum("bh,bj->hj", bias_table, line_hot, precision=HIGHEST)
        line = line[:, ::-1]
        wide = group + rows
        tiled = jnp.broadcast_to(line[:, None, :], (HEADS, rows, wide)).reshape(HEADS, rows * wide)
        skew = tiled[:, rows : rows + rows * (wide - 1)].reshape(HEADS, rows, wide - 1)[:, :, :group]

        normed1_all = norm_apply(x_all.astype(F32), gains[0]).astype(BF)
        normed1 = norm_apply(x_rows, gains[0]).astype(BF)
        query = times(normed1, w_in[0]).astype(BF)
        keys = times(normed1_all, w_in[1]).astype(BF)
        values = times(normed1_all, w_in[2]).astype(BF)
        mem_keys = times(m_all, w_in[4]).astype(BF)
        mem_values = times(m_all, w_in[5]).astype(BF)
        mixed, chances_self = attend(query, keys, values, causal, skew[None], packs)
        hidden1 = x_rows + times(mixed, w_out[0])
        normed2 = norm_apply(hidden1, gains[1]).astype(BF)
        cross_query = times(normed2, w_in[3]).astype(BF)
        cross_mixed, chances_cross = attend(cross_query, mem_keys, mem_values, same, 0.0, packs)
        hidden2 = hidden1 + times(cross_mixed, w_out[1])
        normed3 = norm_apply(hidden2, gains[2]).astype(BF)

    routing = jax.nn.softmax(times(normed3, router), axis=1)
    route = routes[:, 0, 0, :, 0]
    route_hot = (route[:, :, None] == jnp.arange(experts, dtype=jnp.int32)).astype(jnp.int32)
    slot = jnp.sum((jnp.cumsum(route_hot, axis=1) - route_hot) * route_hot, axis=2)
    hot = route_hot.reshape(packs * rows, experts).astype(F32)
    gate = jnp.sum(routing * hot, axis=1)
    target = jnp.where(slot < capacity, (route * packs + jnp.arange(packs)[:, None]) * capacity + slot, -1).reshape(-1)
    dispatch = (target[:, None] == jnp.arange(experts * packs * capacity, dtype=jnp.int32)).astype(BF)

    def swap(a):
        shape = (experts, packs * capacity, width)
        return lax.all_to_all(a.reshape(shape), "expert", split_axis=0, concat_axis=0, tiled=True).reshape(-1, width)

    received = swap(times_left(dispatch, normed3).astype(BF))
    inner = times(received, e_in)
    hidden, pull = jax.vjp(gelu_tanh, inner)
    hidden = hidden.astype(BF)
    result = times(hidden, e_out).astype(BF)
    combined = times(dispatch, swap(result))
    out_rows = (hidden2 + gate[:, None] * combined).astype(BF)
    grad_top = cotangent.reshape(packs * rows, width).astype(F32)
    grad_gate = jnp.sum(grad_top * combined, axis=1)
    grad_result = swap(times_left(dispatch, (gate[:, None] * grad_top).astype(BF)).astype(BF))
    grad_hidden = times_right(grad_result, e_out)
    grad_eout = times_left(hidden, grad_result).astype(BF)
    grad_inner = pull(grad_hidden)[0].astype(BF)
    grad_ein = times_left(received, grad_inner).astype(BF)
    grad_send = swap(times_right(grad_inner, e_in).astype(BF))
    grad_logits = grad_gate[:, None] * routing * (hot - gate[:, None])
    grad_router = jnp.einsum("td,te->de", normed3.astype(F32), grad_logits, precision=HIGHEST)
    grad_normed3 = times(dispatch, grad_send) + jnp.einsum(
        "te,de->td", grad_logits, router.astype(F32), precision=HIGHEST
    )
    back3, gain3 = norm_back(hidden2, gains[2], grad_normed3)
    grad_h2 = grad_top + back3
    shape = (packs, 1, 1, rows, width)
    if fits:
        acts = (
            m_all, normed1_all, normed1, query, keys, values, mem_keys, mem_values, pairs_self, pairs_cross, mixed,
            normed2, cross_query, cross_mixed, hidden1, grad_h2, gain3[None], grad_router.T,
        )
        *shards, grad_x, grad_memory, sums, table = backward(
            rel_buckets, gains, x_rows, w_in.reshape(-1, width), w_out.reshape(-1, width), grad_ein, grad_eout,
            acts, HEADS, buckets,
        )
        return (
            out_rows.reshape(shape),
            grad_x.reshape(shape),
            grad_memory.reshape(shape),
            sums[:3],
            table[:, :HEADS],
            sums[3 : 3 + experts].T,
            shards[0],
            shards[1],
            shards[2][None],
            shards[3][None],
        )
    grad_h2_low = grad_h2.astype(BF)
    grad_wco = times_left(cross_mixed, grad_h2_low)
    grad_cross = times_right(grad_h2_low, w_out[1]).astype(BF)
    grad_cq, grad_ck, grad_cv, _ = attend_back(cross_query, mem_keys, mem_values, chances_cross, grad_cross, packs)
    back2, gain2 = norm_back(hidden1, gains[1], times_right(grad_cq, w_in[3]))
    grad_h1 = grad_h2 + back2
    grad_h1_low = grad_h1.astype(BF)
    grad_wso = times_left(mixed, grad_h1_low)
    grad_mixed = times_right(grad_h1_low, w_out[0]).astype(BF)
    grad_q, grad_k, grad_v, grad_scores = attend_back(query, keys, values, chances_self, grad_mixed, packs)

    total = jnp.sum(grad_scores.astype(F32), axis=0)[:, ::-1]
    padded = jnp.pad(total, ((0, 0), (0, 0), (0, wide - group))).reshape(HEADS, rows * wide)
    diagonal = padded[:, : rows * (wide - 1)].reshape(HEADS, rows, wide - 1).sum(axis=1)
    at = jnp.clip(rank * rows + (rows - 1) - jnp.arange(wide - 1, dtype=jnp.int32), 0, group - 1)
    diagonal_hot = (jnp.take(rel_buckets, at)[:, None] == jnp.arange(buckets)).astype(F32)
    grad_table = jnp.einsum("jb,hj->bh", diagonal_hot, diagonal, precision=HIGHEST)

    def to_owner(a):
        return lax.psum_scatter(a.reshape(packs, group, width), "seq", scatter_dimension=1, tiled=True)

    grad_memory = to_owner((times_right(grad_ck, w_in[4]) + times_right(grad_cv, w_in[5])).astype(BF))
    part1 = to_owner((times_right(grad_k, w_in[1]) + times_right(grad_v, w_in[2])).astype(BF))
    grad_normed1 = times_right(grad_q, w_in[0]) + part1.reshape(packs * rows, width).astype(F32)
    back1, gain1 = norm_back(x_rows, gains[0], grad_normed1)
    grad_x = grad_h1 + back1
    grad_in = jnp.concatenate(
        [
            times_left(normed1, grad_q),
            times_left(normed1_all, grad_k),
            times_left(normed1_all, grad_v),
            times_left(normed2, grad_cq),
            times_left(m_all, grad_ck),
            times_left(m_all, grad_cv),
        ]
    ).astype(BF)
    grad_out = jnp.concatenate([grad_wso, grad_wco]).astype(BF)
    shards = [
        lax.psum_scatter(a, over, scatter_dimension=0, tiled=True).astype(F32)
        for a, over in ((grad_in, everywhere), (grad_out, everywhere), (grad_ein, peers), (grad_eout, peers))
    ]
    small = lax.psum((jnp.stack([gain1, gain2, gain3]), grad_table, grad_router), ("dp", "seq", "expert"))
    shape = (packs, 1, 1, rows, width)
    return (
        out_rows.reshape(shape),
        grad_x.reshape(shape),
        grad_memory.astype(F32).reshape(shape),
        *small,
        shards[0],
        shards[1],
        shards[2][None],
        shards[3][None],
    )


def solution(mesh):
    tokens = P(None, "dp", "expert", "seq", None)
    dense = P(("dp", "seq", "expert"), None)
    expert = P("expert", ("dp", "seq"), None)
    return jax.shard_map(
        per_device,
        mesh=mesh,
        in_specs=(tokens, tokens, tokens, tokens, P(None, "dp", "expert", None), P(), P(), P(), P(),
                  dense, dense, expert, expert),
        out_specs=(tokens, tokens, tokens, P(), P(), P(), dense, dense, expert, expert),
        check_vma=False,
    )
```

```python
import functools

import jax
import jax.numpy as jnp
from jax import lax
from jax.experimental import pallas as pl
from jax.experimental.pallas import tpu as pltpu
from jax.sharding import PartitionSpec as P

HEADS = 12
HEAD = 64

EPS = 1e-06
NEG = -1e30
HIGHEST = lax.Precision.HIGHEST
MESH = pl.DeviceIdType.MESH
BF = jnp.bfloat16
F32 = jnp.float32


class Place:
    def __init__(self):
        self.nz, self.ns, self.ny = (lax.axis_size(a) for a in ("dp", "seq", "expert"))
        self.nx = self.ns // 2
        self.z, self.s, self.y = (lax.axis_index(a) for a in ("dp", "seq", "expert"))
        self.x, self.c = self.s // 2, lax.rem(self.s, 2)

    def device(self, z=None, x=None, c=None, y=None):
        z = self.z if z is None else z
        x = self.x if x is None else x
        c = self.c if c is None else c
        y = self.y if y is None else y
        return (z, x * 2 + c, y)

    def other_x(self):
        return [lax.rem(self.x + k, self.nx) for k in range(1, self.nx)]

    def other_y(self):
        return [lax.rem(self.y + k, self.ny) for k in range(1, self.ny)]

    def by_distance(self, k):
        order = [sorted(range(self.nz), key=lambda d: (abs(d - z), d)) for z in range(self.nz)]
        return self.pick([row[k] for row in order])

    def pick(self, values):
        out = jnp.int32(values[0])
        for z in range(1, self.nz):
            out = jnp.where(self.z == z, jnp.int32(values[z]), out)
        return out

    def greet(self):
        barrier = pltpu.get_barrier_semaphore()
        for x in self.other_x():
            pl.semaphore_signal(barrier, inc=1, device_id=self.device(x=x), device_id_type=MESH)
        for y in self.other_y():
            pl.semaphore_signal(barrier, inc=1, device_id=self.device(y=y), device_id_type=MESH)
        pl.semaphore_signal(barrier, inc=1, device_id=self.device(c=1 - self.c), device_id_type=MESH)

        for k in range(1, self.nz):
            z = lax.rem(self.z + k, self.nz)
            pl.semaphore_signal(barrier, inc=1, device_id=self.device(z=z), device_id_type=MESH)
        pl.semaphore_wait(barrier, self.nx - 1 + self.ny - 1 + 1 + self.nz - 1)


def rms_rows(src, gain, dst, rows, step=64):
    @pl.loop(0, rows // step)
    def _(i):
        at = pl.ds(pl.multiple_of(i * step, step), step)
        value = src[at, :].astype(F32)
        r = lax.rsqrt(jnp.mean(value * value, axis=-1, keepdims=True) + EPS)
        dst[at, :] = (value * r * gain).astype(BF)


def block(weight, index, lanes=slice(None), share=(0, 1)):
    unit, width = weight.shape[-2:]
    count = width // unit // share[1]
    first = pl.multiple_of(index * (width // unit) + share[0] * count, count)
    value = weight[pl.ds(first, count), :, lanes]
    return value.reshape(count * unit, value.shape[-1])


def project(left, weight, index, dst):
    width = dst.shape[-1]
    step = 256 if width % 256 == 0 else width

    @pl.loop(0, width // step)
    def _(j):
        at = pl.ds(pl.multiple_of(j * step, step), step)
        dst[:, at] = jnp.dot(left[...], block(weight, index, at), preferred_element_type=F32).astype(dst.dtype)


def prepare_bias(rel, table, bias, rank, rows, group):
    buckets, heads = table.shape
    wide = group + 128
    lane = lax.broadcasted_iota(jnp.int32, (group, wide), 1)
    shift = jnp.where(lane < group, lane, lane - wide)
    distance = jnp.clip(rank * rows - shift, 0, group - 1)
    hot = (lax.broadcasted_iota(jnp.int32, (group, wide), 0) == distance).astype(F32).astype(BF)
    which = jnp.dot(jnp.broadcast_to(rel[...].astype(F32), (8, group)).astype(BF), hot, preferred_element_type=F32)
    picks = (lax.broadcasted_iota(jnp.int32, (buckets, wide), 0) == which[0:1].astype(jnp.int32)).astype(F32)
    line = lax.dot_general(table[...], picks, (((0,), (0,)), ((), ())), precision=HIGHEST, preferred_element_type=F32)
    for h in range(heads):
        band = pltpu.roll(jnp.broadcast_to(line[h : h + 1], (rows, wide)), 0, 1, stride=1, stride_axis=0)
        bias[h // 2, pl.ds((h % 2) * rows, rows), :] = band[:, :group]


def prepare_masks(lengths, same, causal, rank, rows, group):
    key = lax.broadcasted_iota(jnp.int32, (rows, group), 1)
    query = rank * rows + lax.broadcasted_iota(jnp.int32, (rows, group), 0)
    for p in range(same.shape[0]):
        end = jnp.int32(0)
        kd = jnp.zeros((rows, group), jnp.int32)
        qd = jnp.zeros((rows, group), jnp.int32)
        for n in range(lengths.shape[1]):
            end = end + lengths[p, n]
            kd = kd + jnp.where(key >= end, 1, 0)
            qd = qd + jnp.where(query >= end, 1, 0)
        same[p] = jnp.where(kd == qd, 0.0, NEG)
        causal[p] = jnp.where((kd == qd) & (key <= query), 0.0, NEG)


def two_heads(pair):
    first = lax.broadcasted_iota(jnp.int32, pair.shape, 1) < HEAD
    zero = jnp.zeros_like(pair)
    return jnp.concatenate([jnp.where(first, pair, zero), jnp.where(first, zero, pair)], axis=0)


def one_pair(stacked):
    rows = stacked.shape[0] // 2
    first = lax.broadcasted_iota(jnp.int32, (rows, stacked.shape[1]), 1) < HEAD
    return jnp.where(first, stacked[:rows], stacked[rows:])


def attend_pairs(query, keys, values, bias, mask, chances, mixed):
    packs, pairs, double, group = chances.shape
    rows = double // 2

    def body(i, carry):
        p, j = i // pairs, lax.rem(i, pairs)
        mine = pl.ds(pl.multiple_of(p * rows, rows), rows)
        theirs = pl.ds(pl.multiple_of(p * group, group), group)
        lanes = pl.ds(pl.multiple_of(j * 128, 128), 128)
        scores = lax.dot_general(
            two_heads(query[mine, lanes]), keys[theirs, lanes], (((1,), (1,)), ((), ())), preferred_element_type=F32
        )
        scores = scores * HEAD**-0.5
        if bias is not None:
            scores = scores + bias[j]
        scores = (scores.reshape(2, rows, group) + mask[p][None]).reshape(double, group)
        raised = jnp.exp(scores - jnp.max(scores, axis=1, keepdims=True))
        weights = (raised * (1.0 / jnp.sum(raised, axis=1, keepdims=True))).astype(BF)
        chances[p, j] = weights
        out = jnp.dot(weights, values[theirs, lanes], preferred_element_type=F32)
        mixed[mine, lanes] = one_pair(out).astype(BF)
        return carry

    lax.fori_loop(0, packs * pairs, body, 0, unroll=2)


def add_product(total, left, weight, index):
    width = total.shape[-1]
    step = 256 if width % 256 == 0 else width

    @pl.loop(0, width // step)
    def _(j):
        at = pl.ds(pl.multiple_of(j * step, step), step)
        total[:, at] += jnp.dot(left[...], block(weight, index, at), preferred_element_type=F32)


def product_t(left, weight, index, dst):
    halves = 2
    step = weight.shape[-1] // halves

    @pl.loop(0, halves)
    def _(j):
        rows = block(weight, index, share=(j, halves))
        out = lax.dot_general(left[...], rows, (((1,), (1,)), ((), ())), preferred_element_type=F32)
        dst[:, pl.ds(pl.multiple_of(j * step, step), step)] = out.astype(dst.dtype)


def two_products_t(left1, index1, left2, index2, weight, dst):
    halves = 2
    step = weight.shape[-1] // halves

    @pl.loop(0, halves)
    def _(j):
        out = 0.0
        for left, index in ((left1, index1), (left2, index2)):
            rows = block(weight, index, share=(j, halves))
            out = out + lax.dot_general(left[...], rows, (((1,), (1,)), ((), ())), preferred_element_type=F32)
        dst[:, pl.ds(pl.multiple_of(j * step, step), step)] = out.astype(dst.dtype)


def outer_product(left, right, dst, index):
    unit, width = dst.shape[-2:]
    halves = 2
    step, count = width // halves, width // unit // halves

    @pl.loop(0, halves)
    def _(j):
        part = left[:, pl.ds(pl.multiple_of(j * step, step), step)]
        out = lax.dot_general(part, right[...], (((0,), (0,)), ((), ())), preferred_element_type=F32)
        first = index * (width // unit) + j * count
        dst[pl.ds(first, count)] = out.astype(dst.dtype).reshape(count, unit, width)


def add_into(total, other):
    lead = total.shape[:-2]
    count = 1
    for n in lead:
        count *= n
    rows = total.shape[-2]
    step = next(n for n in ((48, 32, 16) if total.shape[-1] <= 1024 else (16,)) if rows % n == 0)

    def body(i, carry):
        index = []
        rest = i // (rows // step)
        for n in reversed(lead):
            index.insert(0, lax.rem(rest, n))
            rest = rest // n
        r = pl.ds(pl.multiple_of(lax.rem(i, rows // step) * step, 16), step)
        at = (*index, r)
        total[at] = (total[at].astype(F32) + other[at].astype(F32)).astype(total.dtype)
        return carry

    lax.fori_loop(0, count * (rows // step), body, 0)


def norm_back_rows(value, gain, grad, total, gain_grad, step=64):
    gain_grad[...] = jnp.zeros_like(gain_grad)

    @pl.loop(0, value.shape[0] // step)
    def _(i):
        at = pl.ds(pl.multiple_of(i * step, step), step)
        v, g = value[at, :].astype(F32), grad[at, :]
        r = lax.rsqrt(jnp.mean(v * v, axis=-1, keepdims=True) + EPS)
        scaled = g * gain
        total[at, :] += r * scaled - v * (r * r * r) * jnp.mean(scaled * v, axis=-1, keepdims=True)
        gain_grad[...] += jnp.sum(g * v * r, axis=0, keepdims=True)


def attend_pairs_back(query, keys, values, chances, grad, grad_q, grad_k, grad_v, diagonal):
    packs, pairs, double, group = chances.shape
    rows = double // 2
    scale = HEAD**-0.5

    def body(i, carry):
        p, j = i // pairs, lax.rem(i, pairs)
        mine = pl.ds(pl.multiple_of(p * rows, rows), rows)
        theirs = pl.ds(pl.multiple_of(p * group, group), group)
        lanes = pl.ds(pl.multiple_of(j * 128, 128), 128)
        ga = two_heads(grad[mine, lanes])
        low = chances[p, j]
        wide = low.astype(F32)
        gp = lax.dot_general(ga, values[theirs, lanes], (((1,), (1,)), ((), ())), preferred_element_type=F32)
        gs = (wide * (gp - jnp.sum(wide * gp, axis=1, keepdims=True))).astype(BF)
        gq = jnp.dot(gs, keys[theirs, lanes], preferred_element_type=F32)
        grad_q[mine, lanes] = (one_pair(gq) * scale).astype(BF)
        gk = lax.dot_general(gs, two_heads(query[mine, lanes]), (((0,), (0,)), ((), ())), preferred_element_type=F32)
        grad_k[theirs, lanes] = (gk * scale).astype(BF)
        gv = lax.dot_general(low, ga, (((0,), (0,)), ((), ())), preferred_element_type=F32)
        grad_v[theirs, lanes] = gv.astype(BF)
        if diagonal is not None:
            a = lax.broadcasted_iota(jnp.int32, (rows, rows), 0)
            b = lax.broadcasted_iota(jnp.int32, (rows, rows), 1)
            flip = (a + b == rows - 1).astype(F32).astype(BF)
            for half in range(2):
                turned = jnp.dot(flip, gs[half * rows : (half + 1) * rows], preferred_element_type=F32)
                turned = jnp.concatenate([turned, jnp.zeros((rows, 128), F32)], axis=1)
                band = pltpu.roll(turned, 0, 1, stride=1, stride_axis=0)
                diagonal[pl.ds(2 * j + half, 1), :] += jnp.sum(band, axis=0, keepdims=True)
        return carry

    lax.fori_loop(0, packs * pairs, body, 0, unroll=2)


def table_grad(rel, diagonal, rank, rows, group, buckets):
    wide = group + 128
    lane = lax.broadcasted_iota(jnp.int32, (group, wide), 1)
    distance = jnp.clip(rank * rows + rows - 1 - lane, 0, group - 1)
    hot = (lax.broadcasted_iota(jnp.int32, (group, wide), 0) == distance).astype(F32).astype(BF)
    which = jnp.dot(jnp.broadcast_to(rel[...].astype(F32), (8, group)).astype(BF), hot, preferred_element_type=F32)
    picks = (lax.broadcasted_iota(jnp.int32, (buckets, wide), 0) == which[0:1].astype(jnp.int32)).astype(F32)
    return lax.dot_general(picks, diagonal[...], (((1,), (1,)), ((), ())), precision=HIGHEST, preferred_element_type=F32)


def route_slots(route, packs, experts, capacity):
    count = route.shape[0]
    hot = (route[...] == lax.broadcasted_iota(jnp.int32, (count, experts), 1)).astype(F32)
    a = lax.broadcasted_iota(jnp.int32, (count, count), 0)
    b = lax.broadcasted_iota(jnp.int32, (count, count), 1)
    rows = count // packs
    earlier = ((b < a) & (a // rows == b // rows)).astype(F32).astype(BF)
    before = jnp.dot(earlier, hot.astype(BF), preferred_element_type=F32)
    slot = jnp.sum(before * hot, axis=1, keepdims=True).astype(jnp.int32)
    pack = lax.broadcasted_iota(jnp.int32, (count, 1), 0) // rows
    target = jnp.where(slot < capacity, (route[...] * packs + pack) * capacity + slot, -1)
    slots = lax.broadcasted_iota(jnp.int32, (count, experts * packs * capacity), 1)
    return hot, (target == slots).astype(F32).astype(BF)


def gelu_both(z):
    c = 0.7978845608028654
    t = jnp.tanh(c * (z + 0.044715 * (z * z * z)))
    half = 0.5 * (1.0 + t)
    slope = half + 0.5 * z * (1.0 - t * t) * (c * (1.0 + 3 * 0.044715 * (z * z)))
    return z * half, slope


def layer_body(lengths, rel, gains, table, router_t, route, x_ref, m_ref, g_ref, ain, aout, ein, eout,
               out_rows, o0, o1, o2, o3, grad_x, grad_mem, sum_wide, sum_table,
               w, big, ge, c2, c3, y0, y1, x0, x1, x2, x3, z0, z1, z2, z3,
               xo, mo, n1_all, k_, v, kc, vc, gv, n1, q, mixed, n2, qc, cross_mixed, n3, gb, ga, gq,
               pr_self, pr_cross, h1, h2, gn, bias, same, causal, diagonal, gain_row,
               act_core, act_x, wide_sum, table_sum, wide_in, table_in,
               slots_out, slots_in, slots_acc, back_in, hid, gin_,
               act_send, act_recv, line_send, side_send, spread_send, ici_recv, spread_recv, own_sem,
               core_send, core_recv, y_send, y_recv, x_send, x_recv, z_send, z_recv,
               sum_send, sum_recv, small_send, small_recv, swap_send, swap_recv, free_sem):
    at = Place()
    nz, nx, ny = at.nz, at.nx, at.ny
    packs, tok, width = x_ref.shape
    group = xo.shape[0] // packs
    experts = router_t.shape[0]
    unit = ain.shape[1]
    panels = eout.shape[0]
    buckets = table.shape[0]
    gk = xo
    units = (ain.shape[0], aout.shape[0], panels, panels)
    tall = nz * nx * 2
    bases = (0, tall * ny * units[0], 0, tall * panels)
    dense, e_in, e_out = (0, 1), 2, 3
    experts_ = (e_in, e_out)
    waits = []

    def remote(src, dst, ssem, rsem, **where):
        return pltpu.make_async_remote_copy(
            src_ref=src, dst_ref=dst, send_sem=ssem, recv_sem=rsem,
            device_id=at.device(**where), device_id_type=MESH,
        )

    def send(*args, **where):
        one = remote(*args, **where)
        one.start()
        waits.append(one.wait_send)
        return one

    def arrive(ref, sem):
        pltpu.make_async_copy(ref, ref, sem).wait()

    def spot(a, z, x, c, y):
        index = (z * nx + x) * 2 + c
        index = index * ny + y if a in dense else index
        return (w if a in dense else big).at[pl.ds(bases[a] + index * units[a], units[a])]

    shards = {0: ain, 1: aout, 3: eout}
    acts = ((x_ref, xo), (m_ref, mo))

    at.greet()

    def act_rows(full, p, x, c):
        return full.at[pl.ds(pl.multiple_of(p * group + (x * 2 + c) * tok, 16), tok)]

    own_waits = []
    for i, (src, full) in enumerate(acts):
        for p in range(packs):
            dst = act_rows(full, p, at.x, at.c)
            for k, x in enumerate(at.other_x()):
                send(src.at[p], dst, act_send.at[i, p, k], act_recv.at[i, p, at.x, at.c], x=x)
            send(src.at[p], dst, act_send.at[i, p, nx - 1 + at.x], act_recv.at[i, p, at.x, at.c], c=1 - at.c)
            own = pltpu.make_async_copy(src.at[p], dst, own_sem.at[4 + i, p])
            own.start()
            own_waits.append(own.wait)

    def along_line(a, z, src):
        dst = spot(a, z, at.x, at.c, at.y)
        sem = ici_recv.at[a, z, at.x, at.y]
        left = (z >= at.z) & (at.z > 0)
        right = (z <= at.z) & (at.z < nz - 1)

        def one(side):
            return remote(src, dst, line_send.at[a, z, side], sem, z=at.z + 2 * side - 1)

        @pl.when(left)
        def _():
            one(0).start()

        @pl.when(right)
        def _():
            one(1).start()

        def wait():
            @pl.when(left)
            def _():
                one(0).wait_send()

            @pl.when(right)
            def _():
                one(1).wait_send()

        waits.append(wait)

    def to_sides(a, z, src):
        dst = spot(a, z, at.x, at.c, at.y)
        for k, x in enumerate(at.other_x()):
            send(src, dst, side_send.at[a, z, k], ici_recv.at[a, z, at.x, at.y], x=x)
        if a in dense:
            for k, y in enumerate(at.other_y()):
                send(src, dst, side_send.at[a, z, nx - 1 + k], ici_recv.at[a, z, at.x, at.y], y=y)

    def to_core(a, z, x, y, src):
        send(src, spot(a, z, x, at.c, y), spread_send.at[a, z, x, y], spread_recv.at[a, z, x, y], c=1 - at.c)

    zs = [at.by_distance(k) for k in range(nz)]
    for a in dense:
        along_line(a, at.z, shards[a])
    own_ein = spot(e_in, at.z, at.x, at.c, at.y)
    first = bases[e_in] + ((at.z * nx + at.x) * 2 + at.c) * panels
    for f in range(panels):
        big[first + f] = ein[:, f * width : (f + 1) * width]
    shards[2] = own_ein
    for a in experts_:
        along_line(a, at.z, shards[a])

    def shard_events(kind, k):
        for a in kind:
            here = spot(a, zs[k], at.x, at.c, at.y)
            if k:
                arrive(here, ici_recv.at[a, zs[k], at.x, at.y])
                along_line(a, zs[k], here)
            elif a != e_in:
                own = pltpu.make_async_copy(shards[a], here, own_sem.at[a, 0])
                own.start()
                own_waits.append(own.wait)
            src = here if k else shards[a]
            to_sides(a, zs[k], src)
            to_core(a, zs[k], at.x, at.y, src)

    for k in range(nz):
        shard_events(dense, k)
        if k == 0:
            for i, (src, full) in enumerate(acts):
                for p in range(packs):
                    for x in at.other_x():
                        dst = act_rows(full, p, x, at.c)
                        arrive(dst, act_recv.at[i, p, x, at.c])
                        send(dst, dst, act_send.at[i, p, nx - 1 + x], act_recv.at[i, p, x, at.c], c=1 - at.c)

    def diagonal_events(k):
        for a in dense:
            for x in at.other_x():
                here = spot(a, zs[k], x, at.c, at.y)
                arrive(here, ici_recv.at[a, zs[k], x, at.y])
                for j, y in enumerate(at.other_y()):
                    send(here, here, side_send.at[a, zs[k], nx - 1 + ny - 1 + j + (ny - 1) * x],
                         ici_recv.at[a, zs[k], x, at.y], y=y)
                to_core(a, zs[k], x, at.y, here)

    for k in range(nz):
        shard_events(experts_, k)
        diagonal_events(k)

    prepare_bias(rel, table, bias, at.s, tok, group)
    prepare_masks(lengths, same, causal, at.s, tok, group)
    for i, (src, full) in enumerate(acts):
        for p in range(packs):
            for x in range(nx):
                arrive(act_rows(full, p, x, 1 - at.c), act_recv.at[i, p, x, 1 - at.c])
    for wait in own_waits:
        wait()
    rms_rows(xo, gains[0:1], n1_all, packs * group)
    for p in range(packs):
        h1[pl.ds(p * tok, tok), :] = x_ref[p].astype(F32)
        n1[pl.ds(p * tok, tok), :] = n1_all[pl.ds(pl.multiple_of(p * group + at.s * tok, tok), tok), :]
    for k in range(nz):
        for a in dense:
            for y in at.other_y():
                for x in range(nx):
                    here = spot(a, zs[k], x, at.c, y)
                    arrive(here, ici_recv.at[a, zs[k], x, y])
                    to_core(a, zs[k], x, y, here)
    for a in dense:
        for z in range(nz):
            for x in range(nx):
                for y in range(ny):
                    arrive(spot(a, z, x, 1 - at.c, y), spread_recv.at[a, z, x, y])

    project(n1, w, 0, q)
    project(n1_all, w, 1, k_)
    project(n1_all, w, 2, v)
    project(mo, w, 4, kc)
    project(mo, w, 5, vc)
    attend_pairs(q, k_, v, bias, causal, pr_self, mixed)
    add_product(h1, mixed, w, 6)
    rms_rows(h1, gains[1:2], n2, packs * tok)
    project(n2, w, 3, qc)
    attend_pairs(qc, kc, vc, None, same, pr_cross, cross_mixed)
    h2[...] = h1[...]
    add_product(h2, cross_mixed, w, 7)
    rms_rows(h2, gains[2:3], n3, packs * tok)

    each = slots_in.shape[2]
    hot, dispatch = route_slots(route, packs, experts, each // packs)
    logits = lax.dot_general(n3[...], router_t[...].astype(BF), (((1,), (1,)), ((), ())), preferred_element_type=F32)
    raised = jnp.exp(logits - jnp.max(logits, axis=1, keepdims=True))
    routing = raised / jnp.sum(raised, axis=1, keepdims=True)
    gate = jnp.sum(routing * hot, axis=1, keepdims=True)
    top = g_ref[...].astype(F32).reshape(packs * tok, width)

    def by_slot(rows):
        out = lax.dot_general(dispatch, rows, (((0,), (0,)), ((), ())), preferred_element_type=F32)
        return out.astype(BF).reshape(ny, each, width)

    def swap(t, source, target):
        for j, y in enumerate(at.other_y()):
            one = remote(source.at[t % 2, y], target.at[t % 2, at.y], swap_send.at[t, j], swap_recv.at[t, ny - 2 - j], y=y)
            one.start()
            (waits if t >= 2 else swap_waits).append(one.wait_send)

    swap_waits = []

    def swapped(t, target):
        for j, y in enumerate(at.other_y()):
            arrive(target.at[t % 2, y], swap_recv.at[t, j])

    slots_out[0] = by_slot(n3[...])
    swap(0, slots_out, slots_in)
    slots_out[1] = by_slot((gate * top).astype(BF))
    swap(1, slots_out, slots_in)
    for t in range(2):
        slots_in[t, at.y] = slots_out[t, at.y]

    for k in range(nz):
        for a in experts_:
            for x in at.other_x():
                here = spot(a, zs[k], x, at.c, at.y)
                arrive(here, ici_recv.at[a, zs[k], x, at.y])
                to_core(a, zs[k], x, at.y, here)
    for a in experts_:
        for z in range(nz):
            for x in range(nx):
                arrive(spot(a, z, x, 1 - at.c, at.y), spread_recv.at[a, z, x, at.y])
    for t in range(2):
        swapped(t, slots_in)
    for wait in waits:
        wait()
    waits.clear()

    cores, ys, xs, zs_ = {2: c2, 3: c3}, (y0, y1), (x0, x1, x2, x3), (z0, z1, z2, z3)
    outs = (o0, o1, o2, o3)
    far = [sorted(range(nz), key=lambda d: (-abs(d - z), d)) for z in range(nz)]
    order_e = [at.pick([far[z][k] for z in range(nz)]) for k in range(nz)]
    halves = [[d for d in row if d >= nz // 2] + [d for d in row if d < nz // 2] for row in far]
    order_d = [at.pick([halves[z][k] for z in range(nz)]) for k in range(nz)]
    e_waits = []

    def expert_part(a, d, x, c):
        return ge.at[pl.ds(bases[a] + ((d * nx + x) * 2 + c) * panels, panels)]

    def start_expert(a, k):
        for x in range(nx):
            one = remote(expert_part(a, order_e[k], x, 1 - at.c), cores[a].at[k, x], core_send.at[a, k, x],
                         core_recv.at[a, k, x], c=1 - at.c)
            one.start()
            e_waits.append(one.wait_send)

    def core_expert(a, k):
        for x in range(nx):
            arrive(cores[a].at[k, x], core_recv.at[a, k, x])
            add_into(cores[a].at[k, x], expert_part(a, order_e[k], x, at.c))
        for j, x in enumerate(at.other_x()):
            send(cores[a].at[k, x], xs[a].at[k, nx - 2 - j], x_send.at[a, k, j], x_recv.at[a, k, nx - 2 - j], x=x)

    def free_experts():
        for wait in e_waits:
            wait()
        pl.semaphore_signal(free_sem, inc=1, device_id=at.device(c=1 - at.c), device_id_type=MESH)

    def dense_part(a, d, x, c):
        return big.at[pl.ds(bases[a] + ((d * nx + x) * 2 + c) * ny * units[a], ny * units[a])]

    def dense_core(a, k, x, y=None):
        first = bases[a] // 2 + (k * nx + x) * ny * units[a]
        if y is None:
            return ge.at[pl.ds(first, ny * units[a])]
        return ge.at[pl.ds(first + y * units[a], units[a])]

    def start_dense(k):
        for a in dense:
            for x in range(nx):
                send(dense_part(a, order_d[k], x, 1 - at.c), dense_core(a, k, x), core_send.at[a, k, x],
                     core_recv.at[a, k, x], c=1 - at.c)

    def core_dense(k):
        for a in dense:
            for x in range(nx):
                arrive(dense_core(a, k, x), core_recv.at[a, k, x])
                add_into(dense_core(a, k, x), dense_part(a, order_d[k], x, at.c))
                for j, y in enumerate(at.other_y()):
                    send(dense_core(a, k, x, y), ys[a].at[k, ny - 2 - j, x],
                         y_send.at[a, k, j, x], y_recv.at[a, k, ny - 2 - j, x], y=y)

    def y_dense(k):
        for a in dense:
            for x in range(nx):
                for j in range(ny - 1):
                    arrive(ys[a].at[k, j, x], y_recv.at[a, k, j, x])
                    add_into(ys[a].at[k, 0, x], ys[a].at[k, j, x] if j else dense_core(a, k, x, at.y))
            for j, x in enumerate(at.other_x()):
                send(ys[a].at[k, 0, x], xs[a].at[k, nx - 2 - j], x_send.at[a, k, j], x_recv.at[a, k, nx - 2 - j], x=x)

    def write_out(a, total):
        value = total[...].astype(F32)
        if a == e_in:
            for f in range(panels):
                outs[a][:, f * width : (f + 1) * width] = value[f]
        else:
            outs[a][...] = value.reshape(outs[a].shape)

    def x_and_line(kind, k):
        for a in kind:
            d = (order_d if a in dense else order_e)[k]
            total = xs[a].at[k, 0]
            for j in range(nx - 1):
                arrive(xs[a].at[k, j], x_recv.at[a, k, j])
                own = ys[a].at[k, 0, at.x] if a in dense else cores[a].at[k, at.x]
                add_into(total, xs[a].at[k, j] if j else own)
            for side in range(2):
                feeds = (at.z > 0) & (d >= at.z) if side == 0 else (at.z < nz - 1) & (d <= at.z)
                slot = d if side == 0 else jnp.where(d == at.z, nz, d)

                @pl.when(feeds)
                def _(a=a, slot=slot, total=total):
                    arrive(zs_[a].at[slot], z_recv.at[a, slot])
                    add_into(total, zs_[a].at[slot])

            def hop(to, a=a, total=total, d=d):
                slot = d if to > 0 else jnp.where(d == at.z - 1, nz, d)
                return remote(total, zs_[a].at[slot], z_send.at[a, k], z_recv.at[a, slot], z=at.z + to)

            @pl.when(d < at.z)
            def _(hop=hop):
                hop(-1).start()

            @pl.when(d > at.z)
            def _(hop=hop):
                hop(1).start()

            @pl.when(d == at.z)
            def _(a=a, total=total):
                write_out(a, total)

            def wait(hop=hop, d=d):
                @pl.when(d < at.z)
                def _():
                    hop(-1).wait_send()

                @pl.when(d > at.z)
                def _():
                    hop(1).wait_send()

            waits.append(wait)

    def start_act(i):
        for p in range(packs):
            for x in range(nx):
                send(act_rows((kc, k_)[i], p, x, 1 - at.c), act_core.at[i, p, x], sum_send.at[i, p, x],
                     sum_recv.at[i, p, x], c=1 - at.c)

    def core_act(i):
        for p in range(packs):
            for x in range(nx):
                arrive(act_core.at[i, p, x], sum_recv.at[i, p, x])
                add_into(act_core.at[i, p, x], act_rows((kc, k_)[i], p, x, at.c))
        for j, x in enumerate(at.other_x()):
            send(act_core.at[i, :, x], act_x.at[i, nx - 2 - j], sum_send.at[i, packs, j], sum_recv.at[i, packs, nx - 2 - j], x=x)

    def x_act(i):
        for j in range(nx - 1):
            arrive(act_x.at[i, j], sum_recv.at[i, packs, j])
        for p in range(packs):
            out = act_core[i, p, at.x].astype(F32)
            for j in range(nx - 1):
                out = out + act_x[i, j, p].astype(F32)
            if i == 0:
                grad_mem[pl.ds(p * tok, tok), :] = out
            else:
                gn[pl.ds(p * tok, tok), :] += out

    pair_sums = ((wide_sum, wide_in), (table_sum, table_in))
    stages = [("c", [1 - at.c]), ("y", at.other_y()), ("x", at.other_x())]

    def start_small(t):
        axis, peers = stages[t]
        base = [0, 1, ny][t]
        for i, (total, inbox) in enumerate(pair_sums):
            for j, peer in enumerate(peers):
                back = base + len(peers) - 1 - j
                send(total.at[t], inbox.at[back], small_send.at[i, base + j], small_recv.at[i, back], **{axis: peer})

    def end_small(t):
        axis, peers = stages[t]
        base = [0, 1, ny][t]
        for i, (total, inbox) in enumerate(pair_sums):
            out = total[t]
            for j in range(len(peers)):
                arrive(inbox.at[base + j], small_recv.at[i, base + j])
                out = out + inbox[base + j]
            total[t + 1] = out

    tail = ny + nx - 1

    def start_line():
        for i, (total, inbox) in enumerate(pair_sums):
            for j in range(1, nz):
                z = lax.rem(at.z + j, nz)
                send(total.at[3], inbox.at[tail + at.z], small_send.at[i, tail + j], small_recv.at[i, tail + at.z], z=z)

    def end_line():
        for i, (total, inbox) in enumerate(pair_sums):
            for j in range(1, nz):
                z = lax.rem(at.z + j, nz)
                arrive(inbox.at[tail + z], small_recv.at[i, tail + z])
            out = None
            for z in range(nz):
                term = jnp.where(at.z == z, total[3], inbox[tail + z])
                out = term if out is None else out + term
            (sum_wide, sum_table)[i][...] = out

    count = ny * each
    row_units = width // unit
    for k in range(nz):
        f = order_e[k]
        here = slots_in[0].reshape(count, width)
        grad_here = slots_in[1].reshape(count, width)

        def in_rows(start, n, f=f):
            return jnp.concatenate([big[(start + i) * panels + f] for i in range(n)], axis=0)

        first_out = bases[e_out] + f * row_units
        inner = jnp.dot(here, in_rows(0, row_units), preferred_element_type=F32)
        hidden, slope = gelu_both(inner)
        hid[...] = hidden.astype(BF)
        out_panel = big[pl.ds(first_out, row_units)].reshape(width, width)
        grad_hidden = lax.dot_general(grad_here, out_panel, (((1,), (1,)), ((), ())), preferred_element_type=F32)
        gin_[...] = (grad_hidden * slope).astype(BF)
        result = jnp.dot(hid[...], out_panel, preferred_element_type=F32)
        grad_slots = lax.dot_general(gin_[...], in_rows(0, row_units), (((1,), (1,)), ((), ())), preferred_element_type=F32)
        if k:
            slots_acc[0] += result
            slots_acc[1] += grad_slots
        else:
            slots_acc[0] = result
            slots_acc[1] = grad_slots
        grad = lax.dot_general(hid[...], grad_here, (((0,), (0,)), ((), ())), preferred_element_type=F32).astype(BF)
        ge[pl.ds(first_out, row_units)] = grad.reshape(row_units, unit, width)
        start_expert(e_out, k)
        grad = lax.dot_general(here, gin_[...], (((0,), (0,)), ((), ())), preferred_element_type=F32).astype(BF)
        for i in range(row_units):
            ge[i * panels + f] = grad[i * unit : (i + 1) * unit]
        if k:
            core_expert(e_out, k - 1)
    for wait in swap_waits:
        wait()
    for t in range(2):
        slots_out[t] = slots_acc[t].astype(BF).reshape(ny, each, width)
        swap(2 + t, slots_out, back_in)
    for k in range(nz):
        start_expert(e_in, k)
    core_expert(e_out, nz - 1)
    core_expert(e_in, 0)
    for t in range(2):
        swapped(2 + t, back_in)
        back_in[t, at.y] = slots_out[t, at.y]
    combined = jnp.dot(dispatch, back_in[0].reshape(count, width), preferred_element_type=F32)
    rows_out = (h2[...] + gate * combined).astype(BF)
    for p in range(packs):
        out_rows[p] = rows_out[p * tok : (p + 1) * tok]
    grad_gate = jnp.sum(top * combined, axis=1, keepdims=True)
    grad_logits = grad_gate * routing * (hot - gate)
    diagonal[...] = jnp.zeros_like(diagonal)
    for i, (_, inbox) in enumerate(pair_sums):
        inbox[pl.ds(tail + at.z, 1)] = jnp.zeros_like(inbox[pl.ds(0, 1)])
    wide_sum[0] = jnp.zeros_like(wide_sum[0])
    wide_sum[0, pl.ds(3, experts), :] = lax.dot_general(
        grad_logits, n3[...].astype(F32), (((0,), (0,)), ((), ())), precision=HIGHEST, preferred_element_type=F32
    )
    grad_n3 = jnp.dot(dispatch, back_in[1].reshape(count, width), preferred_element_type=F32)
    for e in range(experts):
        grad_n3 = grad_n3 + grad_logits[:, e : e + 1] * router_t[e : e + 1, :]
    gn[...] = grad_n3
    grad_x[...] = top
    norm_back_rows(h2, gains[2:3], gn, grad_x, gain_row)
    wide_sum[0, 2:3, :] = gain_row[...]
    gb[...] = grad_x[...].astype(BF)

    product_t(gb, w, 7, ga)
    core_expert(e_in, 1)
    core_expert(e_in, 2)
    core_expert(e_in, 3)
    free_experts()
    outer_product(cross_mixed, gb, big, 7)
    x_and_line((e_out,), 0)
    attend_pairs_back(qc, kc, vc, pr_cross, ga, gq, gk, gv, None)
    outer_product(n2, gq, big, 3)
    outer_product(mo, gk, big, 4)
    outer_product(mo, gv, big, 5)
    pl.semaphore_wait(free_sem, 1)
    for k in range(nz // 2):
        start_dense(k)
    x_and_line((e_out,), 1)
    two_products_t(gk, 4, gv, 5, w, kc)
    start_act(0)
    product_t(gq, w, 3, gn)
    norm_back_rows(h1, gains[1:2], gn, grad_x, gain_row)
    wide_sum[0, 1:2, :] = gain_row[...]
    gb[...] = grad_x[...].astype(BF)
    product_t(gb, w, 6, ga)
    core_dense(0)
    x_and_line((e_out,), 2)
    outer_product(mixed, gb, big, 6)
    core_act(0)
    core_dense(1)
    x_and_line((e_out,), 3)
    attend_pairs_back(q, k_, v, pr_self, ga, gq, gk, gv, diagonal)
    x_and_line((e_in,), 0)
    outer_product(n1, gq, big, 0)
    outer_product(n1_all, gk, big, 1)
    outer_product(n1_all, gv, big, 2)
    for k in range(nz // 2, nz):
        start_dense(k)
    y_dense(0)
    two_products_t(gk, 1, gv, 2, w, k_)
    start_act(1)
    x_and_line((e_in,), 1)
    y_dense(1)
    for k in range(nz // 2, nz):
        core_dense(k)
    core_act(1)
    product_t(gq, w, 0, gn)
    table_sum[0] = table_grad(rel, diagonal, at.s, tok, group, buckets)
    x_and_line((e_in,), 2)
    x_and_line((e_in,), 3)
    x_act(0)
    x_and_line(dense, 0)
    x_act(1)
    for p in range(packs):
        h1[pl.ds(p * tok, tok), :] = x_ref[p].astype(F32)
    norm_back_rows(h1, gains[0:1], gn, grad_x, gain_row)
    wide_sum[0, 0:1, :] = gain_row[...]
    start_small(0)
    y_dense(2)
    end_small(0)
    start_small(1)
    x_and_line(dense, 1)
    end_small(1)
    start_small(2)
    y_dense(3)
    end_small(2)
    start_line()
    x_and_line(dense, 2)
    end_line()
    x_and_line(dense, 3)
    for wait in waits:
        wait()


def shapes_of(layer_input, routes, attn_in, attn_out, expert_in, expert_out):
    nz, ns, ny = (lax.axis_size(a) for a in ("dp", "seq", "expert"))
    packs, tok, width = layer_input.shape[0], layer_input.shape[3], layer_input.shape[4]
    return nz, ns, ny, packs, tok, width


def fits_kernel(layer_input, routes, attn_in, attn_out, expert_in, expert_out):
    nz, ns, ny, packs, tok, width = shapes_of(layer_input, routes, attn_in, attn_out, expert_in, expert_out)
    unit, hidden = expert_in.shape[1:]
    capacity = (5 * tok + 4 * ny - 1) // (4 * ny)
    return (
        unit % 16 == 0
        and tok % 16 == 0
        and packs * capacity % 16 == 0
        and attn_in.shape[0] % unit == 0
        and attn_out.shape[0] % unit == 0
        and width % (2 * unit) == 0
        and hidden == nz * width
        and expert_in.shape[0] == 1
    )


def layer_kernel(layer_input, memory, cotangent, routes, doc_lengths, rel_buckets, gains, bias_table, router,
                 attn_in, attn_out, expert_in, expert_out):
    nz, ns, ny, packs, tok, width = shapes_of(layer_input, routes, attn_in, attn_out, expert_in, expert_out)
    nx = ns // 2
    group, pairs = ns * tok, width // 128
    unit = expert_in.shape[1]
    panels = expert_in.shape[2] // width
    experts, buckets = router.shape[1], bias_table.shape[0]
    each = packs * ((5 * tok + 4 * experts - 1) // (4 * experts))
    tall = nz * ns
    units = (attn_in.shape[0] // unit, attn_out.shape[0] // unit, panels, panels)
    total = tall * ny * (units[0] + units[1])
    extra = -(-(3 + experts) // 8) * 8
    small = ny + nx - 1 + nz
    mine, every = packs * tok, packs * group
    any_ = pl.BlockSpec(memory_space=pl.ANY)
    vmem = pl.BlockSpec(memory_space=pltpu.VMEM)
    smem = pl.BlockSpec(memory_space=pltpu.SMEM)
    dma = pltpu.SemaphoreType.DMA
    low = lambda *shape: pltpu.VMEM(shape, BF)
    wide = lambda *shape: pltpu.VMEM(shape, F32)
    shape = lambda *dims: jax.ShapeDtypeStruct(dims, F32)
    out_rows, g0, g1, g2, g3, grad_x, grad_mem, sums, table = pl.pallas_call(
        layer_body,
        out_shape=[
            jax.ShapeDtypeStruct((packs, tok, width), BF),
            shape(*attn_in.shape),
            shape(*attn_out.shape),
            shape(*expert_in.shape[1:]),
            shape(*expert_out.shape[1:]),
            shape(mine, width),
            shape(mine, width),
            shape(extra, width),
            shape(buckets, 128),
        ],
        in_specs=[smem, *[vmem] * 8, any_, any_, vmem, any_],
        out_specs=[vmem] * 9,
        scratch_shapes=[
            low(total, unit, width),
            low(total, unit, width),
            low(2 * tall * panels, unit, width),
            *[low(nz, nx, panels, unit, width)] * 2,
            *[low(nz, ny - 1, nx, u, unit, width) for u in units[:2]],
            *[low(nz, nx - 1, u, unit, width) for u in units],
            *[low(nz + 1, u, unit, width) for u in units],
            *[low(every, width)] * 8,
            *[low(mine, width)] * 10,
            *[low(packs, pairs, 2 * tok, group)] * 2,
            *[wide(mine, width)] * 3,
            wide(pairs, 2 * tok, group),
            wide(packs, tok, group),
            wide(packs, tok, group),
            wide(128, group + 128),
            wide(1, width),
            low(2, packs, nx, tok, width),
            low(2, nx - 1, packs, tok, width),
            wide(4, extra, width),
            wide(4, buckets, 128),
            wide(small, extra, width),
            wide(small, buckets, 128),
            low(2, ny, each, width),
            low(2, ny, each, width),
            wide(2, ny * each, width),
            low(2, ny, each, width),
            low(ny * each, width),
            low(ny * each, width),
            dma((2, packs, 2 * nx)),
            dma((2, packs, nx, 2)),
            dma((4, nz, 2)),
            dma((4, nz, nx - 1 + (ny - 1) * (1 + nx))),
            dma((4, nz, nx, ny)),
            dma((4, nz, nx, ny)),
            dma((4, nz, nx, ny)),
            dma((6, packs)),
            dma((4, nz, nx)),
            dma((4, nz, nx)),
            dma((2, nz, ny - 1, nx)),
            dma((2, nz, ny - 1, nx)),
            dma((4, nz, nx - 1)),
            dma((4, nz, nx - 1)),
            dma((4, nz)),
            dma((4, nz + 1)),
            dma((2, packs + 1, nx)),
            dma((2, packs + 1, nx)),
            dma((2, small)),
            dma((2, small)),
            dma((4, ny - 1)),
            dma((4, ny - 1)),
            pltpu.SemaphoreType.REGULAR,
        ],
        compiler_params=pltpu.CompilerParams(
            collective_id=0, has_side_effects=True, vmem_limit_bytes=64 * 2**20
        ),
        name="layer",
    )(
        doc_lengths[:, 0, 0],
        rel_buckets.reshape(1, -1),
        gains,
        bias_table,
        router.T.astype(F32),
        routes.reshape(mine, 1),
        layer_input[:, 0, 0],
        memory[:, 0, 0],
        cotangent[:, 0, 0],
        attn_in.reshape(units[0], unit, width),
        attn_out.reshape(units[1], unit, width),
        expert_in[0],
        expert_out.reshape(panels, unit, width),
    )
    spread = (packs, 1, 1, tok, width)
    return (
        out_rows.reshape(spread),
        grad_x.reshape(spread),
        grad_mem.reshape(spread),
        sums[:3],
        table[:, : 2 * pairs],
        sums[3 : 3 + experts].T,
        g0,
        g1,
        g2[None],
        g3[None],
    )


def norm_apply(value, gain):
    return value * lax.rsqrt(jnp.mean(value * value, axis=-1, keepdims=True) + EPS) * gain


def norm_back(value, gain, grad):
    r = lax.rsqrt(jnp.mean(value * value, axis=-1, keepdims=True) + EPS)
    scaled = grad * gain
    back = r * scaled - value * (r * r * r) * jnp.mean(scaled * value, axis=-1, keepdims=True)
    return back, jnp.sum(grad * value * r, axis=0)


def gelu_tanh(value):
    return jax.nn.gelu(value, approximate=True)


def times(left, right):
    return jnp.dot(left, right, preferred_element_type=F32)


def times_right(left, right):
    return jnp.einsum("te,de->td", left, right, preferred_element_type=F32)


def times_left(left, right):
    return jnp.einsum("td,te->de", left, right, preferred_element_type=F32)


def split(a, packs):
    return a.reshape(packs, -1, HEADS, HEAD)


def attend(query, keys, values, allowed, bias, packs):
    scores = jnp.einsum("pqhd,pkhd->phqk", split(query, packs), split(keys, packs), preferred_element_type=F32)
    masked = jnp.where(allowed[:, None], scores * HEAD**-0.5 + bias, NEG)
    raised = jnp.exp(masked - jnp.max(masked, axis=3, keepdims=True))
    chances = raised / jnp.sum(raised, axis=3, keepdims=True)
    mixed = jnp.einsum("phqk,pkhd->pqhd", chances.astype(BF), split(values, packs), preferred_element_type=F32)
    return mixed.reshape(query.shape).astype(BF), chances


def attend_back(query, keys, values, chances, grad, packs):
    scale = HEAD**-0.5
    g4 = split(grad, packs)
    grad_chances = jnp.einsum("pqhd,pkhd->phqk", g4, split(values, packs), preferred_element_type=F32)
    spread_ = jnp.sum(chances * grad_chances, axis=3, keepdims=True)
    grad_scores = (chances * (grad_chances - spread_)).astype(BF)
    grad_query = jnp.einsum("phqk,pkhd->pqhd", grad_scores, split(keys, packs), preferred_element_type=F32) * scale
    grad_keys = jnp.einsum("phqk,pqhd->pkhd", grad_scores, split(query, packs), preferred_element_type=F32) * scale
    grad_values = jnp.einsum("phqk,pqhd->pkhd", chances.astype(BF), g4, preferred_element_type=F32)
    return (
        grad_query.reshape(query.shape).astype(BF),
        grad_keys.reshape(keys.shape).astype(BF),
        grad_values.reshape(keys.shape).astype(BF),
        grad_scores,
    )


def per_device(layer_input, memory, cotangent, routes, doc_lengths, rel_buckets, gains, bias_table, router,
               attn_in, attn_out, expert_in, expert_out):
    packs, rows, width = layer_input.shape[0], layer_input.shape[3], layer_input.shape[4]
    seqs = lax.axis_size("seq")
    group = rows * seqs
    experts = router.shape[1]
    capacity = (5 * rows + 4 * experts - 1) // (4 * experts)
    buckets = bias_table.shape[0]
    rank = lax.axis_index("seq")

    x_in, m_in, e_in, e_out = layer_input[:, 0, 0], memory[:, 0, 0], expert_in[0], expert_out[0]
    if fits_kernel(layer_input, routes, attn_in, attn_out, expert_in, expert_out):
        return layer_kernel(layer_input, memory, cotangent, routes, doc_lengths, rel_buckets, gains, bias_table, router,
                            attn_in, attn_out, expert_in, expert_out)
    x_rows = x_in.reshape(packs * rows, width).astype(F32)
    everywhere, peers = ("dp", "seq", "expert"), ("dp", "seq")
    x_all, m_all = (lax.all_gather(a, "seq", axis=1, tiled=True) for a in (x_in, m_in))
    w_in, w_out = (lax.all_gather(a, everywhere, axis=0, tiled=True) for a in (attn_in, attn_out))
    e_in, e_out = (lax.all_gather(a, peers, axis=0, tiled=True) for a in (e_in, e_out))
    w_in = w_in.reshape(6, width, width)
    w_out = w_out.reshape(2, width, width)
    x_all = x_all.reshape(packs * group, width)
    m_all = m_all.reshape(packs * group, width)
    wide = group + rows
    query_pos = rank * rows + jnp.arange(rows, dtype=jnp.int32)
    key_pos = jnp.arange(group, dtype=jnp.int32)
    ends = jnp.cumsum(doc_lengths[:, 0, 0], axis=1)
    query_doc = jnp.sum((query_pos[None, :, None] >= ends[:, None, :]).astype(jnp.int32), axis=2)
    key_doc = jnp.sum((key_pos[None, :, None] >= ends[:, None, :]).astype(jnp.int32), axis=2)
    same = query_doc[:, :, None] == key_doc[:, None, :]
    causal = same & (key_pos[None, None, :] <= query_pos[None, :, None])
    bucket_hot = (rel_buckets[:, None] == jnp.arange(buckets, dtype=jnp.int32)).astype(F32)
    line_at = jnp.arange(group + rows, dtype=jnp.int32) - (group - 1) + rank * rows
    line_hot = (jnp.take(rel_buckets, jnp.clip(line_at, 0, group - 1))[None, :] == jnp.arange(buckets)[:, None]).astype(F32)
    line = jnp.einsum("bh,bj->hj", bias_table, line_hot, precision=HIGHEST)
    line = line[:, ::-1]
    wide = group + rows
    tiled = jnp.broadcast_to(line[:, None, :], (HEADS, rows, wide)).reshape(HEADS, rows * wide)
    skew = tiled[:, rows : rows + rows * (wide - 1)].reshape(HEADS, rows, wide - 1)[:, :, :group]

    normed1_all = norm_apply(x_all.astype(F32), gains[0]).astype(BF)
    normed1 = norm_apply(x_rows, gains[0]).astype(BF)
    query = times(normed1, w_in[0]).astype(BF)
    keys = times(normed1_all, w_in[1]).astype(BF)
    values = times(normed1_all, w_in[2]).astype(BF)
    mem_keys = times(m_all, w_in[4]).astype(BF)
    mem_values = times(m_all, w_in[5]).astype(BF)
    mixed, chances_self = attend(query, keys, values, causal, skew[None], packs)
    hidden1 = x_rows + times(mixed, w_out[0])
    normed2 = norm_apply(hidden1, gains[1]).astype(BF)
    cross_query = times(normed2, w_in[3]).astype(BF)
    cross_mixed, chances_cross = attend(cross_query, mem_keys, mem_values, same, 0.0, packs)
    hidden2 = hidden1 + times(cross_mixed, w_out[1])
    normed3 = norm_apply(hidden2, gains[2]).astype(BF)

    routing = jax.nn.softmax(times(normed3, router), axis=1)
    route = routes[:, 0, 0, :, 0]
    route_hot = (route[:, :, None] == jnp.arange(experts, dtype=jnp.int32)).astype(jnp.int32)
    slot = jnp.sum((jnp.cumsum(route_hot, axis=1) - route_hot) * route_hot, axis=2)
    hot = route_hot.reshape(packs * rows, experts).astype(F32)
    gate = jnp.sum(routing * hot, axis=1)
    target = jnp.where(slot < capacity, (route * packs + jnp.arange(packs)[:, None]) * capacity + slot, -1).reshape(-1)
    dispatch = (target[:, None] == jnp.arange(experts * packs * capacity, dtype=jnp.int32)).astype(BF)

    def swap(a):
        shape = (experts, packs * capacity, width)
        return lax.all_to_all(a.reshape(shape), "expert", split_axis=0, concat_axis=0, tiled=True).reshape(-1, width)

    received = swap(times_left(dispatch, normed3).astype(BF))
    inner = times(received, e_in)
    hidden, pull = jax.vjp(gelu_tanh, inner)
    hidden = hidden.astype(BF)
    result = times(hidden, e_out).astype(BF)
    combined = times(dispatch, swap(result))
    out_rows = (hidden2 + gate[:, None] * combined).astype(BF)
    grad_top = cotangent.reshape(packs * rows, width).astype(F32)
    grad_gate = jnp.sum(grad_top * combined, axis=1)
    grad_result = swap(times_left(dispatch, (gate[:, None] * grad_top).astype(BF)).astype(BF))
    grad_hidden = times_right(grad_result, e_out)
    grad_eout = times_left(hidden, grad_result).astype(BF)
    grad_inner = pull(grad_hidden)[0].astype(BF)
    grad_ein = times_left(received, grad_inner).astype(BF)
    grad_send = swap(times_right(grad_inner, e_in).astype(BF))
    grad_logits = grad_gate[:, None] * routing * (hot - gate[:, None])
    grad_router = jnp.einsum("td,te->de", normed3.astype(F32), grad_logits, precision=HIGHEST)
    grad_normed3 = times(dispatch, grad_send) + jnp.einsum(
        "te,de->td", grad_logits, router.astype(F32), precision=HIGHEST
    )
    back3, gain3 = norm_back(hidden2, gains[2], grad_normed3)
    grad_h2 = grad_top + back3
    grad_h2_low = grad_h2.astype(BF)
    grad_wco = times_left(cross_mixed, grad_h2_low)
    grad_cross = times_right(grad_h2_low, w_out[1]).astype(BF)
    grad_cq, grad_ck, grad_cv, _ = attend_back(cross_query, mem_keys, mem_values, chances_cross, grad_cross, packs)
    back2, gain2 = norm_back(hidden1, gains[1], times_right(grad_cq, w_in[3]))
    grad_h1 = grad_h2 + back2
    grad_h1_low = grad_h1.astype(BF)
    grad_wso = times_left(mixed, grad_h1_low)
    grad_mixed = times_right(grad_h1_low, w_out[0]).astype(BF)
    grad_q, grad_k, grad_v, grad_scores = attend_back(query, keys, values, chances_self, grad_mixed, packs)

    total = jnp.sum(grad_scores.astype(F32), axis=0)[:, ::-1]
    padded = jnp.pad(total, ((0, 0), (0, 0), (0, wide - group))).reshape(HEADS, rows * wide)
    diagonal = padded[:, : rows * (wide - 1)].reshape(HEADS, rows, wide - 1).sum(axis=1)
    at = jnp.clip(rank * rows + (rows - 1) - jnp.arange(wide - 1, dtype=jnp.int32), 0, group - 1)
    diagonal_hot = (jnp.take(rel_buckets, at)[:, None] == jnp.arange(buckets)).astype(F32)
    grad_table = jnp.einsum("jb,hj->bh", diagonal_hot, diagonal, precision=HIGHEST)

    def to_owner(a):
        return lax.psum_scatter(a.reshape(packs, group, width), "seq", scatter_dimension=1, tiled=True)

    grad_memory = to_owner((times_right(grad_ck, w_in[4]) + times_right(grad_cv, w_in[5])).astype(BF))
    part1 = to_owner((times_right(grad_k, w_in[1]) + times_right(grad_v, w_in[2])).astype(BF))
    grad_normed1 = times_right(grad_q, w_in[0]) + part1.reshape(packs * rows, width).astype(F32)
    back1, gain1 = norm_back(x_rows, gains[0], grad_normed1)
    grad_x = grad_h1 + back1
    grad_in = jnp.concatenate(
        [
            times_left(normed1, grad_q),
            times_left(normed1_all, grad_k),
            times_left(normed1_all, grad_v),
            times_left(normed2, grad_cq),
            times_left(m_all, grad_ck),
            times_left(m_all, grad_cv),
        ]
    ).astype(BF)
    grad_out = jnp.concatenate([grad_wso, grad_wco]).astype(BF)
    shards = [
        lax.psum_scatter(a, over, scatter_dimension=0, tiled=True).astype(F32)
        for a, over in ((grad_in, everywhere), (grad_out, everywhere), (grad_ein, peers), (grad_eout, peers))
    ]
    small = lax.psum((jnp.stack([gain1, gain2, gain3]), grad_table, grad_router), ("dp", "seq", "expert"))
    shape = (packs, 1, 1, rows, width)
    return (
        out_rows.reshape(shape),
        grad_x.reshape(shape),
        grad_memory.astype(F32).reshape(shape),
        *small,
        shards[0],
        shards[1],
        shards[2][None],
        shards[3][None],
    )


def solution(mesh):
    tokens = P(None, "dp", "expert", "seq", None)
    dense = P(("dp", "seq", "expert"), None)
    expert = P("expert", ("dp", "seq"), None)
    return jax.shard_map(
        per_device,
        mesh=mesh,
        in_specs=(tokens, tokens, tokens, tokens, P(None, "dp", "expert", None), P(), P(), P(), P(),
                  dense, dense, expert, expert),
        out_specs=(tokens, tokens, tokens, P(), P(), P(), dense, dense, expert, expert),
        check_vma=False,
    )
```

```python
import functools

import jax
import jax.numpy as jnp
from jax import lax
from jax.experimental import pallas as pl
from jax.experimental.pallas import tpu as pltpu
from jax.sharding import PartitionSpec as P

HEADS = 12
HEAD = 64

EPS = 1e-06
NEG = -1e30
HIGHEST = lax.Precision.HIGHEST
MESH = pl.DeviceIdType.MESH
BF = jnp.bfloat16
F32 = jnp.float32


class Place:
    def __init__(self):
        self.nz, self.ns, self.ny = (lax.axis_size(a) for a in ("dp", "seq", "expert"))
        self.nx = self.ns // 2
        self.z, self.s, self.y = (lax.axis_index(a) for a in ("dp", "seq", "expert"))
        self.x, self.c = self.s // 2, lax.rem(self.s, 2)

    def device(self, z=None, x=None, c=None, y=None):
        z = self.z if z is None else z
        x = self.x if x is None else x
        c = self.c if c is None else c
        y = self.y if y is None else y
        return (z, x * 2 + c, y)

    def other_x(self):
        return [lax.rem(self.x + k, self.nx) for k in range(1, self.nx)]

    def other_y(self):
        return [lax.rem(self.y + k, self.ny) for k in range(1, self.ny)]

    def by_distance(self, k):
        half = self.nz // 2
        order = [
            sorted(range(self.nz), key=lambda d: (abs(d - z), (d < half) != (z < half), d)) for z in range(self.nz)
        ]
        return self.pick([row[k] for row in order])

    def pick(self, values):
        out = jnp.int32(values[0])
        for z in range(1, self.nz):
            out = jnp.where(self.z == z, jnp.int32(values[z]), out)
        return out

    def greet(self):
        barrier = pltpu.get_barrier_semaphore()
        for x in self.other_x():
            pl.semaphore_signal(barrier, inc=1, device_id=self.device(x=x), device_id_type=MESH)
        for y in self.other_y():
            pl.semaphore_signal(barrier, inc=1, device_id=self.device(y=y), device_id_type=MESH)
        pl.semaphore_signal(barrier, inc=1, device_id=self.device(c=1 - self.c), device_id_type=MESH)

        for k in range(1, self.nz):
            z = lax.rem(self.z + k, self.nz)
            pl.semaphore_signal(barrier, inc=1, device_id=self.device(z=z), device_id_type=MESH)
        pl.semaphore_wait(barrier, self.nx - 1 + self.ny - 1 + 1 + self.nz - 1)


def rms_rows(src, gain, dst, rows, step=64):
    @pl.loop(0, rows // step)
    def _(i):
        at = pl.ds(pl.multiple_of(i * step, step), step)
        value = src[at, :].astype(F32)
        r = lax.rsqrt(jnp.mean(value * value, axis=-1, keepdims=True) + EPS)
        dst[at, :] = (value * r * gain).astype(BF)


def block(weight, index, lanes=slice(None), share=(0, 1)):
    unit, width = weight.shape[-2:]
    count = width // unit // share[1]
    first = pl.multiple_of(index * (width // unit) + share[0] * count, count)
    value = weight[pl.ds(first, count), :, lanes]
    return value.reshape(count * unit, value.shape[-1])


def project(left, weight, index, dst):
    width = dst.shape[-1]
    step = 256 if width % 256 == 0 else width

    @pl.loop(0, width // step)
    def _(j):
        at = pl.ds(pl.multiple_of(j * step, step), step)
        dst[:, at] = jnp.dot(left[...], block(weight, index, at), preferred_element_type=F32).astype(dst.dtype)


def prepare_bias(rel, table, bias, rank, rows, group):
    heads, buckets = table.shape
    wide = group + 128
    lane = lax.broadcasted_iota(jnp.int32, (group, wide), 1)
    shift = jnp.where(lane < group, lane, lane - wide)
    distance = jnp.clip(rank * rows - shift, 0, group - 1)
    hot = (lax.broadcasted_iota(jnp.int32, (group, wide), 0) == distance).astype(F32).astype(BF)
    which = jnp.dot(jnp.broadcast_to(rel[...].astype(F32), (8, group)).astype(BF), hot, preferred_element_type=F32)
    picks = (lax.broadcasted_iota(jnp.int32, (buckets, wide), 0) == which[0:1].astype(jnp.int32)).astype(F32)
    line = jnp.dot(table[...], picks, precision=HIGHEST, preferred_element_type=F32)
    for h in range(heads):
        band = pltpu.roll(jnp.broadcast_to(line[h : h + 1], (rows, wide)), 0, 1, stride=1, stride_axis=0)
        bias[h // 2, pl.ds((h % 2) * rows, rows), :] = band[:, :group]


def prepare_masks(lengths, same, causal, rank, rows, group):
    key = lax.broadcasted_iota(jnp.int32, (rows, group), 1)
    query = rank * rows + lax.broadcasted_iota(jnp.int32, (rows, group), 0)
    for p in range(same.shape[0]):
        end = jnp.int32(0)
        kd = jnp.zeros((rows, group), jnp.int32)
        qd = jnp.zeros((rows, group), jnp.int32)
        for n in range(lengths.shape[1]):
            end = end + lengths[p, n]
            kd = kd + jnp.where(key >= end, 1, 0)
            qd = qd + jnp.where(query >= end, 1, 0)
        same[p] = jnp.where(kd == qd, 0.0, NEG)
        causal[p] = jnp.where((kd == qd) & (key <= query), 0.0, NEG)


def two_heads(pair):
    first = lax.broadcasted_iota(jnp.int32, pair.shape, 1) < HEAD
    zero = jnp.zeros_like(pair)
    return jnp.concatenate([jnp.where(first, pair, zero), jnp.where(first, zero, pair)], axis=0)


def one_pair(stacked):
    rows = stacked.shape[0] // 2
    first = lax.broadcasted_iota(jnp.int32, (rows, stacked.shape[1]), 1) < HEAD
    return jnp.where(first, stacked[:rows], stacked[rows:])


def attend_pairs(query, keys, values, bias, mask, chances, mixed):
    packs, pairs, double, group = chances.shape
    rows = double // 2

    def body(i, carry):
        p, j = i // pairs, lax.rem(i, pairs)
        mine = pl.ds(pl.multiple_of(p * rows, rows), rows)
        theirs = pl.ds(pl.multiple_of(p * group, group), group)
        lanes = pl.ds(pl.multiple_of(j * 128, 128), 128)
        scores = lax.dot_general(
            two_heads(query[mine, lanes]), keys[theirs, lanes], (((1,), (1,)), ((), ())), preferred_element_type=F32
        )
        scores = scores * HEAD**-0.5
        if bias is not None:
            scores = scores + bias[j]
        scores = (scores.reshape(2, rows, group) + mask[p][None]).reshape(double, group)
        raised = jnp.exp(scores - jnp.max(scores, axis=1, keepdims=True))
        weights = (raised * (1.0 / jnp.sum(raised, axis=1, keepdims=True))).astype(BF)
        chances[p, j] = weights
        out = jnp.dot(weights, values[theirs, lanes], preferred_element_type=F32)
        mixed[mine, lanes] = one_pair(out).astype(BF)
        return carry

    lax.fori_loop(0, packs * pairs, body, 0, unroll=6)


def add_product(total, left, weight, index):
    width = total.shape[-1]
    step = 256 if width % 256 == 0 else width

    @pl.loop(0, width // step)
    def _(j):
        at = pl.ds(pl.multiple_of(j * step, step), step)
        total[:, at] += jnp.dot(left[...], block(weight, index, at), preferred_element_type=F32)


def product_t(left, weight, index, dst):
    halves = 2
    step = weight.shape[-1] // halves

    @pl.loop(0, halves)
    def _(j):
        rows = block(weight, index, share=(j, halves))
        out = lax.dot_general(left[...], rows, (((1,), (1,)), ((), ())), preferred_element_type=F32)
        dst[:, pl.ds(pl.multiple_of(j * step, step), step)] = out.astype(dst.dtype)


def two_products_t(left1, index1, left2, index2, weight, dst):
    halves = 2
    step = weight.shape[-1] // halves

    @pl.loop(0, halves)
    def _(j):
        out = 0.0
        for left, index in ((left1, index1), (left2, index2)):
            rows = block(weight, index, share=(j, halves))
            out = out + lax.dot_general(left[...], rows, (((1,), (1,)), ((), ())), preferred_element_type=F32)
        dst[:, pl.ds(pl.multiple_of(j * step, step), step)] = out.astype(dst.dtype)


def outer_product(left, right, dst, index):
    unit, width = dst.shape[-2:]
    halves = 2
    step, count = width // halves, width // unit // halves

    @pl.loop(0, halves)
    def _(j):
        part = left[:, pl.ds(pl.multiple_of(j * step, step), step)]
        out = lax.dot_general(part, right[...], (((0,), (0,)), ((), ())), preferred_element_type=F32)
        first = index * (width // unit) + j * count
        dst[pl.ds(first, count)] = out.astype(dst.dtype).reshape(count, unit, width)


def add_into(total, other):
    lead = total.shape[:-2]
    count = 1
    for n in lead:
        count *= n
    rows = total.shape[-2]
    step = next(n for n in ((48, 32, 16) if total.shape[-1] <= 1024 else (16,)) if rows % n == 0)

    def body(i, carry):
        index = []
        rest = i // (rows // step)
        for n in reversed(lead):
            index.insert(0, lax.rem(rest, n))
            rest = rest // n
        r = pl.ds(pl.multiple_of(lax.rem(i, rows // step) * step, 16), step)
        at = (*index, r)
        total[at] = (total[at].astype(F32) + other[at].astype(F32)).astype(total.dtype)
        return carry

    lax.fori_loop(0, count * (rows // step), body, 0)


def norm_back_rows(value, gain, grad, total, gain_grad, step=64):
    gain_grad[...] = jnp.zeros_like(gain_grad)

    @pl.loop(0, value.shape[0] // step)
    def _(i):
        at = pl.ds(pl.multiple_of(i * step, step), step)
        v, g = value[at, :].astype(F32), grad[at, :]
        r = lax.rsqrt(jnp.mean(v * v, axis=-1, keepdims=True) + EPS)
        scaled = g * gain
        total[at, :] += r * scaled - v * (r * r * r) * jnp.mean(scaled * v, axis=-1, keepdims=True)
        gain_grad[...] += jnp.sum(g * v * r, axis=0, keepdims=True)


def attend_pairs_back(query, keys, values, chances, grad, grad_q, grad_k, grad_v, diagonal):
    packs, pairs, double, group = chances.shape
    rows = double // 2
    scale = HEAD**-0.5

    def body(i, carry):
        p, j = i // pairs, lax.rem(i, pairs)
        mine = pl.ds(pl.multiple_of(p * rows, rows), rows)
        theirs = pl.ds(pl.multiple_of(p * group, group), group)
        lanes = pl.ds(pl.multiple_of(j * 128, 128), 128)
        ga = two_heads(grad[mine, lanes])
        low = chances[p, j]
        wide = low.astype(F32)
        gp = lax.dot_general(ga, values[theirs, lanes], (((1,), (1,)), ((), ())), preferred_element_type=F32)
        gs = (wide * (gp - jnp.sum(wide * gp, axis=1, keepdims=True))).astype(BF)
        gq = jnp.dot(gs, keys[theirs, lanes], preferred_element_type=F32)
        grad_q[mine, lanes] = (one_pair(gq) * scale).astype(BF)
        gk = lax.dot_general(gs, two_heads(query[mine, lanes]), (((0,), (0,)), ((), ())), preferred_element_type=F32)
        grad_k[theirs, lanes] = (gk * scale).astype(BF)
        gv = lax.dot_general(low, ga, (((0,), (0,)), ((), ())), preferred_element_type=F32)
        grad_v[theirs, lanes] = gv.astype(BF)
        if diagonal is not None:
            a = lax.broadcasted_iota(jnp.int32, (rows, rows), 0)
            b = lax.broadcasted_iota(jnp.int32, (rows, rows), 1)
            flip = (a + b == rows - 1).astype(F32).astype(BF)
            for half in range(2):
                turned = jnp.dot(flip, gs[half * rows : (half + 1) * rows], preferred_element_type=F32)
                turned = jnp.concatenate([turned, jnp.zeros((rows, 128), F32)], axis=1)
                band = pltpu.roll(turned, 0, 1, stride=1, stride_axis=0)
                diagonal[pl.ds(2 * j + half, 1), :] += jnp.sum(band, axis=0, keepdims=True)
        return carry

    lax.fori_loop(0, packs * pairs, body, 0, unroll=6)


def table_grad(rel, diagonal, rank, rows, group):
    wide = group + 128
    lane = lax.broadcasted_iota(jnp.int32, (group, wide), 1)
    distance = jnp.clip(rank * rows + rows - 1 - lane, 0, group - 1)
    hot = (lax.broadcasted_iota(jnp.int32, (group, wide), 0) == distance).astype(F32).astype(BF)
    which = jnp.dot(jnp.broadcast_to(rel[...].astype(F32), (8, group)).astype(BF), hot, preferred_element_type=F32)
    picks = (lax.broadcasted_iota(jnp.int32, (128, wide), 0) == which[0:1].astype(jnp.int32)).astype(F32)
    return lax.dot_general(diagonal[...], picks, (((1,), (1,)), ((), ())), precision=HIGHEST, preferred_element_type=F32)


def route_slots(route, experts, capacity):
    packs, _, rows = route.shape
    count = packs * rows
    same = lax.broadcasted_iota(jnp.int32, (rows, rows), 0) == lax.broadcasted_iota(jnp.int32, (rows, rows), 1)
    column = jnp.concatenate(
        [jnp.sum(jnp.where(same, route[p], 0), axis=1, keepdims=True) for p in range(packs)], axis=0
    )
    hot = (column == lax.broadcasted_iota(jnp.int32, (count, experts), 1)).astype(F32)
    a = lax.broadcasted_iota(jnp.int32, (count, count), 0)
    b = lax.broadcasted_iota(jnp.int32, (count, count), 1)
    earlier = ((b < a) & (a // rows == b // rows)).astype(F32).astype(BF)
    before = jnp.dot(earlier, hot.astype(BF), preferred_element_type=F32)
    slot = jnp.sum(before * hot, axis=1, keepdims=True).astype(jnp.int32)
    pack = lax.broadcasted_iota(jnp.int32, (count, 1), 0) // rows
    target = jnp.where(slot < capacity, (column * packs + pack) * capacity + slot, -1)
    slots = lax.broadcasted_iota(jnp.int32, (count, experts * packs * capacity), 1)
    return hot, (target == slots).astype(F32).astype(BF)


def gelu_both(z):
    c = 0.7978845608028654
    t = jnp.tanh(c * (z + 0.044715 * (z * z * z)))
    half = 0.5 * (1.0 + t)
    slope = half + 0.5 * z * (1.0 - t * t) * (c * (1.0 + 3 * 0.044715 * (z * z)))
    return z * half, slope


def continue_waits(waits, hop, d, at):
    def wait():
        @pl.when(d < at.z)
        def _():
            hop(-1).wait_send()

        @pl.when(d > at.z)
        def _():
            hop(1).wait_send()

    waits.append(wait)


def layer_body(lengths, rel, gains, table, router_t, route, x_ref, m_ref, g_ref, ain, aout, ein, eout,
               out_rows, o0, o1, o2, o3, grad_x, grad_mem, sum_gains, sum_router, sum_table,
               w, big, ge, prep, c2, c3, y0, y1, x0, x1, ex_in, z0, z1, z2, z3,
               xo, mo, n1_all, k_, v, kc, vc, gv, n1, q, mixed, n2, qc, cross_mixed, n3, gb, ga, gq,
               pr_self, pr_cross, h1, h2, gn, bias, same, causal, diagonal, gain_row,
               act_core, act_x, wide_sum, table_sum, wide_in, table_in,
               slots_out, slots_in, slots_acc, ret_out, ret_in, back_in, hid, gin_,
               act_send, act_recv, prep_send, prep_recv, line_send, side_send, spread_send, ici_recv, spread_recv, own_sem,
               core_send, core_recv, y_send, y_recv, x_send, x_recv, ex_send, ex_recv, z_send, z_recv, zd_send, zd_recv,
               sum_send, sum_recv, small_send, small_recv, slot_send, slot_recv, free_sem):
    at = Place()
    nz, nx, ny = at.nz, at.nx, at.ny
    packs, tok, width = x_ref.shape
    group = xo.shape[0] // packs
    experts = router_t.shape[0]
    unit = ain.shape[1]
    block_units = eout.shape[0]
    panels = block_units // nx
    columns = ein.shape[1] // (nz * nx)
    buckets = table.shape[1]
    gk = xo
    units = (ain.shape[0], aout.shape[0])
    tall = nz * nx * 2
    bases = (0, tall * ny * units[0], 0, 2 * nz * block_units)
    dense, e_in, e_out = (0, 1), 2, 3
    experts_ = (e_in, e_out)
    waits = []

    def remote(src, dst, ssem, rsem, **where):
        return pltpu.make_async_remote_copy(
            src_ref=src, dst_ref=dst, send_sem=ssem, recv_sem=rsem,
            device_id=at.device(**where), device_id_type=MESH,
        )

    def send(*args, **where):
        one = remote(*args, **where)
        one.start()
        waits.append(one.wait_send)
        return one

    def arrive(ref, sem):
        pltpu.make_async_copy(ref, ref, sem).wait()

    def spot(a, z, x, c, y):
        index = ((z * nx + x) * 2 + c) * ny + y
        return w.at[pl.ds(bases[a] + index * units[a], units[a])]

    def pack_of(a, z, c):
        return big.at[pl.ds(bases[a] + (z * 2 + c) * block_units, block_units)]

    shards = (ain, aout)
    acts = ((x_ref, xo), (m_ref, mo))

    at.greet()

    def act_rows(full, p, x, c):
        return full.at[pl.ds(pl.multiple_of(p * group + (x * 2 + c) * tok, 16), tok)]

    own_waits = []

    def send_acts():
        for i, (src, full) in enumerate(acts):
            for p in range(packs):
                dst = act_rows(full, p, at.x, at.c)
                for k, x in enumerate(at.other_x()):
                    send(src.at[p], dst, act_send.at[i, p, k], act_recv.at[i, p, at.x, at.c], x=x)
                send(src.at[p], dst, act_send.at[i, p, nx - 1 + at.x], act_recv.at[i, p, at.x, at.c], c=1 - at.c)
                own = pltpu.make_async_copy(src.at[p], dst, own_sem.at[4 + i, p])
                own.start()
                own_waits.append(own.wait)

    def along_line(a, z, src):
        dst = spot(a, z, at.x, at.c, at.y) if a in dense else pack_of(a, z, at.c)
        sem = ici_recv.at[a, z, at.x, at.y]
        left = (z >= at.z) & (at.z > 0)
        right = (z <= at.z) & (at.z < nz - 1)

        def one(side):
            return remote(src, dst, line_send.at[a, z, side], sem, z=at.z + 2 * side - 1)

        @pl.when(left)
        def _():
            one(0).start()

        @pl.when(right)
        def _():
            one(1).start()

        def wait():
            @pl.when(left)
            def _():
                one(0).wait_send()

            @pl.when(right)
            def _():
                one(1).wait_send()

        waits.append(wait)

    def to_core(a, z, x, y, src):
        dst = spot(a, z, x, at.c, y) if a in dense else pack_of(a, z, at.c)
        send(src, dst, spread_send.at[a, z, x, y], spread_recv.at[a, z, x, y], c=1 - at.c)

    zs = [at.by_distance(k) for k in range(nz)]

    def dense_events(k):
        z = zs[k]
        for a in dense:
            here = spot(a, z, at.x, at.c, at.y)
            src = here if k else shards[a]
            if k:
                arrive(here, ici_recv.at[a, z, at.x, at.y])
            else:
                own = pltpu.make_async_copy(shards[a], here, own_sem.at[a, 0])
                own.start()
                own_waits.append(own.wait)
            along_line(a, z, src)
            for j, x in enumerate(at.other_x()):
                send(src, here, side_send.at[a, z, j], ici_recv.at[a, z, at.x, at.y], x=x)
            for j, y in enumerate(at.other_y()):
                send(src, here, side_send.at[a, z, nx - 1 + j], ici_recv.at[a, z, at.x, at.y], y=y)
            to_core(a, z, at.x, at.y, src)

    def side_y(k):
        z = zs[k]
        for y in at.other_y():
            for a in dense:
                here = spot(a, z, at.x, at.c, y)
                arrive(here, ici_recv.at[a, z, at.x, y])
                if a == 1:
                    for j, x in enumerate(at.other_x()):
                        send(here, here, side_send.at[a, z, nx - 1 + ny - 1 + j + (nx - 1) * y],
                             ici_recv.at[a, z, at.x, y], x=x)
                to_core(a, z, at.x, y, here)

    def side_x(k):
        z = zs[k]
        for x in at.other_x():
            for a in dense:
                here = spot(a, z, x, at.c, at.y)
                arrive(here, ici_recv.at[a, z, x, at.y])
                if a == 0:
                    for j, y in enumerate(at.other_y()):
                        send(here, here, side_send.at[a, z, nx - 1 + ny - 1 + j + (ny - 1) * x],
                             ici_recv.at[a, z, x, at.y], y=y)
                to_core(a, z, x, at.y, here)

    def corner_events(k):
        z = zs[k]
        for a in dense:
            for y in at.other_y():
                for x in at.other_x():
                    here = spot(a, z, x, at.c, y)
                    arrive(here, ici_recv.at[a, z, x, y])
                    to_core(a, z, x, y, here)

    def act_events():
        for i, (src, full) in enumerate(acts):
            for p in range(packs):
                for x in at.other_x():
                    dst = act_rows(full, p, x, at.c)
                    arrive(dst, act_recv.at[i, p, x, at.c])
                    send(dst, dst, act_send.at[i, p, nx - 1 + x], act_recv.at[i, p, x, at.c], c=1 - at.c)

    def in_unit(z, c, x, n=1):
        return pl.ds(bases[e_in] + ((z * 2 + c) * nx + x) * panels, n * panels)

    def start_prep():
        for x in range(nx):
            for u in range(panels):
                each_z = width // columns
                prep[x, u] = jnp.concatenate(
                    [ein[:, (z * nx + x) * columns : (z * nx + x + 1) * columns] for z in range(u * each_z, (u + 1) * each_z)],
                    axis=1,
                )
        big[in_unit(at.z, at.c, at.x)] = prep[at.x]
        for j, x in enumerate(at.other_x()):
            send(prep.at[x], big.at[in_unit(at.z, at.c, at.x)], prep_send.at[j], prep_recv.at[at.x], x=x)

    def expert_events(k, kinds=experts_):
        z = zs[k]
        for a in kinds:
            here = pack_of(a, z, at.c)
            src = here
            if k:
                arrive(here, ici_recv.at[a, z, at.x, at.y])
            elif a == e_in:
                for x in at.other_x():
                    arrive(big.at[in_unit(at.z, at.c, x)], prep_recv.at[x])
            else:
                src = eout
                own = pltpu.make_async_copy(eout, here, own_sem.at[a, 0])
                own.start()
                own_waits.append(own.wait)
            along_line(a, z, src)
            to_core(a, z, 0, 0, src)

    def first_norm():
        for i, (src, full) in enumerate(acts):
            for p in range(packs):
                for x in range(nx):
                    arrive(act_rows(full, p, x, 1 - at.c), act_recv.at[i, p, x, 1 - at.c])
        for wait in own_waits:
            wait()
        rms_rows(xo, gains[0:1], n1_all, packs * group)
        for p in range(packs):
            h1[pl.ds(p * tok, tok), :] = x_ref[p].astype(F32)
            n1[pl.ds(p * tok, tok), :] = n1_all[pl.ds(pl.multiple_of(p * group + at.s * tok, tok), tok), :]

    places = [((z * 2 + c) * nx + x) * panels for z in range(nz) for x in range(nx) for c in range(2)]
    each = slots_out.shape[2]
    count = ny * each
    row_units = width // unit

    def keys_and_values(for_self):
        @pl.when(for_self)
        def _():
            project(n1_all, w, 1, k_)
            project(n1_all, w, 2, v)

        @pl.when(jnp.logical_not(for_self))
        def _():
            project(mo, w, 4, kc)
            project(mo, w, 5, vc)

    def by_slot(dispatch, rows):
        out = lax.dot_general(dispatch, rows, (((0,), (0,)), ((), ())), preferred_element_type=F32)
        return out.astype(BF).reshape(ny, each, width)

    slot_waits = []

    def slot_copy(late, src, dst, sem_from, sem_to, **where):
        one = remote(src, dst, slot_send.at[sem_from], slot_recv.at[sem_to], **where)
        one.start()
        (waits if late else slot_waits).append(one.wait_send)

    def y_sem(t, j):
        return t * (ny - 1) + j

    def x_sem(t, j, y):
        return 4 * (ny - 1) + (t * (nx - 1) + j) * ny + y

    def ret_sem(t, j, y):
        return 4 * (ny - 1) + 2 * (nx - 1) * ny + (t * (nx - 1) + j) * ny + y

    def send_slots(t):
        for j, y in enumerate(at.other_y()):
            slot_copy(False, slots_out.at[t, y], slots_in.at[t, at.x, at.y], y_sem(t, j), y_sem(t, ny - 2 - j), y=y)
        for j, x in enumerate(at.other_x()):
            slot_copy(False, slots_out.at[t, at.y], slots_in.at[t, at.x, at.y], x_sem(t, j, at.y),
                      x_sem(t, nx - 2 - j, at.y), x=x)
        slots_in[t, at.x, at.y] = slots_out[t, at.y]

    def summed(t, y):
        total = slots_acc[t, at.x, y]
        for j in range(nx - 1):
            arrive(ret_in.at[t, j, y], slot_recv.at[ret_sem(t, j, y)])
            total = total + ret_in[t, j, y].astype(F32)
        return total.astype(BF)

    cores, ys, xs, zs_ = {2: c2, 3: c3}, (y0, y1), (x0, x1), (z0, z1, z2, z3)
    outs = (o0, o1, o2, o3)
    far = [sorted(range(nz), key=lambda d: (-abs(d - z), d)) for z in range(nz)]
    order_e = [at.pick([far[z][k] for z in range(nz)]) for k in range(nz)]
    halves = [[d for d in row if d >= nz // 2] + [d for d in row if d < nz // 2] for row in far]
    order_d = [at.pick([halves[z][k] for z in range(nz)]) for k in range(nz)]
    e_waits = []

    def expert_part(a, d, c):
        return ge.at[pl.ds(bases[a] + (d * 2 + c) * block_units, block_units)]

    def start_expert(a, k):
        one = remote(expert_part(a, order_e[k], 1 - at.c), cores[a].at[k], core_send.at[a, k, 0],
                     core_recv.at[a, k, 0], c=1 - at.c)
        one.start()
        e_waits.append(one.wait_send)

    def core_expert(a, k):
        arrive(cores[a].at[k], core_recv.at[a, k, 0])
        add_into(cores[a].at[k], expert_part(a, order_e[k], at.c))

    def free_experts():
        for wait in e_waits:
            wait()
        pl.semaphore_signal(free_sem, inc=1, device_id=at.device(c=1 - at.c), device_id_type=MESH)

    def dense_part(a, d, x, c):
        return big.at[pl.ds(bases[a] + ((d * nx + x) * 2 + c) * ny * units[a], ny * units[a])]

    def dense_core(a, k, x, y=None, u=None):
        first = bases[a] // 2 + (k * nx + x) * ny * units[a]
        if y is None:
            return ge.at[pl.ds(first, ny * units[a])]
        if u is None:
            return ge.at[pl.ds(first + y * units[a], units[a])]
        return ge.at[pl.ds(first + y * units[a] + u, 1)]

    def xs_in_order():
        return [(x, True) for x in at.other_x()] + [(at.x, False)]

    def start_dense(k):
        for a in dense:
            for x in range(nx):
                send(dense_part(a, order_d[k], x, 1 - at.c), dense_core(a, k, x), core_send.at[a, k, x],
                     core_recv.at[a, k, x], c=1 - at.c)

    def first_dense(k):
        for x, _ in xs_in_order():
            arrive(dense_core(0, k, x), core_recv.at[0, k, x])
            add_into(dense_core(0, k, x), dense_part(0, order_d[k], x, at.c))
            for u in range(units[0]):
                for j, y in enumerate(at.other_y()):
                    send(dense_core(0, k, x, y, u), ys[0].at[k, ny - 2 - j, x, pl.ds(u, 1)],
                         y_send.at[k, j, x, u], y_recv.at[k, ny - 2 - j, x, u], y=y)
        for x, _ in xs_in_order():
            arrive(dense_core(1, k, x), core_recv.at[1, k, x])
            add_into(dense_core(1, k, x), dense_part(1, order_d[k], x, at.c))
        for j, x in enumerate(at.other_x()):
            send(dense_core(1, k, x), xs[1].at[k, nx - 2 - j], x_send.at[k, j, units[0]],
                 x_recv.at[k, nx - 2 - j, units[0]], x=x)

    def second_dense(k):
        for x, away in xs_in_order():
            for u in range(units[0]):
                total = ys[0].at[k, 0, x, pl.ds(u, 1)]
                for j in range(ny - 1):
                    piece = ys[0].at[k, j, x, pl.ds(u, 1)]
                    arrive(piece, y_recv.at[k, j, x, u])
                    add_into(total, piece if j else dense_core(0, k, x, at.y, u))
                if away:
                    j = lax.rem(x - at.x + nx, nx) - 1
                    send(total, xs[0].at[k, nx - 2 - j, pl.ds(u, 1)], x_send.at[k, j, u], x_recv.at[k, nx - 2 - j, u], x=x)
        for j in range(nx - 1):
            arrive(xs[1].at[k, j], x_recv.at[k, j, units[0]])
            add_into(xs[1].at[k, 0], xs[1].at[k, j] if j else dense_core(1, k, at.x))
        for j, y in enumerate(at.other_y()):
            send(xs[1].at[k, 0, pl.ds(y * units[1], units[1])], ys[1].at[k, ny - 2 - j],
                 y_send.at[k, j, nx, 0], y_recv.at[k, ny - 2 - j, nx, 0], y=y)

    def piece_of(k, p):
        return xs[0].at[k, 0, pl.ds(p, 1)] if p < units[0] else ys[1].at[k, 0]

    def inbox_of(slot, p):
        return zs_[0].at[slot, pl.ds(p, 1)] if p < units[0] else zs_[1].at[slot]

    def line_dense(k):
        d = order_d[k]
        for p in range(units[0] + 1):
            total = piece_of(k, p)
            if p < units[0]:
                for j in range(nx - 1):
                    piece = xs[0].at[k, j, pl.ds(p, 1)]
                    arrive(piece, x_recv.at[k, j, p])
                    add_into(total, piece if j else ys[0].at[k, 0, at.x, pl.ds(p, 1)])
            else:
                for j in range(ny - 1):
                    arrive(ys[1].at[k, j], y_recv.at[k, j, nx, 0])
                    add_into(total, ys[1].at[k, j] if j else xs[1].at[k, 0, pl.ds(at.y * units[1], units[1])])
            for side in range(2):

                @pl.when((at.z > 0) & (d > at.z) if side == 0 else (at.z < nz - 1) & (d < at.z))
                def _(total=total, p=p):
                    arrive(inbox_of(d, p), zd_recv.at[d, p])
                    add_into(total, inbox_of(d, p))

            def hop(to, total=total, p=p):
                slot = d if to > 0 else jnp.where(d == at.z - 1, nz, d)
                return remote(total, inbox_of(slot, p), zd_send.at[k, p], zd_recv.at[slot, p], z=at.z + to)

            @pl.when(d < at.z)
            def _(hop=hop):
                hop(-1).start()

            @pl.when(d > at.z)
            def _(hop=hop):
                hop(1).start()

            continue_waits(waits, hop, d, at)

    def finish_dense():
        for k in (nz // 2 - 1, nz - 1):

            @pl.when(order_d[k] == at.z)
            def _(k=k):
                for p in range(units[0] + 1):
                    total = piece_of(k, p)
                    for side, here in enumerate((at.z > 0, at.z < nz - 1)):
                        slot = at.z if side == 0 else nz

                        @pl.when(here)
                        def _(total=total, slot=slot, p=p):
                            arrive(inbox_of(slot, p), zd_recv.at[slot, p])
                            add_into(total, inbox_of(slot, p))

                write_out(0, xs[0].at[k, 0])
                write_out(1, ys[1].at[k, 0])

    def write_out(a, total):
        if a != e_in:
            outs[a][...] = total[...].astype(F32).reshape(outs[a].shape)
            return
        for j, x in enumerate(at.other_x()):
            send(total.at[pl.ds(x * panels, panels)], ex_in.at[nx - 2 - j], ex_send.at[j], ex_recv.at[nx - 2 - j], x=x)

    def finish_expert_in():
        for j in range(nx - 1):
            arrive(ex_in.at[j], ex_recv.at[j])
        total = cores[e_in].at[nz - 1]
        for x in range(nx):
            for u in range(panels):
                value = None
                for j, other in enumerate(at.other_x()):
                    value = ex_in[j, u] if value is None else jnp.where(other == x, ex_in[j, u], value)
                mine = total[pl.ds(at.x * panels + u, 1)][0]
                value = jnp.where(at.x == x, mine.astype(F32), value.astype(F32))
                for i in range(width // columns):
                    z = u * (width // columns) + i
                    outs[e_in][:, (z * nx + x) * columns : (z * nx + x + 1) * columns] = value[:, i * columns : (i + 1) * columns]

    def line(kind, k):
        for a in kind:
            d = order_e[k]
            total = cores[a].at[k]
            for side in range(2):
                feeds = (at.z > 0) & (d >= at.z) if side == 0 else (at.z < nz - 1) & (d <= at.z)
                slot = d if side == 0 else jnp.where(d == at.z, nz, d)

                @pl.when(feeds)
                def _(a=a, slot=slot, total=total):
                    arrive(zs_[a].at[slot], z_recv.at[a, slot])
                    add_into(total, zs_[a].at[slot])

            def hop(to, a=a, total=total, d=d):
                slot = d if to > 0 else jnp.where(d == at.z - 1, nz, d)
                return remote(total, zs_[a].at[slot], z_send.at[a, k], z_recv.at[a, slot], z=at.z + to)

            @pl.when(d < at.z)
            def _(hop=hop):
                hop(-1).start()

            @pl.when(d > at.z)
            def _(hop=hop):
                hop(1).start()

            if k == nz - 1:
                write_out(a, total)
            continue_waits(waits, hop, d, at)

    def start_act(i):
        for p in range(packs):
            for x in range(nx):
                send(act_rows((kc, k_)[i], p, x, 1 - at.c), act_core.at[i, p, x], sum_send.at[i, p, x],
                     sum_recv.at[i, p, x], c=1 - at.c)

    def core_act(i):
        for p in range(packs):
            for x in range(nx):
                arrive(act_core.at[i, p, x], sum_recv.at[i, p, x])
                add_into(act_core.at[i, p, x], act_rows((kc, k_)[i], p, x, at.c))
        for j, x in enumerate(at.other_x()):
            send(act_core.at[i, :, x], act_x.at[i, nx - 2 - j], sum_send.at[i, packs, j], sum_recv.at[i, packs, nx - 2 - j], x=x)

    def x_act(i):
        for j in range(nx - 1):
            arrive(act_x.at[i, j], sum_recv.at[i, packs, j])
        for p in range(packs):
            out = act_core[i, p, at.x].astype(F32)
            for j in range(nx - 1):
                out = out + act_x[i, j, p].astype(F32)
            if i == 0:
                grad_mem[pl.ds(p * tok, tok), :] = out
            else:
                gn[pl.ds(p * tok, tok), :] += out

    pair_sums = ((wide_sum, wide_in), (table_sum, table_in))
    stages = [("c", [1 - at.c]), ("y", at.other_y()), ("x", at.other_x())]

    def start_small(t):
        axis, peers = stages[t]
        base = [0, 1, ny][t]
        for i, (total, inbox) in enumerate(pair_sums):
            for j, peer in enumerate(peers):
                back = base + len(peers) - 1 - j
                send(total.at[t], inbox.at[back], small_send.at[i, base + j], small_recv.at[i, back], **{axis: peer})

    def end_small(t):
        axis, peers = stages[t]
        base = [0, 1, ny][t]
        for i, (total, inbox) in enumerate(pair_sums):
            out = total[t]
            for j in range(len(peers)):
                arrive(inbox.at[base + j], small_recv.at[i, base + j])
                out = out + inbox[base + j]
            total[t + 1] = out

    tail = ny + nx - 1

    def start_line():
        for i, (total, inbox) in enumerate(pair_sums):
            for j in range(1, nz):
                z = lax.rem(at.z + j, nz)
                send(total.at[3], inbox.at[tail + at.z], small_send.at[i, tail + j], small_recv.at[i, tail + at.z], z=z)

    def end_line():
        for i, (total, inbox) in enumerate(pair_sums):
            for j in range(1, nz):
                z = lax.rem(at.z + j, nz)
                arrive(inbox.at[tail + z], small_recv.at[i, tail + z])
            out = None
            for z in range(nz):
                term = jnp.where(at.z == z, total[3], inbox[tail + z])
                out = term if out is None else out + term
            if i == 0:
                sum_gains[...] = out[: sum_gains.shape[0]]
                sum_router[...] = out[sum_gains.shape[0] : sum_gains.shape[0] + experts]
            else:
                sum_table[...] = out[: sum_table.shape[0], : sum_table.shape[1]]

    dense_events(0)
    dense_events(1)
    expert_events(0, (e_out,))
    send_acts()
    side_y(0)
    side_x(0)
    prepare_bias(rel, table, bias, at.s, tok, group)
    prepare_masks(lengths, same, causal, at.s, tok, group)
    hot, dispatch = route_slots(route, experts, each // packs)
    top = g_ref[...].astype(F32).reshape(packs * tok, width)
    start_prep()
    side_y(1)
    dense_events(2)
    side_x(1)
    dense_events(3)
    expert_events(1, (e_out,))
    expert_events(2, (e_out,))
    act_events()
    expert_events(0, (e_in,))
    corner_events(1)
    first_norm()
    corner_events(0)
    side_x(2)
    for a in dense:
        for z in zs[: nz // 2]:
            for x in range(nx):
                for y in range(ny):
                    arrive(spot(a, z, x, 1 - at.c, y), spread_recv.at[a, z, x, y])
    side_y(2)
    keys_and_values(at.z < nz // 2)
    side_x(3)
    side_y(3)
    expert_events(3, (e_out,))
    corner_events(2)
    expert_events(1, (e_in,))
    corner_events(3)
    for a in dense:
        for z in zs[nz // 2 :]:
            for x in range(nx):
                for y in range(ny):
                    arrive(spot(a, z, x, 1 - at.c, y), spread_recv.at[a, z, x, y])
    project(n1, w, 0, q)
    keys_and_values(at.z >= nz // 2)
    attend_pairs(q, k_, v, bias, causal, pr_self, mixed)
    add_product(h1, mixed, w, 6)
    rms_rows(h1, gains[1:2], n2, packs * tok)
    project(n2, w, 3, qc)
    attend_pairs(qc, kc, vc, None, same, pr_cross, cross_mixed)
    h2[...] = h1[...]
    add_product(h2, cross_mixed, w, 7)
    rms_rows(h2, gains[2:3], n3, packs * tok)
    slots_out[0] = by_slot(dispatch, n3[...])
    send_slots(0)
    logits = lax.dot_general(n3[...], router_t[...], (((1,), (1,)), ((), ())), preferred_element_type=F32)
    raised = jnp.exp(logits - jnp.max(logits, axis=1, keepdims=True))
    routing = raised / jnp.sum(raised, axis=1, keepdims=True)
    gate = jnp.sum(routing * hot, axis=1, keepdims=True)
    slots_out[1] = by_slot(dispatch, (gate * top).astype(BF))
    send_slots(1)
    expert_events(2, (e_in,))
    for t in range(2):
        for j, y in enumerate(at.other_y()):
            here = slots_in.at[t, at.x, y]
            arrive(here, slot_recv.at[y_sem(t, j)])
            for i, x in enumerate(at.other_x()):
                slot_copy(False, here, here, x_sem(t, i, y), x_sem(t, nx - 2 - i, y), x=x)
    expert_events(3, (e_in,))
    for t in range(2):
        for i, x in enumerate(at.other_x()):
            for y in range(ny):
                arrive(slots_in.at[t, x, y], slot_recv.at[x_sem(t, i, y)])
    for a in experts_:
        for z in range(nz):
            arrive(pack_of(a, z, 1 - at.c), spread_recv.at[a, z, 0, 0])
    here = slots_in[0].reshape(nx * count, width)
    grad_here = slots_in[1].reshape(nx * count, width)
    for u in range(panels):
        in_panel = jnp.concatenate([big[place + u] for place in places], axis=0)
        out_panel = big[pl.ds(bases[e_out] + u * row_units, row_units)].reshape(width, width)
        inner = jnp.dot(here, in_panel, preferred_element_type=F32)
        hidden, slope = gelu_both(inner)
        hid[u] = hidden.astype(BF)
        grad_hidden = lax.dot_general(grad_here, out_panel, (((1,), (1,)), ((), ())), preferred_element_type=F32)
        gin_[u] = (grad_hidden * slope).astype(BF)
        result = jnp.dot(hid[u], out_panel, preferred_element_type=F32).reshape(nx, ny, each, width)
        grad_slots = lax.dot_general(gin_[u], in_panel, (((1,), (1,)), ((), ())), preferred_element_type=F32)
        grad_slots = grad_slots.reshape(nx, ny, each, width)
        if u:
            slots_acc[0] += result
            slots_acc[1] += grad_slots
        else:
            slots_acc[0] = result
            slots_acc[1] = grad_slots
    for wait in waits:
        wait()
    waits.clear()
    for y in [*at.other_y(), at.y]:
        for t in range(2):
            for j, x in enumerate(at.other_x()):
                ret_out[t, j, y] = slots_acc[t, x, y].astype(BF)
                slot_copy(True, ret_out.at[t, j, y], ret_in.at[t, nx - 2 - j, y], ret_sem(t, j, y),
                          ret_sem(t, nx - 2 - j, y), x=x)
    for u in range(panels):
        grad = lax.dot_general(hid[u], grad_here, (((0,), (0,)), ((), ())), preferred_element_type=F32).astype(BF)
        ge[pl.ds(bases[e_out] + u * row_units, row_units)] = grad.reshape(row_units, unit, width)
    for k in range(nz):
        start_expert(e_out, k)
    for u in range(panels):
        grad = lax.dot_general(here, gin_[u], (((0,), (0,)), ((), ())), preferred_element_type=F32).astype(BF)
        for i, place in enumerate(places):
            ge[place + u] = grad[i * unit : (i + 1) * unit]
    for k in range(nz):
        start_expert(e_in, k)
    core_expert(e_out, 0)
    line((e_out,), 0)
    core_expert(e_out, 2)
    for wait in slot_waits:
        wait()
    for j, y in enumerate(at.other_y()):
        for t in range(2):
            slots_out[t, y] = summed(t, y)
            slot_copy(True, slots_out.at[t, y], back_in.at[t, at.y], y_sem(2 + t, j), y_sem(2 + t, ny - 2 - j), y=y)
    core_expert(e_out, 3)
    core_expert(e_in, 1)
    core_expert(e_out, 1)
    core_expert(e_in, 0)
    core_expert(e_in, 3)
    line((e_in,), 0)
    core_expert(e_in, 2)
    free_experts()
    for t in range(2):
        back_in[t, at.y] = summed(t, at.y)
    for t in range(2):
        for j, y in enumerate(at.other_y()):
            arrive(back_in.at[t, y], slot_recv.at[y_sem(2 + t, j)])
    combined = jnp.dot(dispatch, back_in[0].reshape(count, width), preferred_element_type=F32)
    rows_out = (h2[...] + gate * combined).astype(BF)
    for p in range(packs):
        out_rows[p] = rows_out[p * tok : (p + 1) * tok]
    grad_gate = jnp.sum(top * combined, axis=1, keepdims=True)
    grad_logits = grad_gate * routing * (hot - gate)
    diagonal[...] = jnp.zeros_like(diagonal)
    for i, (_, inbox) in enumerate(pair_sums):
        inbox[pl.ds(tail + at.z, 1)] = jnp.zeros_like(inbox[pl.ds(0, 1)])
    wide_sum[0] = jnp.zeros_like(wide_sum[0])
    wide_sum[0, pl.ds(3, experts), :] = lax.dot_general(
        grad_logits, n3[...].astype(F32), (((0,), (0,)), ((), ())), precision=HIGHEST, preferred_element_type=F32
    )
    grad_n3 = jnp.dot(dispatch, back_in[1].reshape(count, width), preferred_element_type=F32)
    for e in range(experts):
        grad_n3 = grad_n3 + grad_logits[:, e : e + 1] * router_t[e : e + 1, :].astype(F32)
    gn[...] = grad_n3
    grad_x[...] = top
    norm_back_rows(h2, gains[2:3], gn, grad_x, gain_row)
    wide_sum[0, 2:3, :] = gain_row[...]
    gb[...] = grad_x[...].astype(BF)
    product_t(gb, w, 7, ga)
    attend_pairs_back(qc, kc, vc, pr_cross, ga, gq, gk, gv, None)
    outer_product(cross_mixed, gb, big, 7)
    outer_product(n2, gq, big, 3)
    outer_product(mo, gk, big, 4)
    outer_product(mo, gv, big, 5)
    pl.semaphore_wait(free_sem, 1)
    start_dense(0)
    start_dense(1)
    two_products_t(gk, 4, gv, 5, w, kc)
    line((e_in,), 1)
    line((e_in,), 2)
    first_dense(0)
    start_act(0)
    product_t(gq, w, 3, gn)
    norm_back_rows(h1, gains[1:2], gn, grad_x, gain_row)
    wide_sum[0, 1:2, :] = gain_row[...]
    gb[...] = grad_x[...].astype(BF)
    product_t(gb, w, 6, ga)
    core_act(0)
    first_dense(1)
    attend_pairs_back(q, k_, v, pr_self, ga, gq, gk, gv, diagonal)
    two_products_t(gk, 1, gv, 2, w, k_)
    start_act(1)
    outer_product(n1, gq, big, 0)
    outer_product(n1_all, gk, big, 1)
    outer_product(n1_all, gv, big, 2)
    core_act(1)
    line((e_out,), 1)
    line((e_out,), 2)
    outer_product(mixed, gb, big, 6)
    start_dense(2)
    second_dense(0)
    product_t(gq, w, 0, gn)
    table_sum[0] = table_grad(rel, diagonal, at.s, tok, group)
    first_dense(2)
    second_dense(1)
    x_act(1)
    for p in range(packs):
        h1[pl.ds(p * tok, tok), :] = x_ref[p].astype(F32)
    norm_back_rows(h1, gains[0:1], gn, grad_x, gain_row)
    wide_sum[0, 0:1, :] = gain_row[...]
    start_small(0)
    start_dense(3)
    line_dense(0)
    end_small(0)
    start_small(1)
    second_dense(2)
    line((e_in,), 3)
    end_small(1)
    start_small(2)
    first_dense(3)
    line_dense(1)
    line_dense(2)
    line((e_out,), 3)
    end_small(2)
    start_line()
    second_dense(3)
    x_act(0)
    line_dense(3)
    finish_expert_in()
    end_line()
    finish_dense()
    for wait in waits:
        wait()


def shapes_of(layer_input, routes, attn_in, attn_out, expert_in, expert_out):
    nz, ns, ny = (lax.axis_size(a) for a in ("dp", "seq", "expert"))
    packs, tok, width = layer_input.shape[0], layer_input.shape[3], layer_input.shape[4]
    return nz, ns, ny, packs, tok, width


def fits_kernel(layer_input, routes, attn_in, attn_out, expert_in, expert_out):
    nz, ns, ny, packs, tok, width = shapes_of(layer_input, routes, attn_in, attn_out, expert_in, expert_out)
    unit, hidden = expert_in.shape[1:]
    capacity = (5 * tok + 4 * ny - 1) // (4 * ny)
    nx = ns // 2
    return (
        unit % 16 == 0
        and tok % 16 == 0
        and packs * capacity % 16 == 0
        and attn_in.shape[0] % unit == 0
        and attn_out.shape[0] % unit == 0
        and expert_out.shape[1] % (unit * nx) == 0
        and width % (2 * unit) == 0
        and hidden % (nx * width) == 0
        and width % (hidden // (nz * nx)) == 0
        and hidden // (nz * nx) % 128 == 0
        and expert_out.shape[1] * nz * ns == hidden
        and expert_out.shape[1] * width == hidden * unit
        and expert_in.shape[0] == 1
    )


def deliver_body(*refs):
    count = len(refs) // 2
    for i in range(count):
        refs[count + i][...] = refs[i][...]


def deliver(arrays):
    vmem = pl.BlockSpec(memory_space=pltpu.VMEM)
    return pl.pallas_call(
        deliver_body,
        out_shape=[jax.ShapeDtypeStruct(a.shape, a.dtype) for a in arrays],
        in_specs=[vmem] * len(arrays),
        out_specs=[vmem] * len(arrays),
        name="deliver",
    )(*arrays)


def layer_kernel(layer_input, memory, cotangent, routes, doc_lengths, rel_buckets, gains, bias_table, router,
                 attn_in, attn_out, expert_in, expert_out):
    nz, ns, ny, packs, tok, width = shapes_of(layer_input, routes, attn_in, attn_out, expert_in, expert_out)
    nx = ns // 2
    group, pairs = ns * tok, width // 128
    unit = expert_in.shape[1]
    hidden = expert_in.shape[2]
    panels = hidden // width // nx
    pack_units = nx * panels
    experts, buckets = router.shape[1], bias_table.shape[0]
    each = packs * ((5 * tok + 4 * experts - 1) // (4 * experts))
    tall = nz * ns
    units = (attn_in.shape[0] // unit, attn_out.shape[0] // unit)
    total = tall * ny * (units[0] + units[1])
    grads = max(4 * nz * pack_units, total // 2)
    extra = -(-(3 + experts) // 8) * 8
    small = ny + nx - 1 + nz
    mine, every = packs * tok, packs * group
    any_ = pl.BlockSpec(memory_space=pl.ANY)
    vmem = pl.BlockSpec(memory_space=pltpu.VMEM)
    smem = pl.BlockSpec(memory_space=pltpu.SMEM)
    dma = pltpu.SemaphoreType.DMA
    low = lambda *shape: pltpu.VMEM(shape, BF)
    wide = lambda *shape: pltpu.VMEM(shape, F32)
    shape = lambda *dims: jax.ShapeDtypeStruct(dims, F32)
    results = pl.pallas_call(
        layer_body,
        out_shape=[
            jax.ShapeDtypeStruct((packs, tok, width), BF),
            shape(*attn_in.shape),
            shape(*attn_out.shape),
            shape(*expert_in.shape[1:]),
            shape(*expert_out.shape[1:]),
            shape(mine, width),
            shape(mine, width),
            shape(3, width),
            shape(experts, width),
            shape(2 * pairs, buckets),
        ],
        in_specs=[smem, *[vmem] * 8, any_, any_, vmem, any_],
        out_specs=[vmem] * 10,
        scratch_shapes=[
            low(total, unit, width),
            low(total, unit, width),
            low(grads, unit, width),
            low(nx, panels, unit, width),
            *[low(nz, pack_units, unit, width)] * 2,
            low(nz, ny - 1, nx, units[0], unit, width),
            low(nz, ny - 1, units[1], unit, width),
            low(nz, nx - 1, units[0], unit, width),
            low(nz, nx - 1, ny * units[1], unit, width),
            low(nx - 1, panels, unit, width),
            *[low(nz + 1, u, unit, width) for u in (*units, pack_units, pack_units)],
            *[low(every, width)] * 8,
            *[low(mine, width)] * 10,
            *[low(packs, pairs, 2 * tok, group)] * 2,
            *[wide(mine, width)] * 3,
            wide(pairs, 2 * tok, group),
            wide(packs, tok, group),
            wide(packs, tok, group),
            wide(16, group + 128),
            wide(1, width),
            low(2, packs, nx, tok, width),
            low(2, nx - 1, packs, tok, width),
            wide(4, extra, width),
            wide(4, 16, 128),
            wide(small, extra, width),
            wide(small, 16, 128),
            low(2, ny, each, width),
            low(2, nx, ny, each, width),
            wide(2, nx, ny, each, width),
            low(2, nx - 1, ny, each, width),
            low(2, nx - 1, ny, each, width),
            low(2, ny, each, width),
            low(panels, nx * ny * each, width),
            low(panels, nx * ny * each, width),
            dma((2, packs, 2 * nx)),
            dma((2, packs, nx, 2)),
            dma((nx - 1,)),
            dma((nx,)),
            dma((4, nz, 2)),
            dma((2, nz, nx - 1 + ny - 1 + max((ny - 1) * nx, (nx - 1) * ny))),
            dma((4, nz, nx, ny)),
            dma((4, nz, nx, ny)),
            dma((4, nz, nx, ny)),
            dma((6, packs)),
            dma((4, nz, nx)),
            dma((4, nz, nx)),
            dma((nz, ny - 1, nx + 1, units[0])),
            dma((nz, ny - 1, nx + 1, units[0])),
            dma((nz, nx - 1, units[0] + 1)),
            dma((nz, nx - 1, units[0] + 1)),
            dma((nx - 1,)),
            dma((nx - 1,)),
            dma((4, nz)),
            dma((4, nz + 1)),
            dma((nz, units[0] + 1)),
            dma((nz + 1, units[0] + 1)),
            dma((2, packs + 1, nx)),
            dma((2, packs + 1, nx)),
            dma((2, small)),
            dma((2, small)),
            dma((4 * (ny - 1) + 4 * (nx - 1) * ny,)),
            dma((4 * (ny - 1) + 4 * (nx - 1) * ny,)),
            pltpu.SemaphoreType.REGULAR,
        ],
        compiler_params=pltpu.CompilerParams(
            collective_id=0, has_side_effects=True, vmem_limit_bytes=64 * 2**20
        ),
        name="layer",
    )(
        doc_lengths[:, 0, 0],
        rel_buckets.reshape(1, -1),
        gains,
        bias_table.T,
        router.T,
        routes.reshape(packs, 1, tok),
        layer_input[:, 0, 0],
        memory[:, 0, 0],
        cotangent[:, 0, 0],
        attn_in.reshape(units[0], unit, width),
        attn_out.reshape(units[1], unit, width),
        expert_in[0],
        expert_out.reshape(pack_units, unit, width),
    )
    out_rows, g0, g1, g2, g3, grad_x, grad_mem, gains_sum, router_sum, table_sum = deliver(results)
    spread = (packs, 1, 1, tok, width)
    return (
        out_rows.reshape(spread),
        grad_x.reshape(spread),
        grad_mem.reshape(spread),
        gains_sum,
        table_sum.T,
        router_sum.T,
        g0,
        g1,
        g2[None],
        g3[None],
    )


def norm_apply(value, gain):
    return value * lax.rsqrt(jnp.mean(value * value, axis=-1, keepdims=True) + EPS) * gain


def norm_back(value, gain, grad):
    r = lax.rsqrt(jnp.mean(value * value, axis=-1, keepdims=True) + EPS)
    scaled = grad * gain
    back = r * scaled - value * (r * r * r) * jnp.mean(scaled * value, axis=-1, keepdims=True)
    return back, jnp.sum(grad * value * r, axis=0)


def gelu_tanh(value):
    return jax.nn.gelu(value, approximate=True)


def times(left, right):
    return jnp.dot(left, right, preferred_element_type=F32)


def times_right(left, right):
    return jnp.einsum("te,de->td", left, right, preferred_element_type=F32)


def times_left(left, right):
    return jnp.einsum("td,te->de", left, right, preferred_element_type=F32)


def split(a, packs):
    return a.reshape(packs, -1, HEADS, HEAD)


def attend(query, keys, values, allowed, bias, packs):
    scores = jnp.einsum("pqhd,pkhd->phqk", split(query, packs), split(keys, packs), preferred_element_type=F32)
    masked = jnp.where(allowed[:, None], scores * HEAD**-0.5 + bias, NEG)
    raised = jnp.exp(masked - jnp.max(masked, axis=3, keepdims=True))
    chances = raised / jnp.sum(raised, axis=3, keepdims=True)
    mixed = jnp.einsum("phqk,pkhd->pqhd", chances.astype(BF), split(values, packs), preferred_element_type=F32)
    return mixed.reshape(query.shape).astype(BF), chances


def attend_back(query, keys, values, chances, grad, packs):
    scale = HEAD**-0.5
    g4 = split(grad, packs)
    grad_chances = jnp.einsum("pqhd,pkhd->phqk", g4, split(values, packs), preferred_element_type=F32)
    spread_ = jnp.sum(chances * grad_chances, axis=3, keepdims=True)
    grad_scores = (chances * (grad_chances - spread_)).astype(BF)
    grad_query = jnp.einsum("phqk,pkhd->pqhd", grad_scores, split(keys, packs), preferred_element_type=F32) * scale
    grad_keys = jnp.einsum("phqk,pqhd->pkhd", grad_scores, split(query, packs), preferred_element_type=F32) * scale
    grad_values = jnp.einsum("phqk,pqhd->pkhd", chances.astype(BF), g4, preferred_element_type=F32)
    return (
        grad_query.reshape(query.shape).astype(BF),
        grad_keys.reshape(keys.shape).astype(BF),
        grad_values.reshape(keys.shape).astype(BF),
        grad_scores,
    )


def per_device(layer_input, memory, cotangent, routes, doc_lengths, rel_buckets, gains, bias_table, router,
               attn_in, attn_out, expert_in, expert_out):
    packs, rows, width = layer_input.shape[0], layer_input.shape[3], layer_input.shape[4]
    seqs = lax.axis_size("seq")
    group = rows * seqs
    experts = router.shape[1]
    capacity = (5 * rows + 4 * experts - 1) // (4 * experts)
    buckets = bias_table.shape[0]
    rank = lax.axis_index("seq")

    x_in, m_in, e_in, e_out = layer_input[:, 0, 0], memory[:, 0, 0], expert_in[0], expert_out[0]
    if fits_kernel(layer_input, routes, attn_in, attn_out, expert_in, expert_out):
        return layer_kernel(layer_input, memory, cotangent, routes, doc_lengths, rel_buckets, gains, bias_table, router,
                            attn_in, attn_out, expert_in, expert_out)
    x_rows = x_in.reshape(packs * rows, width).astype(F32)
    everywhere, peers = ("dp", "seq", "expert"), ("dp", "seq")
    x_all, m_all = (lax.all_gather(a, "seq", axis=1, tiled=True) for a in (x_in, m_in))
    w_in, w_out = (lax.all_gather(a, everywhere, axis=0, tiled=True) for a in (attn_in, attn_out))
    e_in, e_out = (lax.all_gather(a, peers, axis=0, tiled=True) for a in (e_in, e_out))
    w_in = w_in.reshape(6, width, width)
    w_out = w_out.reshape(2, width, width)
    x_all = x_all.reshape(packs * group, width)
    m_all = m_all.reshape(packs * group, width)
    wide = group + rows
    query_pos = rank * rows + jnp.arange(rows, dtype=jnp.int32)
    key_pos = jnp.arange(group, dtype=jnp.int32)
    ends = jnp.cumsum(doc_lengths[:, 0, 0], axis=1)
    query_doc = jnp.sum((query_pos[None, :, None] >= ends[:, None, :]).astype(jnp.int32), axis=2)
    key_doc = jnp.sum((key_pos[None, :, None] >= ends[:, None, :]).astype(jnp.int32), axis=2)
    same = query_doc[:, :, None] == key_doc[:, None, :]
    causal = same & (key_pos[None, None, :] <= query_pos[None, :, None])
    bucket_hot = (rel_buckets[:, None] == jnp.arange(buckets, dtype=jnp.int32)).astype(F32)
    line_at = jnp.arange(group + rows, dtype=jnp.int32) - (group - 1) + rank * rows
    line_hot = (jnp.take(rel_buckets, jnp.clip(line_at, 0, group - 1))[None, :] == jnp.arange(buckets)[:, None]).astype(F32)
    line = jnp.einsum("bh,bj->hj", bias_table, line_hot, precision=HIGHEST)
    line = line[:, ::-1]
    wide = group + rows
    tiled = jnp.broadcast_to(line[:, None, :], (HEADS, rows, wide)).reshape(HEADS, rows * wide)
    skew = tiled[:, rows : rows + rows * (wide - 1)].reshape(HEADS, rows, wide - 1)[:, :, :group]

    normed1_all = norm_apply(x_all.astype(F32), gains[0]).astype(BF)
    normed1 = norm_apply(x_rows, gains[0]).astype(BF)
    query = times(normed1, w_in[0]).astype(BF)
    keys = times(normed1_all, w_in[1]).astype(BF)
    values = times(normed1_all, w_in[2]).astype(BF)
    mem_keys = times(m_all, w_in[4]).astype(BF)
    mem_values = times(m_all, w_in[5]).astype(BF)
    mixed, chances_self = attend(query, keys, values, causal, skew[None], packs)
    hidden1 = x_rows + times(mixed, w_out[0])
    normed2 = norm_apply(hidden1, gains[1]).astype(BF)
    cross_query = times(normed2, w_in[3]).astype(BF)
    cross_mixed, chances_cross = attend(cross_query, mem_keys, mem_values, same, 0.0, packs)
    hidden2 = hidden1 + times(cross_mixed, w_out[1])
    normed3 = norm_apply(hidden2, gains[2]).astype(BF)

    routing = jax.nn.softmax(times(normed3, router), axis=1)
    route = routes[:, 0, 0, :, 0]
    route_hot = (route[:, :, None] == jnp.arange(experts, dtype=jnp.int32)).astype(jnp.int32)
    slot = jnp.sum((jnp.cumsum(route_hot, axis=1) - route_hot) * route_hot, axis=2)
    hot = route_hot.reshape(packs * rows, experts).astype(F32)
    gate = jnp.sum(routing * hot, axis=1)
    target = jnp.where(slot < capacity, (route * packs + jnp.arange(packs)[:, None]) * capacity + slot, -1).reshape(-1)
    dispatch = (target[:, None] == jnp.arange(experts * packs * capacity, dtype=jnp.int32)).astype(BF)

    def swap(a):
        shape = (experts, packs * capacity, width)
        return lax.all_to_all(a.reshape(shape), "expert", split_axis=0, concat_axis=0, tiled=True).reshape(-1, width)

    received = swap(times_left(dispatch, normed3).astype(BF))
    inner = times(received, e_in)
    hidden, pull = jax.vjp(gelu_tanh, inner)
    hidden = hidden.astype(BF)
    result = times(hidden, e_out).astype(BF)
    combined = times(dispatch, swap(result))
    out_rows = (hidden2 + gate[:, None] * combined).astype(BF)
    grad_top = cotangent.reshape(packs * rows, width).astype(F32)
    grad_gate = jnp.sum(grad_top * combined, axis=1)
    grad_result = swap(times_left(dispatch, (gate[:, None] * grad_top).astype(BF)).astype(BF))
    grad_hidden = times_right(grad_result, e_out)
    grad_eout = times_left(hidden, grad_result).astype(BF)
    grad_inner = pull(grad_hidden)[0].astype(BF)
    grad_ein = times_left(received, grad_inner).astype(BF)
    grad_send = swap(times_right(grad_inner, e_in).astype(BF))
    grad_logits = grad_gate[:, None] * routing * (hot - gate[:, None])
    grad_router = jnp.einsum("td,te->de", normed3.astype(F32), grad_logits, precision=HIGHEST)
    grad_normed3 = times(dispatch, grad_send) + jnp.einsum(
        "te,de->td", grad_logits, router.astype(F32), precision=HIGHEST
    )
    back3, gain3 = norm_back(hidden2, gains[2], grad_normed3)
    grad_h2 = grad_top + back3
    grad_h2_low = grad_h2.astype(BF)
    grad_wco = times_left(cross_mixed, grad_h2_low)
    grad_cross = times_right(grad_h2_low, w_out[1]).astype(BF)
    grad_cq, grad_ck, grad_cv, _ = attend_back(cross_query, mem_keys, mem_values, chances_cross, grad_cross, packs)
    back2, gain2 = norm_back(hidden1, gains[1], times_right(grad_cq, w_in[3]))
    grad_h1 = grad_h2 + back2
    grad_h1_low = grad_h1.astype(BF)
    grad_wso = times_left(mixed, grad_h1_low)
    grad_mixed = times_right(grad_h1_low, w_out[0]).astype(BF)
    grad_q, grad_k, grad_v, grad_scores = attend_back(query, keys, values, chances_self, grad_mixed, packs)

    total = jnp.sum(grad_scores.astype(F32), axis=0)[:, ::-1]
    padded = jnp.pad(total, ((0, 0), (0, 0), (0, wide - group))).reshape(HEADS, rows * wide)
    diagonal = padded[:, : rows * (wide - 1)].reshape(HEADS, rows, wide - 1).sum(axis=1)
    at = jnp.clip(rank * rows + (rows - 1) - jnp.arange(wide - 1, dtype=jnp.int32), 0, group - 1)
    diagonal_hot = (jnp.take(rel_buckets, at)[:, None] == jnp.arange(buckets)).astype(F32)
    grad_table = jnp.einsum("jb,hj->bh", diagonal_hot, diagonal, precision=HIGHEST)

    def to_owner(a):
        return lax.psum_scatter(a.reshape(packs, group, width), "seq", scatter_dimension=1, tiled=True)

    grad_memory = to_owner((times_right(grad_ck, w_in[4]) + times_right(grad_cv, w_in[5])).astype(BF))
    part1 = to_owner((times_right(grad_k, w_in[1]) + times_right(grad_v, w_in[2])).astype(BF))
    grad_normed1 = times_right(grad_q, w_in[0]) + part1.reshape(packs * rows, width).astype(F32)
    back1, gain1 = norm_back(x_rows, gains[0], grad_normed1)
    grad_x = grad_h1 + back1
    grad_in = jnp.concatenate(
        [
            times_left(normed1, grad_q),
            times_left(normed1_all, grad_k),
            times_left(normed1_all, grad_v),
            times_left(normed2, grad_cq),
            times_left(m_all, grad_ck),
            times_left(m_all, grad_cv),
        ]
    ).astype(BF)
    grad_out = jnp.concatenate([grad_wso, grad_wco]).astype(BF)
    shards = [
        lax.psum_scatter(a, over, scatter_dimension=0, tiled=True).astype(F32)
        for a, over in ((grad_in, everywhere), (grad_out, everywhere), (grad_ein, peers), (grad_eout, peers))
    ]
    small = lax.psum((jnp.stack([gain1, gain2, gain3]), grad_table, grad_router), ("dp", "seq", "expert"))
    shape = (packs, 1, 1, rows, width)
    return (
        out_rows.reshape(shape),
        grad_x.reshape(shape),
        grad_memory.astype(F32).reshape(shape),
        *small,
        shards[0],
        shards[1],
        shards[2][None],
        shards[3][None],
    )


def solution(mesh):
    tokens = P(None, "dp", "expert", "seq", None)
    dense = P(("dp", "seq", "expert"), None)
    expert = P("expert", ("dp", "seq"), None)
    return jax.shard_map(
        per_device,
        mesh=mesh,
        in_specs=(tokens, tokens, tokens, tokens, P(None, "dp", "expert", None), P(), P(), P(), P(),
                  dense, dense, expert, expert),
        out_specs=(tokens, tokens, tokens, P(), P(), P(), dense, dense, expert, expert),
        check_vma=False,
    )
```

```python
import functools

import jax
import jax.numpy as jnp
from jax import lax
from jax.experimental import pallas as pl
from jax.experimental.pallas import tpu as pltpu
from jax.sharding import PartitionSpec as P

HEADS = 12
HEAD = 64

EPS = 1e-06
NEG = -1e30
HIGHEST = lax.Precision.HIGHEST
MESH = pl.DeviceIdType.MESH
BF = jnp.bfloat16
F32 = jnp.float32


class Place:
    def __init__(self):
        self.nz, self.ns, self.ny = (lax.axis_size(a) for a in ("dp", "seq", "expert"))
        self.nx = self.ns // 2
        self.z, self.s, self.y = (lax.axis_index(a) for a in ("dp", "seq", "expert"))
        self.x, self.c = self.s // 2, lax.rem(self.s, 2)

    def device(self, z=None, x=None, c=None, y=None):
        z = self.z if z is None else z
        x = self.x if x is None else x
        c = self.c if c is None else c
        y = self.y if y is None else y
        return (z, x * 2 + c, y)

    def other_x(self):
        return [lax.rem(self.x + k, self.nx) for k in range(1, self.nx)]

    def other_y(self):
        return [lax.rem(self.y + k, self.ny) for k in range(1, self.ny)]

    def by_distance(self, k):
        half = self.nz // 2
        order = [
            sorted(range(self.nz), key=lambda d: (abs(d - z), (d < half) != (z < half), d)) for z in range(self.nz)
        ]
        return self.pick([row[k] for row in order])

    def pick(self, values):
        out = jnp.int32(values[0])
        for z in range(1, self.nz):
            out = jnp.where(self.z == z, jnp.int32(values[z]), out)
        return out

    def greet(self):
        barrier = pltpu.get_barrier_semaphore()
        for x in self.other_x():
            pl.semaphore_signal(barrier, inc=1, device_id=self.device(x=x), device_id_type=MESH)
        for y in self.other_y():
            pl.semaphore_signal(barrier, inc=1, device_id=self.device(y=y), device_id_type=MESH)
        pl.semaphore_signal(barrier, inc=1, device_id=self.device(c=1 - self.c), device_id_type=MESH)

        for k in range(1, self.nz):
            z = lax.rem(self.z + k, self.nz)
            pl.semaphore_signal(barrier, inc=1, device_id=self.device(z=z), device_id_type=MESH)
        pl.semaphore_wait(barrier, self.nx - 1 + self.ny - 1 + 1 + self.nz - 1)


def rms_rows(src, gain, dst, rows, step=64):
    @pl.loop(0, rows // step)
    def _(i):
        at = pl.ds(pl.multiple_of(i * step, step), step)
        value = src[at, :].astype(F32)
        r = lax.rsqrt(jnp.mean(value * value, axis=-1, keepdims=True) + EPS)
        dst[at, :] = (value * r * gain).astype(BF)


def block(weight, index, lanes=slice(None), share=(0, 1)):
    unit, width = weight.shape[-2:]
    count = width // unit // share[1]
    first = pl.multiple_of(index * (width // unit) + share[0] * count, count)
    value = weight[pl.ds(first, count), :, lanes]
    return value.reshape(count * unit, value.shape[-1])


def project(left, weight, index, dst):
    width = dst.shape[-1]
    step = 256 if width % 256 == 0 else width

    @pl.loop(0, width // step)
    def _(j):
        at = pl.ds(pl.multiple_of(j * step, step), step)
        dst[:, at] = jnp.dot(left[...], block(weight, index, at), preferred_element_type=F32).astype(dst.dtype)


def prepare_bias(rel, table, bias, rank, rows, group):
    heads, buckets = table.shape
    wide = group + 128
    lane = lax.broadcasted_iota(jnp.int32, (group, wide), 1)
    shift = jnp.where(lane < group, lane, lane - wide)
    distance = jnp.clip(rank * rows - shift, 0, group - 1)
    hot = (lax.broadcasted_iota(jnp.int32, (group, wide), 0) == distance).astype(F32).astype(BF)
    which = jnp.dot(jnp.broadcast_to(rel[...].astype(F32), (8, group)).astype(BF), hot, preferred_element_type=F32)
    picks = (lax.broadcasted_iota(jnp.int32, (buckets, wide), 0) == which[0:1].astype(jnp.int32)).astype(F32)
    line = jnp.dot(table[...], picks, precision=HIGHEST, preferred_element_type=F32)
    for h in range(heads):
        band = pltpu.roll(jnp.broadcast_to(line[h : h + 1], (rows, wide)), 0, 1, stride=1, stride_axis=0)
        bias[h // 2, pl.ds((h % 2) * rows, rows), :] = band[:, :group]


def prepare_masks(lengths, same, causal, rank, rows, group):
    key = lax.broadcasted_iota(jnp.int32, (rows, group), 1)
    query = rank * rows + lax.broadcasted_iota(jnp.int32, (rows, group), 0)
    for p in range(same.shape[0]):
        end = jnp.int32(0)
        kd = jnp.zeros((rows, group), jnp.int32)
        qd = jnp.zeros((rows, group), jnp.int32)
        for n in range(lengths.shape[1]):
            end = end + lengths[p, n]
            kd = kd + jnp.where(key >= end, 1, 0)
            qd = qd + jnp.where(query >= end, 1, 0)
        same[p] = jnp.where(kd == qd, 0.0, NEG)
        causal[p] = jnp.where((kd == qd) & (key <= query), 0.0, NEG)


def two_heads(pair):
    first = lax.broadcasted_iota(jnp.int32, pair.shape, 1) < HEAD
    zero = jnp.zeros_like(pair)
    return jnp.concatenate([jnp.where(first, pair, zero), jnp.where(first, zero, pair)], axis=0)


def one_pair(stacked):
    rows = stacked.shape[0] // 2
    first = lax.broadcasted_iota(jnp.int32, (rows, stacked.shape[1]), 1) < HEAD
    return jnp.where(first, stacked[:rows], stacked[rows:])


def attend_pairs(query, keys, values, bias, mask, chances, mixed):
    packs, pairs, double, group = chances.shape
    rows = double // 2

    def body(i, carry):
        p, j = i // pairs, lax.rem(i, pairs)
        mine = pl.ds(pl.multiple_of(p * rows, rows), rows)
        theirs = pl.ds(pl.multiple_of(p * group, group), group)
        lanes = pl.ds(pl.multiple_of(j * 128, 128), 128)
        scores = lax.dot_general(
            two_heads(query[mine, lanes]), keys[theirs, lanes], (((1,), (1,)), ((), ())), preferred_element_type=F32
        )
        scores = scores * HEAD**-0.5
        if bias is not None:
            scores = scores + bias[j]
        scores = (scores.reshape(2, rows, group) + mask[p][None]).reshape(double, group)
        raised = jnp.exp(scores - jnp.max(scores, axis=1, keepdims=True))
        weights = (raised * (1.0 / jnp.sum(raised, axis=1, keepdims=True))).astype(BF)
        chances[p, j] = weights
        out = jnp.dot(weights, values[theirs, lanes], preferred_element_type=F32)
        mixed[mine, lanes] = one_pair(out).astype(BF)
        return carry

    lax.fori_loop(0, packs * pairs, body, 0, unroll=6)


def add_product(total, left, weight, index):
    width = total.shape[-1]
    step = 256 if width % 256 == 0 else width

    @pl.loop(0, width // step)
    def _(j):
        at = pl.ds(pl.multiple_of(j * step, step), step)
        total[:, at] += jnp.dot(left[...], block(weight, index, at), preferred_element_type=F32)


def product_t(left, weight, index, dst):
    halves = 2
    step = weight.shape[-1] // halves

    @pl.loop(0, halves)
    def _(j):
        rows = block(weight, index, share=(j, halves))
        out = lax.dot_general(left[...], rows, (((1,), (1,)), ((), ())), preferred_element_type=F32)
        dst[:, pl.ds(pl.multiple_of(j * step, step), step)] = out.astype(dst.dtype)


def two_products_t(left1, index1, left2, index2, weight, dst):
    halves = 2
    step = weight.shape[-1] // halves

    @pl.loop(0, halves)
    def _(j):
        out = 0.0
        for left, index in ((left1, index1), (left2, index2)):
            rows = block(weight, index, share=(j, halves))
            out = out + lax.dot_general(left[...], rows, (((1,), (1,)), ((), ())), preferred_element_type=F32)
        dst[:, pl.ds(pl.multiple_of(j * step, step), step)] = out.astype(dst.dtype)


def outer_product(left, right, dst, index):
    unit, width = dst.shape[-2:]
    halves = 2
    step, count = width // halves, width // unit // halves

    @pl.loop(0, halves)
    def _(j):
        part = left[:, pl.ds(pl.multiple_of(j * step, step), step)]
        out = lax.dot_general(part, right[...], (((0,), (0,)), ((), ())), preferred_element_type=F32)
        first = index * (width // unit) + j * count
        dst[pl.ds(first, count)] = out.astype(dst.dtype).reshape(count, unit, width)


def add_into(total, other):
    lead = total.shape[:-2]
    count = 1
    for n in lead:
        count *= n
    rows = total.shape[-2]
    step = next(n for n in ((48, 32, 16) if total.shape[-1] <= 1024 else (16,)) if rows % n == 0)

    def body(i, carry):
        index = []
        rest = i // (rows // step)
        for n in reversed(lead):
            index.insert(0, lax.rem(rest, n))
            rest = rest // n
        r = pl.ds(pl.multiple_of(lax.rem(i, rows // step) * step, 16), step)
        at = (*index, r)
        total[at] = (total[at].astype(F32) + other[at].astype(F32)).astype(total.dtype)
        return carry

    lax.fori_loop(0, count * (rows // step), body, 0)


def norm_back_rows(value, gain, grad, total, gain_grad, step=64):
    gain_grad[...] = jnp.zeros_like(gain_grad)

    @pl.loop(0, value.shape[0] // step)
    def _(i):
        at = pl.ds(pl.multiple_of(i * step, step), step)
        v, g = value[at, :].astype(F32), grad[at, :]
        r = lax.rsqrt(jnp.mean(v * v, axis=-1, keepdims=True) + EPS)
        scaled = g * gain
        total[at, :] += r * scaled - v * (r * r * r) * jnp.mean(scaled * v, axis=-1, keepdims=True)
        gain_grad[...] += jnp.sum(g * v * r, axis=0, keepdims=True)


def attend_pairs_back(query, keys, values, chances, grad, grad_q, grad_k, grad_v, diagonal):
    packs, pairs, double, group = chances.shape
    rows = double // 2
    scale = HEAD**-0.5

    def body(i, carry):
        p, j = i // pairs, lax.rem(i, pairs)
        mine = pl.ds(pl.multiple_of(p * rows, rows), rows)
        theirs = pl.ds(pl.multiple_of(p * group, group), group)
        lanes = pl.ds(pl.multiple_of(j * 128, 128), 128)
        ga = two_heads(grad[mine, lanes])
        low = chances[p, j]
        wide = low.astype(F32)
        gp = lax.dot_general(ga, values[theirs, lanes], (((1,), (1,)), ((), ())), preferred_element_type=F32)
        gs = (wide * (gp - jnp.sum(wide * gp, axis=1, keepdims=True))).astype(BF)
        gq = jnp.dot(gs, keys[theirs, lanes], preferred_element_type=F32)
        grad_q[mine, lanes] = (one_pair(gq) * scale).astype(BF)
        gk = lax.dot_general(gs, two_heads(query[mine, lanes]), (((0,), (0,)), ((), ())), preferred_element_type=F32)
        grad_k[theirs, lanes] = (gk * scale).astype(BF)
        gv = lax.dot_general(low, ga, (((0,), (0,)), ((), ())), preferred_element_type=F32)
        grad_v[theirs, lanes] = gv.astype(BF)
        if diagonal is not None:
            a = lax.broadcasted_iota(jnp.int32, (rows, rows), 0)
            b = lax.broadcasted_iota(jnp.int32, (rows, rows), 1)
            flip = (a + b == rows - 1).astype(F32).astype(BF)
            for half in range(2):
                turned = jnp.dot(flip, gs[half * rows : (half + 1) * rows], preferred_element_type=F32)
                turned = jnp.concatenate([turned, jnp.zeros((rows, 128), F32)], axis=1)
                band = pltpu.roll(turned, 0, 1, stride=1, stride_axis=0)
                diagonal[pl.ds(2 * j + half, 1), :] += jnp.sum(band, axis=0, keepdims=True)
        return carry

    lax.fori_loop(0, packs * pairs, body, 0, unroll=6)


def table_grad(rel, diagonal, rank, rows, group):
    wide = group + 128
    lane = lax.broadcasted_iota(jnp.int32, (group, wide), 1)
    distance = jnp.clip(rank * rows + rows - 1 - lane, 0, group - 1)
    hot = (lax.broadcasted_iota(jnp.int32, (group, wide), 0) == distance).astype(F32).astype(BF)
    which = jnp.dot(jnp.broadcast_to(rel[...].astype(F32), (8, group)).astype(BF), hot, preferred_element_type=F32)
    picks = (lax.broadcasted_iota(jnp.int32, (128, wide), 0) == which[0:1].astype(jnp.int32)).astype(F32)
    return lax.dot_general(diagonal[...], picks, (((1,), (1,)), ((), ())), precision=HIGHEST, preferred_element_type=F32)


def route_slots(route, experts, capacity):
    packs, _, rows = route.shape
    count = packs * rows
    same = lax.broadcasted_iota(jnp.int32, (rows, rows), 0) == lax.broadcasted_iota(jnp.int32, (rows, rows), 1)
    column = jnp.concatenate(
        [jnp.sum(jnp.where(same, route[p], 0), axis=1, keepdims=True) for p in range(packs)], axis=0
    )
    hot = (column == lax.broadcasted_iota(jnp.int32, (count, experts), 1)).astype(F32)
    a = lax.broadcasted_iota(jnp.int32, (count, count), 0)
    b = lax.broadcasted_iota(jnp.int32, (count, count), 1)
    earlier = ((b < a) & (a // rows == b // rows)).astype(F32).astype(BF)
    before = jnp.dot(earlier, hot.astype(BF), preferred_element_type=F32)
    slot = jnp.sum(before * hot, axis=1, keepdims=True).astype(jnp.int32)
    pack = lax.broadcasted_iota(jnp.int32, (count, 1), 0) // rows
    target = jnp.where(slot < capacity, (column * packs + pack) * capacity + slot, -1)
    slots = lax.broadcasted_iota(jnp.int32, (count, experts * packs * capacity), 1)
    return hot, (target == slots).astype(F32).astype(BF)


def gelu_both(z):
    c = 0.7978845608028654
    t = jnp.tanh(c * (z + 0.044715 * (z * z * z)))
    half = 0.5 * (1.0 + t)
    slope = half + 0.5 * z * (1.0 - t * t) * (c * (1.0 + 3 * 0.044715 * (z * z)))
    return z * half, slope


def continue_waits(waits, hop, d, at):
    def wait():
        @pl.when(d < at.z)
        def _():
            hop(-1).wait_send()

        @pl.when(d > at.z)
        def _():
            hop(1).wait_send()

    waits.append(wait)


def layer_body(lengths, rel, gains, table, router_t, route, x_ref, m_ref, g_ref, ain, aout, ein, eout,
               out_rows, o0, o1, o2, o3, grad_x, grad_mem, sum_gains, sum_router, sum_table,
               w, big, ge, prep, c2, c3, y0, y1, x0, x1, ex_in, z0, z1, z2, z3,
               xo, mo, n1_all, k_, v, kc, vc, gv, n1, q, mixed, n2, qc, cross_mixed, n3, gb, ga, gq,
               pr_self, pr_cross, h1, h2, gn, bias, same, causal, diagonal, gain_row,
               act_core, act_x, wide_sum, table_sum, wide_in, table_in,
               slots_out, slots_in, slots_acc, ret_out, ret_in, back_in, hid, gin_,
               act_send, act_recv, prep_send, prep_recv, line_send, side_send, spread_send, ici_recv, spread_recv, own_sem,
               core_send, core_recv, y_send, y_recv, x_send, x_recv, ex_send, ex_recv, z_send, z_recv, zd_send, zd_recv,
               sum_send, sum_recv, small_send, small_recv, slot_send, slot_recv, free_sem):
    at = Place()
    nz, nx, ny = at.nz, at.nx, at.ny
    packs, tok, width = x_ref.shape
    group = xo.shape[0] // packs
    experts = router_t.shape[0]
    unit = ain.shape[1]
    block_units = eout.shape[0]
    panels = block_units // nx
    columns = ein.shape[1] // (nz * nx)
    buckets = table.shape[1]
    gk = xo
    units = (ain.shape[0], aout.shape[0])
    tall = nz * nx * 2
    bases = (0, tall * ny * units[0], 0, 2 * nz * block_units)
    dense, e_in, e_out = (0, 1), 2, 3
    experts_ = (e_in, e_out)
    waits = []

    def remote(src, dst, ssem, rsem, **where):
        return pltpu.make_async_remote_copy(
            src_ref=src, dst_ref=dst, send_sem=ssem, recv_sem=rsem,
            device_id=at.device(**where), device_id_type=MESH,
        )

    def send(*args, **where):
        one = remote(*args, **where)
        if acts_now[0]:
            one.start()
        waits.append(one.wait_send)

    acts_now = [True]

    def at_planes(ends, step, last):
        between = (at.z > 0) & (at.z < nz - 1)
        mark = len(waits)

        @pl.when(jnp.logical_not(between) if ends else between)
        def _():
            step()

        del waits[mark:]
        if last:
            acts_now[0] = False
            step()
            acts_now[0] = True

    def add(total, other):
        if acts_now[0]:
            add_into(total, other)

    def start_when(pred, make):
        if acts_now[0]:

            @pl.when(pred)
            def _():
                make().start()

    def arrive(ref, sem):
        if acts_now[0]:
            pltpu.make_async_copy(ref, ref, sem).wait()

    def spot(a, z, x, c, y):
        index = ((z * nx + x) * 2 + c) * ny + y
        return w.at[pl.ds(bases[a] + index * units[a], units[a])]

    def pack_of(a, z, c):
        return big.at[pl.ds(bases[a] + (z * 2 + c) * block_units, block_units)]

    shards = (ain, aout)
    acts = ((x_ref, xo), (m_ref, mo))

    at.greet()

    def act_rows(full, p, x, c):
        return full.at[pl.ds(pl.multiple_of(p * group + (x * 2 + c) * tok, 16), tok)]

    own_waits = []

    def send_acts():
        for i, (src, full) in enumerate(acts):
            for p in range(packs):
                dst = act_rows(full, p, at.x, at.c)
                for k, x in enumerate(at.other_x()):
                    send(src.at[p], dst, act_send.at[i, p, k], act_recv.at[i, p, at.x, at.c], x=x)
                send(src.at[p], dst, act_send.at[i, p, nx - 1 + at.x], act_recv.at[i, p, at.x, at.c], c=1 - at.c)
                own = pltpu.make_async_copy(src.at[p], dst, own_sem.at[4 + i, p])
                own.start()
                own_waits.append(own.wait)

    def along_line(a, z, src):
        dst = spot(a, z, at.x, at.c, at.y) if a in dense else pack_of(a, z, at.c)
        sem = ici_recv.at[a, z, at.x, at.y]
        left = (z >= at.z) & (at.z > 0)
        right = (z <= at.z) & (at.z < nz - 1)

        def one(side):
            return remote(src, dst, line_send.at[a, z, side], sem, z=at.z + 2 * side - 1)

        start_when(left, lambda: one(0))
        start_when(right, lambda: one(1))

        def wait():
            @pl.when(left)
            def _():
                one(0).wait_send()

            @pl.when(right)
            def _():
                one(1).wait_send()

        waits.append(wait)

    def to_core(a, z, x, y, src):
        dst = spot(a, z, x, at.c, y) if a in dense else pack_of(a, z, at.c)
        send(src, dst, spread_send.at[a, z, x, y], spread_recv.at[a, z, x, y], c=1 - at.c)

    zs = [at.by_distance(k) for k in range(nz)]

    def dense_events(k):
        z = zs[k]
        for a in dense:
            here = spot(a, z, at.x, at.c, at.y)
            src = here if k else shards[a]
            if k:
                arrive(here, ici_recv.at[a, z, at.x, at.y])
            else:
                own = pltpu.make_async_copy(shards[a], here, own_sem.at[a, 0])
                own.start()
                own_waits.append(own.wait)
            along_line(a, z, src)
            for j, x in enumerate(at.other_x()):
                send(src, here, side_send.at[a, z, j], ici_recv.at[a, z, at.x, at.y], x=x)
            for j, y in enumerate(at.other_y()):
                send(src, here, side_send.at[a, z, nx - 1 + j], ici_recv.at[a, z, at.x, at.y], y=y)
            to_core(a, z, at.x, at.y, src)

    def side_y(k):
        z = zs[k]
        for y in at.other_y():
            for a in dense:
                here = spot(a, z, at.x, at.c, y)
                arrive(here, ici_recv.at[a, z, at.x, y])
                if a == 1:
                    for j, x in enumerate(at.other_x()):
                        send(here, here, side_send.at[a, z, nx - 1 + ny - 1 + j + (nx - 1) * y],
                             ici_recv.at[a, z, at.x, y], x=x)
                to_core(a, z, at.x, y, here)

    def side_x(k):
        z = zs[k]
        for x in at.other_x():
            for a in dense:
                here = spot(a, z, x, at.c, at.y)
                arrive(here, ici_recv.at[a, z, x, at.y])
                if a == 0:
                    for j, y in enumerate(at.other_y()):
                        send(here, here, side_send.at[a, z, nx - 1 + ny - 1 + j + (ny - 1) * x],
                             ici_recv.at[a, z, x, at.y], y=y)
                to_core(a, z, x, at.y, here)

    def corner_events(k):
        z = zs[k]
        for a in dense:
            for y in at.other_y():
                for x in at.other_x():
                    here = spot(a, z, x, at.c, y)
                    arrive(here, ici_recv.at[a, z, x, y])
                    to_core(a, z, x, y, here)

    def act_events():
        for i, (src, full) in enumerate(acts):
            for p in range(packs):
                for x in at.other_x():
                    dst = act_rows(full, p, x, at.c)
                    arrive(dst, act_recv.at[i, p, x, at.c])
                    send(dst, dst, act_send.at[i, p, nx - 1 + x], act_recv.at[i, p, x, at.c], c=1 - at.c)

    def in_unit(z, c, x, n=1):
        return pl.ds(bases[e_in] + ((z * 2 + c) * nx + x) * panels, n * panels)

    def start_prep():
        for x in range(nx):
            for u in range(panels):
                each_z = width // columns
                prep[x, u] = jnp.concatenate(
                    [ein[:, (z * nx + x) * columns : (z * nx + x + 1) * columns] for z in range(u * each_z, (u + 1) * each_z)],
                    axis=1,
                )
        big[in_unit(at.z, at.c, at.x)] = prep[at.x]
        for j, x in enumerate(at.other_x()):
            send(prep.at[x], big.at[in_unit(at.z, at.c, at.x)], prep_send.at[j], prep_recv.at[at.x], x=x)

    def expert_events(k, kinds=experts_):
        z = zs[k]
        for a in kinds:
            here = pack_of(a, z, at.c)
            src = here
            if k:
                arrive(here, ici_recv.at[a, z, at.x, at.y])
            elif a == e_in:
                for x in at.other_x():
                    arrive(big.at[in_unit(at.z, at.c, x)], prep_recv.at[x])
            else:
                src = eout
                own = pltpu.make_async_copy(eout, here, own_sem.at[a, 0])
                own.start()
                own_waits.append(own.wait)
            along_line(a, z, src)
            to_core(a, z, 0, 0, src)

    def first_norm():
        for i, (src, full) in enumerate(acts):
            for p in range(packs):
                for x in range(nx):
                    arrive(act_rows(full, p, x, 1 - at.c), act_recv.at[i, p, x, 1 - at.c])
        for wait in own_waits:
            wait()
        rms_rows(xo, gains[0:1], n1_all, packs * group)
        for p in range(packs):
            h1[pl.ds(p * tok, tok), :] = x_ref[p].astype(F32)
            n1[pl.ds(p * tok, tok), :] = n1_all[pl.ds(pl.multiple_of(p * group + at.s * tok, tok), tok), :]

    places = [((z * 2 + c) * nx + x) * panels for z in range(nz) for x in range(nx) for c in range(2)]
    each = slots_out.shape[2]
    count = ny * each
    row_units = width // unit

    def keys_and_values(for_self):
        @pl.when(for_self)
        def _():
            project(n1_all, w, 1, k_)
            project(n1_all, w, 2, v)

        @pl.when(jnp.logical_not(for_self))
        def _():
            project(mo, w, 4, kc)
            project(mo, w, 5, vc)

    def by_slot(dispatch, rows):
        out = lax.dot_general(dispatch, rows, (((0,), (0,)), ((), ())), preferred_element_type=F32)
        return out.astype(BF).reshape(ny, each, width)

    slot_waits = []

    def slot_copy(late, src, dst, sem_from, sem_to, **where):
        one = remote(src, dst, slot_send.at[sem_from], slot_recv.at[sem_to], **where)
        one.start()
        (waits if late else slot_waits).append(one.wait_send)

    def y_sem(t, j):
        return t * (ny - 1) + j

    def x_sem(t, j, y):
        return 4 * (ny - 1) + (t * (nx - 1) + j) * ny + y

    def ret_sem(t, j, y):
        return 4 * (ny - 1) + 2 * (nx - 1) * ny + (t * (nx - 1) + j) * ny + y

    def send_slots(t):
        for j, y in enumerate(at.other_y()):
            slot_copy(False, slots_out.at[t, y], slots_in.at[t, at.x, at.y], y_sem(t, j), y_sem(t, ny - 2 - j), y=y)
        for j, x in enumerate(at.other_x()):
            slot_copy(False, slots_out.at[t, at.y], slots_in.at[t, at.x, at.y], x_sem(t, j, at.y),
                      x_sem(t, nx - 2 - j, at.y), x=x)
        slots_in[t, at.x, at.y] = slots_out[t, at.y]

    def summed(t, y):
        total = slots_acc[t, at.x, y]
        for j in range(nx - 1):
            arrive(ret_in.at[t, j, y], slot_recv.at[ret_sem(t, j, y)])
            total = total + ret_in[t, j, y].astype(F32)
        return total.astype(BF)

    cores, ys, xs, zs_ = {2: c2, 3: c3}, (y0, y1), (x0, x1), (z0, z1, z2, z3)
    outs = (o0, o1, o2, o3)
    far = [sorted(range(nz), key=lambda d: (-abs(d - z), d)) for z in range(nz)]
    order_e = [at.pick([far[z][k] for z in range(nz)]) for k in range(nz)]
    halves = [[d for d in row if d >= nz // 2] + [d for d in row if d < nz // 2] for row in far]
    order_d = [at.pick([halves[z][k] for z in range(nz)]) for k in range(nz)]
    e_waits = []

    def expert_part(a, d, c):
        return ge.at[pl.ds(bases[a] + (d * 2 + c) * block_units, block_units)]

    def start_expert(a, k):
        one = remote(expert_part(a, order_e[k], 1 - at.c), cores[a].at[k], core_send.at[a, k, 0],
                     core_recv.at[a, k, 0], c=1 - at.c)
        one.start()
        e_waits.append(one.wait_send)

    def core_expert(a, k):
        arrive(cores[a].at[k], core_recv.at[a, k, 0])
        add_into(cores[a].at[k], expert_part(a, order_e[k], at.c))

    def free_experts():
        for wait in e_waits:
            wait()
        pl.semaphore_signal(free_sem, inc=1, device_id=at.device(c=1 - at.c), device_id_type=MESH)

    def dense_part(a, d, x, c):
        return big.at[pl.ds(bases[a] + ((d * nx + x) * 2 + c) * ny * units[a], ny * units[a])]

    def dense_core(a, k, x, y=None, u=None):
        first = bases[a] // 2 + (k * nx + x) * ny * units[a]
        if y is None:
            return ge.at[pl.ds(first, ny * units[a])]
        if u is None:
            return ge.at[pl.ds(first + y * units[a], units[a])]
        return ge.at[pl.ds(first + y * units[a] + u, 1)]

    def xs_in_order():
        return [(x, True) for x in at.other_x()] + [(at.x, False)]

    def start_dense(k):
        for a in dense:
            for x in range(nx):
                send(dense_part(a, order_d[k], x, 1 - at.c), dense_core(a, k, x), core_send.at[a, k, x],
                     core_recv.at[a, k, x], c=1 - at.c)

    def first_dense(k):
        for x, _ in xs_in_order():
            arrive(dense_core(0, k, x), core_recv.at[0, k, x])
            add_into(dense_core(0, k, x), dense_part(0, order_d[k], x, at.c))
            for u in range(units[0]):
                for j, y in enumerate(at.other_y()):
                    send(dense_core(0, k, x, y, u), ys[0].at[k, ny - 2 - j, x, pl.ds(u, 1)],
                         y_send.at[k, j, x, u], y_recv.at[k, ny - 2 - j, x, u], y=y)
        for x, _ in xs_in_order():
            arrive(dense_core(1, k, x), core_recv.at[1, k, x])
            add_into(dense_core(1, k, x), dense_part(1, order_d[k], x, at.c))
        for j, x in enumerate(at.other_x()):
            send(dense_core(1, k, x), xs[1].at[k, nx - 2 - j], x_send.at[k, j, units[0]],
                 x_recv.at[k, nx - 2 - j, units[0]], x=x)

    def second_dense(k):
        for x, away in xs_in_order():
            for u in range(units[0]):
                total = ys[0].at[k, 0, x, pl.ds(u, 1)]
                for j in range(ny - 1):
                    piece = ys[0].at[k, j, x, pl.ds(u, 1)]
                    arrive(piece, y_recv.at[k, j, x, u])
                    add_into(total, piece if j else dense_core(0, k, x, at.y, u))
                if away:
                    j = lax.rem(x - at.x + nx, nx) - 1
                    send(total, xs[0].at[k, nx - 2 - j, pl.ds(u, 1)], x_send.at[k, j, u], x_recv.at[k, nx - 2 - j, u], x=x)
        for j in range(nx - 1):
            arrive(xs[1].at[k, j], x_recv.at[k, j, units[0]])
            add_into(xs[1].at[k, 0], xs[1].at[k, j] if j else dense_core(1, k, at.x))
        for j, y in enumerate(at.other_y()):
            send(xs[1].at[k, 0, pl.ds(y * units[1], units[1])], ys[1].at[k, ny - 2 - j],
                 y_send.at[k, j, nx, 0], y_recv.at[k, ny - 2 - j, nx, 0], y=y)

    def piece_of(k, p):
        return xs[0].at[k, 0, pl.ds(p, 1)] if p < units[0] else ys[1].at[k, 0]

    def inbox_of(slot, p):
        return zs_[0].at[slot, pl.ds(p, 1)] if p < units[0] else zs_[1].at[slot]

    def line_dense(k):
        d = order_d[k]
        for p in range(units[0] + 1):
            total = piece_of(k, p)
            if p < units[0]:
                for j in range(nx - 1):
                    piece = xs[0].at[k, j, pl.ds(p, 1)]
                    arrive(piece, x_recv.at[k, j, p])
                    add(total, piece if j else ys[0].at[k, 0, at.x, pl.ds(p, 1)])
            else:
                for j in range(ny - 1):
                    arrive(ys[1].at[k, j], y_recv.at[k, j, nx, 0])
                    add(total, ys[1].at[k, j] if j else xs[1].at[k, 0, pl.ds(at.y * units[1], units[1])])
            for side in range(2):

                @pl.when((at.z > 0) & (d > at.z) if side == 0 else (at.z < nz - 1) & (d < at.z))
                def _(total=total, p=p):
                    arrive(inbox_of(d, p), zd_recv.at[d, p])
                    add(total, inbox_of(d, p))

            def hop(to, total=total, p=p):
                slot = d if to > 0 else jnp.where(d == at.z - 1, nz, d)
                return remote(total, inbox_of(slot, p), zd_send.at[k, p], zd_recv.at[slot, p], z=at.z + to)

            start_when(d < at.z, functools.partial(hop, -1))
            start_when(d > at.z, functools.partial(hop, 1))

            continue_waits(waits, hop, d, at)

    def finish_dense():
        for k in (nz // 2 - 1, nz - 1):

            @pl.when(order_d[k] == at.z)
            def _(k=k):
                for p in range(units[0] + 1):
                    total = piece_of(k, p)
                    for side, here in enumerate((at.z > 0, at.z < nz - 1)):
                        slot = at.z if side == 0 else nz

                        @pl.when(here)
                        def _(total=total, slot=slot, p=p):
                            arrive(inbox_of(slot, p), zd_recv.at[slot, p])
                            add_into(total, inbox_of(slot, p))

                write_out(0, xs[0].at[k, 0])
                write_out(1, ys[1].at[k, 0])

    def write_out(a, total):
        if a != e_in:
            if acts_now[0]:
                outs[a][...] = total[...].astype(F32).reshape(outs[a].shape)
            return
        for j, x in enumerate(at.other_x()):
            send(total.at[pl.ds(x * panels, panels)], ex_in.at[nx - 2 - j], ex_send.at[j], ex_recv.at[nx - 2 - j], x=x)

    def finish_expert_in():
        for j in range(nx - 1):
            arrive(ex_in.at[j], ex_recv.at[j])
        total = cores[e_in].at[nz - 1]
        for x in range(nx):
            for u in range(panels):
                value = None
                for j, other in enumerate(at.other_x()):
                    value = ex_in[j, u] if value is None else jnp.where(other == x, ex_in[j, u], value)
                mine = total[pl.ds(at.x * panels + u, 1)][0]
                value = jnp.where(at.x == x, mine.astype(F32), value.astype(F32))
                for i in range(width // columns):
                    z = u * (width // columns) + i
                    outs[e_in][:, (z * nx + x) * columns : (z * nx + x + 1) * columns] = value[:, i * columns : (i + 1) * columns]

    def line(kind, k):
        for a in kind:
            d = order_e[k]
            total = cores[a].at[k]
            for side in range(2):
                feeds = (at.z > 0) & (d >= at.z) if side == 0 else (at.z < nz - 1) & (d <= at.z)
                slot = d if side == 0 else jnp.where(d == at.z, nz, d)

                @pl.when(feeds)
                def _(a=a, slot=slot, total=total):
                    arrive(zs_[a].at[slot], z_recv.at[a, slot])
                    add(total, zs_[a].at[slot])

            def hop(to, a=a, total=total, d=d):
                slot = d if to > 0 else jnp.where(d == at.z - 1, nz, d)
                return remote(total, zs_[a].at[slot], z_send.at[a, k], z_recv.at[a, slot], z=at.z + to)

            start_when(d < at.z, functools.partial(hop, -1))
            start_when(d > at.z, functools.partial(hop, 1))

            if k == nz - 1:
                write_out(a, total)
            continue_waits(waits, hop, d, at)

    def start_act(i):
        for p in range(packs):
            for x in range(nx):
                send(act_rows((kc, k_)[i], p, x, 1 - at.c), act_core.at[i, p, x], sum_send.at[i, p, x],
                     sum_recv.at[i, p, x], c=1 - at.c)

    def core_act(i):
        for p in range(packs):
            for x in range(nx):
                arrive(act_core.at[i, p, x], sum_recv.at[i, p, x])
                add_into(act_core.at[i, p, x], act_rows((kc, k_)[i], p, x, at.c))
        for j, x in enumerate(at.other_x()):
            send(act_core.at[i, :, x], act_x.at[i, nx - 2 - j], sum_send.at[i, packs, j], sum_recv.at[i, packs, nx - 2 - j], x=x)

    def x_act(i):
        for j in range(nx - 1):
            arrive(act_x.at[i, j], sum_recv.at[i, packs, j])
        for p in range(packs):
            out = act_core[i, p, at.x].astype(F32)
            for j in range(nx - 1):
                out = out + act_x[i, j, p].astype(F32)
            if i == 0:
                grad_mem[pl.ds(p * tok, tok), :] = out
            else:
                gn[pl.ds(p * tok, tok), :] += out

    pair_sums = ((wide_sum, wide_in), (table_sum, table_in))
    stages = [("c", [1 - at.c]), ("y", at.other_y()), ("x", at.other_x())]

    def start_small(t):
        axis, peers = stages[t]
        base = [0, 1, ny][t]
        for i, (total, inbox) in enumerate(pair_sums):
            for j, peer in enumerate(peers):
                back = base + len(peers) - 1 - j
                send(total.at[t], inbox.at[back], small_send.at[i, base + j], small_recv.at[i, back], **{axis: peer})

    def end_small(t):
        axis, peers = stages[t]
        base = [0, 1, ny][t]
        for i, (total, inbox) in enumerate(pair_sums):
            out = total[t]
            for j in range(len(peers)):
                arrive(inbox.at[base + j], small_recv.at[i, base + j])
                out = out + inbox[base + j]
            total[t + 1] = out

    tail = ny + nx - 1

    def start_line():
        for i, (total, inbox) in enumerate(pair_sums):
            for j in range(1, nz):
                z = lax.rem(at.z + j, nz)
                send(total.at[3], inbox.at[tail + at.z], small_send.at[i, tail + j], small_recv.at[i, tail + at.z], z=z)

    def end_line():
        for i, (total, inbox) in enumerate(pair_sums):
            for j in range(1, nz):
                z = lax.rem(at.z + j, nz)
                arrive(inbox.at[tail + z], small_recv.at[i, tail + z])
            out = None
            for z in range(nz):
                term = jnp.where(at.z == z, total[3], inbox[tail + z])
                out = term if out is None else out + term
            if i == 0:
                sum_gains[...] = out[: sum_gains.shape[0]]
                sum_router[...] = out[sum_gains.shape[0] : sum_gains.shape[0] + experts]
            else:
                sum_table[...] = out[: sum_table.shape[0], : sum_table.shape[1]]

    dense_events(0)
    start_prep()
    prepare_bias(rel, table, bias, at.s, tok, group)
    prepare_masks(lengths, same, causal, at.s, tok, group)
    hot, dispatch = route_slots(route, experts, each // packs)
    top = g_ref[...].astype(F32).reshape(packs * tok, width)
    at_planes(False, lambda: dense_events(1), False)
    at_planes(True, lambda: dense_events(1), True)
    side_x(0)
    at_planes(False, lambda: dense_events(2), False)
    side_y(0)
    expert_events(0, (e_out,))
    send_acts()
    at_planes(False, lambda: dense_events(3), False)
    at_planes(True, lambda: dense_events(2), True)
    expert_events(0, (e_in,))
    side_x(1)
    corner_events(0)
    at_planes(True, lambda: dense_events(3), True)
    side_y(1)
    at_planes(False, lambda: expert_events(1, (e_in,)), False)
    at_planes(False, lambda: expert_events(1, (e_out,)), False)
    act_events()
    side_y(2)
    side_x(2)
    at_planes(True, lambda: expert_events(1, (e_in,)), True)
    at_planes(False, lambda: expert_events(2, (e_out,)), False)
    at_planes(False, lambda: expert_events(2, (e_in,)), False)
    at_planes(False, lambda: expert_events(3, (e_in,)), False)
    first_norm()
    side_x(3)
    corner_events(1)
    side_y(3)
    for a in dense:
        for z in zs[: nz // 2]:
            for x in range(nx):
                for y in range(ny):
                    arrive(spot(a, z, x, 1 - at.c, y), spread_recv.at[a, z, x, y])
    at_planes(True, lambda: expert_events(1, (e_out,)), True)
    corner_events(2)
    keys_and_values(at.z < nz // 2)
    corner_events(3)
    at_planes(False, lambda: expert_events(3, (e_out,)), False)
    for a in dense:
        for z in zs[nz // 2 :]:
            for x in range(nx):
                for y in range(ny):
                    arrive(spot(a, z, x, 1 - at.c, y), spread_recv.at[a, z, x, y])
    project(n1, w, 0, q)
    keys_and_values(at.z >= nz // 2)
    at_planes(True, lambda: expert_events(2, (e_out,)), True)
    attend_pairs(q, k_, v, bias, causal, pr_self, mixed)
    add_product(h1, mixed, w, 6)
    rms_rows(h1, gains[1:2], n2, packs * tok)
    project(n2, w, 3, qc)
    attend_pairs(qc, kc, vc, None, same, pr_cross, cross_mixed)
    h2[...] = h1[...]
    add_product(h2, cross_mixed, w, 7)
    rms_rows(h2, gains[2:3], n3, packs * tok)
    slots_out[0] = by_slot(dispatch, n3[...])
    send_slots(0)
    logits = lax.dot_general(n3[...], router_t[...], (((1,), (1,)), ((), ())), preferred_element_type=F32)
    raised = jnp.exp(logits - jnp.max(logits, axis=1, keepdims=True))
    routing = raised / jnp.sum(raised, axis=1, keepdims=True)
    gate = jnp.sum(routing * hot, axis=1, keepdims=True)
    slots_out[1] = by_slot(dispatch, (gate * top).astype(BF))
    send_slots(1)
    at_planes(True, lambda: expert_events(3, (e_out,)), True)
    for t in range(2):
        for j, y in enumerate(at.other_y()):
            here = slots_in.at[t, at.x, y]
            arrive(here, slot_recv.at[y_sem(t, j)])
            for i, x in enumerate(at.other_x()):
                slot_copy(False, here, here, x_sem(t, i, y), x_sem(t, nx - 2 - i, y), x=x)
    at_planes(True, lambda: expert_events(2, (e_in,)), True)
    at_planes(True, lambda: expert_events(3, (e_in,)), True)
    for a in experts_:
        for z in range(nz):
            arrive(pack_of(a, z, 1 - at.c), spread_recv.at[a, z, 0, 0])
    for t in range(2):
        for i, x in enumerate(at.other_x()):
            for y in range(ny):
                arrive(slots_in.at[t, x, y], slot_recv.at[x_sem(t, i, y)])
    for wait in waits:
        wait()
    waits.clear()
    here = slots_in[0].reshape(nx * count, width)
    grad_here = slots_in[1].reshape(nx * count, width)
    for u in range(panels):
        in_panel = jnp.concatenate([big[place + u] for place in places], axis=0)
        out_panel = big[pl.ds(bases[e_out] + u * row_units, row_units)].reshape(width, width)
        inner = jnp.dot(here, in_panel, preferred_element_type=F32)
        hidden, slope = gelu_both(inner)
        hid[u] = hidden.astype(BF)
        grad_hidden = lax.dot_general(grad_here, out_panel, (((1,), (1,)), ((), ())), preferred_element_type=F32)
        gin_[u] = (grad_hidden * slope).astype(BF)
        result = jnp.dot(hid[u], out_panel, preferred_element_type=F32).reshape(nx, ny, each, width)
        grad_slots = lax.dot_general(gin_[u], in_panel, (((1,), (1,)), ((), ())), preferred_element_type=F32)
        grad_slots = grad_slots.reshape(nx, ny, each, width)
        if u:
            slots_acc[0] += result
            slots_acc[1] += grad_slots
        else:
            slots_acc[0] = result
            slots_acc[1] = grad_slots
    for y in [*at.other_y(), at.y]:
        for t in range(2):
            for j, x in enumerate(at.other_x()):
                ret_out[t, j, y] = slots_acc[t, x, y].astype(BF)
                slot_copy(True, ret_out.at[t, j, y], ret_in.at[t, nx - 2 - j, y], ret_sem(t, j, y),
                          ret_sem(t, nx - 2 - j, y), x=x)
    for u in range(panels):
        grad = lax.dot_general(here, gin_[u], (((0,), (0,)), ((), ())), preferred_element_type=F32).astype(BF)
        for i, place in enumerate(places):
            ge[place + u] = grad[i * unit : (i + 1) * unit]
    for k in range(nz):
        start_expert(e_in, k)
    for u in range(panels):
        grad = lax.dot_general(hid[u], grad_here, (((0,), (0,)), ((), ())), preferred_element_type=F32).astype(BF)
        ge[pl.ds(bases[e_out] + u * row_units, row_units)] = grad.reshape(row_units, unit, width)
    for k in range(nz):
        start_expert(e_out, k)
    core_expert(e_in, 0)
    at_planes(True, lambda: line((e_in,), 0), False)
    for wait in slot_waits:
        wait()
    for j, y in enumerate(at.other_y()):
        for t in range(2):
            slots_out[t, y] = summed(t, y)
            slot_copy(True, slots_out.at[t, y], back_in.at[t, at.y], y_sem(2 + t, j), y_sem(2 + t, ny - 2 - j), y=y)
    core_expert(e_out, 0)
    core_expert(e_in, 3)
    core_expert(e_in, 2)
    at_planes(True, lambda: line((e_out,), 0), False)
    core_expert(e_in, 1)
    at_planes(True, lambda: line((e_in,), 1), False)
    core_expert(e_out, 1)
    core_expert(e_out, 3)
    at_planes(True, lambda: line((e_in,), 2), False)
    core_expert(e_out, 2)
    free_experts()
    for t in range(2):
        back_in[t, at.y] = summed(t, at.y)
    for t in range(2):
        for j, y in enumerate(at.other_y()):
            arrive(back_in.at[t, y], slot_recv.at[y_sem(2 + t, j)])
    combined = jnp.dot(dispatch, back_in[0].reshape(count, width), preferred_element_type=F32)
    rows_out = (h2[...] + gate * combined).astype(BF)
    for p in range(packs):
        out_rows[p] = rows_out[p * tok : (p + 1) * tok]
    grad_gate = jnp.sum(top * combined, axis=1, keepdims=True)
    grad_logits = grad_gate * routing * (hot - gate)
    diagonal[...] = jnp.zeros_like(diagonal)
    for i, (_, inbox) in enumerate(pair_sums):
        inbox[pl.ds(tail + at.z, 1)] = jnp.zeros_like(inbox[pl.ds(0, 1)])
    wide_sum[0] = jnp.zeros_like(wide_sum[0])
    wide_sum[0, pl.ds(3, experts), :] = lax.dot_general(
        grad_logits, n3[...].astype(F32), (((0,), (0,)), ((), ())), precision=HIGHEST, preferred_element_type=F32
    )
    grad_n3 = jnp.dot(dispatch, back_in[1].reshape(count, width), preferred_element_type=F32)
    for e in range(experts):
        grad_n3 = grad_n3 + grad_logits[:, e : e + 1] * router_t[e : e + 1, :].astype(F32)
    gn[...] = grad_n3
    grad_x[...] = top
    norm_back_rows(h2, gains[2:3], gn, grad_x, gain_row)
    wide_sum[0, 2:3, :] = gain_row[...]
    gb[...] = grad_x[...].astype(BF)
    at_planes(False, lambda: line((e_in,), 0), True)
    product_t(gb, w, 7, ga)
    attend_pairs_back(qc, kc, vc, pr_cross, ga, gq, gk, gv, None)
    outer_product(n2, gq, big, 3)
    outer_product(mo, gk, big, 4)
    outer_product(mo, gv, big, 5)
    outer_product(cross_mixed, gb, big, 7)
    pl.semaphore_wait(free_sem, 1)
    start_dense(0)
    product_t(gq, w, 3, gn)
    norm_back_rows(h1, gains[1:2], gn, grad_x, gain_row)
    wide_sum[0, 1:2, :] = gain_row[...]
    gb[...] = grad_x[...].astype(BF)
    product_t(gb, w, 6, ga)
    at_planes(False, lambda: line((e_in,), 1), True)
    first_dense(0)
    start_dense(1)
    at_planes(False, lambda: line((e_in,), 2), True)
    at_planes(True, lambda: line((e_out,), 1), False)
    at_planes(True, lambda: line((e_out,), 2), False)
    two_products_t(gk, 4, gv, 5, w, kc)
    at_planes(False, lambda: line((e_out,), 0), True)
    start_act(0)
    first_dense(1)
    attend_pairs_back(q, k_, v, pr_self, ga, gq, gk, gv, diagonal)
    second_dense(0)
    at_planes(False, lambda: line((e_in,), 3), False)
    two_products_t(gk, 1, gv, 2, w, k_)
    start_act(1)
    outer_product(mixed, gb, big, 6)
    at_planes(False, lambda: line((e_out,), 1), True)
    table_sum[0] = table_grad(rel, diagonal, at.s, tok, group)
    at_planes(True, lambda: line((e_in,), 3), True)
    outer_product(n1, gq, big, 0)
    outer_product(n1_all, gk, big, 1)
    outer_product(n1_all, gv, big, 2)
    core_act(1)
    start_dense(2)
    start_dense(3)
    at_planes(False, lambda: line((e_out,), 2), True)
    second_dense(1)
    product_t(gq, w, 0, gn)
    first_dense(2)
    at_planes(True, lambda: line_dense(0), False)
    at_planes(False, lambda: line((e_out,), 3), False)
    x_act(1)
    for p in range(packs):
        h1[pl.ds(p * tok, tok), :] = x_ref[p].astype(F32)
    norm_back_rows(h1, gains[0:1], gn, grad_x, gain_row)
    wide_sum[0, 0:1, :] = gain_row[...]
    start_small(0)
    core_act(0)
    at_planes(False, lambda: line_dense(0), True)
    end_small(0)
    start_small(1)
    second_dense(2)
    end_small(1)
    start_small(2)
    first_dense(3)
    finish_expert_in()
    at_planes(True, lambda: line((e_out,), 3), True)
    x_act(0)
    at_planes(False, lambda: line_dense(1), False)
    at_planes(False, lambda: line_dense(2), False)
    at_planes(True, lambda: line_dense(1), True)
    at_planes(True, lambda: line_dense(2), True)
    end_small(2)
    start_line()
    second_dense(3)
    at_planes(False, lambda: line_dense(3), False)
    at_planes(True, lambda: line_dense(3), True)
    end_line()
    finish_dense()
    for wait in waits:
        wait()


def shapes_of(layer_input, routes, attn_in, attn_out, expert_in, expert_out):
    nz, ns, ny = (lax.axis_size(a) for a in ("dp", "seq", "expert"))
    packs, tok, width = layer_input.shape[0], layer_input.shape[3], layer_input.shape[4]
    return nz, ns, ny, packs, tok, width


def fits_kernel(layer_input, routes, attn_in, attn_out, expert_in, expert_out):
    nz, ns, ny, packs, tok, width = shapes_of(layer_input, routes, attn_in, attn_out, expert_in, expert_out)
    unit, hidden = expert_in.shape[1:]
    capacity = (5 * tok + 4 * ny - 1) // (4 * ny)
    nx = ns // 2
    return (
        unit % 16 == 0
        and tok % 16 == 0
        and packs * capacity % 16 == 0
        and attn_in.shape[0] % unit == 0
        and attn_out.shape[0] % unit == 0
        and expert_out.shape[1] % (unit * nx) == 0
        and width % (2 * unit) == 0
        and hidden % (nx * width) == 0
        and width % (hidden // (nz * nx)) == 0
        and hidden // (nz * nx) % 128 == 0
        and expert_out.shape[1] * nz * ns == hidden
        and expert_out.shape[1] * width == hidden * unit
        and expert_in.shape[0] == 1
    )


def deliver_body(*refs):
    count = len(refs) // 2
    for i in range(count):
        refs[count + i][...] = refs[i][...]


def deliver(arrays):
    vmem = pl.BlockSpec(memory_space=pltpu.VMEM)
    return pl.pallas_call(
        deliver_body,
        out_shape=[jax.ShapeDtypeStruct(a.shape, a.dtype) for a in arrays],
        in_specs=[vmem] * len(arrays),
        out_specs=[vmem] * len(arrays),
        name="deliver",
    )(*arrays)


def layer_kernel(layer_input, memory, cotangent, routes, doc_lengths, rel_buckets, gains, bias_table, router,
                 attn_in, attn_out, expert_in, expert_out):
    nz, ns, ny, packs, tok, width = shapes_of(layer_input, routes, attn_in, attn_out, expert_in, expert_out)
    nx = ns // 2
    group, pairs = ns * tok, width // 128
    unit = expert_in.shape[1]
    hidden = expert_in.shape[2]
    panels = hidden // width // nx
    pack_units = nx * panels
    experts, buckets = router.shape[1], bias_table.shape[0]
    each = packs * ((5 * tok + 4 * experts - 1) // (4 * experts))
    tall = nz * ns
    units = (attn_in.shape[0] // unit, attn_out.shape[0] // unit)
    total = tall * ny * (units[0] + units[1])
    grads = max(4 * nz * pack_units, total // 2)
    extra = -(-(3 + experts) // 8) * 8
    small = ny + nx - 1 + nz
    mine, every = packs * tok, packs * group
    any_ = pl.BlockSpec(memory_space=pl.ANY)
    vmem = pl.BlockSpec(memory_space=pltpu.VMEM)
    smem = pl.BlockSpec(memory_space=pltpu.SMEM)
    dma = pltpu.SemaphoreType.DMA
    low = lambda *shape: pltpu.VMEM(shape, BF)
    wide = lambda *shape: pltpu.VMEM(shape, F32)
    shape = lambda *dims: jax.ShapeDtypeStruct(dims, F32)
    results = pl.pallas_call(
        layer_body,
        out_shape=[
            jax.ShapeDtypeStruct((packs, tok, width), BF),
            shape(*attn_in.shape),
            shape(*attn_out.shape),
            shape(*expert_in.shape[1:]),
            shape(*expert_out.shape[1:]),
            shape(mine, width),
            shape(mine, width),
            shape(3, width),
            shape(experts, width),
            shape(2 * pairs, buckets),
        ],
        in_specs=[smem, *[vmem] * 8, any_, any_, vmem, any_],
        out_specs=[vmem] * 10,
        scratch_shapes=[
            low(total, unit, width),
            low(total, unit, width),
            low(grads, unit, width),
            low(nx, panels, unit, width),
            *[low(nz, pack_units, unit, width)] * 2,
            low(nz, ny - 1, nx, units[0], unit, width),
            low(nz, ny - 1, units[1], unit, width),
            low(nz, nx - 1, units[0], unit, width),
            low(nz, nx - 1, ny * units[1], unit, width),
            low(nx - 1, panels, unit, width),
            *[low(nz + 1, u, unit, width) for u in (*units, pack_units, pack_units)],
            *[low(every, width)] * 8,
            *[low(mine, width)] * 10,
            *[low(packs, pairs, 2 * tok, group)] * 2,
            *[wide(mine, width)] * 3,
            wide(pairs, 2 * tok, group),
            wide(packs, tok, group),
            wide(packs, tok, group),
            wide(16, group + 128),
            wide(1, width),
            low(2, packs, nx, tok, width),
            low(2, nx - 1, packs, tok, width),
            wide(4, extra, width),
            wide(4, 16, 128),
            wide(small, extra, width),
            wide(small, 16, 128),
            low(2, ny, each, width),
            low(2, nx, ny, each, width),
            wide(2, nx, ny, each, width),
            low(2, nx - 1, ny, each, width),
            low(2, nx - 1, ny, each, width),
            low(2, ny, each, width),
            low(panels, nx * ny * each, width),
            low(panels, nx * ny * each, width),
            dma((2, packs, 2 * nx)),
            dma((2, packs, nx, 2)),
            dma((nx - 1,)),
            dma((nx,)),
            dma((4, nz, 2)),
            dma((2, nz, nx - 1 + ny - 1 + max((ny - 1) * nx, (nx - 1) * ny))),
            dma((4, nz, nx, ny)),
            dma((4, nz, nx, ny)),
            dma((4, nz, nx, ny)),
            dma((6, packs)),
            dma((4, nz, nx)),
            dma((4, nz, nx)),
            dma((nz, ny - 1, nx + 1, units[0])),
            dma((nz, ny - 1, nx + 1, units[0])),
            dma((nz, nx - 1, units[0] + 1)),
            dma((nz, nx - 1, units[0] + 1)),
            dma((nx - 1,)),
            dma((nx - 1,)),
            dma((4, nz)),
            dma((4, nz + 1)),
            dma((nz, units[0] + 1)),
            dma((nz + 1, units[0] + 1)),
            dma((2, packs + 1, nx)),
            dma((2, packs + 1, nx)),
            dma((2, small)),
            dma((2, small)),
            dma((4 * (ny - 1) + 4 * (nx - 1) * ny,)),
            dma((4 * (ny - 1) + 4 * (nx - 1) * ny,)),
            pltpu.SemaphoreType.REGULAR,
        ],
        compiler_params=pltpu.CompilerParams(
            collective_id=0, has_side_effects=True, vmem_limit_bytes=64 * 2**20
        ),
        name="layer",
    )(
        doc_lengths[:, 0, 0],
        rel_buckets.reshape(1, -1),
        gains,
        bias_table.T,
        router.T,
        routes.reshape(packs, 1, tok),
        layer_input[:, 0, 0],
        memory[:, 0, 0],
        cotangent[:, 0, 0],
        attn_in.reshape(units[0], unit, width),
        attn_out.reshape(units[1], unit, width),
        expert_in[0],
        expert_out.reshape(pack_units, unit, width),
    )
    out_rows, g0, g1, g2, g3, grad_x, grad_mem, gains_sum, router_sum, table_sum = deliver(results)
    spread = (packs, 1, 1, tok, width)
    return (
        out_rows.reshape(spread),
        grad_x.reshape(spread),
        grad_mem.reshape(spread),
        gains_sum,
        table_sum.T,
        router_sum.T,
        g0,
        g1,
        g2[None],
        g3[None],
    )


def norm_apply(value, gain):
    return value * lax.rsqrt(jnp.mean(value * value, axis=-1, keepdims=True) + EPS) * gain


def norm_back(value, gain, grad):
    r = lax.rsqrt(jnp.mean(value * value, axis=-1, keepdims=True) + EPS)
    scaled = grad * gain
    back = r * scaled - value * (r * r * r) * jnp.mean(scaled * value, axis=-1, keepdims=True)
    return back, jnp.sum(grad * value * r, axis=0)


def gelu_tanh(value):
    return jax.nn.gelu(value, approximate=True)


def times(left, right):
    return jnp.dot(left, right, preferred_element_type=F32)


def times_right(left, right):
    return jnp.einsum("te,de->td", left, right, preferred_element_type=F32)


def times_left(left, right):
    return jnp.einsum("td,te->de", left, right, preferred_element_type=F32)


def split(a, packs):
    return a.reshape(packs, -1, HEADS, HEAD)


def attend(query, keys, values, allowed, bias, packs):
    scores = jnp.einsum("pqhd,pkhd->phqk", split(query, packs), split(keys, packs), preferred_element_type=F32)
    masked = jnp.where(allowed[:, None], scores * HEAD**-0.5 + bias, NEG)
    raised = jnp.exp(masked - jnp.max(masked, axis=3, keepdims=True))
    chances = raised / jnp.sum(raised, axis=3, keepdims=True)
    mixed = jnp.einsum("phqk,pkhd->pqhd", chances.astype(BF), split(values, packs), preferred_element_type=F32)
    return mixed.reshape(query.shape).astype(BF), chances


def attend_back(query, keys, values, chances, grad, packs):
    scale = HEAD**-0.5
    g4 = split(grad, packs)
    grad_chances = jnp.einsum("pqhd,pkhd->phqk", g4, split(values, packs), preferred_element_type=F32)
    spread_ = jnp.sum(chances * grad_chances, axis=3, keepdims=True)
    grad_scores = (chances * (grad_chances - spread_)).astype(BF)
    grad_query = jnp.einsum("phqk,pkhd->pqhd", grad_scores, split(keys, packs), preferred_element_type=F32) * scale
    grad_keys = jnp.einsum("phqk,pqhd->pkhd", grad_scores, split(query, packs), preferred_element_type=F32) * scale
    grad_values = jnp.einsum("phqk,pqhd->pkhd", chances.astype(BF), g4, preferred_element_type=F32)
    return (
        grad_query.reshape(query.shape).astype(BF),
        grad_keys.reshape(keys.shape).astype(BF),
        grad_values.reshape(keys.shape).astype(BF),
        grad_scores,
    )


def per_device(layer_input, memory, cotangent, routes, doc_lengths, rel_buckets, gains, bias_table, router,
               attn_in, attn_out, expert_in, expert_out):
    packs, rows, width = layer_input.shape[0], layer_input.shape[3], layer_input.shape[4]
    seqs = lax.axis_size("seq")
    group = rows * seqs
    experts = router.shape[1]
    capacity = (5 * rows + 4 * experts - 1) // (4 * experts)
    buckets = bias_table.shape[0]
    rank = lax.axis_index("seq")

    x_in, m_in, e_in, e_out = layer_input[:, 0, 0], memory[:, 0, 0], expert_in[0], expert_out[0]
    if fits_kernel(layer_input, routes, attn_in, attn_out, expert_in, expert_out):
        return layer_kernel(layer_input, memory, cotangent, routes, doc_lengths, rel_buckets, gains, bias_table, router,
                            attn_in, attn_out, expert_in, expert_out)
    x_rows = x_in.reshape(packs * rows, width).astype(F32)
    everywhere, peers = ("dp", "seq", "expert"), ("dp", "seq")
    x_all, m_all = (lax.all_gather(a, "seq", axis=1, tiled=True) for a in (x_in, m_in))
    w_in, w_out = (lax.all_gather(a, everywhere, axis=0, tiled=True) for a in (attn_in, attn_out))
    e_in, e_out = (lax.all_gather(a, peers, axis=0, tiled=True) for a in (e_in, e_out))
    w_in = w_in.reshape(6, width, width)
    w_out = w_out.reshape(2, width, width)
    x_all = x_all.reshape(packs * group, width)
    m_all = m_all.reshape(packs * group, width)
    wide = group + rows
    query_pos = rank * rows + jnp.arange(rows, dtype=jnp.int32)
    key_pos = jnp.arange(group, dtype=jnp.int32)
    ends = jnp.cumsum(doc_lengths[:, 0, 0], axis=1)
    query_doc = jnp.sum((query_pos[None, :, None] >= ends[:, None, :]).astype(jnp.int32), axis=2)
    key_doc = jnp.sum((key_pos[None, :, None] >= ends[:, None, :]).astype(jnp.int32), axis=2)
    same = query_doc[:, :, None] == key_doc[:, None, :]
    causal = same & (key_pos[None, None, :] <= query_pos[None, :, None])
    bucket_hot = (rel_buckets[:, None] == jnp.arange(buckets, dtype=jnp.int32)).astype(F32)
    line_at = jnp.arange(group + rows, dtype=jnp.int32) - (group - 1) + rank * rows
    line_hot = (jnp.take(rel_buckets, jnp.clip(line_at, 0, group - 1))[None, :] == jnp.arange(buckets)[:, None]).astype(F32)
    line = jnp.einsum("bh,bj->hj", bias_table, line_hot, precision=HIGHEST)
    line = line[:, ::-1]
    wide = group + rows
    tiled = jnp.broadcast_to(line[:, None, :], (HEADS, rows, wide)).reshape(HEADS, rows * wide)
    skew = tiled[:, rows : rows + rows * (wide - 1)].reshape(HEADS, rows, wide - 1)[:, :, :group]

    normed1_all = norm_apply(x_all.astype(F32), gains[0]).astype(BF)
    normed1 = norm_apply(x_rows, gains[0]).astype(BF)
    query = times(normed1, w_in[0]).astype(BF)
    keys = times(normed1_all, w_in[1]).astype(BF)
    values = times(normed1_all, w_in[2]).astype(BF)
    mem_keys = times(m_all, w_in[4]).astype(BF)
    mem_values = times(m_all, w_in[5]).astype(BF)
    mixed, chances_self = attend(query, keys, values, causal, skew[None], packs)
    hidden1 = x_rows + times(mixed, w_out[0])
    normed2 = norm_apply(hidden1, gains[1]).astype(BF)
    cross_query = times(normed2, w_in[3]).astype(BF)
    cross_mixed, chances_cross = attend(cross_query, mem_keys, mem_values, same, 0.0, packs)
    hidden2 = hidden1 + times(cross_mixed, w_out[1])
    normed3 = norm_apply(hidden2, gains[2]).astype(BF)

    routing = jax.nn.softmax(times(normed3, router), axis=1)
    route = routes[:, 0, 0, :, 0]
    route_hot = (route[:, :, None] == jnp.arange(experts, dtype=jnp.int32)).astype(jnp.int32)
    slot = jnp.sum((jnp.cumsum(route_hot, axis=1) - route_hot) * route_hot, axis=2)
    hot = route_hot.reshape(packs * rows, experts).astype(F32)
    gate = jnp.sum(routing * hot, axis=1)
    target = jnp.where(slot < capacity, (route * packs + jnp.arange(packs)[:, None]) * capacity + slot, -1).reshape(-1)
    dispatch = (target[:, None] == jnp.arange(experts * packs * capacity, dtype=jnp.int32)).astype(BF)

    def swap(a):
        shape = (experts, packs * capacity, width)
        return lax.all_to_all(a.reshape(shape), "expert", split_axis=0, concat_axis=0, tiled=True).reshape(-1, width)

    received = swap(times_left(dispatch, normed3).astype(BF))
    inner = times(received, e_in)
    hidden, pull = jax.vjp(gelu_tanh, inner)
    hidden = hidden.astype(BF)
    result = times(hidden, e_out).astype(BF)
    combined = times(dispatch, swap(result))
    out_rows = (hidden2 + gate[:, None] * combined).astype(BF)
    grad_top = cotangent.reshape(packs * rows, width).astype(F32)
    grad_gate = jnp.sum(grad_top * combined, axis=1)
    grad_result = swap(times_left(dispatch, (gate[:, None] * grad_top).astype(BF)).astype(BF))
    grad_hidden = times_right(grad_result, e_out)
    grad_eout = times_left(hidden, grad_result).astype(BF)
    grad_inner = pull(grad_hidden)[0].astype(BF)
    grad_ein = times_left(received, grad_inner).astype(BF)
    grad_send = swap(times_right(grad_inner, e_in).astype(BF))
    grad_logits = grad_gate[:, None] * routing * (hot - gate[:, None])
    grad_router = jnp.einsum("td,te->de", normed3.astype(F32), grad_logits, precision=HIGHEST)
    grad_normed3 = times(dispatch, grad_send) + jnp.einsum(
        "te,de->td", grad_logits, router.astype(F32), precision=HIGHEST
    )
    back3, gain3 = norm_back(hidden2, gains[2], grad_normed3)
    grad_h2 = grad_top + back3
    grad_h2_low = grad_h2.astype(BF)
    grad_wco = times_left(cross_mixed, grad_h2_low)
    grad_cross = times_right(grad_h2_low, w_out[1]).astype(BF)
    grad_cq, grad_ck, grad_cv, _ = attend_back(cross_query, mem_keys, mem_values, chances_cross, grad_cross, packs)
    back2, gain2 = norm_back(hidden1, gains[1], times_right(grad_cq, w_in[3]))
    grad_h1 = grad_h2 + back2
    grad_h1_low = grad_h1.astype(BF)
    grad_wso = times_left(mixed, grad_h1_low)
    grad_mixed = times_right(grad_h1_low, w_out[0]).astype(BF)
    grad_q, grad_k, grad_v, grad_scores = attend_back(query, keys, values, chances_self, grad_mixed, packs)

    total = jnp.sum(grad_scores.astype(F32), axis=0)[:, ::-1]
    padded = jnp.pad(total, ((0, 0), (0, 0), (0, wide - group))).reshape(HEADS, rows * wide)
    diagonal = padded[:, : rows * (wide - 1)].reshape(HEADS, rows, wide - 1).sum(axis=1)
    at = jnp.clip(rank * rows + (rows - 1) - jnp.arange(wide - 1, dtype=jnp.int32), 0, group - 1)
    diagonal_hot = (jnp.take(rel_buckets, at)[:, None] == jnp.arange(buckets)).astype(F32)
    grad_table = jnp.einsum("jb,hj->bh", diagonal_hot, diagonal, precision=HIGHEST)

    def to_owner(a):
        return lax.psum_scatter(a.reshape(packs, group, width), "seq", scatter_dimension=1, tiled=True)

    grad_memory = to_owner((times_right(grad_ck, w_in[4]) + times_right(grad_cv, w_in[5])).astype(BF))
    part1 = to_owner((times_right(grad_k, w_in[1]) + times_right(grad_v, w_in[2])).astype(BF))
    grad_normed1 = times_right(grad_q, w_in[0]) + part1.reshape(packs * rows, width).astype(F32)
    back1, gain1 = norm_back(x_rows, gains[0], grad_normed1)
    grad_x = grad_h1 + back1
    grad_in = jnp.concatenate(
        [
            times_left(normed1, grad_q),
            times_left(normed1_all, grad_k),
            times_left(normed1_all, grad_v),
            times_left(normed2, grad_cq),
            times_left(m_all, grad_ck),
            times_left(m_all, grad_cv),
        ]
    ).astype(BF)
    grad_out = jnp.concatenate([grad_wso, grad_wco]).astype(BF)
    shards = [
        lax.psum_scatter(a, over, scatter_dimension=0, tiled=True).astype(F32)
        for a, over in ((grad_in, everywhere), (grad_out, everywhere), (grad_ein, peers), (grad_eout, peers))
    ]
    small = lax.psum((jnp.stack([gain1, gain2, gain3]), grad_table, grad_router), ("dp", "seq", "expert"))
    shape = (packs, 1, 1, rows, width)
    return (
        out_rows.reshape(shape),
        grad_x.reshape(shape),
        grad_memory.astype(F32).reshape(shape),
        *small,
        shards[0],
        shards[1],
        shards[2][None],
        shards[3][None],
    )


def solution(mesh):
    tokens = P(None, "dp", "expert", "seq", None)
    dense = P(("dp", "seq", "expert"), None)
    expert = P("expert", ("dp", "seq"), None)
    return jax.shard_map(
        per_device,
        mesh=mesh,
        in_specs=(tokens, tokens, tokens, tokens, P(None, "dp", "expert", None), P(), P(), P(), P(),
                  dense, dense, expert, expert),
        out_specs=(tokens, tokens, tokens, P(), P(), P(), dense, dense, expert, expert),
        check_vma=False,
    )
```

```python
import functools

import jax
import jax.numpy as jnp
from jax import lax
from jax.experimental import pallas as pl
from jax.experimental.pallas import tpu as pltpu
from jax.sharding import PartitionSpec as P

HEADS = 12
HEAD = 64

EPS = 1e-06
NEG = -1e30
HIGHEST = lax.Precision.HIGHEST
MESH = pl.DeviceIdType.MESH
BF = jnp.bfloat16
F32 = jnp.float32


class Place:
    def __init__(self):
        self.nz, self.ns, self.ny = (lax.axis_size(a) for a in ("dp", "seq", "expert"))
        self.nx = self.ns // 2
        self.z, self.s, self.y = (lax.axis_index(a) for a in ("dp", "seq", "expert"))
        self.x, self.c = self.s // 2, lax.rem(self.s, 2)

    def device(self, z=None, x=None, c=None, y=None):
        z = self.z if z is None else z
        x = self.x if x is None else x
        c = self.c if c is None else c
        y = self.y if y is None else y
        return (z, x * 2 + c, y)

    def other_x(self):
        return [lax.rem(self.x + k, self.nx) for k in range(1, self.nx)]

    def other_y(self):
        return [lax.rem(self.y + k, self.ny) for k in range(1, self.ny)]

    def by_distance(self, k):
        half = self.nz // 2
        order = [
            sorted(range(self.nz), key=lambda d: (abs(d - z), (d < half) != (z < half), d)) for z in range(self.nz)
        ]
        return self.pick([row[k] for row in order])

    def pick(self, values):
        out = jnp.int32(values[0])
        for z in range(1, self.nz):
            out = jnp.where(self.z == z, jnp.int32(values[z]), out)
        return out

    def greet(self):
        barrier = pltpu.get_barrier_semaphore()
        for x in self.other_x():
            pl.semaphore_signal(barrier, inc=1, device_id=self.device(x=x), device_id_type=MESH)
        for y in self.other_y():
            pl.semaphore_signal(barrier, inc=1, device_id=self.device(y=y), device_id_type=MESH)
        pl.semaphore_signal(barrier, inc=1, device_id=self.device(c=1 - self.c), device_id_type=MESH)

        for k in range(1, self.nz):
            z = lax.rem(self.z + k, self.nz)
            pl.semaphore_signal(barrier, inc=1, device_id=self.device(z=z), device_id_type=MESH)
        pl.semaphore_wait(barrier, self.nx - 1 + self.ny - 1 + 1 + self.nz - 1)


def rms_rows(src, gain, dst, rows, step=64):
    @pl.loop(0, rows // step)
    def _(i):
        at = pl.ds(pl.multiple_of(i * step, step), step)
        value = src[at, :].astype(F32)
        r = lax.rsqrt(jnp.mean(value * value, axis=-1, keepdims=True) + EPS)
        dst[at, :] = (value * r * gain).astype(BF)


def block(weight, index, lanes=slice(None), share=(0, 1)):
    unit, width = weight.shape[-2:]
    count = width // unit // share[1]
    first = pl.multiple_of(index * (width // unit) + share[0] * count, count)
    value = weight[pl.ds(first, count), :, lanes]
    return value.reshape(count * unit, value.shape[-1])


def project(left, weight, index, dst):
    width = dst.shape[-1]
    step = 256 if width % 256 == 0 else width

    @pl.loop(0, width // step)
    def _(j):
        at = pl.ds(pl.multiple_of(j * step, step), step)
        dst[:, at] = jnp.dot(left[...], block(weight, index, at), preferred_element_type=F32).astype(dst.dtype)


def prepare_bias(rel, table, bias, rank, rows, group):
    heads, buckets = table.shape
    wide = group + 128
    lane = lax.broadcasted_iota(jnp.int32, (group, wide), 1)
    shift = jnp.where(lane < group, lane, lane - wide)
    distance = jnp.clip(rank * rows - shift, 0, group - 1)
    hot = (lax.broadcasted_iota(jnp.int32, (group, wide), 0) == distance).astype(F32).astype(BF)
    which = jnp.dot(jnp.broadcast_to(rel[...].astype(F32), (8, group)).astype(BF), hot, preferred_element_type=F32)
    picks = (lax.broadcasted_iota(jnp.int32, (buckets, wide), 0) == which[0:1].astype(jnp.int32)).astype(F32)
    line = jnp.dot(table[...], picks, precision=HIGHEST, preferred_element_type=F32)
    for h in range(heads):
        band = pltpu.roll(jnp.broadcast_to(line[h : h + 1], (rows, wide)), 0, 1, stride=1, stride_axis=0)
        bias[h // 2, pl.ds((h % 2) * rows, rows), :] = band[:, :group]


def prepare_masks(lengths, same, causal, rank, rows, group):
    key = lax.broadcasted_iota(jnp.int32, (rows, group), 1)
    query = rank * rows + lax.broadcasted_iota(jnp.int32, (rows, group), 0)
    for p in range(same.shape[0]):
        end = jnp.int32(0)
        kd = jnp.zeros((rows, group), jnp.int32)
        qd = jnp.zeros((rows, group), jnp.int32)
        for n in range(lengths.shape[1]):
            end = end + lengths[p, n]
            kd = kd + jnp.where(key >= end, 1, 0)
            qd = qd + jnp.where(query >= end, 1, 0)
        same[p] = jnp.where(kd == qd, 0.0, NEG)
        causal[p] = jnp.where((kd == qd) & (key <= query), 0.0, NEG)


def two_heads(pair):
    first = lax.broadcasted_iota(jnp.int32, pair.shape, 1) < HEAD
    zero = jnp.zeros_like(pair)
    return jnp.concatenate([jnp.where(first, pair, zero), jnp.where(first, zero, pair)], axis=0)


def one_pair(stacked):
    rows = stacked.shape[0] // 2
    first = lax.broadcasted_iota(jnp.int32, (rows, stacked.shape[1]), 1) < HEAD
    return jnp.where(first, stacked[:rows], stacked[rows:])


def attend_pairs(query, keys, values, bias, mask, chances, mixed):
    packs, pairs, double, group = chances.shape
    rows = double // 2

    def body(i, carry):
        p, j = i // pairs, lax.rem(i, pairs)
        mine = pl.ds(pl.multiple_of(p * rows, rows), rows)
        theirs = pl.ds(pl.multiple_of(p * group, group), group)
        lanes = pl.ds(pl.multiple_of(j * 128, 128), 128)
        scores = lax.dot_general(
            two_heads(query[mine, lanes]), keys[theirs, lanes], (((1,), (1,)), ((), ())), preferred_element_type=F32
        )
        scores = scores * HEAD**-0.5
        if bias is not None:
            scores = scores + bias[j]
        scores = (scores.reshape(2, rows, group) + mask[p][None]).reshape(double, group)
        raised = jnp.exp(scores - jnp.max(scores, axis=1, keepdims=True))
        weights = (raised * (1.0 / jnp.sum(raised, axis=1, keepdims=True))).astype(BF)
        chances[p, j] = weights
        out = jnp.dot(weights, values[theirs, lanes], preferred_element_type=F32)
        mixed[mine, lanes] = one_pair(out).astype(BF)
        return carry

    lax.fori_loop(0, packs * pairs, body, 0, unroll=12)


def add_product(total, left, weight, index):
    width = total.shape[-1]
    step = 256 if width % 256 == 0 else width

    @pl.loop(0, width // step)
    def _(j):
        at = pl.ds(pl.multiple_of(j * step, step), step)
        total[:, at] += jnp.dot(left[...], block(weight, index, at), preferred_element_type=F32)


def product_t(left, weight, index, dst):
    halves = 2
    step = weight.shape[-1] // halves

    @pl.loop(0, halves)
    def _(j):
        rows = block(weight, index, share=(j, halves))
        out = lax.dot_general(left[...], rows, (((1,), (1,)), ((), ())), preferred_element_type=F32)
        dst[:, pl.ds(pl.multiple_of(j * step, step), step)] = out.astype(dst.dtype)


def two_products_t(left1, index1, left2, index2, weight, dst):
    halves = 2
    step = weight.shape[-1] // halves

    @pl.loop(0, halves)
    def _(j):
        out = 0.0
        for left, index in ((left1, index1), (left2, index2)):
            rows = block(weight, index, share=(j, halves))
            out = out + lax.dot_general(left[...], rows, (((1,), (1,)), ((), ())), preferred_element_type=F32)
        dst[:, pl.ds(pl.multiple_of(j * step, step), step)] = out.astype(dst.dtype)


def outer_product(left, right, dst, index):
    unit, width = dst.shape[-2:]
    halves = 2
    step, count = width // halves, width // unit // halves

    @pl.loop(0, halves)
    def _(j):
        part = left[:, pl.ds(pl.multiple_of(j * step, step), step)]
        out = lax.dot_general(part, right[...], (((0,), (0,)), ((), ())), preferred_element_type=F32)
        first = index * (width // unit) + j * count
        dst[pl.ds(first, count)] = out.astype(dst.dtype).reshape(count, unit, width)


def add_into(total, other):
    lead = total.shape[:-2]
    count = 1
    for n in lead:
        count *= n
    rows = total.shape[-2]
    step = next(n for n in ((48, 32, 16) if total.shape[-1] <= 1024 else (16,)) if rows % n == 0)

    def body(i, carry):
        index = []
        rest = i // (rows // step)
        for n in reversed(lead):
            index.insert(0, lax.rem(rest, n))
            rest = rest // n
        r = pl.ds(pl.multiple_of(lax.rem(i, rows // step) * step, 16), step)
        at = (*index, r)
        total[at] = (total[at].astype(F32) + other[at].astype(F32)).astype(total.dtype)
        return carry

    lax.fori_loop(0, count * (rows // step), body, 0)


def norm_back_rows(value, gain, grad, total, gain_grad, step=64):
    gain_grad[...] = jnp.zeros_like(gain_grad)

    @pl.loop(0, value.shape[0] // step)
    def _(i):
        at = pl.ds(pl.multiple_of(i * step, step), step)
        v, g = value[at, :].astype(F32), grad[at, :]
        r = lax.rsqrt(jnp.mean(v * v, axis=-1, keepdims=True) + EPS)
        scaled = g * gain
        total[at, :] += r * scaled - v * (r * r * r) * jnp.mean(scaled * v, axis=-1, keepdims=True)
        gain_grad[...] += jnp.sum(g * v * r, axis=0, keepdims=True)


def attend_pairs_back(query, keys, values, chances, grad, grad_q, grad_k, grad_v, diagonal):
    packs, pairs, double, group = chances.shape
    rows = double // 2
    scale = HEAD**-0.5

    def body(i, carry):
        p, j = i // pairs, lax.rem(i, pairs)
        mine = pl.ds(pl.multiple_of(p * rows, rows), rows)
        theirs = pl.ds(pl.multiple_of(p * group, group), group)
        lanes = pl.ds(pl.multiple_of(j * 128, 128), 128)
        ga = two_heads(grad[mine, lanes])
        low = chances[p, j]
        wide = low.astype(F32)
        gp = lax.dot_general(ga, values[theirs, lanes], (((1,), (1,)), ((), ())), preferred_element_type=F32)
        gs = (wide * (gp - jnp.sum(wide * gp, axis=1, keepdims=True))).astype(BF)
        gq = jnp.dot(gs, keys[theirs, lanes], preferred_element_type=F32)
        grad_q[mine, lanes] = (one_pair(gq) * scale).astype(BF)
        gk = lax.dot_general(gs, two_heads(query[mine, lanes]), (((0,), (0,)), ((), ())), preferred_element_type=F32)
        grad_k[theirs, lanes] = (gk * scale).astype(BF)
        gv = lax.dot_general(low, ga, (((0,), (0,)), ((), ())), preferred_element_type=F32)
        grad_v[theirs, lanes] = gv.astype(BF)
        if diagonal is not None:
            a = lax.broadcasted_iota(jnp.int32, (rows, rows), 0)
            b = lax.broadcasted_iota(jnp.int32, (rows, rows), 1)
            flip = (a + b == rows - 1).astype(F32).astype(BF)
            for half in range(2):
                turned = jnp.dot(flip, gs[half * rows : (half + 1) * rows], preferred_element_type=F32)
                turned = jnp.concatenate([turned, jnp.zeros((rows, 128), F32)], axis=1)
                band = pltpu.roll(turned, 0, 1, stride=1, stride_axis=0)
                diagonal[pl.ds(2 * j + half, 1), :] += jnp.sum(band, axis=0, keepdims=True)
        return carry

    lax.fori_loop(0, packs * pairs, body, 0, unroll=12)


def table_grad(rel, diagonal, rank, rows, group):
    wide = group + 128
    lane = lax.broadcasted_iota(jnp.int32, (group, wide), 1)
    distance = jnp.clip(rank * rows + rows - 1 - lane, 0, group - 1)
    hot = (lax.broadcasted_iota(jnp.int32, (group, wide), 0) == distance).astype(F32).astype(BF)
    which = jnp.dot(jnp.broadcast_to(rel[...].astype(F32), (8, group)).astype(BF), hot, preferred_element_type=F32)
    picks = (lax.broadcasted_iota(jnp.int32, (128, wide), 0) == which[0:1].astype(jnp.int32)).astype(F32)
    return lax.dot_general(diagonal[...], picks, (((1,), (1,)), ((), ())), precision=HIGHEST, preferred_element_type=F32)


def route_slots(route, experts, capacity):
    packs, _, rows = route.shape
    count = packs * rows
    same = lax.broadcasted_iota(jnp.int32, (rows, rows), 0) == lax.broadcasted_iota(jnp.int32, (rows, rows), 1)
    column = jnp.concatenate(
        [jnp.sum(jnp.where(same, route[p], 0), axis=1, keepdims=True) for p in range(packs)], axis=0
    )
    hot = (column == lax.broadcasted_iota(jnp.int32, (count, experts), 1)).astype(F32)
    a = lax.broadcasted_iota(jnp.int32, (count, count), 0)
    b = lax.broadcasted_iota(jnp.int32, (count, count), 1)
    earlier = ((b < a) & (a // rows == b // rows)).astype(F32).astype(BF)
    before = jnp.dot(earlier, hot.astype(BF), preferred_element_type=F32)
    slot = jnp.sum(before * hot, axis=1, keepdims=True).astype(jnp.int32)
    pack = lax.broadcasted_iota(jnp.int32, (count, 1), 0) // rows
    target = jnp.where(slot < capacity, (column * packs + pack) * capacity + slot, -1)
    slots = lax.broadcasted_iota(jnp.int32, (count, experts * packs * capacity), 1)
    return hot, (target == slots).astype(F32).astype(BF)


def gelu_both(z):
    c = 0.7978845608028654
    t = jnp.tanh(c * (z + 0.044715 * (z * z * z)))
    half = 0.5 * (1.0 + t)
    slope = half + 0.5 * z * (1.0 - t * t) * (c * (1.0 + 3 * 0.044715 * (z * z)))
    return z * half, slope


def continue_waits(waits, hop, d, at):
    def wait():
        @pl.when(d < at.z)
        def _():
            hop(-1).wait_send()

        @pl.when(d > at.z)
        def _():
            hop(1).wait_send()

    waits.append(wait)


def layer_body(lengths, rel, gains, table, router_t, route, x_ref, m_ref, g_ref, ain, aout, ein, eout,
               out_rows, o0, o1, o2, o3, grad_x, grad_mem, sum_gains, sum_router, sum_table,
               w, big, ge, prep, c2, c3, y0, y1, x0, x1, ex_in, z0, z1, z2, z3,
               xo, mo, n1_all, k_, v, kc, vc, gv, n1, q, mixed, n2, qc, cross_mixed, n3, gb, ga, gq,
               pr_self, pr_cross, h1, h2, gn, bias, same, causal, diagonal, gain_row,
               act_core, act_x, wide_sum, table_sum, wide_in, table_in,
               slots_out, slots_in, slots_acc, ret_out, ret_in, back_in, hid, gin_,
               act_send, act_recv, prep_send, prep_recv, line_send, side_send, spread_send, ici_recv, spread_recv, own_sem,
               core_send, core_recv, y_send, y_recv, x_send, x_recv, ex_send, ex_recv, z_send, z_recv, zd_send, zd_recv,
               sum_send, sum_recv, small_send, small_recv, slot_send, slot_recv, free_sem):
    at = Place()
    nz, nx, ny = at.nz, at.nx, at.ny
    packs, tok, width = x_ref.shape
    group = xo.shape[0] // packs
    experts = router_t.shape[0]
    unit = ain.shape[1]
    block_units = eout.shape[0]
    panels = block_units // nx
    columns = ein.shape[1] // (nz * nx)
    buckets = table.shape[1]
    gk = xo
    units = (ain.shape[0], aout.shape[0])
    tall = nz * nx * 2
    bases = (0, tall * ny * units[0], 0, 2 * nz * block_units)
    dense, e_in, e_out = (0, 1), 2, 3
    experts_ = (e_in, e_out)
    waits = []

    def remote(src, dst, ssem, rsem, **where):
        return pltpu.make_async_remote_copy(
            src_ref=src, dst_ref=dst, send_sem=ssem, recv_sem=rsem,
            device_id=at.device(**where), device_id_type=MESH,
        )

    def send(*args, **where):
        one = remote(*args, **where)
        if acts_now[0]:
            one.start()
        waits.append(one.wait_send)

    acts_now = [True]

    def at_planes(ends, step, last):
        between = (at.z > 0) & (at.z < nz - 1)
        mark = len(waits)

        @pl.when(jnp.logical_not(between) if ends else between)
        def _():
            step()

        del waits[mark:]
        if last:
            acts_now[0] = False
            step()
            acts_now[0] = True

    def add(total, other):
        if acts_now[0]:
            add_into(total, other)

    def start_when(pred, make):
        if acts_now[0]:

            @pl.when(pred)
            def _():
                make().start()

    def arrive(ref, sem):
        if acts_now[0]:
            pltpu.make_async_copy(ref, ref, sem).wait()

    def spot(a, z, x, c, y):
        index = ((z * nx + x) * 2 + c) * ny + y
        return w.at[pl.ds(bases[a] + index * units[a], units[a])]

    def pack_of(a, z, c):
        return big.at[pl.ds(bases[a] + (z * 2 + c) * block_units, block_units)]

    shards = (ain, aout)
    acts = ((x_ref, xo), (m_ref, mo))

    at.greet()

    def act_rows(full, p, x, c):
        return full.at[pl.ds(pl.multiple_of(p * group + (x * 2 + c) * tok, 16), tok)]

    own_waits = []

    def send_acts():
        for i, (src, full) in enumerate(acts):
            for p in range(packs):
                dst = act_rows(full, p, at.x, at.c)
                for k, x in enumerate(at.other_x()):
                    send(src.at[p], dst, act_send.at[i, p, k], act_recv.at[i, p, at.x, at.c], x=x)
                send(src.at[p], dst, act_send.at[i, p, nx - 1 + at.x], act_recv.at[i, p, at.x, at.c], c=1 - at.c)
                own = pltpu.make_async_copy(src.at[p], dst, own_sem.at[4 + i, p])
                own.start()
                own_waits.append(own.wait)

    def along_line(a, z, src):
        dst = spot(a, z, at.x, at.c, at.y) if a in dense else pack_of(a, z, at.c)
        sem = ici_recv.at[a, z, at.x, at.y]
        left = (z >= at.z) & (at.z > 0)
        right = (z <= at.z) & (at.z < nz - 1)

        def one(side):
            return remote(src, dst, line_send.at[a, z, side], sem, z=at.z + 2 * side - 1)

        start_when(left, lambda: one(0))
        start_when(right, lambda: one(1))

        def wait():
            @pl.when(left)
            def _():
                one(0).wait_send()

            @pl.when(right)
            def _():
                one(1).wait_send()

        waits.append(wait)

    def to_core(a, z, x, y, src):
        dst = spot(a, z, x, at.c, y) if a in dense else pack_of(a, z, at.c)
        send(src, dst, spread_send.at[a, z, x, y], spread_recv.at[a, z, x, y], c=1 - at.c)

    zs = [at.by_distance(k) for k in range(nz)]

    def dense_events(k):
        z = zs[k]
        for a in dense:
            here = spot(a, z, at.x, at.c, at.y)
            src = here if k else shards[a]
            if k:
                arrive(here, ici_recv.at[a, z, at.x, at.y])
            else:
                own = pltpu.make_async_copy(shards[a], here, own_sem.at[a, 0])
                own.start()
                own_waits.append(own.wait)
            along_line(a, z, src)
            for j, x in enumerate(at.other_x()):
                send(src, here, side_send.at[a, z, j], ici_recv.at[a, z, at.x, at.y], x=x)
            for j, y in enumerate(at.other_y()):
                send(src, here, side_send.at[a, z, nx - 1 + j], ici_recv.at[a, z, at.x, at.y], y=y)
            to_core(a, z, at.x, at.y, src)

    def side_y(k):
        z = zs[k]
        for y in at.other_y():
            for a in dense:
                here = spot(a, z, at.x, at.c, y)
                arrive(here, ici_recv.at[a, z, at.x, y])
                if a == 1:
                    for j, x in enumerate(at.other_x()):
                        send(here, here, side_send.at[a, z, nx - 1 + ny - 1 + j + (nx - 1) * y],
                             ici_recv.at[a, z, at.x, y], x=x)
                to_core(a, z, at.x, y, here)

    def side_x(k):
        z = zs[k]
        for x in at.other_x():
            for a in dense:
                here = spot(a, z, x, at.c, at.y)
                arrive(here, ici_recv.at[a, z, x, at.y])
                if a == 0:
                    for j, y in enumerate(at.other_y()):
                        send(here, here, side_send.at[a, z, nx - 1 + ny - 1 + j + (ny - 1) * x],
                             ici_recv.at[a, z, x, at.y], y=y)
                to_core(a, z, x, at.y, here)

    def corner_events(k):
        z = zs[k]
        for a in dense:
            for y in at.other_y():
                for x in at.other_x():
                    here = spot(a, z, x, at.c, y)
                    arrive(here, ici_recv.at[a, z, x, y])
                    to_core(a, z, x, y, here)

    def act_events():
        for i, (src, full) in enumerate(acts):
            for p in range(packs):
                for x in at.other_x():
                    dst = act_rows(full, p, x, at.c)
                    arrive(dst, act_recv.at[i, p, x, at.c])
                    send(dst, dst, act_send.at[i, p, nx - 1 + x], act_recv.at[i, p, x, at.c], c=1 - at.c)

    def in_unit(z, c, x, n=1):
        return pl.ds(bases[e_in] + ((z * 2 + c) * nx + x) * panels, n * panels)

    def start_prep():
        for x in range(nx):
            for u in range(panels):
                each_z = width // columns
                prep[x, u] = jnp.concatenate(
                    [ein[:, (z * nx + x) * columns : (z * nx + x + 1) * columns] for z in range(u * each_z, (u + 1) * each_z)],
                    axis=1,
                )
        big[in_unit(at.z, at.c, at.x)] = prep[at.x]
        for j, x in enumerate(at.other_x()):
            send(prep.at[x], big.at[in_unit(at.z, at.c, at.x)], prep_send.at[j], prep_recv.at[at.x], x=x)

    def expert_events(k, kinds=experts_):
        z = zs[k]
        for a in kinds:
            here = pack_of(a, z, at.c)
            src = here
            if k:
                arrive(here, ici_recv.at[a, z, at.x, at.y])
            elif a == e_in:
                for x in at.other_x():
                    arrive(big.at[in_unit(at.z, at.c, x)], prep_recv.at[x])
            else:
                src = eout
                own = pltpu.make_async_copy(eout, here, own_sem.at[a, 0])
                own.start()
                own_waits.append(own.wait)
            along_line(a, z, src)
            to_core(a, z, 0, 0, src)

    def first_norm():
        for i, (src, full) in enumerate(acts):
            for p in range(packs):
                for x in range(nx):
                    arrive(act_rows(full, p, x, 1 - at.c), act_recv.at[i, p, x, 1 - at.c])
        for wait in own_waits:
            wait()
        rms_rows(xo, gains[0:1], n1_all, packs * group)
        for p in range(packs):
            h1[pl.ds(p * tok, tok), :] = x_ref[p].astype(F32)
            n1[pl.ds(p * tok, tok), :] = n1_all[pl.ds(pl.multiple_of(p * group + at.s * tok, tok), tok), :]

    places = [((z * 2 + c) * nx + x) * panels for z in range(nz) for x in range(nx) for c in range(2)]
    each = slots_out.shape[2]
    count = ny * each
    row_units = width // unit

    def keys_and_values(for_self):
        @pl.when(for_self)
        def _():
            project(n1_all, w, 1, k_)
            project(n1_all, w, 2, v)

        @pl.when(jnp.logical_not(for_self))
        def _():
            project(mo, w, 4, kc)
            project(mo, w, 5, vc)

    def by_slot(dispatch, rows):
        out = lax.dot_general(dispatch, rows, (((0,), (0,)), ((), ())), preferred_element_type=F32)
        return out.astype(BF).reshape(ny, each, width)

    slot_waits = []

    def slot_copy(late, src, dst, sem_from, sem_to, **where):
        one = remote(src, dst, slot_send.at[sem_from], slot_recv.at[sem_to], **where)
        one.start()
        (waits if late else slot_waits).append(one.wait_send)

    def y_sem(t, j):
        return t * (ny - 1) + j

    def x_sem(t, j, y):
        return 4 * (ny - 1) + (t * (nx - 1) + j) * ny + y

    def ret_sem(t, j, y):
        return 4 * (ny - 1) + 2 * (nx - 1) * ny + (t * (nx - 1) + j) * ny + y

    def send_slots(t):
        for j, y in enumerate(at.other_y()):
            slot_copy(False, slots_out.at[t, y], slots_in.at[t, at.x, at.y], y_sem(t, j), y_sem(t, ny - 2 - j), y=y)
        for j, x in enumerate(at.other_x()):
            slot_copy(False, slots_out.at[t, at.y], slots_in.at[t, at.x, at.y], x_sem(t, j, at.y),
                      x_sem(t, nx - 2 - j, at.y), x=x)
        slots_in[t, at.x, at.y] = slots_out[t, at.y]

    def summed(t, y):
        total = slots_acc[t, at.x, y]
        for j in range(nx - 1):
            arrive(ret_in.at[t, j, y], slot_recv.at[ret_sem(t, j, y)])
            total = total + ret_in[t, j, y].astype(F32)
        return total.astype(BF)

    cores, ys, xs, zs_ = {2: c2, 3: c3}, (y0, y1), (x0, x1), (z0, z1, z2, z3)
    outs = (o0, o1, o2, o3)
    far = [sorted(range(nz), key=lambda d: (-abs(d - z), d)) for z in range(nz)]
    order_e = [at.pick([far[z][k] for z in range(nz)]) for k in range(nz)]
    halves = [[d for d in row if d >= nz // 2] + [d for d in row if d < nz // 2] for row in far]
    order_d = [at.pick([halves[z][k] for z in range(nz)]) for k in range(nz)]
    e_waits = []

    def expert_part(a, d, c):
        return ge.at[pl.ds(bases[a] + (d * 2 + c) * block_units, block_units)]

    def start_expert(a, k):
        one = remote(expert_part(a, order_e[k], 1 - at.c), cores[a].at[k], core_send.at[a, k, 0],
                     core_recv.at[a, k, 0], c=1 - at.c)
        one.start()
        e_waits.append(one.wait_send)

    def core_expert(a, k):
        arrive(cores[a].at[k], core_recv.at[a, k, 0])
        add_into(cores[a].at[k], expert_part(a, order_e[k], at.c))

    def free_experts():
        for wait in e_waits:
            wait()
        pl.semaphore_signal(free_sem, inc=1, device_id=at.device(c=1 - at.c), device_id_type=MESH)

    def dense_part(a, d, x, c):
        return big.at[pl.ds(bases[a] + ((d * nx + x) * 2 + c) * ny * units[a], ny * units[a])]

    def dense_core(a, k, x, y=None, u=None):
        first = bases[a] // 2 + (k * nx + x) * ny * units[a]
        if y is None:
            return ge.at[pl.ds(first, ny * units[a])]
        if u is None:
            return ge.at[pl.ds(first + y * units[a], units[a])]
        return ge.at[pl.ds(first + y * units[a] + u, 1)]

    def xs_in_order():
        return [(x, True) for x in at.other_x()] + [(at.x, False)]

    def start_dense(k, a):
        for x in range(nx):
            send(dense_part(a, order_d[k], x, 1 - at.c), dense_core(a, k, x), core_send.at[a, k, x],
                     core_recv.at[a, k, x], c=1 - at.c)

    def first_dense(k, a):
        if a == 0:
            for x, _ in xs_in_order():
                arrive(dense_core(0, k, x), core_recv.at[0, k, x])
                add_into(dense_core(0, k, x), dense_part(0, order_d[k], x, at.c))
                for u in range(units[0]):
                    for j, y in enumerate(at.other_y()):
                        send(dense_core(0, k, x, y, u), ys[0].at[k, ny - 2 - j, x, pl.ds(u, 1)],
                             y_send.at[k, j, x, u], y_recv.at[k, ny - 2 - j, x, u], y=y)
            return
        for x, _ in xs_in_order():
            arrive(dense_core(1, k, x), core_recv.at[1, k, x])
            add_into(dense_core(1, k, x), dense_part(1, order_d[k], x, at.c))
        for j, x in enumerate(at.other_x()):
            send(dense_core(1, k, x), xs[1].at[k, nx - 2 - j], x_send.at[k, j, units[0]],
                 x_recv.at[k, nx - 2 - j, units[0]], x=x)

    def second_dense(k, a):
        if a == 0:
            for x, away in xs_in_order():
                for u in range(units[0]):
                    total = ys[0].at[k, 0, x, pl.ds(u, 1)]
                    for j in range(ny - 1):
                        piece = ys[0].at[k, j, x, pl.ds(u, 1)]
                        arrive(piece, y_recv.at[k, j, x, u])
                        add_into(total, piece if j else dense_core(0, k, x, at.y, u))
                    if away:
                        j = lax.rem(x - at.x + nx, nx) - 1
                        send(total, xs[0].at[k, nx - 2 - j, pl.ds(u, 1)], x_send.at[k, j, u], x_recv.at[k, nx - 2 - j, u], x=x)
            return
        for j in range(nx - 1):
            arrive(xs[1].at[k, j], x_recv.at[k, j, units[0]])
            add_into(xs[1].at[k, 0], xs[1].at[k, j] if j else dense_core(1, k, at.x))
        for j, y in enumerate(at.other_y()):
            send(xs[1].at[k, 0, pl.ds(y * units[1], units[1])], ys[1].at[k, ny - 2 - j],
                 y_send.at[k, j, nx, 0], y_recv.at[k, ny - 2 - j, nx, 0], y=y)

    def piece_of(k, p):
        return xs[0].at[k, 0, pl.ds(p, 1)] if p < units[0] else ys[1].at[k, 0]

    def inbox_of(slot, p):
        return zs_[0].at[slot, pl.ds(p, 1)] if p < units[0] else zs_[1].at[slot]

    def line_dense(k, a):
        d = order_d[k]
        for p in range(units[0]) if a == 0 else [units[0]]:
            total = piece_of(k, p)
            if p < units[0]:
                for j in range(nx - 1):
                    piece = xs[0].at[k, j, pl.ds(p, 1)]
                    arrive(piece, x_recv.at[k, j, p])
                    add(total, piece if j else ys[0].at[k, 0, at.x, pl.ds(p, 1)])
            else:
                for j in range(ny - 1):
                    arrive(ys[1].at[k, j], y_recv.at[k, j, nx, 0])
                    add(total, ys[1].at[k, j] if j else xs[1].at[k, 0, pl.ds(at.y * units[1], units[1])])
            for side in range(2):

                @pl.when((at.z > 0) & (d > at.z) if side == 0 else (at.z < nz - 1) & (d < at.z))
                def _(total=total, p=p):
                    arrive(inbox_of(d, p), zd_recv.at[d, p])
                    add(total, inbox_of(d, p))

            def hop(to, total=total, p=p):
                slot = d if to > 0 else jnp.where(d == at.z - 1, nz, d)
                return remote(total, inbox_of(slot, p), zd_send.at[k, p], zd_recv.at[slot, p], z=at.z + to)

            start_when(d < at.z, functools.partial(hop, -1))
            start_when(d > at.z, functools.partial(hop, 1))

            continue_waits(waits, hop, d, at)

    def finish_dense():
        for k in (nz // 2 - 1, nz - 1):

            @pl.when(order_d[k] == at.z)
            def _(k=k):
                for p in range(units[0] + 1):
                    total = piece_of(k, p)
                    for side, here in enumerate((at.z > 0, at.z < nz - 1)):
                        slot = at.z if side == 0 else nz

                        @pl.when(here)
                        def _(total=total, slot=slot, p=p):
                            arrive(inbox_of(slot, p), zd_recv.at[slot, p])
                            add_into(total, inbox_of(slot, p))

                write_out(0, xs[0].at[k, 0])
                write_out(1, ys[1].at[k, 0])

    def write_out(a, total):
        if a != e_in:
            if acts_now[0]:
                outs[a][...] = total[...].astype(F32).reshape(outs[a].shape)
            return
        for j, x in enumerate(at.other_x()):
            send(total.at[pl.ds(x * panels, panels)], ex_in.at[nx - 2 - j], ex_send.at[j], ex_recv.at[nx - 2 - j], x=x)

    def finish_expert_in():
        for j in range(nx - 1):
            arrive(ex_in.at[j], ex_recv.at[j])
        total = cores[e_in].at[nz - 1]
        for x in range(nx):
            for u in range(panels):
                value = None
                for j, other in enumerate(at.other_x()):
                    value = ex_in[j, u] if value is None else jnp.where(other == x, ex_in[j, u], value)
                mine = total[pl.ds(at.x * panels + u, 1)][0]
                value = jnp.where(at.x == x, mine.astype(F32), value.astype(F32))
                for i in range(width // columns):
                    z = u * (width // columns) + i
                    outs[e_in][:, (z * nx + x) * columns : (z * nx + x + 1) * columns] = value[:, i * columns : (i + 1) * columns]

    def line(kind, k):
        for a in kind:
            d = order_e[k]
            total = cores[a].at[k]
            for side in range(2):
                feeds = (at.z > 0) & (d >= at.z) if side == 0 else (at.z < nz - 1) & (d <= at.z)
                slot = d if side == 0 else jnp.where(d == at.z, nz, d)

                @pl.when(feeds)
                def _(a=a, slot=slot, total=total):
                    arrive(zs_[a].at[slot], z_recv.at[a, slot])
                    add(total, zs_[a].at[slot])

            def hop(to, a=a, total=total, d=d):
                slot = d if to > 0 else jnp.where(d == at.z - 1, nz, d)
                return remote(total, zs_[a].at[slot], z_send.at[a, k], z_recv.at[a, slot], z=at.z + to)

            start_when(d < at.z, functools.partial(hop, -1))
            start_when(d > at.z, functools.partial(hop, 1))

            if k == nz - 1:
                write_out(a, total)
            continue_waits(waits, hop, d, at)

    def start_act(i):
        for p in range(packs):
            for x in range(nx):
                send(act_rows((kc, k_)[i], p, x, 1 - at.c), act_core.at[i, p, x], sum_send.at[i, p, x],
                     sum_recv.at[i, p, x], c=1 - at.c)

    def core_act(i):
        for p in range(packs):
            for x in range(nx):
                arrive(act_core.at[i, p, x], sum_recv.at[i, p, x])
                add_into(act_core.at[i, p, x], act_rows((kc, k_)[i], p, x, at.c))
        for j, x in enumerate(at.other_x()):
            send(act_core.at[i, :, x], act_x.at[i, nx - 2 - j], sum_send.at[i, packs, j], sum_recv.at[i, packs, nx - 2 - j], x=x)

    def x_act(i):
        for j in range(nx - 1):
            arrive(act_x.at[i, j], sum_recv.at[i, packs, j])
        for p in range(packs):
            out = act_core[i, p, at.x].astype(F32)
            for j in range(nx - 1):
                out = out + act_x[i, j, p].astype(F32)
            if i == 0:
                grad_mem[pl.ds(p * tok, tok), :] = out
            else:
                gn[pl.ds(p * tok, tok), :] += out

    pair_sums = ((wide_sum, wide_in), (table_sum, table_in))
    stages = [("c", [1 - at.c]), ("y", at.other_y()), ("x", at.other_x())]

    def start_small(t):
        axis, peers = stages[t]
        base = [0, 1, ny][t]
        for i, (total, inbox) in enumerate(pair_sums):
            for j, peer in enumerate(peers):
                back = base + len(peers) - 1 - j
                send(total.at[t], inbox.at[back], small_send.at[i, base + j], small_recv.at[i, back], **{axis: peer})

    def end_small(t):
        axis, peers = stages[t]
        base = [0, 1, ny][t]
        for i, (total, inbox) in enumerate(pair_sums):
            out = total[t]
            for j in range(len(peers)):
                arrive(inbox.at[base + j], small_recv.at[i, base + j])
                out = out + inbox[base + j]
            total[t + 1] = out

    tail = ny + nx - 1

    def start_line():
        for i, (total, inbox) in enumerate(pair_sums):
            for j in range(1, nz):
                z = lax.rem(at.z + j, nz)
                send(total.at[3], inbox.at[tail + at.z], small_send.at[i, tail + j], small_recv.at[i, tail + at.z], z=z)

    def end_line():
        for i, (total, inbox) in enumerate(pair_sums):
            for j in range(1, nz):
                z = lax.rem(at.z + j, nz)
                arrive(inbox.at[tail + z], small_recv.at[i, tail + z])
            out = None
            for z in range(nz):
                term = jnp.where(at.z == z, total[3], inbox[tail + z])
                out = term if out is None else out + term
            if i == 0:
                sum_gains[...] = out[: sum_gains.shape[0]]
                sum_router[...] = out[sum_gains.shape[0] : sum_gains.shape[0] + experts]
            else:
                sum_table[...] = out[: sum_table.shape[0], : sum_table.shape[1]]

    dense_events(0)
    start_prep()
    at_planes(False, lambda: dense_events(1), False)
    send_acts()
    side_x(0)
    side_y(0)
    at_planes(False, lambda: dense_events(2), False)
    at_planes(False, lambda: dense_events(3), False)
    at_planes(True, lambda: dense_events(1), True)
    expert_events(0, (e_in,))
    expert_events(0, (e_out,))
    at_planes(False, lambda: expert_events(1, (e_in,)), False)
    prepare_bias(rel, table, bias, at.s, tok, group)
    prepare_masks(lengths, same, causal, at.s, tok, group)
    hot, dispatch = route_slots(route, experts, each // packs)
    top = g_ref[...].astype(F32).reshape(packs * tok, width)
    at_planes(True, lambda: dense_events(2), True)
    act_events()
    at_planes(True, lambda: dense_events(3), True)
    at_planes(False, lambda: expert_events(2, (e_in,)), False)
    side_y(1)
    at_planes(False, lambda: expert_events(1, (e_out,)), False)
    side_x(1)
    side_y(2)
    first_norm()
    at_planes(True, lambda: expert_events(1, (e_in,)), True)
    at_planes(False, lambda: expert_events(2, (e_out,)), False)
    corner_events(0)
    side_x(2)
    side_y(3)
    side_x(3)
    at_planes(True, lambda: expert_events(1, (e_out,)), True)
    corner_events(1)
    at_planes(True, lambda: expert_events(2, (e_in,)), True)
    for a in dense:
        for z in zs[: nz // 2]:
            for x in range(nx):
                for y in range(ny):
                    arrive(spot(a, z, x, 1 - at.c, y), spread_recv.at[a, z, x, y])
    at_planes(False, lambda: expert_events(3, (e_out,)), False)
    corner_events(2)
    keys_and_values(at.z < nz // 2)
    corner_events(3)
    at_planes(False, lambda: expert_events(3, (e_in,)), False)
    for a in dense:
        for z in zs[nz // 2 :]:
            for x in range(nx):
                for y in range(ny):
                    arrive(spot(a, z, x, 1 - at.c, y), spread_recv.at[a, z, x, y])
    project(n1, w, 0, q)
    keys_and_values(at.z >= nz // 2)
    attend_pairs(q, k_, v, bias, causal, pr_self, mixed)
    add_product(h1, mixed, w, 6)
    rms_rows(h1, gains[1:2], n2, packs * tok)
    project(n2, w, 3, qc)
    attend_pairs(qc, kc, vc, None, same, pr_cross, cross_mixed)
    h2[...] = h1[...]
    add_product(h2, cross_mixed, w, 7)
    rms_rows(h2, gains[2:3], n3, packs * tok)
    slots_out[0] = by_slot(dispatch, n3[...])
    send_slots(0)
    logits = lax.dot_general(n3[...], router_t[...], (((1,), (1,)), ((), ())), preferred_element_type=F32)
    raised = jnp.exp(logits - jnp.max(logits, axis=1, keepdims=True))
    routing = raised / jnp.sum(raised, axis=1, keepdims=True)
    gate = jnp.sum(routing * hot, axis=1, keepdims=True)
    slots_out[1] = by_slot(dispatch, (gate * top).astype(BF))
    send_slots(1)
    for t in range(2):
        for j, y in enumerate(at.other_y()):
            here = slots_in.at[t, at.x, y]
            arrive(here, slot_recv.at[y_sem(t, j)])
            for i, x in enumerate(at.other_x()):
                slot_copy(False, here, here, x_sem(t, i, y), x_sem(t, nx - 2 - i, y), x=x)
    at_planes(True, lambda: expert_events(2, (e_out,)), True)
    at_planes(True, lambda: expert_events(3, (e_out,)), True)
    at_planes(True, lambda: expert_events(3, (e_in,)), True)
    for a in experts_:
        for z in range(nz):
            arrive(pack_of(a, z, 1 - at.c), spread_recv.at[a, z, 0, 0])
    for t in range(2):
        for i, x in enumerate(at.other_x()):
            for y in range(ny):
                arrive(slots_in.at[t, x, y], slot_recv.at[x_sem(t, i, y)])
    for wait in waits:
        wait()
    waits.clear()
    here = slots_in[0].reshape(nx * count, width)
    grad_here = slots_in[1].reshape(nx * count, width)
    for u in range(panels):
        in_panel = jnp.concatenate([big[place + u] for place in places], axis=0)
        out_panel = big[pl.ds(bases[e_out] + u * row_units, row_units)].reshape(width, width)
        inner = jnp.dot(here, in_panel, preferred_element_type=F32)
        hidden, slope = gelu_both(inner)
        hid[u] = hidden.astype(BF)
        grad_hidden = lax.dot_general(grad_here, out_panel, (((1,), (1,)), ((), ())), preferred_element_type=F32)
        gin_[u] = (grad_hidden * slope).astype(BF)
        result = jnp.dot(hid[u], out_panel, preferred_element_type=F32).reshape(nx, ny, each, width)
        grad_slots = lax.dot_general(gin_[u], in_panel, (((1,), (1,)), ((), ())), preferred_element_type=F32)
        grad_slots = grad_slots.reshape(nx, ny, each, width)
        if u:
            slots_acc[0] += result
            slots_acc[1] += grad_slots
        else:
            slots_acc[0] = result
            slots_acc[1] = grad_slots
    for y in [*at.other_y(), at.y]:
        for t in range(2):
            for j, x in enumerate(at.other_x()):
                ret_out[t, j, y] = slots_acc[t, x, y].astype(BF)
                slot_copy(True, ret_out.at[t, j, y], ret_in.at[t, nx - 2 - j, y], ret_sem(t, j, y),
                          ret_sem(t, nx - 2 - j, y), x=x)
    for u in range(panels):
        grad = lax.dot_general(here, gin_[u], (((0,), (0,)), ((), ())), preferred_element_type=F32).astype(BF)
        for i, place in enumerate(places):
            ge[place + u] = grad[i * unit : (i + 1) * unit]
    for k in range(nz):
        start_expert(e_in, k)
    for u in range(panels):
        grad = lax.dot_general(hid[u], grad_here, (((0,), (0,)), ((), ())), preferred_element_type=F32).astype(BF)
        ge[pl.ds(bases[e_out] + u * row_units, row_units)] = grad.reshape(row_units, unit, width)
    for k in range(nz):
        start_expert(e_out, k)
    core_expert(e_in, 0)
    for wait in slot_waits:
        wait()
    for j, y in enumerate(at.other_y()):
        for t in range(2):
            slots_out[t, y] = summed(t, y)
            slot_copy(True, slots_out.at[t, y], back_in.at[t, at.y], y_sem(2 + t, j), y_sem(2 + t, ny - 2 - j), y=y)
    core_expert(e_out, 0)
    at_planes(True, lambda: line((e_out,), 0), False)
    core_expert(e_in, 3)
    core_expert(e_out, 1)
    core_expert(e_out, 2)
    at_planes(True, lambda: line((e_in,), 0), False)
    at_planes(True, lambda: line((e_out,), 1), False)
    core_expert(e_out, 3)
    core_expert(e_in, 2)
    core_expert(e_in, 1)
    free_experts()
    for t in range(2):
        back_in[t, at.y] = summed(t, at.y)
    for t in range(2):
        for j, y in enumerate(at.other_y()):
            arrive(back_in.at[t, y], slot_recv.at[y_sem(2 + t, j)])
    combined = jnp.dot(dispatch, back_in[0].reshape(count, width), preferred_element_type=F32)
    rows_out = (h2[...] + gate * combined).astype(BF)
    for p in range(packs):
        out_rows[p] = rows_out[p * tok : (p + 1) * tok]
    grad_gate = jnp.sum(top * combined, axis=1, keepdims=True)
    grad_logits = grad_gate * routing * (hot - gate)
    diagonal[...] = jnp.zeros_like(diagonal)
    for i, (_, inbox) in enumerate(pair_sums):
        inbox[pl.ds(tail + at.z, 1)] = jnp.zeros_like(inbox[pl.ds(0, 1)])
    wide_sum[0] = jnp.zeros_like(wide_sum[0])
    wide_sum[0, pl.ds(3, experts), :] = lax.dot_general(
        grad_logits, n3[...].astype(F32), (((0,), (0,)), ((), ())), precision=HIGHEST, preferred_element_type=F32
    )
    grad_n3 = jnp.dot(dispatch, back_in[1].reshape(count, width), preferred_element_type=F32)
    for e in range(experts):
        grad_n3 = grad_n3 + grad_logits[:, e : e + 1] * router_t[e : e + 1, :].astype(F32)
    gn[...] = grad_n3
    grad_x[...] = top
    norm_back_rows(h2, gains[2:3], gn, grad_x, gain_row)
    wide_sum[0, 2:3, :] = gain_row[...]
    gb[...] = grad_x[...].astype(BF)
    product_t(gb, w, 7, ga)
    attend_pairs_back(qc, kc, vc, pr_cross, ga, gq, gk, gv, None)
    outer_product(n2, gq, big, 3)
    outer_product(mo, gk, big, 4)
    outer_product(mo, gv, big, 5)
    pl.semaphore_wait(free_sem, 1)
    start_dense(0, 0)
    outer_product(cross_mixed, gb, big, 7)
    start_dense(0, 1)
    two_products_t(gk, 4, gv, 5, w, kc)
    first_dense(0, 0)
    start_dense(1, 1)
    first_dense(0, 1)
    at_planes(True, lambda: line((e_out,), 2), False)
    at_planes(False, lambda: line((e_in,), 0), True)
    product_t(gq, w, 3, gn)
    norm_back_rows(h1, gains[1:2], gn, grad_x, gain_row)
    wide_sum[0, 1:2, :] = gain_row[...]
    at_planes(True, lambda: line((e_in,), 1), False)
    gb[...] = grad_x[...].astype(BF)
    product_t(gb, w, 6, ga)
    first_dense(1, 1)
    outer_product(mixed, gb, big, 6)
    start_dense(3, 1)
    start_dense(2, 1)
    start_dense(1, 0)
    attend_pairs_back(q, k_, v, pr_self, ga, gq, gk, gv, diagonal)
    first_dense(2, 1)
    first_dense(1, 0)
    at_planes(True, lambda: line((e_in,), 2), False)
    second_dense(0, 1)
    at_planes(False, lambda: line((e_out,), 0), True)
    first_dense(3, 1)
    two_products_t(gk, 1, gv, 2, w, k_)
    start_act(1)
    outer_product(n1, gq, big, 0)
    outer_product(n1_all, gk, big, 1)
    outer_product(n1_all, gv, big, 2)
    table_sum[0] = table_grad(rel, diagonal, at.s, tok, group)
    core_act(1)
    start_dense(2, 0)
    start_act(0)
    second_dense(2, 1)
    second_dense(0, 0)
    product_t(gq, w, 0, gn)
    first_dense(2, 0)
    second_dense(3, 1)
    core_act(0)
    start_dense(3, 0)
    at_planes(False, lambda: line((e_out,), 1), True)
    at_planes(False, lambda: line((e_in,), 1), True)
    at_planes(False, lambda: line((e_in,), 2), True)
    second_dense(1, 0)
    x_act(1)
    for p in range(packs):
        h1[pl.ds(p * tok, tok), :] = x_ref[p].astype(F32)
    norm_back_rows(h1, gains[0:1], gn, grad_x, gain_row)
    wide_sum[0, 0:1, :] = gain_row[...]
    at_planes(True, lambda: line_dense(0, 0), False)
    start_small(0)
    end_small(0)
    start_small(1)
    first_dense(3, 0)
    at_planes(False, lambda: line_dense(0, 0), True)
    second_dense(1, 1)
    at_planes(True, lambda: line_dense(0, 1), False)
    at_planes(True, lambda: line_dense(2, 1), False)
    second_dense(2, 0)
    at_planes(False, lambda: line_dense(0, 1), True)
    at_planes(False, lambda: line((e_out,), 2), True)
    at_planes(True, lambda: line_dense(1, 0), False)
    at_planes(False, lambda: line_dense(2, 1), True)
    at_planes(False, lambda: line((e_in,), 3), False)
    at_planes(False, lambda: line_dense(1, 0), True)
    at_planes(True, lambda: line((e_in,), 3), True)
    x_act(0)
    end_small(1)
    start_small(2)
    at_planes(True, lambda: line_dense(2, 0), False)
    at_planes(True, lambda: line_dense(3, 1), False)
    at_planes(False, lambda: line_dense(2, 0), True)
    second_dense(3, 0)
    at_planes(True, lambda: line_dense(3, 0), False)
    at_planes(True, lambda: line_dense(1, 1), False)
    at_planes(True, lambda: line((e_out,), 3), False)
    at_planes(False, lambda: line_dense(3, 1), True)
    finish_expert_in()
    at_planes(False, lambda: line((e_out,), 3), True)
    end_small(2)
    start_line()
    at_planes(False, lambda: line_dense(1, 1), True)
    at_planes(False, lambda: line_dense(3, 0), True)
    end_line()
    finish_dense()
    for wait in waits:
        wait()


def shapes_of(layer_input, routes, attn_in, attn_out, expert_in, expert_out):
    nz, ns, ny = (lax.axis_size(a) for a in ("dp", "seq", "expert"))
    packs, tok, width = layer_input.shape[0], layer_input.shape[3], layer_input.shape[4]
    return nz, ns, ny, packs, tok, width


def fits_kernel(layer_input, routes, attn_in, attn_out, expert_in, expert_out):
    nz, ns, ny, packs, tok, width = shapes_of(layer_input, routes, attn_in, attn_out, expert_in, expert_out)
    unit, hidden = expert_in.shape[1:]
    capacity = (5 * tok + 4 * ny - 1) // (4 * ny)
    nx = ns // 2
    return (
        unit % 16 == 0
        and tok % 16 == 0
        and packs * capacity % 16 == 0
        and attn_in.shape[0] % unit == 0
        and attn_out.shape[0] % unit == 0
        and expert_out.shape[1] % (unit * nx) == 0
        and width % (2 * unit) == 0
        and hidden % (nx * width) == 0
        and width % (hidden // (nz * nx)) == 0
        and hidden // (nz * nx) % 128 == 0
        and expert_out.shape[1] * nz * ns == hidden
        and expert_out.shape[1] * width == hidden * unit
        and expert_in.shape[0] == 1
    )


def deliver_body(*refs):
    count = (len(refs) - 2) // 3
    came, gone = refs[-2:]
    copies = []
    for i in range(count):
        place = refs[2 * count + i]
        copies.append((
            pltpu.make_async_copy(refs[i], place, came.at[i]),
            pltpu.make_async_copy(place, refs[count + i], gone.at[i]),
        ))
    for first, _ in copies:
        first.start()
    for first, second in copies:
        first.wait()
        second.start()
    for _, second in copies:
        second.wait()


def deliver(arrays):
    any_ = pl.BlockSpec(memory_space=pl.ANY)
    count = len(arrays)
    return pl.pallas_call(
        deliver_body,
        out_shape=[jax.ShapeDtypeStruct(a.shape, a.dtype) for a in arrays],
        in_specs=[any_] * count,
        out_specs=[any_] * count,
        scratch_shapes=[
            *[pltpu.VMEM(a.shape, a.dtype) for a in arrays],
            pltpu.SemaphoreType.DMA((count,)),
            pltpu.SemaphoreType.DMA((count,)),
        ],
        name="deliver",
    )(*arrays)


def layer_kernel(layer_input, memory, cotangent, routes, doc_lengths, rel_buckets, gains, bias_table, router,
                 attn_in, attn_out, expert_in, expert_out):
    nz, ns, ny, packs, tok, width = shapes_of(layer_input, routes, attn_in, attn_out, expert_in, expert_out)
    nx = ns // 2
    group, pairs = ns * tok, width // 128
    unit = expert_in.shape[1]
    hidden = expert_in.shape[2]
    panels = hidden // width // nx
    pack_units = nx * panels
    experts, buckets = router.shape[1], bias_table.shape[0]
    each = packs * ((5 * tok + 4 * experts - 1) // (4 * experts))
    tall = nz * ns
    units = (attn_in.shape[0] // unit, attn_out.shape[0] // unit)
    total = tall * ny * (units[0] + units[1])
    grads = max(4 * nz * pack_units, total // 2)
    extra = -(-(3 + experts) // 8) * 8
    small = ny + nx - 1 + nz
    mine, every = packs * tok, packs * group
    any_ = pl.BlockSpec(memory_space=pl.ANY)
    vmem = pl.BlockSpec(memory_space=pltpu.VMEM)
    smem = pl.BlockSpec(memory_space=pltpu.SMEM)
    dma = pltpu.SemaphoreType.DMA
    low = lambda *shape: pltpu.VMEM(shape, BF)
    wide = lambda *shape: pltpu.VMEM(shape, F32)
    shape = lambda *dims: jax.ShapeDtypeStruct(dims, F32)
    results = pl.pallas_call(
        layer_body,
        out_shape=[
            jax.ShapeDtypeStruct((packs, tok, width), BF),
            shape(*attn_in.shape),
            shape(*attn_out.shape),
            shape(*expert_in.shape[1:]),
            shape(*expert_out.shape[1:]),
            shape(mine, width),
            shape(mine, width),
            shape(3, width),
            shape(experts, width),
            shape(2 * pairs, buckets),
        ],
        in_specs=[smem, *[vmem] * 8, any_, any_, vmem, any_],
        out_specs=[vmem] * 10,
        scratch_shapes=[
            low(total, unit, width),
            low(total, unit, width),
            low(grads, unit, width),
            low(nx, panels, unit, width),
            *[low(nz, pack_units, unit, width)] * 2,
            low(nz, ny - 1, nx, units[0], unit, width),
            low(nz, ny - 1, units[1], unit, width),
            low(nz, nx - 1, units[0], unit, width),
            low(nz, nx - 1, ny * units[1], unit, width),
            low(nx - 1, panels, unit, width),
            *[low(nz + 1, u, unit, width) for u in (*units, pack_units, pack_units)],
            *[low(every, width)] * 8,
            *[low(mine, width)] * 10,
            *[low(packs, pairs, 2 * tok, group)] * 2,
            *[wide(mine, width)] * 3,
            wide(pairs, 2 * tok, group),
            wide(packs, tok, group),
            wide(packs, tok, group),
            wide(16, group + 128),
            wide(1, width),
            low(2, packs, nx, tok, width),
            low(2, nx - 1, packs, tok, width),
            wide(4, extra, width),
            wide(4, 16, 128),
            wide(small, extra, width),
            wide(small, 16, 128),
            low(2, ny, each, width),
            low(2, nx, ny, each, width),
            wide(2, nx, ny, each, width),
            low(2, nx - 1, ny, each, width),
            low(2, nx - 1, ny, each, width),
            low(2, ny, each, width),
            low(panels, nx * ny * each, width),
            low(panels, nx * ny * each, width),
            dma((2, packs, 2 * nx)),
            dma((2, packs, nx, 2)),
            dma((nx - 1,)),
            dma((nx,)),
            dma((4, nz, 2)),
            dma((2, nz, nx - 1 + ny - 1 + max((ny - 1) * nx, (nx - 1) * ny))),
            dma((4, nz, nx, ny)),
            dma((4, nz, nx, ny)),
            dma((4, nz, nx, ny)),
            dma((6, packs)),
            dma((4, nz, nx)),
            dma((4, nz, nx)),
            dma((nz, ny - 1, nx + 1, units[0])),
            dma((nz, ny - 1, nx + 1, units[0])),
            dma((nz, nx - 1, units[0] + 1)),
            dma((nz, nx - 1, units[0] + 1)),
            dma((nx - 1,)),
            dma((nx - 1,)),
            dma((4, nz)),
            dma((4, nz + 1)),
            dma((nz, units[0] + 1)),
            dma((nz + 1, units[0] + 1)),
            dma((2, packs + 1, nx)),
            dma((2, packs + 1, nx)),
            dma((2, small)),
            dma((2, small)),
            dma((4 * (ny - 1) + 4 * (nx - 1) * ny,)),
            dma((4 * (ny - 1) + 4 * (nx - 1) * ny,)),
            pltpu.SemaphoreType.REGULAR,
        ],
        compiler_params=pltpu.CompilerParams(
            collective_id=0, has_side_effects=True, vmem_limit_bytes=64 * 2**20
        ),
        name="layer",
    )(
        doc_lengths[:, 0, 0],
        rel_buckets.reshape(1, -1),
        gains,
        bias_table.T,
        router.T,
        routes.reshape(packs, 1, tok),
        layer_input[:, 0, 0],
        memory[:, 0, 0],
        cotangent[:, 0, 0],
        attn_in.reshape(units[0], unit, width),
        attn_out.reshape(units[1], unit, width),
        expert_in[0],
        expert_out.reshape(pack_units, unit, width),
    )
    out_rows, g0, g1, g2, g3, grad_x, grad_mem, gains_sum, router_sum, table_sum = deliver(results)
    spread = (packs, 1, 1, tok, width)
    return (
        out_rows.reshape(spread),
        grad_x.reshape(spread),
        grad_mem.reshape(spread),
        gains_sum,
        table_sum.T,
        router_sum.T,
        g0,
        g1,
        g2[None],
        g3[None],
    )


def norm_apply(value, gain):
    return value * lax.rsqrt(jnp.mean(value * value, axis=-1, keepdims=True) + EPS) * gain


def norm_back(value, gain, grad):
    r = lax.rsqrt(jnp.mean(value * value, axis=-1, keepdims=True) + EPS)
    scaled = grad * gain
    back = r * scaled - value * (r * r * r) * jnp.mean(scaled * value, axis=-1, keepdims=True)
    return back, jnp.sum(grad * value * r, axis=0)


def gelu_tanh(value):
    return jax.nn.gelu(value, approximate=True)


def times(left, right):
    return jnp.dot(left, right, preferred_element_type=F32)


def times_right(left, right):
    return jnp.einsum("te,de->td", left, right, preferred_element_type=F32)


def times_left(left, right):
    return jnp.einsum("td,te->de", left, right, preferred_element_type=F32)


def split(a, packs):
    return a.reshape(packs, -1, HEADS, HEAD)


def attend(query, keys, values, allowed, bias, packs):
    scores = jnp.einsum("pqhd,pkhd->phqk", split(query, packs), split(keys, packs), preferred_element_type=F32)
    masked = jnp.where(allowed[:, None], scores * HEAD**-0.5 + bias, NEG)
    raised = jnp.exp(masked - jnp.max(masked, axis=3, keepdims=True))
    chances = raised / jnp.sum(raised, axis=3, keepdims=True)
    mixed = jnp.einsum("phqk,pkhd->pqhd", chances.astype(BF), split(values, packs), preferred_element_type=F32)
    return mixed.reshape(query.shape).astype(BF), chances


def attend_back(query, keys, values, chances, grad, packs):
    scale = HEAD**-0.5
    g4 = split(grad, packs)
    grad_chances = jnp.einsum("pqhd,pkhd->phqk", g4, split(values, packs), preferred_element_type=F32)
    spread_ = jnp.sum(chances * grad_chances, axis=3, keepdims=True)
    grad_scores = (chances * (grad_chances - spread_)).astype(BF)
    grad_query = jnp.einsum("phqk,pkhd->pqhd", grad_scores, split(keys, packs), preferred_element_type=F32) * scale
    grad_keys = jnp.einsum("phqk,pqhd->pkhd", grad_scores, split(query, packs), preferred_element_type=F32) * scale
    grad_values = jnp.einsum("phqk,pqhd->pkhd", chances.astype(BF), g4, preferred_element_type=F32)
    return (
        grad_query.reshape(query.shape).astype(BF),
        grad_keys.reshape(keys.shape).astype(BF),
        grad_values.reshape(keys.shape).astype(BF),
        grad_scores,
    )


def per_device(layer_input, memory, cotangent, routes, doc_lengths, rel_buckets, gains, bias_table, router,
               attn_in, attn_out, expert_in, expert_out):
    packs, rows, width = layer_input.shape[0], layer_input.shape[3], layer_input.shape[4]
    seqs = lax.axis_size("seq")
    group = rows * seqs
    experts = router.shape[1]
    capacity = (5 * rows + 4 * experts - 1) // (4 * experts)
    buckets = bias_table.shape[0]
    rank = lax.axis_index("seq")

    x_in, m_in, e_in, e_out = layer_input[:, 0, 0], memory[:, 0, 0], expert_in[0], expert_out[0]
    if fits_kernel(layer_input, routes, attn_in, attn_out, expert_in, expert_out):
        return layer_kernel(layer_input, memory, cotangent, routes, doc_lengths, rel_buckets, gains, bias_table, router,
                            attn_in, attn_out, expert_in, expert_out)
    x_rows = x_in.reshape(packs * rows, width).astype(F32)
    everywhere, peers = ("dp", "seq", "expert"), ("dp", "seq")
    x_all, m_all = (lax.all_gather(a, "seq", axis=1, tiled=True) for a in (x_in, m_in))
    w_in, w_out = (lax.all_gather(a, everywhere, axis=0, tiled=True) for a in (attn_in, attn_out))
    e_in, e_out = (lax.all_gather(a, peers, axis=0, tiled=True) for a in (e_in, e_out))
    w_in = w_in.reshape(6, width, width)
    w_out = w_out.reshape(2, width, width)
    x_all = x_all.reshape(packs * group, width)
    m_all = m_all.reshape(packs * group, width)
    wide = group + rows
    query_pos = rank * rows + jnp.arange(rows, dtype=jnp.int32)
    key_pos = jnp.arange(group, dtype=jnp.int32)
    ends = jnp.cumsum(doc_lengths[:, 0, 0], axis=1)
    query_doc = jnp.sum((query_pos[None, :, None] >= ends[:, None, :]).astype(jnp.int32), axis=2)
    key_doc = jnp.sum((key_pos[None, :, None] >= ends[:, None, :]).astype(jnp.int32), axis=2)
    same = query_doc[:, :, None] == key_doc[:, None, :]
    causal = same & (key_pos[None, None, :] <= query_pos[None, :, None])
    bucket_hot = (rel_buckets[:, None] == jnp.arange(buckets, dtype=jnp.int32)).astype(F32)
    line_at = jnp.arange(group + rows, dtype=jnp.int32) - (group - 1) + rank * rows
    line_hot = (jnp.take(rel_buckets, jnp.clip(line_at, 0, group - 1))[None, :] == jnp.arange(buckets)[:, None]).astype(F32)
    line = jnp.einsum("bh,bj->hj", bias_table, line_hot, precision=HIGHEST)
    line = line[:, ::-1]
    wide = group + rows
    tiled = jnp.broadcast_to(line[:, None, :], (HEADS, rows, wide)).reshape(HEADS, rows * wide)
    skew = tiled[:, rows : rows + rows * (wide - 1)].reshape(HEADS, rows, wide - 1)[:, :, :group]

    normed1_all = norm_apply(x_all.astype(F32), gains[0]).astype(BF)
    normed1 = norm_apply(x_rows, gains[0]).astype(BF)
    query = times(normed1, w_in[0]).astype(BF)
    keys = times(normed1_all, w_in[1]).astype(BF)
    values = times(normed1_all, w_in[2]).astype(BF)
    mem_keys = times(m_all, w_in[4]).astype(BF)
    mem_values = times(m_all, w_in[5]).astype(BF)
    mixed, chances_self = attend(query, keys, values, causal, skew[None], packs)
    hidden1 = x_rows + times(mixed, w_out[0])
    normed2 = norm_apply(hidden1, gains[1]).astype(BF)
    cross_query = times(normed2, w_in[3]).astype(BF)
    cross_mixed, chances_cross = attend(cross_query, mem_keys, mem_values, same, 0.0, packs)
    hidden2 = hidden1 + times(cross_mixed, w_out[1])
    normed3 = norm_apply(hidden2, gains[2]).astype(BF)

    routing = jax.nn.softmax(times(normed3, router), axis=1)
    route = routes[:, 0, 0, :, 0]
    route_hot = (route[:, :, None] == jnp.arange(experts, dtype=jnp.int32)).astype(jnp.int32)
    slot = jnp.sum((jnp.cumsum(route_hot, axis=1) - route_hot) * route_hot, axis=2)
    hot = route_hot.reshape(packs * rows, experts).astype(F32)
    gate = jnp.sum(routing * hot, axis=1)
    target = jnp.where(slot < capacity, (route * packs + jnp.arange(packs)[:, None]) * capacity + slot, -1).reshape(-1)
    dispatch = (target[:, None] == jnp.arange(experts * packs * capacity, dtype=jnp.int32)).astype(BF)

    def swap(a):
        shape = (experts, packs * capacity, width)
        return lax.all_to_all(a.reshape(shape), "expert", split_axis=0, concat_axis=0, tiled=True).reshape(-1, width)

    received = swap(times_left(dispatch, normed3).astype(BF))
    inner = times(received, e_in)
    hidden, pull = jax.vjp(gelu_tanh, inner)
    hidden = hidden.astype(BF)
    result = times(hidden, e_out).astype(BF)
    combined = times(dispatch, swap(result))
    out_rows = (hidden2 + gate[:, None] * combined).astype(BF)
    grad_top = cotangent.reshape(packs * rows, width).astype(F32)
    grad_gate = jnp.sum(grad_top * combined, axis=1)
    grad_result = swap(times_left(dispatch, (gate[:, None] * grad_top).astype(BF)).astype(BF))
    grad_hidden = times_right(grad_result, e_out)
    grad_eout = times_left(hidden, grad_result).astype(BF)
    grad_inner = pull(grad_hidden)[0].astype(BF)
    grad_ein = times_left(received, grad_inner).astype(BF)
    grad_send = swap(times_right(grad_inner, e_in).astype(BF))
    grad_logits = grad_gate[:, None] * routing * (hot - gate[:, None])
    grad_router = jnp.einsum("td,te->de", normed3.astype(F32), grad_logits, precision=HIGHEST)
    grad_normed3 = times(dispatch, grad_send) + jnp.einsum(
        "te,de->td", grad_logits, router.astype(F32), precision=HIGHEST
    )
    back3, gain3 = norm_back(hidden2, gains[2], grad_normed3)
    grad_h2 = grad_top + back3
    grad_h2_low = grad_h2.astype(BF)
    grad_wco = times_left(cross_mixed, grad_h2_low)
    grad_cross = times_right(grad_h2_low, w_out[1]).astype(BF)
    grad_cq, grad_ck, grad_cv, _ = attend_back(cross_query, mem_keys, mem_values, chances_cross, grad_cross, packs)
    back2, gain2 = norm_back(hidden1, gains[1], times_right(grad_cq, w_in[3]))
    grad_h1 = grad_h2 + back2
    grad_h1_low = grad_h1.astype(BF)
    grad_wso = times_left(mixed, grad_h1_low)
    grad_mixed = times_right(grad_h1_low, w_out[0]).astype(BF)
    grad_q, grad_k, grad_v, grad_scores = attend_back(query, keys, values, chances_self, grad_mixed, packs)

    total = jnp.sum(grad_scores.astype(F32), axis=0)[:, ::-1]
    padded = jnp.pad(total, ((0, 0), (0, 0), (0, wide - group))).reshape(HEADS, rows * wide)
    diagonal = padded[:, : rows * (wide - 1)].reshape(HEADS, rows, wide - 1).sum(axis=1)
    at = jnp.clip(rank * rows + (rows - 1) - jnp.arange(wide - 1, dtype=jnp.int32), 0, group - 1)
    diagonal_hot = (jnp.take(rel_buckets, at)[:, None] == jnp.arange(buckets)).astype(F32)
    grad_table = jnp.einsum("jb,hj->bh", diagonal_hot, diagonal, precision=HIGHEST)

    def to_owner(a):
        return lax.psum_scatter(a.reshape(packs, group, width), "seq", scatter_dimension=1, tiled=True)

    grad_memory = to_owner((times_right(grad_ck, w_in[4]) + times_right(grad_cv, w_in[5])).astype(BF))
    part1 = to_owner((times_right(grad_k, w_in[1]) + times_right(grad_v, w_in[2])).astype(BF))
    grad_normed1 = times_right(grad_q, w_in[0]) + part1.reshape(packs * rows, width).astype(F32)
    back1, gain1 = norm_back(x_rows, gains[0], grad_normed1)
    grad_x = grad_h1 + back1
    grad_in = jnp.concatenate(
        [
            times_left(normed1, grad_q),
            times_left(normed1_all, grad_k),
            times_left(normed1_all, grad_v),
            times_left(normed2, grad_cq),
            times_left(m_all, grad_ck),
            times_left(m_all, grad_cv),
        ]
    ).astype(BF)
    grad_out = jnp.concatenate([grad_wso, grad_wco]).astype(BF)
    shards = [
        lax.psum_scatter(a, over, scatter_dimension=0, tiled=True).astype(F32)
        for a, over in ((grad_in, everywhere), (grad_out, everywhere), (grad_ein, peers), (grad_eout, peers))
    ]
    small = lax.psum((jnp.stack([gain1, gain2, gain3]), grad_table, grad_router), ("dp", "seq", "expert"))
    shape = (packs, 1, 1, rows, width)
    return (
        out_rows.reshape(shape),
        grad_x.reshape(shape),
        grad_memory.astype(F32).reshape(shape),
        *small,
        shards[0],
        shards[1],
        shards[2][None],
        shards[3][None],
    )


def solution(mesh):
    tokens = P(None, "dp", "expert", "seq", None)
    dense = P(("dp", "seq", "expert"), None)
    expert = P("expert", ("dp", "seq"), None)
    return jax.shard_map(
        per_device,
        mesh=mesh,
        in_specs=(tokens, tokens, tokens, tokens, P(None, "dp", "expert", None), P(), P(), P(), P(),
                  dense, dense, expert, expert),
        out_specs=(tokens, tokens, tokens, P(), P(), P(), dense, dense, expert, expert),
        check_vma=False,
    )
```

```python
import functools

import jax
import jax.numpy as jnp
from jax import lax
from jax.experimental import pallas as pl
from jax.experimental.pallas import tpu as pltpu
from jax.sharding import PartitionSpec as P

HEADS = 12
HEAD = 64

EPS = 1e-06
NEG = -1e30
HIGHEST = lax.Precision.HIGHEST
MESH = pl.DeviceIdType.MESH
BF = jnp.bfloat16
F32 = jnp.float32


class Place:
    def __init__(self):
        self.nz, self.ns, self.ny = (lax.axis_size(a) for a in ("dp", "seq", "expert"))
        self.nx = self.ns // 2
        self.z, self.s, self.y = (lax.axis_index(a) for a in ("dp", "seq", "expert"))
        self.x, self.c = self.s // 2, lax.rem(self.s, 2)

    def device(self, z=None, x=None, c=None, y=None):
        z = self.z if z is None else z
        x = self.x if x is None else x
        c = self.c if c is None else c
        y = self.y if y is None else y
        return (z, x * 2 + c, y)

    def other_x(self):
        return [lax.rem(self.x + k, self.nx) for k in range(1, self.nx)]

    def other_y(self):
        return [lax.rem(self.y + k, self.ny) for k in range(1, self.ny)]

    def by_distance(self, k):
        half = self.nz // 2
        order = [
            sorted(range(self.nz), key=lambda d: (abs(d - z), (d < half) != (z < half), d)) for z in range(self.nz)
        ]
        return self.pick([row[k] for row in order])

    def pick(self, values):
        out = jnp.int32(values[0])
        for z in range(1, self.nz):
            out = jnp.where(self.z == z, jnp.int32(values[z]), out)
        return out

    def greet(self):
        barrier = pltpu.get_barrier_semaphore()
        for x in self.other_x():
            pl.semaphore_signal(barrier, inc=1, device_id=self.device(x=x), device_id_type=MESH)
        for y in self.other_y():
            pl.semaphore_signal(barrier, inc=1, device_id=self.device(y=y), device_id_type=MESH)
        pl.semaphore_signal(barrier, inc=1, device_id=self.device(c=1 - self.c), device_id_type=MESH)

        for k in range(1, self.nz):
            z = lax.rem(self.z + k, self.nz)
            pl.semaphore_signal(barrier, inc=1, device_id=self.device(z=z), device_id_type=MESH)
        pl.semaphore_wait(barrier, self.nx - 1 + self.ny - 1 + 1 + self.nz - 1)


def rms_rows(src, gain, dst, rows, step=64):
    @pl.loop(0, rows // step)
    def _(i):
        at = pl.ds(pl.multiple_of(i * step, step), step)
        value = src[at, :].astype(F32)
        r = lax.rsqrt(jnp.mean(value * value, axis=-1, keepdims=True) + EPS)
        dst[at, :] = (value * r * gain).astype(BF)


def block(weight, index, lanes=slice(None), share=(0, 1)):
    unit, width = weight.shape[-2:]
    count = width // unit // share[1]
    first = pl.multiple_of(index * (width // unit) + share[0] * count, count)
    value = weight[pl.ds(first, count), :, lanes]
    return value.reshape(count * unit, value.shape[-1])


def project(left, weight, index, dst):
    width = dst.shape[-1]
    step = 256 if width % 256 == 0 else width

    @pl.loop(0, width // step)
    def _(j):
        at = pl.ds(pl.multiple_of(j * step, step), step)
        dst[:, at] = jnp.dot(left[...], block(weight, index, at), preferred_element_type=F32).astype(dst.dtype)


def prepare_bias(rel, table, bias, rank, rows, group):
    heads, buckets = table.shape
    wide = group + 128
    lane = lax.broadcasted_iota(jnp.int32, (group, wide), 1)
    shift = jnp.where(lane < group, lane, lane - wide)
    distance = jnp.clip(rank * rows - shift, 0, group - 1)
    hot = (lax.broadcasted_iota(jnp.int32, (group, wide), 0) == distance).astype(F32).astype(BF)
    which = jnp.dot(jnp.broadcast_to(rel[...].astype(F32), (8, group)).astype(BF), hot, preferred_element_type=F32)
    picks = (lax.broadcasted_iota(jnp.int32, (buckets, wide), 0) == which[0:1].astype(jnp.int32)).astype(F32)
    line = jnp.dot(table[...], picks, precision=HIGHEST, preferred_element_type=F32)
    for h in range(heads):
        band = pltpu.roll(jnp.broadcast_to(line[h : h + 1], (rows, wide)), 0, 1, stride=1, stride_axis=0)
        bias[h // 2, pl.ds((h % 2) * rows, rows), :] = band[:, :group]


def prepare_masks(lengths, same, causal, rank, rows, group):
    key = lax.broadcasted_iota(jnp.int32, (rows, group), 1)
    query = rank * rows + lax.broadcasted_iota(jnp.int32, (rows, group), 0)
    for p in range(same.shape[0]):
        end = jnp.int32(0)
        kd = jnp.zeros((rows, group), jnp.int32)
        qd = jnp.zeros((rows, group), jnp.int32)
        for n in range(lengths.shape[1]):
            end = end + lengths[p, n]
            kd = kd + jnp.where(key >= end, 1, 0)
            qd = qd + jnp.where(query >= end, 1, 0)
        same[p] = jnp.where(kd == qd, 0.0, NEG)
        causal[p] = jnp.where((kd == qd) & (key <= query), 0.0, NEG)


def two_heads(pair):
    first = lax.broadcasted_iota(jnp.int32, pair.shape, 1) < HEAD
    zero = jnp.zeros_like(pair)
    return jnp.concatenate([jnp.where(first, pair, zero), jnp.where(first, zero, pair)], axis=0)


def one_pair(stacked):
    rows = stacked.shape[0] // 2
    first = lax.broadcasted_iota(jnp.int32, (rows, stacked.shape[1]), 1) < HEAD
    return jnp.where(first, stacked[:rows], stacked[rows:])


def attend_pairs(query, keys, values, bias, mask, chances, mixed):
    packs, pairs, double, group = chances.shape
    rows = double // 2

    def body(i, carry):
        p, j = i // pairs, lax.rem(i, pairs)
        mine = pl.ds(pl.multiple_of(p * rows, rows), rows)
        theirs = pl.ds(pl.multiple_of(p * group, group), group)
        lanes = pl.ds(pl.multiple_of(j * 128, 128), 128)
        scores = lax.dot_general(
            two_heads(query[mine, lanes]), keys[theirs, lanes], (((1,), (1,)), ((), ())), preferred_element_type=F32
        )
        scores = scores * HEAD**-0.5
        if bias is not None:
            scores = scores + bias[j]
        scores = (scores.reshape(2, rows, group) + mask[p][None]).reshape(double, group)
        raised = jnp.exp(scores - jnp.max(scores, axis=1, keepdims=True))
        weights = (raised * (1.0 / jnp.sum(raised, axis=1, keepdims=True))).astype(BF)
        chances[p, j] = weights
        out = jnp.dot(weights, values[theirs, lanes], preferred_element_type=F32)
        mixed[mine, lanes] = one_pair(out).astype(BF)
        return carry

    lax.fori_loop(0, packs * pairs, body, 0, unroll=12)


def add_product(total, left, weight, index):
    width = total.shape[-1]
    step = 256 if width % 256 == 0 else width

    @pl.loop(0, width // step)
    def _(j):
        at = pl.ds(pl.multiple_of(j * step, step), step)
        total[:, at] += jnp.dot(left[...], block(weight, index, at), preferred_element_type=F32)


def product_t(left, weight, index, dst):
    halves = 2
    step = weight.shape[-1] // halves

    @pl.loop(0, halves)
    def _(j):
        rows = block(weight, index, share=(j, halves))
        out = lax.dot_general(left[...], rows, (((1,), (1,)), ((), ())), preferred_element_type=F32)
        dst[:, pl.ds(pl.multiple_of(j * step, step), step)] = out.astype(dst.dtype)


def two_products_t(left1, index1, left2, index2, weight, dst):
    halves = 2
    step = weight.shape[-1] // halves

    @pl.loop(0, halves)
    def _(j):
        out = 0.0
        for left, index in ((left1, index1), (left2, index2)):
            rows = block(weight, index, share=(j, halves))
            out = out + lax.dot_general(left[...], rows, (((1,), (1,)), ((), ())), preferred_element_type=F32)
        dst[:, pl.ds(pl.multiple_of(j * step, step), step)] = out.astype(dst.dtype)


def outer_product(left, right, dst, index):
    unit, width = dst.shape[-2:]
    halves = 2
    step, count = width // halves, width // unit // halves

    @pl.loop(0, halves)
    def _(j):
        part = left[:, pl.ds(pl.multiple_of(j * step, step), step)]
        out = lax.dot_general(part, right[...], (((0,), (0,)), ((), ())), preferred_element_type=F32)
        first = index * (width // unit) + j * count
        dst[pl.ds(first, count)] = out.astype(dst.dtype).reshape(count, unit, width)


def add_into(total, other):
    lead = total.shape[:-2]
    count = 1
    for n in lead:
        count *= n
    rows = total.shape[-2]
    step = next(n for n in ((48, 32, 16) if total.shape[-1] <= 1024 else (16,)) if rows % n == 0)

    def body(i, carry):
        index = []
        rest = i // (rows // step)
        for n in reversed(lead):
            index.insert(0, lax.rem(rest, n))
            rest = rest // n
        r = pl.ds(pl.multiple_of(lax.rem(i, rows // step) * step, 16), step)
        at = (*index, r)
        total[at] = (total[at].astype(F32) + other[at].astype(F32)).astype(total.dtype)
        return carry

    lax.fori_loop(0, count * (rows // step), body, 0)


def norm_back_rows(value, gain, grad, total, gain_grad, step=64):
    gain_grad[...] = jnp.zeros_like(gain_grad)

    @pl.loop(0, value.shape[0] // step)
    def _(i):
        at = pl.ds(pl.multiple_of(i * step, step), step)
        v, g = value[at, :].astype(F32), grad[at, :]
        r = lax.rsqrt(jnp.mean(v * v, axis=-1, keepdims=True) + EPS)
        scaled = g * gain
        total[at, :] += r * scaled - v * (r * r * r) * jnp.mean(scaled * v, axis=-1, keepdims=True)
        gain_grad[...] += jnp.sum(g * v * r, axis=0, keepdims=True)


def attend_pairs_back(query, keys, values, chances, grad, grad_q, grad_k, grad_v, diagonal):
    packs, pairs, double, group = chances.shape
    rows = double // 2
    scale = HEAD**-0.5

    def body(i, carry):
        p, j = i // pairs, lax.rem(i, pairs)
        mine = pl.ds(pl.multiple_of(p * rows, rows), rows)
        theirs = pl.ds(pl.multiple_of(p * group, group), group)
        lanes = pl.ds(pl.multiple_of(j * 128, 128), 128)
        ga = two_heads(grad[mine, lanes])
        low = chances[p, j]
        wide = low.astype(F32)
        gp = lax.dot_general(ga, values[theirs, lanes], (((1,), (1,)), ((), ())), preferred_element_type=F32)
        gs = (wide * (gp - jnp.sum(wide * gp, axis=1, keepdims=True))).astype(BF)
        gq = jnp.dot(gs, keys[theirs, lanes], preferred_element_type=F32)
        grad_q[mine, lanes] = (one_pair(gq) * scale).astype(BF)
        gk = lax.dot_general(gs, two_heads(query[mine, lanes]), (((0,), (0,)), ((), ())), preferred_element_type=F32)
        grad_k[theirs, lanes] = (gk * scale).astype(BF)
        gv = lax.dot_general(low, ga, (((0,), (0,)), ((), ())), preferred_element_type=F32)
        grad_v[theirs, lanes] = gv.astype(BF)
        if diagonal is not None:
            a = lax.broadcasted_iota(jnp.int32, (rows, rows), 0)
            b = lax.broadcasted_iota(jnp.int32, (rows, rows), 1)
            flip = (a + b == rows - 1).astype(F32).astype(BF)
            for half in range(2):
                turned = jnp.dot(flip, gs[half * rows : (half + 1) * rows], preferred_element_type=F32)
                turned = jnp.concatenate([turned, jnp.zeros((rows, 128), F32)], axis=1)
                band = pltpu.roll(turned, 0, 1, stride=1, stride_axis=0)
                diagonal[pl.ds(2 * j + half, 1), :] += jnp.sum(band, axis=0, keepdims=True)
        return carry

    lax.fori_loop(0, packs * pairs, body, 0, unroll=12)


def table_grad(rel, diagonal, rank, rows, group):
    wide = group + 128
    lane = lax.broadcasted_iota(jnp.int32, (group, wide), 1)
    distance = jnp.clip(rank * rows + rows - 1 - lane, 0, group - 1)
    hot = (lax.broadcasted_iota(jnp.int32, (group, wide), 0) == distance).astype(F32).astype(BF)
    which = jnp.dot(jnp.broadcast_to(rel[...].astype(F32), (8, group)).astype(BF), hot, preferred_element_type=F32)
    picks = (lax.broadcasted_iota(jnp.int32, (128, wide), 0) == which[0:1].astype(jnp.int32)).astype(F32)
    return lax.dot_general(diagonal[...], picks, (((1,), (1,)), ((), ())), precision=HIGHEST, preferred_element_type=F32)


def route_slots(route, experts, capacity):
    packs, _, rows = route.shape
    count = packs * rows
    same = lax.broadcasted_iota(jnp.int32, (rows, rows), 0) == lax.broadcasted_iota(jnp.int32, (rows, rows), 1)
    column = jnp.concatenate(
        [jnp.sum(jnp.where(same, route[p], 0), axis=1, keepdims=True) for p in range(packs)], axis=0
    )
    hot = (column == lax.broadcasted_iota(jnp.int32, (count, experts), 1)).astype(F32)
    a = lax.broadcasted_iota(jnp.int32, (count, count), 0)
    b = lax.broadcasted_iota(jnp.int32, (count, count), 1)
    earlier = ((b < a) & (a // rows == b // rows)).astype(F32).astype(BF)
    before = jnp.dot(earlier, hot.astype(BF), preferred_element_type=F32)
    slot = jnp.sum(before * hot, axis=1, keepdims=True).astype(jnp.int32)
    pack = lax.broadcasted_iota(jnp.int32, (count, 1), 0) // rows
    target = jnp.where(slot < capacity, (column * packs + pack) * capacity + slot, -1)
    slots = lax.broadcasted_iota(jnp.int32, (count, experts * packs * capacity), 1)
    return hot, (target == slots).astype(F32).astype(BF)


def chances_of(rows, router_t, own):
    logits = lax.dot_general(rows, router_t[...], (((1,), (1,)), ((), ())), preferred_element_type=F32)
    raised = jnp.exp(logits - jnp.max(logits, axis=1, keepdims=True))
    mine = (lax.broadcasted_iota(jnp.int32, (1, logits.shape[1]), 1) == own).astype(F32)
    return mine, raised / jnp.sum(raised, axis=1, keepdims=True)


def gelu_both(z):
    c = 0.7978845608028654
    t = jnp.tanh(c * (z + 0.044715 * (z * z * z)))
    half = 0.5 * (1.0 + t)
    slope = half + 0.5 * z * (1.0 - t * t) * (c * (1.0 + 3 * 0.044715 * (z * z)))
    return z * half, slope


def continue_waits(waits, hop, d, at):
    def wait():
        @pl.when(d < at.z)
        def _():
            hop(-1).wait_send()

        @pl.when(d > at.z)
        def _():
            hop(1).wait_send()

    waits.append(wait)


def layer_body(lengths, rel, gains, table, router_t, route, x_ref, m_ref, g_ref, ain, aout, ein, eout,
               out_rows, o0, o1, o2, o3, grad_x, grad_mem, sum_gains, sum_router, sum_table,
               w, big, ge, prep, c2, c3, y0, y1, x0, x1, ex_in, z0, z1, z2, z3,
               xo, mo, n1_all, k_, v, kc, vc, gv, n1, q, mixed, n2, qc, cross_mixed, n3, gb, ga, gq,
               pr_self, pr_cross, h1, h2, gn, bias, same, causal, diagonal, gain_row,
               act_core, act_x, wide_sum, table_sum, wide_in, table_in,
               slots_out, slots_in, slots_acc, ret_out, ret_in, back_in, grad_here, hid, gin_,
               act_send, act_recv, prep_send, prep_recv, line_send, side_send, spread_send, ici_recv, spread_recv, own_sem,
               core_send, core_recv, y_send, y_recv, x_send, x_recv, ex_send, ex_recv, z_send, z_recv, zd_send, zd_recv,
               sum_send, sum_recv, small_send, small_recv, slot_send, slot_recv, free_sem):
    at = Place()
    nz, nx, ny = at.nz, at.nx, at.ny
    packs, tok, width = x_ref.shape
    group = xo.shape[0] // packs
    experts = router_t.shape[0]
    unit = ain.shape[1]
    block_units = eout.shape[0]
    panels = block_units // nx
    columns = ein.shape[1] // (nz * nx)
    buckets = table.shape[1]
    gk = xo
    units = (ain.shape[0], aout.shape[0])
    tall = nz * nx * 2
    bases = (0, tall * ny * units[0], 0, 2 * nz * block_units)
    dense, e_in, e_out = (0, 1), 2, 3
    experts_ = (e_in, e_out)
    waits = []

    def remote(src, dst, ssem, rsem, **where):
        return pltpu.make_async_remote_copy(
            src_ref=src, dst_ref=dst, send_sem=ssem, recv_sem=rsem,
            device_id=at.device(**where), device_id_type=MESH,
        )

    def send(*args, **where):
        one = remote(*args, **where)
        if acts_now[0]:
            one.start()
        waits.append(one.wait_send)

    acts_now = [True]

    def at_planes(ends, step, last):
        between = (at.z > 0) & (at.z < nz - 1)
        mark = len(waits)

        @pl.when(jnp.logical_not(between) if ends else between)
        def _():
            step()

        del waits[mark:]
        if last:
            acts_now[0] = False
            step()
            acts_now[0] = True

    def add(total, other):
        if acts_now[0]:
            add_into(total, other)

    def start_when(pred, make):
        if acts_now[0]:

            @pl.when(pred)
            def _():
                make().start()

    def arrive(ref, sem):
        if acts_now[0]:
            pltpu.make_async_copy(ref, ref, sem).wait()

    def spot(a, z, x, c, y):
        index = ((z * nx + x) * 2 + c) * ny + y
        return w.at[pl.ds(bases[a] + index * units[a], units[a])]

    def pack_of(a, z, c):
        return big.at[pl.ds(bases[a] + (z * 2 + c) * block_units, block_units)]

    shards = (ain, aout)
    acts = ((x_ref, xo), (m_ref, mo))

    at.greet()

    def act_rows(full, p, x, c):
        return full.at[pl.ds(pl.multiple_of(p * group + (x * 2 + c) * tok, 16), tok)]

    own_waits = []

    def send_acts():
        for i, (src, full) in enumerate(acts):
            for p in range(packs):
                dst = act_rows(full, p, at.x, at.c)
                for k, x in enumerate(at.other_x()):
                    send(src.at[p], dst, act_send.at[i, p, k], act_recv.at[i, p, at.x, at.c], x=x)
                send(src.at[p], dst, act_send.at[i, p, nx - 1 + at.x], act_recv.at[i, p, at.x, at.c], c=1 - at.c)
                own = pltpu.make_async_copy(src.at[p], dst, own_sem.at[4 + i, p])
                own.start()
                own_waits.append(own.wait)

    def along_line(a, z, src):
        dst = spot(a, z, at.x, at.c, at.y) if a in dense else pack_of(a, z, at.c)
        sem = ici_recv.at[a, z, at.x, at.y]
        left = (z >= at.z) & (at.z > 0)
        right = (z <= at.z) & (at.z < nz - 1)

        def one(side):
            return remote(src, dst, line_send.at[a, z, side], sem, z=at.z + 2 * side - 1)

        start_when(left, lambda: one(0))
        start_when(right, lambda: one(1))

        def wait():
            @pl.when(left)
            def _():
                one(0).wait_send()

            @pl.when(right)
            def _():
                one(1).wait_send()

        waits.append(wait)

    def to_core(a, z, x, y, src):
        dst = spot(a, z, x, at.c, y) if a in dense else pack_of(a, z, at.c)
        send(src, dst, spread_send.at[a, z, x, y], spread_recv.at[a, z, x, y], c=1 - at.c)

    zs = [at.by_distance(k) for k in range(nz)]

    def dense_events(k):
        z = zs[k]
        for a in dense:
            here = spot(a, z, at.x, at.c, at.y)
            src = here if k else shards[a]
            if k:
                arrive(here, ici_recv.at[a, z, at.x, at.y])
            else:
                own = pltpu.make_async_copy(shards[a], here, own_sem.at[a, 0])
                own.start()
                own_waits.append(own.wait)
            along_line(a, z, src)
            for j, x in enumerate(at.other_x()):
                send(src, here, side_send.at[a, z, j], ici_recv.at[a, z, at.x, at.y], x=x)
            for j, y in enumerate(at.other_y()):
                send(src, here, side_send.at[a, z, nx - 1 + j], ici_recv.at[a, z, at.x, at.y], y=y)
            to_core(a, z, at.x, at.y, src)

    def side_y(k):
        z = zs[k]
        for y in at.other_y():
            for a in dense:
                here = spot(a, z, at.x, at.c, y)
                arrive(here, ici_recv.at[a, z, at.x, y])
                if a == 1:
                    for j, x in enumerate(at.other_x()):
                        send(here, here, side_send.at[a, z, nx - 1 + ny - 1 + j + (nx - 1) * y],
                             ici_recv.at[a, z, at.x, y], x=x)
                to_core(a, z, at.x, y, here)

    def side_x(k):
        z = zs[k]
        for x in at.other_x():
            for a in dense:
                here = spot(a, z, x, at.c, at.y)
                arrive(here, ici_recv.at[a, z, x, at.y])
                if a == 0:
                    for j, y in enumerate(at.other_y()):
                        send(here, here, side_send.at[a, z, nx - 1 + ny - 1 + j + (ny - 1) * x],
                             ici_recv.at[a, z, x, at.y], y=y)
                to_core(a, z, x, at.y, here)

    def corner_events(k):
        z = zs[k]
        for a in dense:
            for y in at.other_y():
                for x in at.other_x():
                    here = spot(a, z, x, at.c, y)
                    arrive(here, ici_recv.at[a, z, x, y])
                    to_core(a, z, x, y, here)

    def act_events():
        for i, (src, full) in enumerate(acts):
            for p in range(packs):
                for x in at.other_x():
                    dst = act_rows(full, p, x, at.c)
                    arrive(dst, act_recv.at[i, p, x, at.c])
                    send(dst, dst, act_send.at[i, p, nx - 1 + x], act_recv.at[i, p, x, at.c], c=1 - at.c)

    def in_unit(z, c, x, n=1):
        return pl.ds(bases[e_in] + ((z * 2 + c) * nx + x) * panels, n * panels)

    def start_prep():
        for x in range(nx):
            for u in range(panels):
                each_z = width // columns
                prep[x, u] = jnp.concatenate(
                    [ein[:, (z * nx + x) * columns : (z * nx + x + 1) * columns] for z in range(u * each_z, (u + 1) * each_z)],
                    axis=1,
                )
        big[in_unit(at.z, at.c, at.x)] = prep[at.x]
        for j, x in enumerate(at.other_x()):
            send(prep.at[x], big.at[in_unit(at.z, at.c, at.x)], prep_send.at[j], prep_recv.at[at.x], x=x)

    def expert_events(k, kinds=experts_):
        z = zs[k]
        for a in kinds:
            here = pack_of(a, z, at.c)
            src = here
            if k:
                arrive(here, ici_recv.at[a, z, at.x, at.y])
            elif a == e_in:
                for x in at.other_x():
                    arrive(big.at[in_unit(at.z, at.c, x)], prep_recv.at[x])
            else:
                src = eout
                own = pltpu.make_async_copy(eout, here, own_sem.at[a, 0])
                own.start()
                own_waits.append(own.wait)
            along_line(a, z, src)
            to_core(a, z, 0, 0, src)

    def first_norm():
        for i, (src, full) in enumerate(acts):
            for p in range(packs):
                for x in range(nx):
                    arrive(act_rows(full, p, x, 1 - at.c), act_recv.at[i, p, x, 1 - at.c])
        for wait in own_waits:
            wait()
        rms_rows(xo, gains[0:1], n1_all, packs * group)
        for p in range(packs):
            h1[pl.ds(p * tok, tok), :] = x_ref[p].astype(F32)
            n1[pl.ds(p * tok, tok), :] = n1_all[pl.ds(pl.multiple_of(p * group + at.s * tok, tok), tok), :]

    places = [((z * 2 + c) * nx + x) * panels for z in range(nz) for x in range(nx) for c in range(2)]
    each = slots_out.shape[2]
    count = ny * each
    row_units = width // unit

    def keys_and_values(for_self):
        @pl.when(for_self)
        def _():
            project(n1_all, w, 1, k_)
            project(n1_all, w, 2, v)

        @pl.when(jnp.logical_not(for_self))
        def _():
            project(mo, w, 4, kc)
            project(mo, w, 5, vc)

    def by_slot(dispatch, rows):
        out = lax.dot_general(dispatch, rows, (((0,), (0,)), ((), ())), preferred_element_type=F32)
        return out.astype(BF).reshape(ny, each, width)

    slot_waits = []

    def slot_copy(late, src, dst, sem_from, sem_to, **where):
        one = remote(src, dst, slot_send.at[sem_from], slot_recv.at[sem_to], **where)
        one.start()
        (waits if late else slot_waits).append(one.wait_send)

    def y_sem(t, j):
        return t * (ny - 1) + j

    def x_sem(t, j, y):
        return 4 * (ny - 1) + (t * (nx - 1) + j) * ny + y

    def ret_sem(t, j, y):
        return 4 * (ny - 1) + 2 * (nx - 1) * ny + (t * (nx - 1) + j) * ny + y

    def send_slots(t):
        for j, y in enumerate(at.other_y()):
            slot_copy(False, slots_out.at[t, y], slots_in.at[t, at.x, at.y], y_sem(t, j), y_sem(t, ny - 2 - j), y=y)
        for j, x in enumerate(at.other_x()):
            slot_copy(False, slots_out.at[t, at.y], slots_in.at[t, at.x, at.y], x_sem(t, j, at.y),
                      x_sem(t, nx - 2 - j, at.y), x=x)
        slots_in[t, at.x, at.y] = slots_out[t, at.y]

    def summed(t, y):
        total = slots_acc[t, at.x, y]
        for j in range(nx - 1):
            arrive(ret_in.at[t, j, y], slot_recv.at[ret_sem(t, j, y)])
            total = total + ret_in[t, j, y].astype(F32)
        return total.astype(BF)

    cores, ys, xs, zs_ = {2: c2, 3: c3}, (y0, y1), (x0, x1), (z0, z1, z2, z3)
    outs = (o0, o1, o2, o3)
    far = [sorted(range(nz), key=lambda d: (-abs(d - z), d)) for z in range(nz)]
    order_e = [at.pick([far[z][k] for z in range(nz)]) for k in range(nz)]
    halves = [[d for d in row if d >= nz // 2] + [d for d in row if d < nz // 2] for row in far]
    order_d = [at.pick([halves[z][k] for z in range(nz)]) for k in range(nz)]
    e_waits = []

    def expert_part(a, d, c):
        return ge.at[pl.ds(bases[a] + (d * 2 + c) * block_units, block_units)]

    def start_expert(a, k):
        one = remote(expert_part(a, order_e[k], 1 - at.c), cores[a].at[k], core_send.at[a, k, 0],
                     core_recv.at[a, k, 0], c=1 - at.c)
        one.start()
        e_waits.append(one.wait_send)

    def core_expert(a, k):
        arrive(cores[a].at[k], core_recv.at[a, k, 0])
        add_into(cores[a].at[k], expert_part(a, order_e[k], at.c))

    def free_experts():
        for wait in e_waits:
            wait()
        pl.semaphore_signal(free_sem, inc=1, device_id=at.device(c=1 - at.c), device_id_type=MESH)

    def dense_part(a, d, x, c):
        return big.at[pl.ds(bases[a] + ((d * nx + x) * 2 + c) * ny * units[a], ny * units[a])]

    def dense_core(a, k, x, y=None, u=None):
        first = bases[a] // 2 + (k * nx + x) * ny * units[a]
        if y is None:
            return ge.at[pl.ds(first, ny * units[a])]
        if u is None:
            return ge.at[pl.ds(first + y * units[a], units[a])]
        return ge.at[pl.ds(first + y * units[a] + u, 1)]

    def xs_in_order():
        return [(x, True) for x in at.other_x()] + [(at.x, False)]

    def start_dense(k, a):
        for x in range(nx):
            send(dense_part(a, order_d[k], x, 1 - at.c), dense_core(a, k, x), core_send.at[a, k, x],
                     core_recv.at[a, k, x], c=1 - at.c)

    def first_dense(k, a):
        if a == 0:
            for x, _ in xs_in_order():
                arrive(dense_core(0, k, x), core_recv.at[0, k, x])
                add_into(dense_core(0, k, x), dense_part(0, order_d[k], x, at.c))
                for u in range(units[0]):
                    for j, y in enumerate(at.other_y()):
                        send(dense_core(0, k, x, y, u), ys[0].at[k, ny - 2 - j, x, pl.ds(u, 1)],
                             y_send.at[k, j, x, u], y_recv.at[k, ny - 2 - j, x, u], y=y)
            return
        for x, _ in xs_in_order():
            arrive(dense_core(1, k, x), core_recv.at[1, k, x])
            add_into(dense_core(1, k, x), dense_part(1, order_d[k], x, at.c))
        for j, x in enumerate(at.other_x()):
            send(dense_core(1, k, x), xs[1].at[k, nx - 2 - j], x_send.at[k, j, units[0]],
                 x_recv.at[k, nx - 2 - j, units[0]], x=x)

    def second_dense(k, a):
        if a == 0:
            for x, away in xs_in_order():
                for u in range(units[0]):
                    total = ys[0].at[k, 0, x, pl.ds(u, 1)]
                    for j in range(ny - 1):
                        piece = ys[0].at[k, j, x, pl.ds(u, 1)]
                        arrive(piece, y_recv.at[k, j, x, u])
                        add_into(total, piece if j else dense_core(0, k, x, at.y, u))
                    if away:
                        j = lax.rem(x - at.x + nx, nx) - 1
                        send(total, xs[0].at[k, nx - 2 - j, pl.ds(u, 1)], x_send.at[k, j, u], x_recv.at[k, nx - 2 - j, u], x=x)
            return
        for j in range(nx - 1):
            arrive(xs[1].at[k, j], x_recv.at[k, j, units[0]])
            add_into(xs[1].at[k, 0], xs[1].at[k, j] if j else dense_core(1, k, at.x))
        for j, y in enumerate(at.other_y()):
            send(xs[1].at[k, 0, pl.ds(y * units[1], units[1])], ys[1].at[k, ny - 2 - j],
                 y_send.at[k, j, nx, 0], y_recv.at[k, ny - 2 - j, nx, 0], y=y)

    def piece_of(k, p):
        return xs[0].at[k, 0, pl.ds(p, 1)] if p < units[0] else ys[1].at[k, 0]

    def inbox_of(slot, p):
        return zs_[0].at[slot, pl.ds(p, 1)] if p < units[0] else zs_[1].at[slot]

    def line_dense(k, a):
        d = order_d[k]
        for p in range(units[0]) if a == 0 else [units[0]]:
            total = piece_of(k, p)
            if p < units[0]:
                for j in range(nx - 1):
                    piece = xs[0].at[k, j, pl.ds(p, 1)]
                    arrive(piece, x_recv.at[k, j, p])
                    add(total, piece if j else ys[0].at[k, 0, at.x, pl.ds(p, 1)])
            else:
                for j in range(ny - 1):
                    arrive(ys[1].at[k, j], y_recv.at[k, j, nx, 0])
                    add(total, ys[1].at[k, j] if j else xs[1].at[k, 0, pl.ds(at.y * units[1], units[1])])
            for side in range(2):

                @pl.when((at.z > 0) & (d > at.z) if side == 0 else (at.z < nz - 1) & (d < at.z))
                def _(total=total, p=p):
                    arrive(inbox_of(d, p), zd_recv.at[d, p])
                    add(total, inbox_of(d, p))

            def hop(to, total=total, p=p):
                slot = d if to > 0 else jnp.where(d == at.z - 1, nz, d)
                return remote(total, inbox_of(slot, p), zd_send.at[k, p], zd_recv.at[slot, p], z=at.z + to)

            start_when(d < at.z, functools.partial(hop, -1))
            start_when(d > at.z, functools.partial(hop, 1))

            continue_waits(waits, hop, d, at)

    def finish_dense():
        for k in (nz // 2 - 1, nz - 1):

            @pl.when(order_d[k] == at.z)
            def _(k=k):
                for p in range(units[0] + 1):
                    total = piece_of(k, p)
                    for side, here in enumerate((at.z > 0, at.z < nz - 1)):
                        slot = at.z if side == 0 else nz

                        @pl.when(here)
                        def _(total=total, slot=slot, p=p):
                            arrive(inbox_of(slot, p), zd_recv.at[slot, p])
                            add_into(total, inbox_of(slot, p))

                write_out(0, xs[0].at[k, 0])
                write_out(1, ys[1].at[k, 0])

    def write_out(a, total):
        if a != e_in:
            if acts_now[0]:
                outs[a][...] = total[...].astype(F32).reshape(outs[a].shape)
            return
        for j, x in enumerate(at.other_x()):
            send(total.at[pl.ds(x * panels, panels)], ex_in.at[nx - 2 - j], ex_send.at[j], ex_recv.at[nx - 2 - j], x=x)

    def finish_expert_in():
        for j in range(nx - 1):
            arrive(ex_in.at[j], ex_recv.at[j])
        total = cores[e_in].at[nz - 1]
        for x in range(nx):
            for u in range(panels):
                value = None
                for j, other in enumerate(at.other_x()):
                    value = ex_in[j, u] if value is None else jnp.where(other == x, ex_in[j, u], value)
                mine = total[pl.ds(at.x * panels + u, 1)][0]
                value = jnp.where(at.x == x, mine.astype(F32), value.astype(F32))
                for i in range(width // columns):
                    z = u * (width // columns) + i
                    outs[e_in][:, (z * nx + x) * columns : (z * nx + x + 1) * columns] = value[:, i * columns : (i + 1) * columns]

    def line(kind, k):
        for a in kind:
            d = order_e[k]
            total = cores[a].at[k]
            for side in range(2):
                feeds = (at.z > 0) & (d >= at.z) if side == 0 else (at.z < nz - 1) & (d <= at.z)
                slot = d if side == 0 else jnp.where(d == at.z, nz, d)

                @pl.when(feeds)
                def _(a=a, slot=slot, total=total):
                    arrive(zs_[a].at[slot], z_recv.at[a, slot])
                    add(total, zs_[a].at[slot])

            def hop(to, a=a, total=total, d=d):
                slot = d if to > 0 else jnp.where(d == at.z - 1, nz, d)
                return remote(total, zs_[a].at[slot], z_send.at[a, k], z_recv.at[a, slot], z=at.z + to)

            start_when(d < at.z, functools.partial(hop, -1))
            start_when(d > at.z, functools.partial(hop, 1))

            if k == nz - 1:
                write_out(a, total)
            continue_waits(waits, hop, d, at)

    def start_act(i):
        for p in range(packs):
            for x in range(nx):
                send(act_rows((kc, k_)[i], p, x, 1 - at.c), act_core.at[i, p, x], sum_send.at[i, p, x],
                     sum_recv.at[i, p, x], c=1 - at.c)

    def core_act(i):
        for p in range(packs):
            for x in range(nx):
                arrive(act_core.at[i, p, x], sum_recv.at[i, p, x])
                add_into(act_core.at[i, p, x], act_rows((kc, k_)[i], p, x, at.c))
        for j, x in enumerate(at.other_x()):
            send(act_core.at[i, :, x], act_x.at[i, nx - 2 - j], sum_send.at[i, packs, j], sum_recv.at[i, packs, nx - 2 - j], x=x)

    def x_act(i):
        for j in range(nx - 1):
            arrive(act_x.at[i, j], sum_recv.at[i, packs, j])
        for p in range(packs):
            out = act_core[i, p, at.x].astype(F32)
            for j in range(nx - 1):
                out = out + act_x[i, j, p].astype(F32)
            if i == 0:
                grad_mem[pl.ds(p * tok, tok), :] = out
            else:
                gn[pl.ds(p * tok, tok), :] += out

    pair_sums = ((wide_sum, wide_in), (table_sum, table_in))
    stages = [("c", [1 - at.c]), ("y", at.other_y()), ("x", at.other_x())]

    def start_small(t):
        axis, peers = stages[t]
        base = [0, 1, ny][t]
        for i, (total, inbox) in enumerate(pair_sums):
            for j, peer in enumerate(peers):
                back = base + len(peers) - 1 - j
                send(total.at[t], inbox.at[back], small_send.at[i, base + j], small_recv.at[i, back], **{axis: peer})

    def end_small(t):
        axis, peers = stages[t]
        base = [0, 1, ny][t]
        for i, (total, inbox) in enumerate(pair_sums):
            out = total[t]
            for j in range(len(peers)):
                arrive(inbox.at[base + j], small_recv.at[i, base + j])
                out = out + inbox[base + j]
            total[t + 1] = out

    tail = ny + nx - 1

    def start_line():
        for i, (total, inbox) in enumerate(pair_sums):
            for j in range(1, nz):
                z = lax.rem(at.z + j, nz)
                send(total.at[3], inbox.at[tail + at.z], small_send.at[i, tail + j], small_recv.at[i, tail + at.z], z=z)

    def end_line():
        for i, (total, inbox) in enumerate(pair_sums):
            for j in range(1, nz):
                z = lax.rem(at.z + j, nz)
                arrive(inbox.at[tail + z], small_recv.at[i, tail + z])
            out = None
            for z in range(nz):
                term = jnp.where(at.z == z, total[3], inbox[tail + z])
                out = term if out is None else out + term
            if i == 0:
                sum_gains[...] = out[: sum_gains.shape[0]]
                sum_router[...] = out[sum_gains.shape[0] : sum_gains.shape[0] + experts]
            else:
                sum_table[...] = out[: sum_table.shape[0], : sum_table.shape[1]]

    dense_events(0)
    start_prep()
    at_planes(False, lambda: dense_events(1), False)
    at_planes(False, lambda: dense_events(2), False)
    at_planes(False, lambda: dense_events(3), False)
    side_x(0)
    at_planes(True, lambda: dense_events(1), True)
    expert_events(0, (e_out,))
    side_y(0)
    side_x(1)
    at_planes(True, lambda: dense_events(2), True)
    at_planes(True, lambda: dense_events(3), True)
    expert_events(0, (e_in,))
    send_acts()
    at_planes(False, lambda: expert_events(1, (e_out,)), False)
    side_y(1)
    prepare_bias(rel, table, bias, at.s, tok, group)
    prepare_masks(lengths, same, causal, at.s, tok, group)
    hot, dispatch = route_slots(route, experts, each // packs)
    top = g_ref[...].astype(F32).reshape(packs * tok, width)
    side_x(2)
    side_x(3)
    at_planes(True, lambda: expert_events(1, (e_out,)), True)
    side_y(2)
    at_planes(False, lambda: expert_events(1, (e_in,)), False)
    side_y(3)
    slots_out[1] = by_slot(dispatch, g_ref[...].reshape(packs * tok, width))
    send_slots(1)
    at_planes(True, lambda: expert_events(1, (e_in,)), True)
    at_planes(False, lambda: expert_events(2, (e_out,)), False)
    at_planes(False, lambda: expert_events(3, (e_out,)), False)
    act_events()
    corner_events(0)
    at_planes(True, lambda: expert_events(2, (e_out,)), True)
    corner_events(1)
    first_norm()
    at_planes(False, lambda: expert_events(2, (e_in,)), False)
    corner_events(2)
    at_planes(False, lambda: expert_events(3, (e_in,)), False)
    for a in dense:
        for z in zs[: nz // 2]:
            for x in range(nx):
                for y in range(ny):
                    arrive(spot(a, z, x, 1 - at.c, y), spread_recv.at[a, z, x, y])
    corner_events(3)
    keys_and_values(at.z < nz // 2)
    for a in dense:
        for z in zs[nz // 2 :]:
            for x in range(nx):
                for y in range(ny):
                    arrive(spot(a, z, x, 1 - at.c, y), spread_recv.at[a, z, x, y])
    keys_and_values(at.z >= nz // 2)
    for j, y in enumerate(at.other_y()):
        here = slots_in.at[1, at.x, y]
        arrive(here, slot_recv.at[y_sem(1, j)])
        for i, x in enumerate(at.other_x()):
            slot_copy(False, here, here, x_sem(1, i, y), x_sem(1, nx - 2 - i, y), x=x)
    project(n1, w, 0, q)
    attend_pairs(q, k_, v, bias, causal, pr_self, mixed)
    add_product(h1, mixed, w, 6)
    rms_rows(h1, gains[1:2], n2, packs * tok)
    project(n2, w, 3, qc)
    attend_pairs(qc, kc, vc, None, same, pr_cross, cross_mixed)
    h2[...] = h1[...]
    add_product(h2, cross_mixed, w, 7)
    rms_rows(h2, gains[2:3], n3, packs * tok)
    slots_out[0] = by_slot(dispatch, n3[...])
    send_slots(0)
    at_planes(True, lambda: expert_events(3, (e_out,)), True)
    for j, y in enumerate(at.other_y()):
        here = slots_in.at[0, at.x, y]
        arrive(here, slot_recv.at[y_sem(0, j)])
        for i, x in enumerate(at.other_x()):
            slot_copy(False, here, here, x_sem(0, i, y), x_sem(0, nx - 2 - i, y), x=x)
    at_planes(True, lambda: expert_events(2, (e_in,)), True)
    at_planes(True, lambda: expert_events(3, (e_in,)), True)
    for a in experts_:
        for z in range(nz):
            arrive(pack_of(a, z, 1 - at.c), spread_recv.at[a, z, 0, 0])
    for t in range(2):
        for i, x in enumerate(at.other_x()):
            for y in range(ny):
                arrive(slots_in.at[t, x, y], slot_recv.at[x_sem(t, i, y)])
    here = slots_in[0].reshape(nx * count, width)
    g_here = slots_in[1].reshape(nx * count, width).astype(F32)
    mine, chances = chances_of(here, router_t, at.y)
    gate_here = jnp.sum(chances * mine, axis=1, keepdims=True)
    grad_here[...] = (gate_here * g_here).astype(BF)
    for u in range(panels):
        in_panel = jnp.concatenate([big[place + u] for place in places], axis=0)
        out_panel = big[pl.ds(bases[e_out] + u * row_units, row_units)].reshape(width, width)
        inner = jnp.dot(here, in_panel, preferred_element_type=F32)
        hidden, slope = gelu_both(inner)
        hid[u] = hidden.astype(BF)
        grad_hidden = lax.dot_general(grad_here[...], out_panel, (((1,), (1,)), ((), ())), preferred_element_type=F32)
        gin_[u] = (grad_hidden * slope).astype(BF)
        result = jnp.dot(hid[u], out_panel, preferred_element_type=F32).reshape(nx, ny, each, width)
        grad_slots = lax.dot_general(gin_[u], in_panel, (((1,), (1,)), ((), ())), preferred_element_type=F32)
        grad_slots = grad_slots.reshape(nx, ny, each, width)
        if u:
            slots_acc[0] += result
            slots_acc[1] += grad_slots
        else:
            slots_acc[0] = result
            slots_acc[1] = grad_slots
    grad_gate = jnp.sum(g_here * slots_acc[0].reshape(nx * count, width), axis=1, keepdims=True)
    grad_logits = grad_gate * chances * (mine - gate_here)
    extra_grad = 0.0
    for e in range(experts):
        extra_grad = extra_grad + grad_logits[:, e : e + 1] * router_t[e : e + 1, :].astype(F32)
    slots_acc[1] += extra_grad.reshape(nx, ny, each, width)
    for wait in waits:
        wait()
    waits.clear()
    for y in [*at.other_y(), at.y]:
        for j, x in enumerate(at.other_x()):
            ret_out[1, j, y] = slots_acc[1, x, y].astype(BF)
            slot_copy(True, ret_out.at[1, j, y], ret_in.at[1, nx - 2 - j, y], ret_sem(1, j, y), ret_sem(1, nx - 2 - j, y), x=x)
    for u in range(panels):
        grad = lax.dot_general(here, gin_[u], (((0,), (0,)), ((), ())), preferred_element_type=F32).astype(BF)
        for i, place in enumerate(places):
            ge[place + u] = grad[i * unit : (i + 1) * unit]
    for k in range(nz):
        start_expert(e_in, k)
    router_grad = lax.dot_general(
        grad_logits, here.astype(F32), (((0,), (0,)), ((), ())), precision=HIGHEST, preferred_element_type=F32
    )
    for u in range(panels):
        grad = lax.dot_general(hid[u], grad_here[...], (((0,), (0,)), ((), ())), preferred_element_type=F32).astype(BF)
        ge[pl.ds(bases[e_out] + u * row_units, row_units)] = grad.reshape(row_units, unit, width)
    for k in range(nz):
        start_expert(e_out, k)
    for y in [*at.other_y(), at.y]:
        for j, x in enumerate(at.other_x()):
            ret_out[0, j, y] = slots_acc[0, x, y].astype(BF)
            slot_copy(True, ret_out.at[0, j, y], ret_in.at[0, nx - 2 - j, y], ret_sem(0, j, y), ret_sem(0, nx - 2 - j, y), x=x)
    core_expert(e_in, 0)
    at_planes(True, lambda: line((e_in,), 0), False)
    for wait in slot_waits:
        wait()
    for j, y in enumerate(at.other_y()):
        slots_out[1, y] = summed(1, y)
        slot_copy(True, slots_out.at[1, y], back_in.at[1, at.y], y_sem(3, j), y_sem(3, ny - 2 - j), y=y)
    core_expert(e_out, 0)
    core_expert(e_in, 1)
    core_expert(e_out, 1)
    back_in[1, at.y] = summed(1, at.y)
    core_expert(e_in, 3)
    core_expert(e_out, 2)
    core_expert(e_out, 3)
    at_planes(True, lambda: line((e_out,), 0), False)
    core_expert(e_in, 2)
    free_experts()
    for j, y in enumerate(at.other_y()):
        arrive(back_in.at[1, y], slot_recv.at[y_sem(3, j)])
    diagonal[...] = jnp.zeros_like(diagonal)
    for i, (_, inbox) in enumerate(pair_sums):
        inbox[pl.ds(tail + at.z, 1)] = jnp.zeros_like(inbox[pl.ds(0, 1)])
    wide_sum[0] = jnp.zeros_like(wide_sum[0])
    wide_sum[0, pl.ds(3, experts), :] = router_grad
    gn[...] = jnp.dot(dispatch, back_in[1].reshape(count, width), preferred_element_type=F32)
    grad_x[...] = top
    norm_back_rows(h2, gains[2:3], gn, grad_x, gain_row)
    wide_sum[0, 2:3, :] = gain_row[...]
    gb[...] = grad_x[...].astype(BF)
    product_t(gb, w, 7, ga)
    attend_pairs_back(qc, kc, vc, pr_cross, ga, gq, gk, gv, None)
    outer_product(n2, gq, big, 3)
    outer_product(mo, gk, big, 4)
    outer_product(mo, gv, big, 5)
    pl.semaphore_wait(free_sem, 1)
    start_dense(1, 0)
    for j, y in enumerate(at.other_y()):
        slots_out[0, y] = summed(0, y)
        slot_copy(True, slots_out.at[0, y], back_in.at[0, at.y], y_sem(2, j), y_sem(2, ny - 2 - j), y=y)
    at_planes(True, lambda: line((e_in,), 1), False)
    product_t(gq, w, 3, gn)
    norm_back_rows(h1, gains[1:2], gn, grad_x, gain_row)
    wide_sum[0, 1:2, :] = gain_row[...]
    back_in[0, at.y] = summed(0, at.y)
    outer_product(cross_mixed, gb, big, 7)
    start_dense(0, 1)
    first_dense(1, 0)
    start_dense(1, 1)
    gb[...] = grad_x[...].astype(BF)
    product_t(gb, w, 6, ga)
    outer_product(mixed, gb, big, 6)
    at_planes(True, lambda: line((e_out,), 1), False)
    first_dense(0, 1)
    start_dense(3, 1)
    at_planes(False, lambda: line((e_in,), 0), True)
    start_dense(0, 0)
    at_planes(False, lambda: line((e_out,), 0), True)
    start_dense(2, 1)
    two_products_t(gk, 4, gv, 5, w, kc)
    first_dense(1, 1)
    at_planes(True, lambda: line((e_out,), 2), False)
    first_dense(3, 1)
    attend_pairs_back(q, k_, v, pr_self, ga, gq, gk, gv, diagonal)
    second_dense(0, 1)
    first_dense(2, 1)
    first_dense(0, 0)
    start_act(0)
    at_planes(False, lambda: line((e_in,), 1), True)
    two_products_t(gk, 1, gv, 2, w, k_)
    at_planes(True, lambda: line((e_in,), 2), False)
    start_act(1)
    outer_product(n1, gq, big, 0)
    outer_product(n1_all, gk, big, 1)
    outer_product(n1_all, gv, big, 2)
    start_dense(2, 0)
    core_act(1)
    table_sum[0] = table_grad(rel, diagonal, at.s, tok, group)
    start_dense(3, 0)
    product_t(gq, w, 0, gn)
    for j, y in enumerate(at.other_y()):
        arrive(back_in.at[0, y], slot_recv.at[y_sem(2, j)])
    _, routing = chances_of(n3[...], router_t, at.y)
    gate = jnp.sum(routing * hot, axis=1, keepdims=True)
    combined = jnp.dot(dispatch, back_in[0].reshape(count, width), preferred_element_type=F32)
    rows_out = (h2[...] + gate * combined).astype(BF)
    for p in range(packs):
        out_rows[p] = rows_out[p * tok : (p + 1) * tok]
    at_planes(False, lambda: line((e_out,), 1), True)
    second_dense(3, 1)
    first_dense(2, 0)
    second_dense(2, 1)
    second_dense(0, 0)
    at_planes(False, lambda: line((e_in,), 2), True)
    x_act(1)
    for p in range(packs):
        h1[pl.ds(p * tok, tok), :] = x_ref[p].astype(F32)
    norm_back_rows(h1, gains[0:1], gn, grad_x, gain_row)
    wide_sum[0, 0:1, :] = gain_row[...]
    at_planes(True, lambda: line_dense(0, 1), False)
    core_act(0)
    second_dense(1, 0)
    at_planes(True, lambda: line_dense(0, 0), False)
    start_small(0)
    end_small(0)
    start_small(1)
    first_dense(3, 0)
    at_planes(False, lambda: line_dense(3, 1), False)
    at_planes(True, lambda: line_dense(3, 1), True)
    at_planes(False, lambda: line_dense(0, 0), True)
    second_dense(2, 0)
    at_planes(False, lambda: line_dense(0, 1), True)
    at_planes(True, lambda: line_dense(1, 0), False)
    at_planes(True, lambda: line((e_in,), 3), False)
    x_act(0)
    end_small(1)
    start_small(2)
    second_dense(1, 1)
    at_planes(False, lambda: line((e_in,), 3), True)
    at_planes(True, lambda: line_dense(2, 0), False)
    at_planes(False, lambda: line((e_out,), 2), True)
    at_planes(False, lambda: line_dense(1, 0), True)
    at_planes(True, lambda: line_dense(2, 1), False)
    at_planes(False, lambda: line_dense(2, 0), True)
    second_dense(3, 0)
    at_planes(False, lambda: line_dense(2, 1), True)
    at_planes(True, lambda: line_dense(3, 0), False)
    at_planes(True, lambda: line_dense(1, 1), False)
    end_small(2)
    start_line()
    at_planes(False, lambda: line_dense(1, 1), True)
    at_planes(False, lambda: line((e_out,), 3), False)
    at_planes(False, lambda: line_dense(3, 0), True)
    finish_expert_in()
    end_line()
    finish_dense()
    at_planes(True, lambda: line((e_out,), 3), True)
    for wait in waits:
        wait()


def shapes_of(layer_input, routes, attn_in, attn_out, expert_in, expert_out):
    nz, ns, ny = (lax.axis_size(a) for a in ("dp", "seq", "expert"))
    packs, tok, width = layer_input.shape[0], layer_input.shape[3], layer_input.shape[4]
    return nz, ns, ny, packs, tok, width


def fits_kernel(layer_input, routes, attn_in, attn_out, expert_in, expert_out):
    nz, ns, ny, packs, tok, width = shapes_of(layer_input, routes, attn_in, attn_out, expert_in, expert_out)
    unit, hidden = expert_in.shape[1:]
    capacity = (5 * tok + 4 * ny - 1) // (4 * ny)
    nx = ns // 2
    return (
        unit % 16 == 0
        and tok % 16 == 0
        and packs * capacity % 16 == 0
        and attn_in.shape[0] % unit == 0
        and attn_out.shape[0] % unit == 0
        and expert_out.shape[1] % (unit * nx) == 0
        and width % (2 * unit) == 0
        and hidden % (nx * width) == 0
        and width % (hidden // (nz * nx)) == 0
        and hidden // (nz * nx) % 128 == 0
        and expert_out.shape[1] * nz * ns == hidden
        and expert_out.shape[1] * width == hidden * unit
        and expert_in.shape[0] == 1
    )


def deliver_body(*refs):
    count = (len(refs) - 2) // 3
    came, gone = refs[-2:]
    copies = []
    for i in range(count):
        place = refs[2 * count + i]
        copies.append((
            pltpu.make_async_copy(refs[i], place, came.at[i]),
            pltpu.make_async_copy(place, refs[count + i], gone.at[i]),
        ))
    for first, _ in copies:
        first.start()
    for first, second in copies:
        first.wait()
        second.start()
    for _, second in copies:
        second.wait()


def deliver(arrays):
    any_ = pl.BlockSpec(memory_space=pl.ANY)
    count = len(arrays)
    return pl.pallas_call(
        deliver_body,
        out_shape=[jax.ShapeDtypeStruct(a.shape, a.dtype) for a in arrays],
        in_specs=[any_] * count,
        out_specs=[any_] * count,
        scratch_shapes=[
            *[pltpu.VMEM(a.shape, a.dtype) for a in arrays],
            pltpu.SemaphoreType.DMA((count,)),
            pltpu.SemaphoreType.DMA((count,)),
        ],
        name="deliver",
    )(*arrays)


def layer_kernel(layer_input, memory, cotangent, routes, doc_lengths, rel_buckets, gains, bias_table, router,
                 attn_in, attn_out, expert_in, expert_out):
    nz, ns, ny, packs, tok, width = shapes_of(layer_input, routes, attn_in, attn_out, expert_in, expert_out)
    nx = ns // 2
    group, pairs = ns * tok, width // 128
    unit = expert_in.shape[1]
    hidden = expert_in.shape[2]
    panels = hidden // width // nx
    pack_units = nx * panels
    experts, buckets = router.shape[1], bias_table.shape[0]
    each = packs * ((5 * tok + 4 * experts - 1) // (4 * experts))
    tall = nz * ns
    units = (attn_in.shape[0] // unit, attn_out.shape[0] // unit)
    total = tall * ny * (units[0] + units[1])
    grads = max(4 * nz * pack_units, total // 2)
    extra = -(-(3 + experts) // 8) * 8
    small = ny + nx - 1 + nz
    mine, every = packs * tok, packs * group
    any_ = pl.BlockSpec(memory_space=pl.ANY)
    vmem = pl.BlockSpec(memory_space=pltpu.VMEM)
    smem = pl.BlockSpec(memory_space=pltpu.SMEM)
    dma = pltpu.SemaphoreType.DMA
    low = lambda *shape: pltpu.VMEM(shape, BF)
    wide = lambda *shape: pltpu.VMEM(shape, F32)
    shape = lambda *dims: jax.ShapeDtypeStruct(dims, F32)
    results = pl.pallas_call(
        layer_body,
        out_shape=[
            jax.ShapeDtypeStruct((packs, tok, width), BF),
            shape(*attn_in.shape),
            shape(*attn_out.shape),
            shape(*expert_in.shape[1:]),
            shape(*expert_out.shape[1:]),
            shape(mine, width),
            shape(mine, width),
            shape(3, width),
            shape(experts, width),
            shape(2 * pairs, buckets),
        ],
        in_specs=[smem, *[vmem] * 8, any_, any_, vmem, any_],
        out_specs=[vmem] * 10,
        scratch_shapes=[
            low(total, unit, width),
            low(total, unit, width),
            low(grads, unit, width),
            low(nx, panels, unit, width),
            *[low(nz, pack_units, unit, width)] * 2,
            low(nz, ny - 1, nx, units[0], unit, width),
            low(nz, ny - 1, units[1], unit, width),
            low(nz, nx - 1, units[0], unit, width),
            low(nz, nx - 1, ny * units[1], unit, width),
            low(nx - 1, panels, unit, width),
            *[low(nz + 1, u, unit, width) for u in (*units, pack_units, pack_units)],
            *[low(every, width)] * 8,
            *[low(mine, width)] * 10,
            *[low(packs, pairs, 2 * tok, group)] * 2,
            *[wide(mine, width)] * 3,
            wide(pairs, 2 * tok, group),
            wide(packs, tok, group),
            wide(packs, tok, group),
            wide(16, group + 128),
            wide(1, width),
            low(2, packs, nx, tok, width),
            low(2, nx - 1, packs, tok, width),
            wide(4, extra, width),
            wide(4, 16, 128),
            wide(small, extra, width),
            wide(small, 16, 128),
            low(2, ny, each, width),
            low(2, nx, ny, each, width),
            wide(2, nx, ny, each, width),
            low(2, nx - 1, ny, each, width),
            low(2, nx - 1, ny, each, width),
            low(2, ny, each, width),
            low(nx * ny * each, width),
            low(panels, nx * ny * each, width),
            low(panels, nx * ny * each, width),
            dma((2, packs, 2 * nx)),
            dma((2, packs, nx, 2)),
            dma((nx - 1,)),
            dma((nx,)),
            dma((4, nz, 2)),
            dma((2, nz, nx - 1 + ny - 1 + max((ny - 1) * nx, (nx - 1) * ny))),
            dma((4, nz, nx, ny)),
            dma((4, nz, nx, ny)),
            dma((4, nz, nx, ny)),
            dma((6, packs)),
            dma((4, nz, nx)),
            dma((4, nz, nx)),
            dma((nz, ny - 1, nx + 1, units[0])),
            dma((nz, ny - 1, nx + 1, units[0])),
            dma((nz, nx - 1, units[0] + 1)),
            dma((nz, nx - 1, units[0] + 1)),
            dma((nx - 1,)),
            dma((nx - 1,)),
            dma((4, nz)),
            dma((4, nz + 1)),
            dma((nz, units[0] + 1)),
            dma((nz + 1, units[0] + 1)),
            dma((2, packs + 1, nx)),
            dma((2, packs + 1, nx)),
            dma((2, small)),
            dma((2, small)),
            dma((4 * (ny - 1) + 4 * (nx - 1) * ny,)),
            dma((4 * (ny - 1) + 4 * (nx - 1) * ny,)),
            pltpu.SemaphoreType.REGULAR,
        ],
        compiler_params=pltpu.CompilerParams(
            collective_id=0, has_side_effects=True, vmem_limit_bytes=64 * 2**20
        ),
        name="layer",
    )(
        doc_lengths[:, 0, 0],
        rel_buckets.reshape(1, -1),
        gains,
        bias_table.T,
        router.T,
        routes.reshape(packs, 1, tok),
        layer_input[:, 0, 0],
        memory[:, 0, 0],
        cotangent[:, 0, 0],
        attn_in.reshape(units[0], unit, width),
        attn_out.reshape(units[1], unit, width),
        expert_in[0],
        expert_out.reshape(pack_units, unit, width),
    )
    out_rows, g0, g1, g2, g3, grad_x, grad_mem, gains_sum, router_sum, table_sum = deliver(results)
    spread = (packs, 1, 1, tok, width)
    return (
        out_rows.reshape(spread),
        grad_x.reshape(spread),
        grad_mem.reshape(spread),
        gains_sum,
        table_sum.T,
        router_sum.T,
        g0,
        g1,
        g2[None],
        g3[None],
    )


def norm_apply(value, gain):
    return value * lax.rsqrt(jnp.mean(value * value, axis=-1, keepdims=True) + EPS) * gain


def norm_back(value, gain, grad):
    r = lax.rsqrt(jnp.mean(value * value, axis=-1, keepdims=True) + EPS)
    scaled = grad * gain
    back = r * scaled - value * (r * r * r) * jnp.mean(scaled * value, axis=-1, keepdims=True)
    return back, jnp.sum(grad * value * r, axis=0)


def gelu_tanh(value):
    return jax.nn.gelu(value, approximate=True)


def times(left, right):
    return jnp.dot(left, right, preferred_element_type=F32)


def times_right(left, right):
    return jnp.einsum("te,de->td", left, right, preferred_element_type=F32)


def times_left(left, right):
    return jnp.einsum("td,te->de", left, right, preferred_element_type=F32)


def split(a, packs):
    return a.reshape(packs, -1, HEADS, HEAD)


def attend(query, keys, values, allowed, bias, packs):
    scores = jnp.einsum("pqhd,pkhd->phqk", split(query, packs), split(keys, packs), preferred_element_type=F32)
    masked = jnp.where(allowed[:, None], scores * HEAD**-0.5 + bias, NEG)
    raised = jnp.exp(masked - jnp.max(masked, axis=3, keepdims=True))
    chances = raised / jnp.sum(raised, axis=3, keepdims=True)
    mixed = jnp.einsum("phqk,pkhd->pqhd", chances.astype(BF), split(values, packs), preferred_element_type=F32)
    return mixed.reshape(query.shape).astype(BF), chances


def attend_back(query, keys, values, chances, grad, packs):
    scale = HEAD**-0.5
    g4 = split(grad, packs)
    grad_chances = jnp.einsum("pqhd,pkhd->phqk", g4, split(values, packs), preferred_element_type=F32)
    spread_ = jnp.sum(chances * grad_chances, axis=3, keepdims=True)
    grad_scores = (chances * (grad_chances - spread_)).astype(BF)
    grad_query = jnp.einsum("phqk,pkhd->pqhd", grad_scores, split(keys, packs), preferred_element_type=F32) * scale
    grad_keys = jnp.einsum("phqk,pqhd->pkhd", grad_scores, split(query, packs), preferred_element_type=F32) * scale
    grad_values = jnp.einsum("phqk,pqhd->pkhd", chances.astype(BF), g4, preferred_element_type=F32)
    return (
        grad_query.reshape(query.shape).astype(BF),
        grad_keys.reshape(keys.shape).astype(BF),
        grad_values.reshape(keys.shape).astype(BF),
        grad_scores,
    )


def per_device(layer_input, memory, cotangent, routes, doc_lengths, rel_buckets, gains, bias_table, router,
               attn_in, attn_out, expert_in, expert_out):
    packs, rows, width = layer_input.shape[0], layer_input.shape[3], layer_input.shape[4]
    seqs = lax.axis_size("seq")
    group = rows * seqs
    experts = router.shape[1]
    capacity = (5 * rows + 4 * experts - 1) // (4 * experts)
    buckets = bias_table.shape[0]
    rank = lax.axis_index("seq")

    x_in, m_in, e_in, e_out = layer_input[:, 0, 0], memory[:, 0, 0], expert_in[0], expert_out[0]
    if fits_kernel(layer_input, routes, attn_in, attn_out, expert_in, expert_out):
        return layer_kernel(layer_input, memory, cotangent, routes, doc_lengths, rel_buckets, gains, bias_table, router,
                            attn_in, attn_out, expert_in, expert_out)
    x_rows = x_in.reshape(packs * rows, width).astype(F32)
    everywhere, peers = ("dp", "seq", "expert"), ("dp", "seq")
    x_all, m_all = (lax.all_gather(a, "seq", axis=1, tiled=True) for a in (x_in, m_in))
    w_in, w_out = (lax.all_gather(a, everywhere, axis=0, tiled=True) for a in (attn_in, attn_out))
    e_in, e_out = (lax.all_gather(a, peers, axis=0, tiled=True) for a in (e_in, e_out))
    w_in = w_in.reshape(6, width, width)
    w_out = w_out.reshape(2, width, width)
    x_all = x_all.reshape(packs * group, width)
    m_all = m_all.reshape(packs * group, width)
    wide = group + rows
    query_pos = rank * rows + jnp.arange(rows, dtype=jnp.int32)
    key_pos = jnp.arange(group, dtype=jnp.int32)
    ends = jnp.cumsum(doc_lengths[:, 0, 0], axis=1)
    query_doc = jnp.sum((query_pos[None, :, None] >= ends[:, None, :]).astype(jnp.int32), axis=2)
    key_doc = jnp.sum((key_pos[None, :, None] >= ends[:, None, :]).astype(jnp.int32), axis=2)
    same = query_doc[:, :, None] == key_doc[:, None, :]
    causal = same & (key_pos[None, None, :] <= query_pos[None, :, None])
    bucket_hot = (rel_buckets[:, None] == jnp.arange(buckets, dtype=jnp.int32)).astype(F32)
    line_at = jnp.arange(group + rows, dtype=jnp.int32) - (group - 1) + rank * rows
    line_hot = (jnp.take(rel_buckets, jnp.clip(line_at, 0, group - 1))[None, :] == jnp.arange(buckets)[:, None]).astype(F32)
    line = jnp.einsum("bh,bj->hj", bias_table, line_hot, precision=HIGHEST)
    line = line[:, ::-1]
    wide = group + rows
    tiled = jnp.broadcast_to(line[:, None, :], (HEADS, rows, wide)).reshape(HEADS, rows * wide)
    skew = tiled[:, rows : rows + rows * (wide - 1)].reshape(HEADS, rows, wide - 1)[:, :, :group]

    normed1_all = norm_apply(x_all.astype(F32), gains[0]).astype(BF)
    normed1 = norm_apply(x_rows, gains[0]).astype(BF)
    query = times(normed1, w_in[0]).astype(BF)
    keys = times(normed1_all, w_in[1]).astype(BF)
    values = times(normed1_all, w_in[2]).astype(BF)
    mem_keys = times(m_all, w_in[4]).astype(BF)
    mem_values = times(m_all, w_in[5]).astype(BF)
    mixed, chances_self = attend(query, keys, values, causal, skew[None], packs)
    hidden1 = x_rows + times(mixed, w_out[0])
    normed2 = norm_apply(hidden1, gains[1]).astype(BF)
    cross_query = times(normed2, w_in[3]).astype(BF)
    cross_mixed, chances_cross = attend(cross_query, mem_keys, mem_values, same, 0.0, packs)
    hidden2 = hidden1 + times(cross_mixed, w_out[1])
    normed3 = norm_apply(hidden2, gains[2]).astype(BF)

    routing = jax.nn.softmax(times(normed3, router), axis=1)
    route = routes[:, 0, 0, :, 0]
    route_hot = (route[:, :, None] == jnp.arange(experts, dtype=jnp.int32)).astype(jnp.int32)
    slot = jnp.sum((jnp.cumsum(route_hot, axis=1) - route_hot) * route_hot, axis=2)
    hot = route_hot.reshape(packs * rows, experts).astype(F32)
    gate = jnp.sum(routing * hot, axis=1)
    target = jnp.where(slot < capacity, (route * packs + jnp.arange(packs)[:, None]) * capacity + slot, -1).reshape(-1)
    dispatch = (target[:, None] == jnp.arange(experts * packs * capacity, dtype=jnp.int32)).astype(BF)

    def swap(a):
        shape = (experts, packs * capacity, width)
        return lax.all_to_all(a.reshape(shape), "expert", split_axis=0, concat_axis=0, tiled=True).reshape(-1, width)

    received = swap(times_left(dispatch, normed3).astype(BF))
    inner = times(received, e_in)
    hidden, pull = jax.vjp(gelu_tanh, inner)
    hidden = hidden.astype(BF)
    result = times(hidden, e_out).astype(BF)
    combined = times(dispatch, swap(result))
    out_rows = (hidden2 + gate[:, None] * combined).astype(BF)
    grad_top = cotangent.reshape(packs * rows, width).astype(F32)
    grad_gate = jnp.sum(grad_top * combined, axis=1)
    grad_result = swap(times_left(dispatch, (gate[:, None] * grad_top).astype(BF)).astype(BF))
    grad_hidden = times_right(grad_result, e_out)
    grad_eout = times_left(hidden, grad_result).astype(BF)
    grad_inner = pull(grad_hidden)[0].astype(BF)
    grad_ein = times_left(received, grad_inner).astype(BF)
    grad_send = swap(times_right(grad_inner, e_in).astype(BF))
    grad_logits = grad_gate[:, None] * routing * (hot - gate[:, None])
    grad_router = jnp.einsum("td,te->de", normed3.astype(F32), grad_logits, precision=HIGHEST)
    grad_normed3 = times(dispatch, grad_send) + jnp.einsum(
        "te,de->td", grad_logits, router.astype(F32), precision=HIGHEST
    )
    back3, gain3 = norm_back(hidden2, gains[2], grad_normed3)
    grad_h2 = grad_top + back3
    grad_h2_low = grad_h2.astype(BF)
    grad_wco = times_left(cross_mixed, grad_h2_low)
    grad_cross = times_right(grad_h2_low, w_out[1]).astype(BF)
    grad_cq, grad_ck, grad_cv, _ = attend_back(cross_query, mem_keys, mem_values, chances_cross, grad_cross, packs)
    back2, gain2 = norm_back(hidden1, gains[1], times_right(grad_cq, w_in[3]))
    grad_h1 = grad_h2 + back2
    grad_h1_low = grad_h1.astype(BF)
    grad_wso = times_left(mixed, grad_h1_low)
    grad_mixed = times_right(grad_h1_low, w_out[0]).astype(BF)
    grad_q, grad_k, grad_v, grad_scores = attend_back(query, keys, values, chances_self, grad_mixed, packs)

    total = jnp.sum(grad_scores.astype(F32), axis=0)[:, ::-1]
    padded = jnp.pad(total, ((0, 0), (0, 0), (0, wide - group))).reshape(HEADS, rows * wide)
    diagonal = padded[:, : rows * (wide - 1)].reshape(HEADS, rows, wide - 1).sum(axis=1)
    at = jnp.clip(rank * rows + (rows - 1) - jnp.arange(wide - 1, dtype=jnp.int32), 0, group - 1)
    diagonal_hot = (jnp.take(rel_buckets, at)[:, None] == jnp.arange(buckets)).astype(F32)
    grad_table = jnp.einsum("jb,hj->bh", diagonal_hot, diagonal, precision=HIGHEST)

    def to_owner(a):
        return lax.psum_scatter(a.reshape(packs, group, width), "seq", scatter_dimension=1, tiled=True)

    grad_memory = to_owner((times_right(grad_ck, w_in[4]) + times_right(grad_cv, w_in[5])).astype(BF))
    part1 = to_owner((times_right(grad_k, w_in[1]) + times_right(grad_v, w_in[2])).astype(BF))
    grad_normed1 = times_right(grad_q, w_in[0]) + part1.reshape(packs * rows, width).astype(F32)
    back1, gain1 = norm_back(x_rows, gains[0], grad_normed1)
    grad_x = grad_h1 + back1
    grad_in = jnp.concatenate(
        [
            times_left(normed1, grad_q),
            times_left(normed1_all, grad_k),
            times_left(normed1_all, grad_v),
            times_left(normed2, grad_cq),
            times_left(m_all, grad_ck),
            times_left(m_all, grad_cv),
        ]
    ).astype(BF)
    grad_out = jnp.concatenate([grad_wso, grad_wco]).astype(BF)
    shards = [
        lax.psum_scatter(a, over, scatter_dimension=0, tiled=True).astype(F32)
        for a, over in ((grad_in, everywhere), (grad_out, everywhere), (grad_ein, peers), (grad_eout, peers))
    ]
    small = lax.psum((jnp.stack([gain1, gain2, gain3]), grad_table, grad_router), ("dp", "seq", "expert"))
    shape = (packs, 1, 1, rows, width)
    return (
        out_rows.reshape(shape),
        grad_x.reshape(shape),
        grad_memory.astype(F32).reshape(shape),
        *small,
        shards[0],
        shards[1],
        shards[2][None],
        shards[3][None],
    )


def solution(mesh):
    tokens = P(None, "dp", "expert", "seq", None)
    dense = P(("dp", "seq", "expert"), None)
    expert = P("expert", ("dp", "seq"), None)
    return jax.shard_map(
        per_device,
        mesh=mesh,
        in_specs=(tokens, tokens, tokens, tokens, P(None, "dp", "expert", None), P(), P(), P(), P(),
                  dense, dense, expert, expert),
        out_specs=(tokens, tokens, tokens, P(), P(), P(), dense, dense, expert, expert),
        check_vma=False,
    )
```

```python
import functools

import jax
import jax.numpy as jnp
from jax import lax
from jax.experimental import pallas as pl
from jax.experimental.pallas import tpu as pltpu
from jax.sharding import PartitionSpec as P

HEADS = 12
HEAD = 64

EPS = 1e-06
NEG = -1e30
HIGHEST = lax.Precision.HIGHEST
MESH = pl.DeviceIdType.MESH
BF = jnp.bfloat16
F32 = jnp.float32


class Place:
    def __init__(self):
        self.nz, self.ns, self.ny = (lax.axis_size(a) for a in ("dp", "seq", "expert"))
        self.nx = self.ns // 2
        self.z, self.s, self.y = (lax.axis_index(a) for a in ("dp", "seq", "expert"))
        self.x, self.c = self.s // 2, lax.rem(self.s, 2)

    def device(self, z=None, x=None, c=None, y=None):
        z = self.z if z is None else z
        x = self.x if x is None else x
        c = self.c if c is None else c
        y = self.y if y is None else y
        return (z, x * 2 + c, y)

    def other_x(self):
        return [lax.rem(self.x + k, self.nx) for k in range(1, self.nx)]

    def other_y(self):
        return [lax.rem(self.y + k, self.ny) for k in range(1, self.ny)]

    def by_distance(self, k):
        half = self.nz // 2
        order = [
            sorted(range(self.nz), key=lambda d: (abs(d - z), (d < half) != (z < half), d)) for z in range(self.nz)
        ]
        return self.pick([row[k] for row in order])

    def pick(self, values):
        out = jnp.int32(values[0])
        for z in range(1, self.nz):
            out = jnp.where(self.z == z, jnp.int32(values[z]), out)
        return out

    def greet(self):
        barrier = pltpu.get_barrier_semaphore()
        for x in self.other_x():
            pl.semaphore_signal(barrier, inc=1, device_id=self.device(x=x), device_id_type=MESH)
        for y in self.other_y():
            pl.semaphore_signal(barrier, inc=1, device_id=self.device(y=y), device_id_type=MESH)
        pl.semaphore_signal(barrier, inc=1, device_id=self.device(c=1 - self.c), device_id_type=MESH)

        for k in range(1, self.nz):
            z = lax.rem(self.z + k, self.nz)
            pl.semaphore_signal(barrier, inc=1, device_id=self.device(z=z), device_id_type=MESH)
        pl.semaphore_wait(barrier, self.nx - 1 + self.ny - 1 + 1 + self.nz - 1)


def rms_rows(src, gain, dst, rows, step=64):
    @pl.loop(0, rows // step)
    def _(i):
        at = pl.ds(pl.multiple_of(i * step, step), step)
        value = src[at, :].astype(F32)
        r = lax.rsqrt(jnp.mean(value * value, axis=-1, keepdims=True) + EPS)
        dst[at, :] = (value * r * gain).astype(BF)


def block(weight, index, lanes=slice(None), share=(0, 1)):
    unit, width = weight.shape[-2:]
    count = width // unit // share[1]
    first = pl.multiple_of(index * (width // unit) + share[0] * count, count)
    value = weight[pl.ds(first, count), :, lanes]
    return value.reshape(count * unit, value.shape[-1])


def project(left, weight, index, dst):
    width = dst.shape[-1]
    step = 256 if width % 256 == 0 else width

    @pl.loop(0, width // step)
    def _(j):
        at = pl.ds(pl.multiple_of(j * step, step), step)
        dst[:, at] = jnp.dot(left[...], block(weight, index, at), preferred_element_type=F32).astype(dst.dtype)


def prepare_bias(rel, table, bias, rank, rows, group):
    heads, buckets = table.shape
    wide = group + 128
    lane = lax.broadcasted_iota(jnp.int32, (group, wide), 1)
    shift = jnp.where(lane < group, lane, lane - wide)
    distance = jnp.clip(rank * rows - shift, 0, group - 1)
    hot = (lax.broadcasted_iota(jnp.int32, (group, wide), 0) == distance).astype(F32).astype(BF)
    which = jnp.dot(jnp.broadcast_to(rel[...].astype(F32), (8, group)).astype(BF), hot, preferred_element_type=F32)
    picks = (lax.broadcasted_iota(jnp.int32, (buckets, wide), 0) == which[0:1].astype(jnp.int32)).astype(F32)
    line = jnp.dot(table[...], picks, precision=HIGHEST, preferred_element_type=F32)
    for h in range(heads):
        band = pltpu.roll(jnp.broadcast_to(line[h : h + 1], (rows, wide)), 0, 1, stride=1, stride_axis=0)
        bias[h // 2, pl.ds((h % 2) * rows, rows), :] = band[:, :group]


def prepare_masks(lengths, same, causal, rank, rows, group):
    key = lax.broadcasted_iota(jnp.int32, (rows, group), 1)
    query = rank * rows + lax.broadcasted_iota(jnp.int32, (rows, group), 0)
    for p in range(same.shape[0]):
        end = jnp.int32(0)
        kd = jnp.zeros((rows, group), jnp.int32)
        qd = jnp.zeros((rows, group), jnp.int32)
        for n in range(lengths.shape[1]):
            end = end + lengths[p, n]
            kd = kd + jnp.where(key >= end, 1, 0)
            qd = qd + jnp.where(query >= end, 1, 0)
        same[p] = jnp.where(kd == qd, 0.0, NEG)
        causal[p] = jnp.where((kd == qd) & (key <= query), 0.0, NEG)


def two_heads(pair):
    first = lax.broadcasted_iota(jnp.int32, pair.shape, 1) < HEAD
    zero = jnp.zeros_like(pair)
    return jnp.concatenate([jnp.where(first, pair, zero), jnp.where(first, zero, pair)], axis=0)


def one_pair(stacked):
    rows = stacked.shape[0] // 2
    first = lax.broadcasted_iota(jnp.int32, (rows, stacked.shape[1]), 1) < HEAD
    return jnp.where(first, stacked[:rows], stacked[rows:])


def attend_pairs(query, keys, values, bias, mask, chances, mixed):
    packs, pairs, double, group = chances.shape
    rows = double // 2

    def body(i, carry):
        p, j = i // pairs, lax.rem(i, pairs)
        mine = pl.ds(pl.multiple_of(p * rows, rows), rows)
        theirs = pl.ds(pl.multiple_of(p * group, group), group)
        lanes = pl.ds(pl.multiple_of(j * 128, 128), 128)
        scores = lax.dot_general(
            two_heads(query[mine, lanes]), keys[theirs, lanes], (((1,), (1,)), ((), ())), preferred_element_type=F32
        )
        scores = scores * HEAD**-0.5
        if bias is not None:
            scores = scores + bias[j]
        scores = (scores.reshape(2, rows, group) + mask[p][None]).reshape(double, group)
        raised = jnp.exp(scores - jnp.max(scores, axis=1, keepdims=True))
        weights = (raised * (1.0 / jnp.sum(raised, axis=1, keepdims=True))).astype(BF)
        chances[p, j] = weights
        out = jnp.dot(weights, values[theirs, lanes], preferred_element_type=F32)
        mixed[mine, lanes] = one_pair(out).astype(BF)
        return carry

    lax.fori_loop(0, packs * pairs, body, 0, unroll=12)


def add_product(total, left, weight, index):
    width = total.shape[-1]
    step = 256 if width % 256 == 0 else width

    @pl.loop(0, width // step)
    def _(j):
        at = pl.ds(pl.multiple_of(j * step, step), step)
        total[:, at] += jnp.dot(left[...], block(weight, index, at), preferred_element_type=F32)


def product_t(left, weight, index, dst):
    halves = 2
    step = weight.shape[-1] // halves

    @pl.loop(0, halves)
    def _(j):
        rows = block(weight, index, share=(j, halves))
        out = lax.dot_general(left[...], rows, (((1,), (1,)), ((), ())), preferred_element_type=F32)
        dst[:, pl.ds(pl.multiple_of(j * step, step), step)] = out.astype(dst.dtype)


def two_products_t(left1, index1, left2, index2, weight, dst):
    halves = 2
    step = weight.shape[-1] // halves

    @pl.loop(0, halves)
    def _(j):
        out = 0.0
        for left, index in ((left1, index1), (left2, index2)):
            rows = block(weight, index, share=(j, halves))
            out = out + lax.dot_general(left[...], rows, (((1,), (1,)), ((), ())), preferred_element_type=F32)
        dst[:, pl.ds(pl.multiple_of(j * step, step), step)] = out.astype(dst.dtype)


def outer_product(left, right, dst, index):
    unit, width = dst.shape[-2:]
    halves = 2
    step, count = width // halves, width // unit // halves

    @pl.loop(0, halves)
    def _(j):
        part = left[:, pl.ds(pl.multiple_of(j * step, step), step)]
        out = lax.dot_general(part, right[...], (((0,), (0,)), ((), ())), preferred_element_type=F32)
        first = index * (width // unit) + j * count
        dst[pl.ds(first, count)] = out.astype(dst.dtype).reshape(count, unit, width)


def add_into(total, other):
    lead = total.shape[:-2]
    count = 1
    for n in lead:
        count *= n
    rows = total.shape[-2]
    step = next(n for n in ((48, 32, 16) if total.shape[-1] <= 1024 else (16,)) if rows % n == 0)

    def body(i, carry):
        index = []
        rest = i // (rows // step)
        for n in reversed(lead):
            index.insert(0, lax.rem(rest, n))
            rest = rest // n
        r = pl.ds(pl.multiple_of(lax.rem(i, rows // step) * step, 16), step)
        at = (*index, r)
        total[at] = (total[at].astype(F32) + other[at].astype(F32)).astype(total.dtype)
        return carry

    lax.fori_loop(0, count * (rows // step), body, 0)


def norm_back_rows(value, gain, grad, total, gain_grad, step=64):
    gain_grad[...] = jnp.zeros_like(gain_grad)

    @pl.loop(0, value.shape[0] // step)
    def _(i):
        at = pl.ds(pl.multiple_of(i * step, step), step)
        v, g = value[at, :].astype(F32), grad[at, :]
        r = lax.rsqrt(jnp.mean(v * v, axis=-1, keepdims=True) + EPS)
        scaled = g * gain
        total[at, :] += r * scaled - v * (r * r * r) * jnp.mean(scaled * v, axis=-1, keepdims=True)
        gain_grad[...] += jnp.sum(g * v * r, axis=0, keepdims=True)


def attend_pairs_back(query, keys, values, chances, grad, grad_q, grad_k, grad_v, diagonal):
    packs, pairs, double, group = chances.shape
    rows = double // 2
    scale = HEAD**-0.5

    def body(i, carry):
        p, j = i // pairs, lax.rem(i, pairs)
        mine = pl.ds(pl.multiple_of(p * rows, rows), rows)
        theirs = pl.ds(pl.multiple_of(p * group, group), group)
        lanes = pl.ds(pl.multiple_of(j * 128, 128), 128)
        ga = two_heads(grad[mine, lanes])
        low = chances[p, j]
        wide = low.astype(F32)
        gp = lax.dot_general(ga, values[theirs, lanes], (((1,), (1,)), ((), ())), preferred_element_type=F32)
        gs = (wide * (gp - jnp.sum(wide * gp, axis=1, keepdims=True))).astype(BF)
        gq = jnp.dot(gs, keys[theirs, lanes], preferred_element_type=F32)
        grad_q[mine, lanes] = (one_pair(gq) * scale).astype(BF)
        gk = lax.dot_general(gs, two_heads(query[mine, lanes]), (((0,), (0,)), ((), ())), preferred_element_type=F32)
        grad_k[theirs, lanes] = (gk * scale).astype(BF)
        gv = lax.dot_general(low, ga, (((0,), (0,)), ((), ())), preferred_element_type=F32)
        grad_v[theirs, lanes] = gv.astype(BF)
        if diagonal is not None:
            a = lax.broadcasted_iota(jnp.int32, (rows, rows), 0)
            b = lax.broadcasted_iota(jnp.int32, (rows, rows), 1)
            flip = (a + b == rows - 1).astype(F32).astype(BF)
            for half in range(2):
                turned = jnp.dot(flip, gs[half * rows : (half + 1) * rows], preferred_element_type=F32)
                turned = jnp.concatenate([turned, jnp.zeros((rows, 128), F32)], axis=1)
                band = pltpu.roll(turned, 0, 1, stride=1, stride_axis=0)
                diagonal[pl.ds(2 * j + half, 1), :] += jnp.sum(band, axis=0, keepdims=True)
        return carry

    lax.fori_loop(0, packs * pairs, body, 0, unroll=12)


def table_grad(rel, diagonal, rank, rows, group):
    wide = group + 128
    lane = lax.broadcasted_iota(jnp.int32, (group, wide), 1)
    distance = jnp.clip(rank * rows + rows - 1 - lane, 0, group - 1)
    hot = (lax.broadcasted_iota(jnp.int32, (group, wide), 0) == distance).astype(F32).astype(BF)
    which = jnp.dot(jnp.broadcast_to(rel[...].astype(F32), (8, group)).astype(BF), hot, preferred_element_type=F32)
    picks = (lax.broadcasted_iota(jnp.int32, (128, wide), 0) == which[0:1].astype(jnp.int32)).astype(F32)
    return lax.dot_general(diagonal[...], picks, (((1,), (1,)), ((), ())), precision=HIGHEST, preferred_element_type=F32)


def route_slots(route, experts, capacity):
    packs, _, rows = route.shape
    count = packs * rows
    same = lax.broadcasted_iota(jnp.int32, (rows, rows), 0) == lax.broadcasted_iota(jnp.int32, (rows, rows), 1)
    column = jnp.concatenate(
        [jnp.sum(jnp.where(same, route[p], 0), axis=1, keepdims=True) for p in range(packs)], axis=0
    )
    hot = (column == lax.broadcasted_iota(jnp.int32, (count, experts), 1)).astype(F32)
    a = lax.broadcasted_iota(jnp.int32, (count, count), 0)
    b = lax.broadcasted_iota(jnp.int32, (count, count), 1)
    earlier = ((b < a) & (a // rows == b // rows)).astype(F32).astype(BF)
    before = jnp.dot(earlier, hot.astype(BF), preferred_element_type=F32)
    slot = jnp.sum(before * hot, axis=1, keepdims=True).astype(jnp.int32)
    pack = lax.broadcasted_iota(jnp.int32, (count, 1), 0) // rows
    target = jnp.where(slot < capacity, (column * packs + pack) * capacity + slot, -1)
    slots = lax.broadcasted_iota(jnp.int32, (count, experts * packs * capacity), 1)
    return hot, (target == slots).astype(F32).astype(BF)


def chances_of(rows, router_t, own):
    logits = lax.dot_general(rows, router_t[...], (((1,), (1,)), ((), ())), preferred_element_type=F32)
    raised = jnp.exp(logits - jnp.max(logits, axis=1, keepdims=True))
    mine = (lax.broadcasted_iota(jnp.int32, (1, logits.shape[1]), 1) == own).astype(F32)
    return mine, raised / jnp.sum(raised, axis=1, keepdims=True)


def gelu_both(z):
    c = 0.7978845608028654
    t = jnp.tanh(c * (z + 0.044715 * (z * z * z)))
    half = 0.5 * (1.0 + t)
    slope = half + 0.5 * z * (1.0 - t * t) * (c * (1.0 + 3 * 0.044715 * (z * z)))
    return z * half, slope


def continue_waits(waits, hop, d, at):
    def wait():
        @pl.when(d < at.z)
        def _():
            hop(-1).wait_send()

        @pl.when(d > at.z)
        def _():
            hop(1).wait_send()

    waits.append(wait)


def layer_body(lengths, rel, gains, table, router_t, route, x_ref, m_ref, g_hbm, ain, aout, ein_hbm, eout,
               out_rows, o0, o1, o2, o3, grad_x, grad_mem, sum_gains, sum_router, sum_table,
               w, big, ge, prep, c2, c3, y0, y1, x0, x1, ex_in, z0, z1, z2, z3,
               xo, mo, n1_all, k_, v, kc, vc, gv, n1, q, mixed, n2, qc, cross_mixed, n3, gb, ga, gq,
               pr_self, pr_cross, h1, h2, gn, bias, same, causal, diagonal, gain_row,
               act_core, act_x, wide_sum, table_sum, wide_in, table_in,
               slots_out, slots_in, slots_acc, ret_out, ret_in, back_in, grad_here, hid, gin_,
               act_send, act_recv, prep_send, prep_recv, line_send, side_send, spread_send, ici_recv, spread_recv, own_sem,
               core_send, core_recv, y_send, y_recv, x_send, x_recv, ex_send, ex_recv, z_send, z_recv, zd_send, zd_recv,
               sum_send, sum_recv, small_send, small_recv, slot_send, slot_recv, free_sem, g_ref, ein, x_keep, load_sem):
    at = Place()
    nz, nx, ny = at.nz, at.nx, at.ny
    packs, tok, width = x_ref.shape
    group = xo.shape[0] // packs
    experts = router_t.shape[0]
    unit = ain.shape[1]
    block_units = eout.shape[0]
    panels = block_units // nx
    columns = ein.shape[1] // (nz * nx)
    buckets = table.shape[1]
    gk = xo
    units = (ain.shape[0], aout.shape[0])
    tall = nz * nx * 2
    bases = (0, tall * ny * units[0], 0, 2 * nz * block_units)
    dense, e_in, e_out = (0, 1), 2, 3
    experts_ = (e_in, e_out)
    waits = []

    def remote(src, dst, ssem, rsem, **where):
        return pltpu.make_async_remote_copy(
            src_ref=src, dst_ref=dst, send_sem=ssem, recv_sem=rsem,
            device_id=at.device(**where), device_id_type=MESH,
        )

    def send(*args, **where):
        one = remote(*args, **where)
        if acts_now[0]:
            one.start()
        waits.append(one.wait_send)

    acts_now = [True]

    def at_planes(ends, step, last):
        between = (at.z > 0) & (at.z < nz - 1)
        mark = len(waits)

        @pl.when(jnp.logical_not(between) if ends else between)
        def _():
            step()

        del waits[mark:]
        if last:
            acts_now[0] = False
            step()
            acts_now[0] = True

    def add(total, other):
        if acts_now[0]:
            add_into(total, other)

    def start_when(pred, make):
        if acts_now[0]:

            @pl.when(pred)
            def _():
                make().start()

    def arrive(ref, sem):
        if acts_now[0]:
            pltpu.make_async_copy(ref, ref, sem).wait()

    def spot(a, z, x, c, y):
        index = ((z * nx + x) * 2 + c) * ny + y
        return w.at[pl.ds(bases[a] + index * units[a], units[a])]

    def pack_of(a, z, c):
        return big.at[pl.ds(bases[a] + (z * 2 + c) * block_units, block_units)]

    shards = (ain, aout)
    acts = ((x_ref, xo), (m_ref, mo))

    load_g = pltpu.make_async_copy(g_hbm, g_ref, load_sem.at[0])
    load_e = pltpu.make_async_copy(ein_hbm, ein, load_sem.at[1])
    load_g.start()
    load_e.start()
    at.greet()

    def act_rows(full, p, x, c):
        return full.at[pl.ds(pl.multiple_of(p * group + (x * 2 + c) * tok, 16), tok)]

    own_waits = []

    def send_acts():
        for i, (src, full) in enumerate(acts):
            for p in range(packs):
                dst = act_rows(full, p, at.x, at.c)
                for k, x in enumerate(at.other_x()):
                    send(src.at[p], dst, act_send.at[i, p, k], act_recv.at[i, p, at.x, at.c], x=x)
                send(src.at[p], dst, act_send.at[i, p, nx - 1 + at.x], act_recv.at[i, p, at.x, at.c], c=1 - at.c)
                own = pltpu.make_async_copy(src.at[p], dst, own_sem.at[4 + i, p])
                own.start()
                own_waits.append(own.wait)

    def along_line(a, z, src):
        dst = spot(a, z, at.x, at.c, at.y) if a in dense else pack_of(a, z, at.c)
        sem = ici_recv.at[a, z, at.x, at.y]
        left = (z >= at.z) & (at.z > 0)
        right = (z <= at.z) & (at.z < nz - 1)

        def one(side):
            return remote(src, dst, line_send.at[a, z, side], sem, z=at.z + 2 * side - 1)

        start_when(left, lambda: one(0))
        start_when(right, lambda: one(1))

        def wait():
            @pl.when(left)
            def _():
                one(0).wait_send()

            @pl.when(right)
            def _():
                one(1).wait_send()

        waits.append(wait)

    def to_core(a, z, x, y, src):
        dst = spot(a, z, x, at.c, y) if a in dense else pack_of(a, z, at.c)
        send(src, dst, spread_send.at[a, z, x, y], spread_recv.at[a, z, x, y], c=1 - at.c)

    zs = [at.by_distance(k) for k in range(nz)]

    def dense_events(k):
        z = zs[k]
        for a in dense:
            here = spot(a, z, at.x, at.c, at.y)
            src = here if k else shards[a]
            if k:
                arrive(here, ici_recv.at[a, z, at.x, at.y])
            else:
                own = pltpu.make_async_copy(shards[a], here, own_sem.at[a, 0])
                own.start()
                own_waits.append(own.wait)
            along_line(a, z, src)
            for j, x in enumerate(at.other_x()):
                send(src, here, side_send.at[a, z, j], ici_recv.at[a, z, at.x, at.y], x=x)
            for j, y in enumerate(at.other_y()):
                send(src, here, side_send.at[a, z, nx - 1 + j], ici_recv.at[a, z, at.x, at.y], y=y)
            to_core(a, z, at.x, at.y, src)

    def side_y(k):
        z = zs[k]
        for y in at.other_y():
            for a in dense:
                here = spot(a, z, at.x, at.c, y)
                arrive(here, ici_recv.at[a, z, at.x, y])
                if a == 1:
                    for j, x in enumerate(at.other_x()):
                        send(here, here, side_send.at[a, z, nx - 1 + ny - 1 + j + (nx - 1) * y],
                             ici_recv.at[a, z, at.x, y], x=x)
                to_core(a, z, at.x, y, here)

    def side_x(k):
        z = zs[k]
        for x in at.other_x():
            for a in dense:
                here = spot(a, z, x, at.c, at.y)
                arrive(here, ici_recv.at[a, z, x, at.y])
                if a == 0:
                    for j, y in enumerate(at.other_y()):
                        send(here, here, side_send.at[a, z, nx - 1 + ny - 1 + j + (ny - 1) * x],
                             ici_recv.at[a, z, x, at.y], y=y)
                to_core(a, z, x, at.y, here)

    def corner_events(k):
        z = zs[k]
        for a in dense:
            for y in at.other_y():
                for x in at.other_x():
                    here = spot(a, z, x, at.c, y)
                    arrive(here, ici_recv.at[a, z, x, y])
                    to_core(a, z, x, y, here)

    def act_events():
        for i, (src, full) in enumerate(acts):
            for p in range(packs):
                for x in at.other_x():
                    dst = act_rows(full, p, x, at.c)
                    arrive(dst, act_recv.at[i, p, x, at.c])
                    send(dst, dst, act_send.at[i, p, nx - 1 + x], act_recv.at[i, p, x, at.c], c=1 - at.c)

    def in_unit(z, c, x, n=1):
        return pl.ds(bases[e_in] + ((z * 2 + c) * nx + x) * panels, n * panels)

    def start_prep():
        load_e.wait()
        for x in range(nx):
            for u in range(panels):
                each_z = width // columns
                prep[x, u] = jnp.concatenate(
                    [ein[:, (z * nx + x) * columns : (z * nx + x + 1) * columns] for z in range(u * each_z, (u + 1) * each_z)],
                    axis=1,
                )
        big[in_unit(at.z, at.c, at.x)] = prep[at.x]
        for j, x in enumerate(at.other_x()):
            send(prep.at[x], big.at[in_unit(at.z, at.c, at.x)], prep_send.at[j], prep_recv.at[at.x], x=x)

    def expert_events(k, kinds=experts_):
        z = zs[k]
        for a in kinds:
            here = pack_of(a, z, at.c)
            src = here
            if k:
                arrive(here, ici_recv.at[a, z, at.x, at.y])
            elif a == e_in:
                for x in at.other_x():
                    arrive(big.at[in_unit(at.z, at.c, x)], prep_recv.at[x])
            else:
                src = eout
                own = pltpu.make_async_copy(eout, here, own_sem.at[a, 0])
                own.start()
                own_waits.append(own.wait)
            along_line(a, z, src)
            to_core(a, z, 0, 0, src)

    def first_norm():
        for i, (src, full) in enumerate(acts):
            for p in range(packs):
                for x in range(nx):
                    arrive(act_rows(full, p, x, 1 - at.c), act_recv.at[i, p, x, 1 - at.c])
        for wait in own_waits:
            wait()
        rms_rows(xo, gains[0:1], n1_all, packs * group)
        for p in range(packs):
            x_keep[pl.ds(p * tok, tok), :] = xo[pl.ds(pl.multiple_of(p * group + at.s * tok, tok), tok), :]
            n1[pl.ds(p * tok, tok), :] = n1_all[pl.ds(pl.multiple_of(p * group + at.s * tok, tok), tok), :]
        h1[...] = x_keep[...].astype(F32)

    places = [((z * 2 + c) * nx + x) * panels for z in range(nz) for x in range(nx) for c in range(2)]
    each = slots_out.shape[2]
    count = ny * each
    row_units = width // unit

    def keys_and_values(for_self):
        @pl.when(for_self)
        def _():
            project(n1_all, w, 1, k_)
            project(n1_all, w, 2, v)

        @pl.when(jnp.logical_not(for_self))
        def _():
            project(mo, w, 4, kc)
            project(mo, w, 5, vc)

    def by_slot(dispatch, rows):
        out = lax.dot_general(dispatch, rows, (((0,), (0,)), ((), ())), preferred_element_type=F32)
        return out.astype(BF).reshape(ny, each, width)

    slot_waits = []

    def slot_copy(late, src, dst, sem_from, sem_to, **where):
        one = remote(src, dst, slot_send.at[sem_from], slot_recv.at[sem_to], **where)
        one.start()
        (waits if late else slot_waits).append(one.wait_send)

    def y_sem(t, j):
        return t * (ny - 1) + j

    def x_sem(t, j, y):
        return 4 * (ny - 1) + (t * (nx - 1) + j) * ny + y

    def ret_sem(t, j, y):
        return 4 * (ny - 1) + 2 * (nx - 1) * ny + (t * (nx - 1) + j) * ny + y

    def send_slots(t):
        for j, y in enumerate(at.other_y()):
            slot_copy(False, slots_out.at[t, y], slots_in.at[t, at.x, at.y], y_sem(t, j), y_sem(t, ny - 2 - j), y=y)
        for j, x in enumerate(at.other_x()):
            slot_copy(False, slots_out.at[t, at.y], slots_in.at[t, at.x, at.y], x_sem(t, j, at.y),
                      x_sem(t, nx - 2 - j, at.y), x=x)
        slots_in[t, at.x, at.y] = slots_out[t, at.y]

    def summed(t, y):
        total = slots_acc[t, at.x, y]
        for j in range(nx - 1):
            arrive(ret_in.at[t, j, y], slot_recv.at[ret_sem(t, j, y)])
            total = total + ret_in[t, j, y].astype(F32)
        return total.astype(BF)

    cores, ys, xs, zs_ = {2: c2, 3: c3}, (y0, y1), (x0, x1), (z0, z1, z2, z3)
    outs = (o0, o1, o2, o3)
    far = [sorted(range(nz), key=lambda d: (-abs(d - z), d)) for z in range(nz)]
    order_e = [at.pick([far[z][k] for z in range(nz)]) for k in range(nz)]
    halves = [[d for d in row if d >= nz // 2] + [d for d in row if d < nz // 2] for row in far]
    order_d = [at.pick([halves[z][k] for z in range(nz)]) for k in range(nz)]
    e_waits = []

    def expert_part(a, d, c):
        return ge.at[pl.ds(bases[a] + (d * 2 + c) * block_units, block_units)]

    def start_expert(a, k):
        one = remote(expert_part(a, order_e[k], 1 - at.c), cores[a].at[k], core_send.at[a, k, 0],
                     core_recv.at[a, k, 0], c=1 - at.c)
        one.start()
        e_waits.append(one.wait_send)

    def core_expert(a, k):
        arrive(cores[a].at[k], core_recv.at[a, k, 0])
        add_into(cores[a].at[k], expert_part(a, order_e[k], at.c))

    def free_experts():
        for wait in e_waits:
            wait()
        pl.semaphore_signal(free_sem, inc=1, device_id=at.device(c=1 - at.c), device_id_type=MESH)

    def dense_part(a, d, x, c):
        return big.at[pl.ds(bases[a] + ((d * nx + x) * 2 + c) * ny * units[a], ny * units[a])]

    def dense_core(a, k, x, y=None, u=None):
        first = bases[a] // 2 + (k * nx + x) * ny * units[a]
        if y is None:
            return ge.at[pl.ds(first, ny * units[a])]
        if u is None:
            return ge.at[pl.ds(first + y * units[a], units[a])]
        return ge.at[pl.ds(first + y * units[a] + u, 1)]

    def xs_in_order():
        return [(x, True) for x in at.other_x()] + [(at.x, False)]

    def start_dense(k, a):
        for x in range(nx):
            send(dense_part(a, order_d[k], x, 1 - at.c), dense_core(a, k, x), core_send.at[a, k, x],
                     core_recv.at[a, k, x], c=1 - at.c)

    def first_dense(k, a):
        if a == 0:
            for x, _ in xs_in_order():
                arrive(dense_core(0, k, x), core_recv.at[0, k, x])
                add_into(dense_core(0, k, x), dense_part(0, order_d[k], x, at.c))
                for u in range(units[0]):
                    for j, y in enumerate(at.other_y()):
                        send(dense_core(0, k, x, y, u), ys[0].at[k, ny - 2 - j, x, pl.ds(u, 1)],
                             y_send.at[k, j, x, u], y_recv.at[k, ny - 2 - j, x, u], y=y)
            return
        for x, _ in xs_in_order():
            arrive(dense_core(1, k, x), core_recv.at[1, k, x])
            add_into(dense_core(1, k, x), dense_part(1, order_d[k], x, at.c))
        for j, x in enumerate(at.other_x()):
            send(dense_core(1, k, x), xs[1].at[k, nx - 2 - j], x_send.at[k, j, units[0]],
                 x_recv.at[k, nx - 2 - j, units[0]], x=x)

    def second_dense(k, a):
        if a == 0:
            for x, away in xs_in_order():
                for u in range(units[0]):
                    total = ys[0].at[k, 0, x, pl.ds(u, 1)]
                    for j in range(ny - 1):
                        piece = ys[0].at[k, j, x, pl.ds(u, 1)]
                        arrive(piece, y_recv.at[k, j, x, u])
                        add_into(total, piece if j else dense_core(0, k, x, at.y, u))
                    if away:
                        j = lax.rem(x - at.x + nx, nx) - 1
                        send(total, xs[0].at[k, nx - 2 - j, pl.ds(u, 1)], x_send.at[k, j, u], x_recv.at[k, nx - 2 - j, u], x=x)
            return
        for j in range(nx - 1):
            arrive(xs[1].at[k, j], x_recv.at[k, j, units[0]])
            add_into(xs[1].at[k, 0], xs[1].at[k, j] if j else dense_core(1, k, at.x))
        for j, y in enumerate(at.other_y()):
            send(xs[1].at[k, 0, pl.ds(y * units[1], units[1])], ys[1].at[k, ny - 2 - j],
                 y_send.at[k, j, nx, 0], y_recv.at[k, ny - 2 - j, nx, 0], y=y)

    def piece_of(k, p):
        return xs[0].at[k, 0, pl.ds(p, 1)] if p < units[0] else ys[1].at[k, 0]

    def inbox_of(slot, p):
        return zs_[0].at[slot, pl.ds(p, 1)] if p < units[0] else zs_[1].at[slot]

    def line_dense(k, a):
        d = order_d[k]
        for p in range(units[0]) if a == 0 else [units[0]]:
            total = piece_of(k, p)
            if p < units[0]:
                for j in range(nx - 1):
                    piece = xs[0].at[k, j, pl.ds(p, 1)]
                    arrive(piece, x_recv.at[k, j, p])
                    add(total, piece if j else ys[0].at[k, 0, at.x, pl.ds(p, 1)])
            else:
                for j in range(ny - 1):
                    arrive(ys[1].at[k, j], y_recv.at[k, j, nx, 0])
                    add(total, ys[1].at[k, j] if j else xs[1].at[k, 0, pl.ds(at.y * units[1], units[1])])
            for side in range(2):

                @pl.when((at.z > 0) & (d > at.z) if side == 0 else (at.z < nz - 1) & (d < at.z))
                def _(total=total, p=p):
                    arrive(inbox_of(d, p), zd_recv.at[d, p])
                    add(total, inbox_of(d, p))

            def hop(to, total=total, p=p):
                slot = d if to > 0 else jnp.where(d == at.z - 1, nz, d)
                return remote(total, inbox_of(slot, p), zd_send.at[k, p], zd_recv.at[slot, p], z=at.z + to)

            start_when(d < at.z, functools.partial(hop, -1))
            start_when(d > at.z, functools.partial(hop, 1))

            continue_waits(waits, hop, d, at)

    def finish_dense():
        for k in (nz // 2 - 1, nz - 1):

            @pl.when(order_d[k] == at.z)
            def _(k=k):
                for p in range(units[0] + 1):
                    total = piece_of(k, p)
                    for side, here in enumerate((at.z > 0, at.z < nz - 1)):
                        slot = at.z if side == 0 else nz

                        @pl.when(here)
                        def _(total=total, slot=slot, p=p):
                            arrive(inbox_of(slot, p), zd_recv.at[slot, p])
                            add_into(total, inbox_of(slot, p))

                write_out(0, xs[0].at[k, 0])
                write_out(1, ys[1].at[k, 0])

    def write_out(a, total):
        if a != e_in:
            if acts_now[0]:
                outs[a][...] = total[...].astype(F32).reshape(outs[a].shape)
            return
        for j, x in enumerate(at.other_x()):
            send(total.at[pl.ds(x * panels, panels)], ex_in.at[nx - 2 - j], ex_send.at[j], ex_recv.at[nx - 2 - j], x=x)

    def finish_expert_in():
        for j in range(nx - 1):
            arrive(ex_in.at[j], ex_recv.at[j])
        total = cores[e_in].at[nz - 1]
        for x in range(nx):
            for u in range(panels):
                value = None
                for j, other in enumerate(at.other_x()):
                    value = ex_in[j, u] if value is None else jnp.where(other == x, ex_in[j, u], value)
                mine = total[pl.ds(at.x * panels + u, 1)][0]
                value = jnp.where(at.x == x, mine.astype(F32), value.astype(F32))
                for i in range(width // columns):
                    z = u * (width // columns) + i
                    outs[e_in][:, (z * nx + x) * columns : (z * nx + x + 1) * columns] = value[:, i * columns : (i + 1) * columns]

    def line(kind, k):
        for a in kind:
            d = order_e[k]
            total = cores[a].at[k]
            for side in range(2):
                feeds = (at.z > 0) & (d >= at.z) if side == 0 else (at.z < nz - 1) & (d <= at.z)
                slot = d if side == 0 else jnp.where(d == at.z, nz, d)

                @pl.when(feeds)
                def _(a=a, slot=slot, total=total):
                    arrive(zs_[a].at[slot], z_recv.at[a, slot])
                    add(total, zs_[a].at[slot])

            def hop(to, a=a, total=total, d=d):
                slot = d if to > 0 else jnp.where(d == at.z - 1, nz, d)
                return remote(total, zs_[a].at[slot], z_send.at[a, k], z_recv.at[a, slot], z=at.z + to)

            start_when(d < at.z, functools.partial(hop, -1))
            start_when(d > at.z, functools.partial(hop, 1))

            if k == nz - 1:
                write_out(a, total)
            continue_waits(waits, hop, d, at)

    def start_act(i):
        for p in range(packs):
            for x in range(nx):
                send(act_rows((kc, k_)[i], p, x, 1 - at.c), act_core.at[i, p, x], sum_send.at[i, p, x],
                     sum_recv.at[i, p, x], c=1 - at.c)

    def core_act(i):
        for p in range(packs):
            for x in range(nx):
                arrive(act_core.at[i, p, x], sum_recv.at[i, p, x])
                add_into(act_core.at[i, p, x], act_rows((kc, k_)[i], p, x, at.c))
        for j, x in enumerate(at.other_x()):
            send(act_core.at[i, :, x], act_x.at[i, nx - 2 - j], sum_send.at[i, packs, j], sum_recv.at[i, packs, nx - 2 - j], x=x)

    def x_act(i):
        for j in range(nx - 1):
            arrive(act_x.at[i, j], sum_recv.at[i, packs, j])
        for p in range(packs):
            out = act_core[i, p, at.x].astype(F32)
            for j in range(nx - 1):
                out = out + act_x[i, j, p].astype(F32)
            if i == 0:
                grad_mem[pl.ds(p * tok, tok), :] = out
            else:
                gn[pl.ds(p * tok, tok), :] += out

    pair_sums = ((wide_sum, wide_in), (table_sum, table_in))
    stages = [("c", [1 - at.c]), ("y", at.other_y()), ("x", at.other_x())]

    def start_small(t):
        axis, peers = stages[t]
        base = [0, 1, ny][t]
        for i, (total, inbox) in enumerate(pair_sums):
            for j, peer in enumerate(peers):
                back = base + len(peers) - 1 - j
                send(total.at[t], inbox.at[back], small_send.at[i, base + j], small_recv.at[i, back], **{axis: peer})

    def end_small(t):
        axis, peers = stages[t]
        base = [0, 1, ny][t]
        for i, (total, inbox) in enumerate(pair_sums):
            out = total[t]
            for j in range(len(peers)):
                arrive(inbox.at[base + j], small_recv.at[i, base + j])
                out = out + inbox[base + j]
            total[t + 1] = out

    tail = ny + nx - 1

    def start_line():
        for i, (total, inbox) in enumerate(pair_sums):
            for j in range(1, nz):
                z = lax.rem(at.z + j, nz)
                send(total.at[3], inbox.at[tail + at.z], small_send.at[i, tail + j], small_recv.at[i, tail + at.z], z=z)

    def end_line():
        for i, (total, inbox) in enumerate(pair_sums):
            for j in range(1, nz):
                z = lax.rem(at.z + j, nz)
                arrive(inbox.at[tail + z], small_recv.at[i, tail + z])
            out = None
            for z in range(nz):
                term = jnp.where(at.z == z, total[3], inbox[tail + z])
                out = term if out is None else out + term
            if i == 0:
                sum_gains[...] = out[: sum_gains.shape[0]]
                sum_router[...] = out[sum_gains.shape[0] : sum_gains.shape[0] + experts]
            else:
                sum_table[...] = out[: sum_table.shape[0], : sum_table.shape[1]]

    dense_events(0)
    start_prep()
    at_planes(False, lambda: dense_events(1), False)
    at_planes(False, lambda: dense_events(2), False)
    at_planes(False, lambda: dense_events(3), False)
    side_x(0)
    at_planes(True, lambda: dense_events(1), True)
    expert_events(0, (e_out,))
    side_y(0)
    side_x(1)
    at_planes(True, lambda: dense_events(2), True)
    at_planes(True, lambda: dense_events(3), True)
    expert_events(0, (e_in,))
    send_acts()
    at_planes(False, lambda: expert_events(1, (e_out,)), False)
    side_y(1)
    prepare_bias(rel, table, bias, at.s, tok, group)
    prepare_masks(lengths, same, causal, at.s, tok, group)
    hot, dispatch = route_slots(route, experts, each // packs)
    load_g.wait()
    top = g_ref[...].astype(F32).reshape(packs * tok, width)
    side_x(2)
    side_x(3)
    at_planes(True, lambda: expert_events(1, (e_out,)), True)
    side_y(2)
    at_planes(False, lambda: expert_events(1, (e_in,)), False)
    side_y(3)
    slots_out[1] = by_slot(dispatch, g_ref[...].reshape(packs * tok, width))
    send_slots(1)
    at_planes(True, lambda: expert_events(1, (e_in,)), True)
    at_planes(False, lambda: expert_events(2, (e_out,)), False)
    at_planes(False, lambda: expert_events(3, (e_out,)), False)
    act_events()
    corner_events(0)
    at_planes(True, lambda: expert_events(2, (e_out,)), True)
    corner_events(1)
    first_norm()
    at_planes(False, lambda: expert_events(2, (e_in,)), False)
    corner_events(2)
    at_planes(False, lambda: expert_events(3, (e_in,)), False)
    for a in dense:
        for z in zs[: nz // 2]:
            for x in range(nx):
                for y in range(ny):
                    arrive(spot(a, z, x, 1 - at.c, y), spread_recv.at[a, z, x, y])
    corner_events(3)
    keys_and_values(at.z < nz // 2)
    for a in dense:
        for z in zs[nz // 2 :]:
            for x in range(nx):
                for y in range(ny):
                    arrive(spot(a, z, x, 1 - at.c, y), spread_recv.at[a, z, x, y])
    keys_and_values(at.z >= nz // 2)
    for j, y in enumerate(at.other_y()):
        here = slots_in.at[1, at.x, y]
        arrive(here, slot_recv.at[y_sem(1, j)])
        for i, x in enumerate(at.other_x()):
            slot_copy(False, here, here, x_sem(1, i, y), x_sem(1, nx - 2 - i, y), x=x)
    project(n1, w, 0, q)
    attend_pairs(q, k_, v, bias, causal, pr_self, mixed)
    add_product(h1, mixed, w, 6)
    rms_rows(h1, gains[1:2], n2, packs * tok)
    project(n2, w, 3, qc)
    attend_pairs(qc, kc, vc, None, same, pr_cross, cross_mixed)
    h2[...] = h1[...]
    add_product(h2, cross_mixed, w, 7)
    rms_rows(h2, gains[2:3], n3, packs * tok)
    slots_out[0] = by_slot(dispatch, n3[...])
    send_slots(0)
    at_planes(True, lambda: expert_events(3, (e_out,)), True)
    for j, y in enumerate(at.other_y()):
        here = slots_in.at[0, at.x, y]
        arrive(here, slot_recv.at[y_sem(0, j)])
        for i, x in enumerate(at.other_x()):
            slot_copy(False, here, here, x_sem(0, i, y), x_sem(0, nx - 2 - i, y), x=x)
    at_planes(True, lambda: expert_events(2, (e_in,)), True)
    at_planes(True, lambda: expert_events(3, (e_in,)), True)
    for a in experts_:
        for z in range(nz):
            arrive(pack_of(a, z, 1 - at.c), spread_recv.at[a, z, 0, 0])
    for t in range(2):
        for i, x in enumerate(at.other_x()):
            for y in range(ny):
                arrive(slots_in.at[t, x, y], slot_recv.at[x_sem(t, i, y)])
    here = slots_in[0].reshape(nx * count, width)
    g_here = slots_in[1].reshape(nx * count, width).astype(F32)
    mine, chances = chances_of(here, router_t, at.y)
    gate_here = jnp.sum(chances * mine, axis=1, keepdims=True)
    grad_here[...] = (gate_here * g_here).astype(BF)
    for u in range(panels):
        in_panel = jnp.concatenate([big[place + u] for place in places], axis=0)
        out_panel = big[pl.ds(bases[e_out] + u * row_units, row_units)].reshape(width, width)
        inner = jnp.dot(here, in_panel, preferred_element_type=F32)
        hidden, slope = gelu_both(inner)
        hid[u] = hidden.astype(BF)
        grad_hidden = lax.dot_general(grad_here[...], out_panel, (((1,), (1,)), ((), ())), preferred_element_type=F32)
        gin_[u] = (grad_hidden * slope).astype(BF)
        result = jnp.dot(hid[u], out_panel, preferred_element_type=F32).reshape(nx, ny, each, width)
        grad_slots = lax.dot_general(gin_[u], in_panel, (((1,), (1,)), ((), ())), preferred_element_type=F32)
        grad_slots = grad_slots.reshape(nx, ny, each, width)
        if u:
            slots_acc[0] += result
            slots_acc[1] += grad_slots
        else:
            slots_acc[0] = result
            slots_acc[1] = grad_slots
    grad_gate = jnp.sum(g_here * slots_acc[0].reshape(nx * count, width), axis=1, keepdims=True)
    grad_logits = grad_gate * chances * (mine - gate_here)
    extra_grad = 0.0
    for e in range(experts):
        extra_grad = extra_grad + grad_logits[:, e : e + 1] * router_t[e : e + 1, :].astype(F32)
    slots_acc[1] += extra_grad.reshape(nx, ny, each, width)
    for wait in waits:
        wait()
    waits.clear()
    for y in [*at.other_y(), at.y]:
        for j, x in enumerate(at.other_x()):
            ret_out[1, j, y] = slots_acc[1, x, y].astype(BF)
            slot_copy(True, ret_out.at[1, j, y], ret_in.at[1, nx - 2 - j, y], ret_sem(1, j, y), ret_sem(1, nx - 2 - j, y), x=x)
    for u in range(panels):
        grad = lax.dot_general(here, gin_[u], (((0,), (0,)), ((), ())), preferred_element_type=F32).astype(BF)
        for i, place in enumerate(places):
            ge[place + u] = grad[i * unit : (i + 1) * unit]
    for k in range(nz):
        start_expert(e_in, k)
    router_grad = lax.dot_general(
        grad_logits, here.astype(F32), (((0,), (0,)), ((), ())), precision=HIGHEST, preferred_element_type=F32
    )
    for u in range(panels):
        grad = lax.dot_general(hid[u], grad_here[...], (((0,), (0,)), ((), ())), preferred_element_type=F32).astype(BF)
        ge[pl.ds(bases[e_out] + u * row_units, row_units)] = grad.reshape(row_units, unit, width)
    for k in range(nz):
        start_expert(e_out, k)
    for y in [*at.other_y(), at.y]:
        for j, x in enumerate(at.other_x()):
            ret_out[0, j, y] = slots_acc[0, x, y].astype(BF)
            slot_copy(True, ret_out.at[0, j, y], ret_in.at[0, nx - 2 - j, y], ret_sem(0, j, y), ret_sem(0, nx - 2 - j, y), x=x)
    core_expert(e_in, 0)
    at_planes(True, lambda: line((e_in,), 0), False)
    for wait in slot_waits:
        wait()
    for j, y in enumerate(at.other_y()):
        slots_out[1, y] = summed(1, y)
        slot_copy(True, slots_out.at[1, y], back_in.at[1, at.y], y_sem(3, j), y_sem(3, ny - 2 - j), y=y)
    core_expert(e_out, 0)
    core_expert(e_in, 1)
    core_expert(e_out, 1)
    back_in[1, at.y] = summed(1, at.y)
    core_expert(e_in, 3)
    core_expert(e_out, 2)
    core_expert(e_out, 3)
    at_planes(True, lambda: line((e_out,), 0), False)
    core_expert(e_in, 2)
    free_experts()
    for j, y in enumerate(at.other_y()):
        arrive(back_in.at[1, y], slot_recv.at[y_sem(3, j)])
    diagonal[...] = jnp.zeros_like(diagonal)
    for i, (_, inbox) in enumerate(pair_sums):
        inbox[pl.ds(tail + at.z, 1)] = jnp.zeros_like(inbox[pl.ds(0, 1)])
    wide_sum[0] = jnp.zeros_like(wide_sum[0])
    wide_sum[0, pl.ds(3, experts), :] = router_grad
    gn[...] = jnp.dot(dispatch, back_in[1].reshape(count, width), preferred_element_type=F32)
    grad_x[...] = top
    norm_back_rows(h2, gains[2:3], gn, grad_x, gain_row)
    wide_sum[0, 2:3, :] = gain_row[...]
    gb[...] = grad_x[...].astype(BF)
    product_t(gb, w, 7, ga)
    attend_pairs_back(qc, kc, vc, pr_cross, ga, gq, gk, gv, None)
    outer_product(n2, gq, big, 3)
    outer_product(mo, gk, big, 4)
    outer_product(mo, gv, big, 5)
    pl.semaphore_wait(free_sem, 1)
    start_dense(1, 0)
    for j, y in enumerate(at.other_y()):
        slots_out[0, y] = summed(0, y)
        slot_copy(True, slots_out.at[0, y], back_in.at[0, at.y], y_sem(2, j), y_sem(2, ny - 2 - j), y=y)
    at_planes(True, lambda: line((e_in,), 1), False)
    product_t(gq, w, 3, gn)
    norm_back_rows(h1, gains[1:2], gn, grad_x, gain_row)
    wide_sum[0, 1:2, :] = gain_row[...]
    back_in[0, at.y] = summed(0, at.y)
    outer_product(cross_mixed, gb, big, 7)
    start_dense(0, 1)
    first_dense(1, 0)
    start_dense(1, 1)
    gb[...] = grad_x[...].astype(BF)
    product_t(gb, w, 6, ga)
    outer_product(mixed, gb, big, 6)
    at_planes(True, lambda: line((e_out,), 1), False)
    first_dense(0, 1)
    start_dense(3, 1)
    at_planes(False, lambda: line((e_in,), 0), True)
    start_dense(0, 0)
    at_planes(False, lambda: line((e_out,), 0), True)
    start_dense(2, 1)
    two_products_t(gk, 4, gv, 5, w, kc)
    first_dense(1, 1)
    at_planes(True, lambda: line((e_out,), 2), False)
    first_dense(3, 1)
    attend_pairs_back(q, k_, v, pr_self, ga, gq, gk, gv, diagonal)
    second_dense(0, 1)
    first_dense(2, 1)
    first_dense(0, 0)
    start_act(0)
    at_planes(False, lambda: line((e_in,), 1), True)
    two_products_t(gk, 1, gv, 2, w, k_)
    at_planes(True, lambda: line((e_in,), 2), False)
    start_act(1)
    outer_product(n1, gq, big, 0)
    outer_product(n1_all, gk, big, 1)
    outer_product(n1_all, gv, big, 2)
    start_dense(2, 0)
    core_act(1)
    table_sum[0] = table_grad(rel, diagonal, at.s, tok, group)
    start_dense(3, 0)
    product_t(gq, w, 0, gn)
    for j, y in enumerate(at.other_y()):
        arrive(back_in.at[0, y], slot_recv.at[y_sem(2, j)])
    _, routing = chances_of(n3[...], router_t, at.y)
    gate = jnp.sum(routing * hot, axis=1, keepdims=True)
    combined = jnp.dot(dispatch, back_in[0].reshape(count, width), preferred_element_type=F32)
    rows_out = (h2[...] + gate * combined).astype(BF)
    for p in range(packs):
        out_rows[p] = rows_out[p * tok : (p + 1) * tok]
    at_planes(False, lambda: line((e_out,), 1), True)
    second_dense(3, 1)
    first_dense(2, 0)
    second_dense(2, 1)
    second_dense(0, 0)
    at_planes(False, lambda: line((e_in,), 2), True)
    x_act(1)
    h1[...] = x_keep[...].astype(F32)
    norm_back_rows(h1, gains[0:1], gn, grad_x, gain_row)
    wide_sum[0, 0:1, :] = gain_row[...]
    at_planes(True, lambda: line_dense(0, 1), False)
    core_act(0)
    second_dense(1, 0)
    at_planes(True, lambda: line_dense(0, 0), False)
    start_small(0)
    end_small(0)
    start_small(1)
    first_dense(3, 0)
    at_planes(False, lambda: line_dense(3, 1), False)
    at_planes(True, lambda: line_dense(3, 1), True)
    at_planes(False, lambda: line_dense(0, 0), True)
    second_dense(2, 0)
    at_planes(False, lambda: line_dense(0, 1), True)
    at_planes(True, lambda: line_dense(1, 0), False)
    at_planes(True, lambda: line((e_in,), 3), False)
    x_act(0)
    end_small(1)
    start_small(2)
    second_dense(1, 1)
    at_planes(False, lambda: line((e_in,), 3), True)
    at_planes(True, lambda: line_dense(2, 0), False)
    at_planes(False, lambda: line((e_out,), 2), True)
    at_planes(False, lambda: line_dense(1, 0), True)
    at_planes(True, lambda: line_dense(2, 1), False)
    at_planes(False, lambda: line_dense(2, 0), True)
    second_dense(3, 0)
    at_planes(False, lambda: line_dense(2, 1), True)
    at_planes(True, lambda: line_dense(3, 0), False)
    at_planes(True, lambda: line_dense(1, 1), False)
    end_small(2)
    start_line()
    at_planes(False, lambda: line_dense(1, 1), True)
    at_planes(False, lambda: line((e_out,), 3), False)
    at_planes(False, lambda: line_dense(3, 0), True)
    finish_expert_in()
    end_line()
    finish_dense()
    at_planes(True, lambda: line((e_out,), 3), True)
    for wait in waits:
        wait()


def shapes_of(layer_input, routes, attn_in, attn_out, expert_in, expert_out):
    nz, ns, ny = (lax.axis_size(a) for a in ("dp", "seq", "expert"))
    packs, tok, width = layer_input.shape[0], layer_input.shape[3], layer_input.shape[4]
    return nz, ns, ny, packs, tok, width


def fits_kernel(layer_input, routes, attn_in, attn_out, expert_in, expert_out):
    nz, ns, ny, packs, tok, width = shapes_of(layer_input, routes, attn_in, attn_out, expert_in, expert_out)
    unit, hidden = expert_in.shape[1:]
    capacity = (5 * tok + 4 * ny - 1) // (4 * ny)
    nx = ns // 2
    return (
        unit % 16 == 0
        and tok % 16 == 0
        and packs * capacity % 16 == 0
        and attn_in.shape[0] % unit == 0
        and attn_out.shape[0] % unit == 0
        and expert_out.shape[1] % (unit * nx) == 0
        and width % (2 * unit) == 0
        and hidden % (nx * width) == 0
        and width % (hidden // (nz * nx)) == 0
        and hidden // (nz * nx) % 128 == 0
        and expert_out.shape[1] * nz * ns == hidden
        and expert_out.shape[1] * width == hidden * unit
        and expert_in.shape[0] == 1
    )


def deliver_body(*refs):
    count = (len(refs) - 2) // 3
    came, gone = refs[-2:]
    copies = []
    for i in range(count):
        place = refs[2 * count + i]
        copies.append((
            pltpu.make_async_copy(refs[i], place, came.at[i]),
            pltpu.make_async_copy(place, refs[count + i], gone.at[i]),
        ))
    for first, _ in copies:
        first.start()
    for first, second in copies:
        first.wait()
        second.start()
    for _, second in copies:
        second.wait()


def deliver(arrays):
    any_ = pl.BlockSpec(memory_space=pl.ANY)
    count = len(arrays)
    return pl.pallas_call(
        deliver_body,
        out_shape=[jax.ShapeDtypeStruct(a.shape, a.dtype) for a in arrays],
        in_specs=[any_] * count,
        out_specs=[any_] * count,
        scratch_shapes=[
            *[pltpu.VMEM(a.shape, a.dtype) for a in arrays],
            pltpu.SemaphoreType.DMA((count,)),
            pltpu.SemaphoreType.DMA((count,)),
        ],
        name="deliver",
    )(*arrays)


def layer_kernel(layer_input, memory, cotangent, routes, doc_lengths, rel_buckets, gains, bias_table, router,
                 attn_in, attn_out, expert_in, expert_out):
    nz, ns, ny, packs, tok, width = shapes_of(layer_input, routes, attn_in, attn_out, expert_in, expert_out)
    nx = ns // 2
    group, pairs = ns * tok, width // 128
    unit = expert_in.shape[1]
    hidden = expert_in.shape[2]
    panels = hidden // width // nx
    pack_units = nx * panels
    experts, buckets = router.shape[1], bias_table.shape[0]
    each = packs * ((5 * tok + 4 * experts - 1) // (4 * experts))
    tall = nz * ns
    units = (attn_in.shape[0] // unit, attn_out.shape[0] // unit)
    total = tall * ny * (units[0] + units[1])
    grads = max(4 * nz * pack_units, total // 2)
    extra = -(-(3 + experts) // 8) * 8
    small = ny + nx - 1 + nz
    mine, every = packs * tok, packs * group
    any_ = pl.BlockSpec(memory_space=pl.ANY)
    vmem = pl.BlockSpec(memory_space=pltpu.VMEM)
    smem = pl.BlockSpec(memory_space=pltpu.SMEM)
    dma = pltpu.SemaphoreType.DMA
    low = lambda *shape: pltpu.VMEM(shape, BF)
    wide = lambda *shape: pltpu.VMEM(shape, F32)
    shape = lambda *dims: jax.ShapeDtypeStruct(dims, F32)
    results = pl.pallas_call(
        layer_body,
        out_shape=[
            jax.ShapeDtypeStruct((packs, tok, width), BF),
            shape(*attn_in.shape),
            shape(*attn_out.shape),
            shape(*expert_in.shape[1:]),
            shape(*expert_out.shape[1:]),
            shape(mine, width),
            shape(mine, width),
            shape(3, width),
            shape(experts, width),
            shape(2 * pairs, buckets),
        ],
        in_specs=[smem, *[vmem] * 5, *[any_] * 7],
        out_specs=[vmem] * 10,
        scratch_shapes=[
            low(total, unit, width),
            low(total, unit, width),
            low(grads, unit, width),
            low(nx, panels, unit, width),
            *[low(nz, pack_units, unit, width)] * 2,
            low(nz, ny - 1, nx, units[0], unit, width),
            low(nz, ny - 1, units[1], unit, width),
            low(nz, nx - 1, units[0], unit, width),
            low(nz, nx - 1, ny * units[1], unit, width),
            low(nx - 1, panels, unit, width),
            *[low(nz + 1, u, unit, width) for u in (*units, pack_units, pack_units)],
            *[low(every, width)] * 8,
            *[low(mine, width)] * 10,
            *[low(packs, pairs, 2 * tok, group)] * 2,
            *[wide(mine, width)] * 3,
            wide(pairs, 2 * tok, group),
            wide(packs, tok, group),
            wide(packs, tok, group),
            wide(16, group + 128),
            wide(1, width),
            low(2, packs, nx, tok, width),
            low(2, nx - 1, packs, tok, width),
            wide(4, extra, width),
            wide(4, 16, 128),
            wide(small, extra, width),
            wide(small, 16, 128),
            low(2, ny, each, width),
            low(2, nx, ny, each, width),
            wide(2, nx, ny, each, width),
            low(2, nx - 1, ny, each, width),
            low(2, nx - 1, ny, each, width),
            low(2, ny, each, width),
            low(nx * ny * each, width),
            low(panels, nx * ny * each, width),
            low(panels, nx * ny * each, width),
            dma((2, packs, 2 * nx)),
            dma((2, packs, nx, 2)),
            dma((nx - 1,)),
            dma((nx,)),
            dma((4, nz, 2)),
            dma((2, nz, nx - 1 + ny - 1 + max((ny - 1) * nx, (nx - 1) * ny))),
            dma((4, nz, nx, ny)),
            dma((4, nz, nx, ny)),
            dma((4, nz, nx, ny)),
            dma((6, packs)),
            dma((4, nz, nx)),
            dma((4, nz, nx)),
            dma((nz, ny - 1, nx + 1, units[0])),
            dma((nz, ny - 1, nx + 1, units[0])),
            dma((nz, nx - 1, units[0] + 1)),
            dma((nz, nx - 1, units[0] + 1)),
            dma((nx - 1,)),
            dma((nx - 1,)),
            dma((4, nz)),
            dma((4, nz + 1)),
            dma((nz, units[0] + 1)),
            dma((nz + 1, units[0] + 1)),
            dma((2, packs + 1, nx)),
            dma((2, packs + 1, nx)),
            dma((2, small)),
            dma((2, small)),
            dma((4 * (ny - 1) + 4 * (nx - 1) * ny,)),
            dma((4 * (ny - 1) + 4 * (nx - 1) * ny,)),
            pltpu.SemaphoreType.REGULAR,
            low(packs, tok, width),
            low(unit, hidden),
            low(mine, width),
            dma((2,)),
        ],
        compiler_params=pltpu.CompilerParams(
            collective_id=0, has_side_effects=True, vmem_limit_bytes=64 * 2**20
        ),
        name="layer",
    )(
        doc_lengths[:, 0, 0],
        rel_buckets.reshape(1, -1),
        gains,
        bias_table.T,
        router.T,
        routes.reshape(packs, 1, tok),
        layer_input[:, 0, 0],
        memory[:, 0, 0],
        cotangent[:, 0, 0],
        attn_in.reshape(units[0], unit, width),
        attn_out.reshape(units[1], unit, width),
        expert_in[0],
        expert_out.reshape(pack_units, unit, width),
    )
    out_rows, g0, g1, g2, g3, grad_x, grad_mem, gains_sum, router_sum, table_sum = deliver(results)
    spread = (packs, 1, 1, tok, width)
    return (
        out_rows.reshape(spread),
        grad_x.reshape(spread),
        grad_mem.reshape(spread),
        gains_sum,
        table_sum.T,
        router_sum.T,
        g0,
        g1,
        g2[None],
        g3[None],
    )


def norm_apply(value, gain):
    return value * lax.rsqrt(jnp.mean(value * value, axis=-1, keepdims=True) + EPS) * gain


def norm_back(value, gain, grad):
    r = lax.rsqrt(jnp.mean(value * value, axis=-1, keepdims=True) + EPS)
    scaled = grad * gain
    back = r * scaled - value * (r * r * r) * jnp.mean(scaled * value, axis=-1, keepdims=True)
    return back, jnp.sum(grad * value * r, axis=0)


def gelu_tanh(value):
    return jax.nn.gelu(value, approximate=True)


def times(left, right):
    return jnp.dot(left, right, preferred_element_type=F32)


def times_right(left, right):
    return jnp.einsum("te,de->td", left, right, preferred_element_type=F32)


def times_left(left, right):
    return jnp.einsum("td,te->de", left, right, preferred_element_type=F32)


def split(a, packs):
    return a.reshape(packs, -1, HEADS, HEAD)


def attend(query, keys, values, allowed, bias, packs):
    scores = jnp.einsum("pqhd,pkhd->phqk", split(query, packs), split(keys, packs), preferred_element_type=F32)
    masked = jnp.where(allowed[:, None], scores * HEAD**-0.5 + bias, NEG)
    raised = jnp.exp(masked - jnp.max(masked, axis=3, keepdims=True))
    chances = raised / jnp.sum(raised, axis=3, keepdims=True)
    mixed = jnp.einsum("phqk,pkhd->pqhd", chances.astype(BF), split(values, packs), preferred_element_type=F32)
    return mixed.reshape(query.shape).astype(BF), chances


def attend_back(query, keys, values, chances, grad, packs):
    scale = HEAD**-0.5
    g4 = split(grad, packs)
    grad_chances = jnp.einsum("pqhd,pkhd->phqk", g4, split(values, packs), preferred_element_type=F32)
    spread_ = jnp.sum(chances * grad_chances, axis=3, keepdims=True)
    grad_scores = (chances * (grad_chances - spread_)).astype(BF)
    grad_query = jnp.einsum("phqk,pkhd->pqhd", grad_scores, split(keys, packs), preferred_element_type=F32) * scale
    grad_keys = jnp.einsum("phqk,pqhd->pkhd", grad_scores, split(query, packs), preferred_element_type=F32) * scale
    grad_values = jnp.einsum("phqk,pqhd->pkhd", chances.astype(BF), g4, preferred_element_type=F32)
    return (
        grad_query.reshape(query.shape).astype(BF),
        grad_keys.reshape(keys.shape).astype(BF),
        grad_values.reshape(keys.shape).astype(BF),
        grad_scores,
    )


def per_device(layer_input, memory, cotangent, routes, doc_lengths, rel_buckets, gains, bias_table, router,
               attn_in, attn_out, expert_in, expert_out):
    packs, rows, width = layer_input.shape[0], layer_input.shape[3], layer_input.shape[4]
    seqs = lax.axis_size("seq")
    group = rows * seqs
    experts = router.shape[1]
    capacity = (5 * rows + 4 * experts - 1) // (4 * experts)
    buckets = bias_table.shape[0]
    rank = lax.axis_index("seq")

    x_in, m_in, e_in, e_out = layer_input[:, 0, 0], memory[:, 0, 0], expert_in[0], expert_out[0]
    if fits_kernel(layer_input, routes, attn_in, attn_out, expert_in, expert_out):
        return layer_kernel(layer_input, memory, cotangent, routes, doc_lengths, rel_buckets, gains, bias_table, router,
                            attn_in, attn_out, expert_in, expert_out)
    x_rows = x_in.reshape(packs * rows, width).astype(F32)
    everywhere, peers = ("dp", "seq", "expert"), ("dp", "seq")
    x_all, m_all = (lax.all_gather(a, "seq", axis=1, tiled=True) for a in (x_in, m_in))
    w_in, w_out = (lax.all_gather(a, everywhere, axis=0, tiled=True) for a in (attn_in, attn_out))
    e_in, e_out = (lax.all_gather(a, peers, axis=0, tiled=True) for a in (e_in, e_out))
    w_in = w_in.reshape(6, width, width)
    w_out = w_out.reshape(2, width, width)
    x_all = x_all.reshape(packs * group, width)
    m_all = m_all.reshape(packs * group, width)
    wide = group + rows
    query_pos = rank * rows + jnp.arange(rows, dtype=jnp.int32)
    key_pos = jnp.arange(group, dtype=jnp.int32)
    ends = jnp.cumsum(doc_lengths[:, 0, 0], axis=1)
    query_doc = jnp.sum((query_pos[None, :, None] >= ends[:, None, :]).astype(jnp.int32), axis=2)
    key_doc = jnp.sum((key_pos[None, :, None] >= ends[:, None, :]).astype(jnp.int32), axis=2)
    same = query_doc[:, :, None] == key_doc[:, None, :]
    causal = same & (key_pos[None, None, :] <= query_pos[None, :, None])
    bucket_hot = (rel_buckets[:, None] == jnp.arange(buckets, dtype=jnp.int32)).astype(F32)
    line_at = jnp.arange(group + rows, dtype=jnp.int32) - (group - 1) + rank * rows
    line_hot = (jnp.take(rel_buckets, jnp.clip(line_at, 0, group - 1))[None, :] == jnp.arange(buckets)[:, None]).astype(F32)
    line = jnp.einsum("bh,bj->hj", bias_table, line_hot, precision=HIGHEST)
    line = line[:, ::-1]
    wide = group + rows
    tiled = jnp.broadcast_to(line[:, None, :], (HEADS, rows, wide)).reshape(HEADS, rows * wide)
    skew = tiled[:, rows : rows + rows * (wide - 1)].reshape(HEADS, rows, wide - 1)[:, :, :group]

    normed1_all = norm_apply(x_all.astype(F32), gains[0]).astype(BF)
    normed1 = norm_apply(x_rows, gains[0]).astype(BF)
    query = times(normed1, w_in[0]).astype(BF)
    keys = times(normed1_all, w_in[1]).astype(BF)
    values = times(normed1_all, w_in[2]).astype(BF)
    mem_keys = times(m_all, w_in[4]).astype(BF)
    mem_values = times(m_all, w_in[5]).astype(BF)
    mixed, chances_self = attend(query, keys, values, causal, skew[None], packs)
    hidden1 = x_rows + times(mixed, w_out[0])
    normed2 = norm_apply(hidden1, gains[1]).astype(BF)
    cross_query = times(normed2, w_in[3]).astype(BF)
    cross_mixed, chances_cross = attend(cross_query, mem_keys, mem_values, same, 0.0, packs)
    hidden2 = hidden1 + times(cross_mixed, w_out[1])
    normed3 = norm_apply(hidden2, gains[2]).astype(BF)

    routing = jax.nn.softmax(times(normed3, router), axis=1)
    route = routes[:, 0, 0, :, 0]
    route_hot = (route[:, :, None] == jnp.arange(experts, dtype=jnp.int32)).astype(jnp.int32)
    slot = jnp.sum((jnp.cumsum(route_hot, axis=1) - route_hot) * route_hot, axis=2)
    hot = route_hot.reshape(packs * rows, experts).astype(F32)
    gate = jnp.sum(routing * hot, axis=1)
    target = jnp.where(slot < capacity, (route * packs + jnp.arange(packs)[:, None]) * capacity + slot, -1).reshape(-1)
    dispatch = (target[:, None] == jnp.arange(experts * packs * capacity, dtype=jnp.int32)).astype(BF)

    def swap(a):
        shape = (experts, packs * capacity, width)
        return lax.all_to_all(a.reshape(shape), "expert", split_axis=0, concat_axis=0, tiled=True).reshape(-1, width)

    received = swap(times_left(dispatch, normed3).astype(BF))
    inner = times(received, e_in)
    hidden, pull = jax.vjp(gelu_tanh, inner)
    hidden = hidden.astype(BF)
    result = times(hidden, e_out).astype(BF)
    combined = times(dispatch, swap(result))
    out_rows = (hidden2 + gate[:, None] * combined).astype(BF)
    grad_top = cotangent.reshape(packs * rows, width).astype(F32)
    grad_gate = jnp.sum(grad_top * combined, axis=1)
    grad_result = swap(times_left(dispatch, (gate[:, None] * grad_top).astype(BF)).astype(BF))
    grad_hidden = times_right(grad_result, e_out)
    grad_eout = times_left(hidden, grad_result).astype(BF)
    grad_inner = pull(grad_hidden)[0].astype(BF)
    grad_ein = times_left(received, grad_inner).astype(BF)
    grad_send = swap(times_right(grad_inner, e_in).astype(BF))
    grad_logits = grad_gate[:, None] * routing * (hot - gate[:, None])
    grad_router = jnp.einsum("td,te->de", normed3.astype(F32), grad_logits, precision=HIGHEST)
    grad_normed3 = times(dispatch, grad_send) + jnp.einsum(
        "te,de->td", grad_logits, router.astype(F32), precision=HIGHEST
    )
    back3, gain3 = norm_back(hidden2, gains[2], grad_normed3)
    grad_h2 = grad_top + back3
    grad_h2_low = grad_h2.astype(BF)
    grad_wco = times_left(cross_mixed, grad_h2_low)
    grad_cross = times_right(grad_h2_low, w_out[1]).astype(BF)
    grad_cq, grad_ck, grad_cv, _ = attend_back(cross_query, mem_keys, mem_values, chances_cross, grad_cross, packs)
    back2, gain2 = norm_back(hidden1, gains[1], times_right(grad_cq, w_in[3]))
    grad_h1 = grad_h2 + back2
    grad_h1_low = grad_h1.astype(BF)
    grad_wso = times_left(mixed, grad_h1_low)
    grad_mixed = times_right(grad_h1_low, w_out[0]).astype(BF)
    grad_q, grad_k, grad_v, grad_scores = attend_back(query, keys, values, chances_self, grad_mixed, packs)

    total = jnp.sum(grad_scores.astype(F32), axis=0)[:, ::-1]
    padded = jnp.pad(total, ((0, 0), (0, 0), (0, wide - group))).reshape(HEADS, rows * wide)
    diagonal = padded[:, : rows * (wide - 1)].reshape(HEADS, rows, wide - 1).sum(axis=1)
    at = jnp.clip(rank * rows + (rows - 1) - jnp.arange(wide - 1, dtype=jnp.int32), 0, group - 1)
    diagonal_hot = (jnp.take(rel_buckets, at)[:, None] == jnp.arange(buckets)).astype(F32)
    grad_table = jnp.einsum("jb,hj->bh", diagonal_hot, diagonal, precision=HIGHEST)

    def to_owner(a):
        return lax.psum_scatter(a.reshape(packs, group, width), "seq", scatter_dimension=1, tiled=True)

    grad_memory = to_owner((times_right(grad_ck, w_in[4]) + times_right(grad_cv, w_in[5])).astype(BF))
    part1 = to_owner((times_right(grad_k, w_in[1]) + times_right(grad_v, w_in[2])).astype(BF))
    grad_normed1 = times_right(grad_q, w_in[0]) + part1.reshape(packs * rows, width).astype(F32)
    back1, gain1 = norm_back(x_rows, gains[0], grad_normed1)
    grad_x = grad_h1 + back1
    grad_in = jnp.concatenate(
        [
            times_left(normed1, grad_q),
            times_left(normed1_all, grad_k),
            times_left(normed1_all, grad_v),
            times_left(normed2, grad_cq),
            times_left(m_all, grad_ck),
            times_left(m_all, grad_cv),
        ]
    ).astype(BF)
    grad_out = jnp.concatenate([grad_wso, grad_wco]).astype(BF)
    shards = [
        lax.psum_scatter(a, over, scatter_dimension=0, tiled=True).astype(F32)
        for a, over in ((grad_in, everywhere), (grad_out, everywhere), (grad_ein, peers), (grad_eout, peers))
    ]
    small = lax.psum((jnp.stack([gain1, gain2, gain3]), grad_table, grad_router), ("dp", "seq", "expert"))
    shape = (packs, 1, 1, rows, width)
    return (
        out_rows.reshape(shape),
        grad_x.reshape(shape),
        grad_memory.astype(F32).reshape(shape),
        *small,
        shards[0],
        shards[1],
        shards[2][None],
        shards[3][None],
    )


def solution(mesh):
    tokens = P(None, "dp", "expert", "seq", None)
    dense = P(("dp", "seq", "expert"), None)
    expert = P("expert", ("dp", "seq"), None)
    return jax.shard_map(
        per_device,
        mesh=mesh,
        in_specs=(tokens, tokens, tokens, tokens, P(None, "dp", "expert", None), P(), P(), P(), P(),
                  dense, dense, expert, expert),
        out_specs=(tokens, tokens, tokens, P(), P(), P(), dense, dense, expert, expert),
        check_vma=False,
    )
```

```python
import functools

import jax
import jax.numpy as jnp
from jax import lax
from jax.experimental import pallas as pl
from jax.experimental.pallas import tpu as pltpu
from jax.sharding import PartitionSpec as P

HEADS = 12
HEAD = 64

EPS = 1e-06
NEG = -1e30
HIGHEST = lax.Precision.HIGHEST
MESH = pl.DeviceIdType.MESH
BF = jnp.bfloat16
F32 = jnp.float32


class Place:
    def __init__(self):
        self.nz, self.ns, self.ny = (lax.axis_size(a) for a in ("dp", "seq", "expert"))
        self.nx = self.ns // 2
        self.z, self.s, self.y = (lax.axis_index(a) for a in ("dp", "seq", "expert"))
        self.x, self.c = self.s // 2, lax.rem(self.s, 2)

    def device(self, z=None, x=None, c=None, y=None):
        z = self.z if z is None else z
        x = self.x if x is None else x
        c = self.c if c is None else c
        y = self.y if y is None else y
        return (z, x * 2 + c, y)

    def other_x(self):
        return [lax.rem(self.x + k, self.nx) for k in range(1, self.nx)]

    def other_y(self):
        return [lax.rem(self.y + k, self.ny) for k in range(1, self.ny)]

    def by_distance(self, k):
        half = self.nz // 2
        order = [
            sorted(range(self.nz), key=lambda d: (abs(d - z), (d < half) != (z < half), d)) for z in range(self.nz)
        ]
        return self.pick([row[k] for row in order])

    def pick(self, values):
        out = jnp.int32(values[0])
        for z in range(1, self.nz):
            out = jnp.where(self.z == z, jnp.int32(values[z]), out)
        return out

    def greet(self):
        barrier = pltpu.get_barrier_semaphore()
        for x in self.other_x():
            pl.semaphore_signal(barrier, inc=1, device_id=self.device(x=x), device_id_type=MESH)
        for y in self.other_y():
            pl.semaphore_signal(barrier, inc=1, device_id=self.device(y=y), device_id_type=MESH)
        pl.semaphore_signal(barrier, inc=1, device_id=self.device(c=1 - self.c), device_id_type=MESH)

        for k in range(1, self.nz):
            z = lax.rem(self.z + k, self.nz)
            pl.semaphore_signal(barrier, inc=1, device_id=self.device(z=z), device_id_type=MESH)
        pl.semaphore_wait(barrier, self.nx - 1 + self.ny - 1 + 1 + self.nz - 1)


def rms_rows(src, gain, dst, rows, step=64):
    @pl.loop(0, rows // step)
    def _(i):
        at = pl.ds(pl.multiple_of(i * step, step), step)
        value = src[at, :].astype(F32)
        r = lax.rsqrt(jnp.mean(value * value, axis=-1, keepdims=True) + EPS)
        dst[at, :] = (value * r * gain).astype(BF)


def block(weight, index, lanes=slice(None), share=(0, 1)):
    unit, width = weight.shape[-2:]
    count = width // unit // share[1]
    first = pl.multiple_of(index * (width // unit) + share[0] * count, count)
    value = weight[pl.ds(first, count), :, lanes]
    return value.reshape(count * unit, value.shape[-1])


def project(left, weight, index, dst):
    width = dst.shape[-1]
    step = 256 if width % 256 == 0 else width

    @pl.loop(0, width // step)
    def _(j):
        at = pl.ds(pl.multiple_of(j * step, step), step)
        dst[:, at] = jnp.dot(left[...], block(weight, index, at), preferred_element_type=F32).astype(dst.dtype)


def prepare_bias(rel, table, bias, rank, rows, group):
    heads, buckets = table.shape
    wide = group + 128
    lane = lax.broadcasted_iota(jnp.int32, (group, wide), 1)
    shift = jnp.where(lane < group, lane, lane - wide)
    distance = jnp.clip(rank * rows - shift, 0, group - 1)
    hot = (lax.broadcasted_iota(jnp.int32, (group, wide), 0) == distance).astype(F32).astype(BF)
    which = jnp.dot(jnp.broadcast_to(rel[...].astype(F32), (8, group)).astype(BF), hot, preferred_element_type=F32)
    picks = (lax.broadcasted_iota(jnp.int32, (buckets, wide), 0) == which[0:1].astype(jnp.int32)).astype(F32)
    line = jnp.dot(table[...], picks, precision=HIGHEST, preferred_element_type=F32)
    for h in range(heads):
        band = pltpu.roll(jnp.broadcast_to(line[h : h + 1], (rows, wide)), 0, 1, stride=1, stride_axis=0)
        bias[h // 2, pl.ds((h % 2) * rows, rows), :] = band[:, :group]


def prepare_masks(lengths, same, causal, rank, rows, group):
    key = lax.broadcasted_iota(jnp.int32, (rows, group), 1)
    query = rank * rows + lax.broadcasted_iota(jnp.int32, (rows, group), 0)
    for p in range(same.shape[0]):
        end = jnp.int32(0)
        kd = jnp.zeros((rows, group), jnp.int32)
        qd = jnp.zeros((rows, group), jnp.int32)
        for n in range(lengths.shape[1]):
            end = end + lengths[p, n]
            kd = kd + jnp.where(key >= end, 1, 0)
            qd = qd + jnp.where(query >= end, 1, 0)
        same[p] = jnp.where(kd == qd, 0.0, NEG)
        causal[p] = jnp.where((kd == qd) & (key <= query), 0.0, NEG)


def two_heads(pair):
    first = lax.broadcasted_iota(jnp.int32, pair.shape, 1) < HEAD
    zero = jnp.zeros_like(pair)
    return jnp.concatenate([jnp.where(first, pair, zero), jnp.where(first, zero, pair)], axis=0)


def one_pair(stacked):
    rows = stacked.shape[0] // 2
    first = lax.broadcasted_iota(jnp.int32, (rows, stacked.shape[1]), 1) < HEAD
    return jnp.where(first, stacked[:rows], stacked[rows:])


def attend_pairs(query, keys, values, bias, mask, chances, mixed):
    packs, pairs, double, group = chances.shape
    rows = double // 2

    def body(i, carry):
        p, j = i // pairs, lax.rem(i, pairs)
        mine = pl.ds(pl.multiple_of(p * rows, rows), rows)
        theirs = pl.ds(pl.multiple_of(p * group, group), group)
        lanes = pl.ds(pl.multiple_of(j * 128, 128), 128)
        scores = lax.dot_general(
            two_heads(query[mine, lanes]), keys[theirs, lanes], (((1,), (1,)), ((), ())), preferred_element_type=F32
        )
        scores = scores * HEAD**-0.5
        if bias is not None:
            scores = scores + bias[j]
        scores = (scores.reshape(2, rows, group) + mask[p][None]).reshape(double, group)
        raised = jnp.exp(scores - jnp.max(scores, axis=1, keepdims=True))
        weights = (raised * (1.0 / jnp.sum(raised, axis=1, keepdims=True))).astype(BF)
        chances[p, j] = weights
        out = jnp.dot(weights, values[theirs, lanes], preferred_element_type=F32)
        mixed[mine, lanes] = one_pair(out).astype(BF)
        return carry

    lax.fori_loop(0, packs * pairs, body, 0, unroll=12)


def add_product(total, left, weight, index):
    width = total.shape[-1]
    step = 256 if width % 256 == 0 else width

    @pl.loop(0, width // step)
    def _(j):
        at = pl.ds(pl.multiple_of(j * step, step), step)
        total[:, at] += jnp.dot(left[...], block(weight, index, at), preferred_element_type=F32)


def product_t(left, weight, index, dst):
    halves = 2
    step = weight.shape[-1] // halves

    @pl.loop(0, halves)
    def _(j):
        rows = block(weight, index, share=(j, halves))
        out = lax.dot_general(left[...], rows, (((1,), (1,)), ((), ())), preferred_element_type=F32)
        dst[:, pl.ds(pl.multiple_of(j * step, step), step)] = out.astype(dst.dtype)


def two_products_t(left1, index1, left2, index2, weight, dst):
    halves = 2
    step = weight.shape[-1] // halves

    @pl.loop(0, halves)
    def _(j):
        out = 0.0
        for left, index in ((left1, index1), (left2, index2)):
            rows = block(weight, index, share=(j, halves))
            out = out + lax.dot_general(left[...], rows, (((1,), (1,)), ((), ())), preferred_element_type=F32)
        dst[:, pl.ds(pl.multiple_of(j * step, step), step)] = out.astype(dst.dtype)


def outer_product(left, right, dst, index):
    unit, width = dst.shape[-2:]
    halves = 2
    step, count = width // halves, width // unit // halves

    @pl.loop(0, halves)
    def _(j):
        part = left[:, pl.ds(pl.multiple_of(j * step, step), step)]
        out = lax.dot_general(part, right[...], (((0,), (0,)), ((), ())), preferred_element_type=F32)
        first = index * (width // unit) + j * count
        dst[pl.ds(first, count)] = out.astype(dst.dtype).reshape(count, unit, width)


def add_into(total, other):
    lead = total.shape[:-2]
    count = 1
    for n in lead:
        count *= n
    rows = total.shape[-2]
    step = next(n for n in ((48, 32, 16) if total.shape[-1] <= 1024 else (16,)) if rows % n == 0)

    def body(i, carry):
        index = []
        rest = i // (rows // step)
        for n in reversed(lead):
            index.insert(0, lax.rem(rest, n))
            rest = rest // n
        r = pl.ds(pl.multiple_of(lax.rem(i, rows // step) * step, 16), step)
        at = (*index, r)
        total[at] = (total[at].astype(F32) + other[at].astype(F32)).astype(total.dtype)
        return carry

    lax.fori_loop(0, count * (rows // step), body, 0, unroll=min(count * (rows // step), 4))


def norm_back_rows(value, gain, grad, total, gain_grad, step=64):
    gain_grad[...] = jnp.zeros_like(gain_grad)

    @pl.loop(0, value.shape[0] // step)
    def _(i):
        at = pl.ds(pl.multiple_of(i * step, step), step)
        v, g = value[at, :].astype(F32), grad[at, :]
        r = lax.rsqrt(jnp.mean(v * v, axis=-1, keepdims=True) + EPS)
        scaled = g * gain
        total[at, :] += r * scaled - v * (r * r * r) * jnp.mean(scaled * v, axis=-1, keepdims=True)
        gain_grad[...] += jnp.sum(g * v * r, axis=0, keepdims=True)


def attend_pairs_back(query, keys, values, chances, grad, grad_q, grad_k, grad_v, diagonal):
    packs, pairs, double, group = chances.shape
    rows = double // 2
    scale = HEAD**-0.5

    def body(i, carry):
        p, j = i // pairs, lax.rem(i, pairs)
        mine = pl.ds(pl.multiple_of(p * rows, rows), rows)
        theirs = pl.ds(pl.multiple_of(p * group, group), group)
        lanes = pl.ds(pl.multiple_of(j * 128, 128), 128)
        ga = two_heads(grad[mine, lanes])
        low = chances[p, j]
        wide = low.astype(F32)
        gp = lax.dot_general(ga, values[theirs, lanes], (((1,), (1,)), ((), ())), preferred_element_type=F32)
        gs = (wide * (gp - jnp.sum(wide * gp, axis=1, keepdims=True))).astype(BF)
        gq = jnp.dot(gs, keys[theirs, lanes], preferred_element_type=F32)
        grad_q[mine, lanes] = (one_pair(gq) * scale).astype(BF)
        gk = lax.dot_general(gs, two_heads(query[mine, lanes]), (((0,), (0,)), ((), ())), preferred_element_type=F32)
        grad_k[theirs, lanes] = (gk * scale).astype(BF)
        gv = lax.dot_general(low, ga, (((0,), (0,)), ((), ())), preferred_element_type=F32)
        grad_v[theirs, lanes] = gv.astype(BF)
        if diagonal is not None:
            a = lax.broadcasted_iota(jnp.int32, (rows, rows), 0)
            b = lax.broadcasted_iota(jnp.int32, (rows, rows), 1)
            flip = (a + b == rows - 1).astype(F32).astype(BF)
            for half in range(2):
                turned = jnp.dot(flip, gs[half * rows : (half + 1) * rows], preferred_element_type=F32)
                turned = jnp.concatenate([turned, jnp.zeros((rows, 128), F32)], axis=1)
                band = pltpu.roll(turned, 0, 1, stride=1, stride_axis=0)
                diagonal[pl.ds(2 * j + half, 1), :] += jnp.sum(band, axis=0, keepdims=True)
        return carry

    lax.fori_loop(0, packs * pairs, body, 0, unroll=12)


def table_grad(rel, diagonal, rank, rows, group):
    wide = group + 128
    lane = lax.broadcasted_iota(jnp.int32, (group, wide), 1)
    distance = jnp.clip(rank * rows + rows - 1 - lane, 0, group - 1)
    hot = (lax.broadcasted_iota(jnp.int32, (group, wide), 0) == distance).astype(F32).astype(BF)
    which = jnp.dot(jnp.broadcast_to(rel[...].astype(F32), (8, group)).astype(BF), hot, preferred_element_type=F32)
    picks = (lax.broadcasted_iota(jnp.int32, (128, wide), 0) == which[0:1].astype(jnp.int32)).astype(F32)
    return lax.dot_general(diagonal[...], picks, (((1,), (1,)), ((), ())), precision=HIGHEST, preferred_element_type=F32)


def route_slots(route, experts, capacity):
    packs, _, rows = route.shape
    count = packs * rows
    same = lax.broadcasted_iota(jnp.int32, (rows, rows), 0) == lax.broadcasted_iota(jnp.int32, (rows, rows), 1)
    column = jnp.concatenate(
        [jnp.sum(jnp.where(same, route[p], 0), axis=1, keepdims=True) for p in range(packs)], axis=0
    )
    hot = (column == lax.broadcasted_iota(jnp.int32, (count, experts), 1)).astype(F32)
    a = lax.broadcasted_iota(jnp.int32, (count, count), 0)
    b = lax.broadcasted_iota(jnp.int32, (count, count), 1)
    earlier = ((b < a) & (a // rows == b // rows)).astype(F32).astype(BF)
    before = jnp.dot(earlier, hot.astype(BF), preferred_element_type=F32)
    slot = jnp.sum(before * hot, axis=1, keepdims=True).astype(jnp.int32)
    pack = lax.broadcasted_iota(jnp.int32, (count, 1), 0) // rows
    target = jnp.where(slot < capacity, (column * packs + pack) * capacity + slot, -1)
    slots = lax.broadcasted_iota(jnp.int32, (count, experts * packs * capacity), 1)
    return hot, (target == slots).astype(F32).astype(BF)


def chances_of(rows, router_t, own):
    logits = lax.dot_general(rows, router_t[...], (((1,), (1,)), ((), ())), preferred_element_type=F32)
    raised = jnp.exp(logits - jnp.max(logits, axis=1, keepdims=True))
    mine = (lax.broadcasted_iota(jnp.int32, (1, logits.shape[1]), 1) == own).astype(F32)
    return mine, raised / jnp.sum(raised, axis=1, keepdims=True)


def gelu_both(z):
    c = 0.7978845608028654
    t = jnp.tanh(c * (z + 0.044715 * (z * z * z)))
    half = 0.5 * (1.0 + t)
    slope = half + 0.5 * z * (1.0 - t * t) * (c * (1.0 + 3 * 0.044715 * (z * z)))
    return z * half, slope


def continue_waits(waits, hop, d, at):
    def wait():
        @pl.when(d < at.z)
        def _():
            hop(-1).wait_send()

        @pl.when(d > at.z)
        def _():
            hop(1).wait_send()

    waits.append(wait)


def layer_body(lengths, rel, gains, table, router_t, route, x_ref, m_ref, g_hbm, ain, aout, ein_hbm, eout,
               out_rows, o0, o1, o2, o3, grad_x, grad_mem, sum_gains, sum_router, sum_table,
               w, big, ge, prep, c2, c3, y0, y1, x0, x1, ex_in, z0, z1, z2, z3,
               xo, mo, n1_all, k_, v, kc, vc, gv, n1, q, mixed, n2, qc, cross_mixed, n3, gb, ga, gq,
               pr_self, pr_cross, h1, h2, gn, bias, same, causal, diagonal, gain_row,
               act_core, act_x, wide_sum, table_sum, wide_in, table_in,
               slots_out, slots_in, slots_acc, ret_out, ret_in, back_in, grad_here, hid, gin_,
               act_send, act_recv, prep_send, prep_recv, line_send, side_send, spread_send, ici_recv, spread_recv, own_sem,
               core_send, core_recv, y_send, y_recv, x_send, x_recv, ex_send, ex_recv, z_send, z_recv, zd_send, zd_recv,
               sum_send, sum_recv, small_send, small_recv, slot_send, slot_recv, free_sem, g_ref, ein, x_keep, load_sem):
    at = Place()
    nz, nx, ny = at.nz, at.nx, at.ny
    packs, tok, width = x_ref.shape
    group = xo.shape[0] // packs
    experts = router_t.shape[0]
    unit = ain.shape[1]
    block_units = eout.shape[0]
    panels = block_units // nx
    columns = ein.shape[1] // (nz * nx)
    buckets = table.shape[1]
    gk = xo
    units = (ain.shape[0], aout.shape[0])
    tall = nz * nx * 2
    bases = (0, tall * ny * units[0], 0, 2 * nz * block_units)
    dense, e_in, e_out = (0, 1), 2, 3
    experts_ = (e_in, e_out)
    waits = []

    def remote(src, dst, ssem, rsem, **where):
        return pltpu.make_async_remote_copy(
            src_ref=src, dst_ref=dst, send_sem=ssem, recv_sem=rsem,
            device_id=at.device(**where), device_id_type=MESH,
        )

    def send(*args, **where):
        one = remote(*args, **where)
        if acts_now[0]:
            one.start()
        waits.append(one.wait_send)

    acts_now = [True]

    def at_planes(ends, step, last):
        between = (at.z > 0) & (at.z < nz - 1)
        mark = len(waits)

        @pl.when(jnp.logical_not(between) if ends else between)
        def _():
            step()

        del waits[mark:]
        if last:
            acts_now[0] = False
            step()
            acts_now[0] = True

    def add(total, other):
        if acts_now[0]:
            add_into(total, other)

    def start_when(pred, make):
        if acts_now[0]:

            @pl.when(pred)
            def _():
                make().start()

    def arrive(ref, sem):
        if acts_now[0]:
            pltpu.make_async_copy(ref, ref, sem).wait()

    def spot(a, z, x, c, y):
        index = ((z * nx + x) * 2 + c) * ny + y
        return w.at[pl.ds(bases[a] + index * units[a], units[a])]

    def pack_of(a, z, c):
        return big.at[pl.ds(bases[a] + (z * 2 + c) * block_units, block_units)]

    shards = (ain, aout)
    acts = ((x_ref, xo), (m_ref, mo))

    load_g = pltpu.make_async_copy(g_hbm, g_ref, load_sem.at[0])
    load_e = pltpu.make_async_copy(ein_hbm, ein, load_sem.at[1])
    load_g.start()
    load_e.start()
    at.greet()

    def act_rows(full, p, x, c):
        return full.at[pl.ds(pl.multiple_of(p * group + (x * 2 + c) * tok, 16), tok)]

    own_waits = []

    def send_acts():
        for i, (src, full) in enumerate(acts):
            for p in range(packs):
                dst = act_rows(full, p, at.x, at.c)
                for k, x in enumerate(at.other_x()):
                    send(src.at[p], dst, act_send.at[i, p, k], act_recv.at[i, p, at.x, at.c], x=x)
                send(src.at[p], dst, act_send.at[i, p, nx - 1 + at.x], act_recv.at[i, p, at.x, at.c], c=1 - at.c)
                own = pltpu.make_async_copy(src.at[p], dst, own_sem.at[4 + i, p])
                own.start()
                own_waits.append(own.wait)

    def along_line(a, z, src):
        dst = spot(a, z, at.x, at.c, at.y) if a in dense else pack_of(a, z, at.c)
        sem = ici_recv.at[a, z, at.x, at.y]
        left = (z >= at.z) & (at.z > 0)
        right = (z <= at.z) & (at.z < nz - 1)

        def one(side):
            return remote(src, dst, line_send.at[a, z, side], sem, z=at.z + 2 * side - 1)

        start_when(left, lambda: one(0))
        start_when(right, lambda: one(1))

        def wait():
            @pl.when(left)
            def _():
                one(0).wait_send()

            @pl.when(right)
            def _():
                one(1).wait_send()

        waits.append(wait)

    def to_core(a, z, x, y, src):
        dst = spot(a, z, x, at.c, y) if a in dense else pack_of(a, z, at.c)
        send(src, dst, spread_send.at[a, z, x, y], spread_recv.at[a, z, x, y], c=1 - at.c)

    zs = [at.by_distance(k) for k in range(nz)]

    def dense_events(k):
        z = zs[k]
        for a in dense:
            here = spot(a, z, at.x, at.c, at.y)
            src = here if k else shards[a]
            if k:
                arrive(here, ici_recv.at[a, z, at.x, at.y])
            else:
                own = pltpu.make_async_copy(shards[a], here, own_sem.at[a, 0])
                own.start()
                own_waits.append(own.wait)
            along_line(a, z, src)
            for j, x in enumerate(at.other_x()):
                send(src, here, side_send.at[a, z, j], ici_recv.at[a, z, at.x, at.y], x=x)
            for j, y in enumerate(at.other_y()):
                send(src, here, side_send.at[a, z, nx - 1 + j], ici_recv.at[a, z, at.x, at.y], y=y)
            to_core(a, z, at.x, at.y, src)

    def side_y(k):
        z = zs[k]
        for y in at.other_y():
            for a in dense:
                here = spot(a, z, at.x, at.c, y)
                arrive(here, ici_recv.at[a, z, at.x, y])
                if a == 1:
                    for j, x in enumerate(at.other_x()):
                        send(here, here, side_send.at[a, z, nx - 1 + ny - 1 + j + (nx - 1) * y],
                             ici_recv.at[a, z, at.x, y], x=x)
                to_core(a, z, at.x, y, here)

    def side_x(k):
        z = zs[k]
        for x in at.other_x():
            for a in dense:
                here = spot(a, z, x, at.c, at.y)
                arrive(here, ici_recv.at[a, z, x, at.y])
                if a == 0:
                    for j, y in enumerate(at.other_y()):
                        send(here, here, side_send.at[a, z, nx - 1 + ny - 1 + j + (ny - 1) * x],
                             ici_recv.at[a, z, x, at.y], y=y)
                to_core(a, z, x, at.y, here)

    def corner_events(k):
        z = zs[k]
        for a in dense:
            for y in at.other_y():
                for x in at.other_x():
                    here = spot(a, z, x, at.c, y)
                    arrive(here, ici_recv.at[a, z, x, y])
                    to_core(a, z, x, y, here)

    def act_events():
        for i, (src, full) in enumerate(acts):
            for p in range(packs):
                for x in at.other_x():
                    dst = act_rows(full, p, x, at.c)
                    arrive(dst, act_recv.at[i, p, x, at.c])
                    send(dst, dst, act_send.at[i, p, nx - 1 + x], act_recv.at[i, p, x, at.c], c=1 - at.c)

    def in_unit(z, c, x, n=1):
        return pl.ds(bases[e_in] + ((z * 2 + c) * nx + x) * panels, n * panels)

    def start_prep():
        load_e.wait()
        for x in range(nx):
            for u in range(panels):
                each_z = width // columns
                prep[x, u] = jnp.concatenate(
                    [ein[:, (z * nx + x) * columns : (z * nx + x + 1) * columns] for z in range(u * each_z, (u + 1) * each_z)],
                    axis=1,
                )
        big[in_unit(at.z, at.c, at.x)] = prep[at.x]
        for j, x in enumerate(at.other_x()):
            send(prep.at[x], big.at[in_unit(at.z, at.c, at.x)], prep_send.at[j], prep_recv.at[at.x], x=x)

    def expert_events(k, kinds=experts_):
        z = zs[k]
        for a in kinds:
            here = pack_of(a, z, at.c)
            src = here
            if k:
                arrive(here, ici_recv.at[a, z, at.x, at.y])
            elif a == e_in:
                for x in at.other_x():
                    arrive(big.at[in_unit(at.z, at.c, x)], prep_recv.at[x])
            else:
                src = eout
                own = pltpu.make_async_copy(eout, here, own_sem.at[a, 0])
                own.start()
                own_waits.append(own.wait)
            along_line(a, z, src)
            to_core(a, z, 0, 0, src)

    def first_norm():
        for i, (src, full) in enumerate(acts):
            for p in range(packs):
                for x in range(nx):
                    arrive(act_rows(full, p, x, 1 - at.c), act_recv.at[i, p, x, 1 - at.c])
        for wait in own_waits:
            wait()
        rms_rows(xo, gains[0:1], n1_all, packs * group)
        for p in range(packs):
            x_keep[pl.ds(p * tok, tok), :] = xo[pl.ds(pl.multiple_of(p * group + at.s * tok, tok), tok), :]
            n1[pl.ds(p * tok, tok), :] = n1_all[pl.ds(pl.multiple_of(p * group + at.s * tok, tok), tok), :]
        h1[...] = x_keep[...].astype(F32)

    places = [((z * 2 + c) * nx + x) * panels for z in range(nz) for x in range(nx) for c in range(2)]
    each = slots_out.shape[2]
    count = ny * each
    row_units = width // unit

    def keys_and_values(for_self):
        @pl.when(for_self)
        def _():
            project(n1_all, w, 1, k_)
            project(n1_all, w, 2, v)

        @pl.when(jnp.logical_not(for_self))
        def _():
            project(mo, w, 4, kc)
            project(mo, w, 5, vc)

    def by_slot(dispatch, rows):
        out = lax.dot_general(dispatch, rows, (((0,), (0,)), ((), ())), preferred_element_type=F32)
        return out.astype(BF).reshape(ny, each, width)

    slot_waits = []

    def slot_copy(late, src, dst, sem_from, sem_to, **where):
        one = remote(src, dst, slot_send.at[sem_from], slot_recv.at[sem_to], **where)
        one.start()
        (waits if late else slot_waits).append(one.wait_send)

    def y_sem(t, j):
        return t * (ny - 1) + j

    def x_sem(t, j, y):
        return 4 * (ny - 1) + (t * (nx - 1) + j) * ny + y

    def ret_sem(t, j, y):
        return 4 * (ny - 1) + 2 * (nx - 1) * ny + (t * (nx - 1) + j) * ny + y

    def send_slots(t):
        for j, y in enumerate(at.other_y()):
            slot_copy(False, slots_out.at[t, y], slots_in.at[t, at.x, at.y], y_sem(t, j), y_sem(t, ny - 2 - j), y=y)
        for j, x in enumerate(at.other_x()):
            slot_copy(False, slots_out.at[t, at.y], slots_in.at[t, at.x, at.y], x_sem(t, j, at.y),
                      x_sem(t, nx - 2 - j, at.y), x=x)
        slots_in[t, at.x, at.y] = slots_out[t, at.y]

    def summed(t, y):
        total = slots_acc[t, at.x, y]
        for j in range(nx - 1):
            arrive(ret_in.at[t, j, y], slot_recv.at[ret_sem(t, j, y)])
            total = total + ret_in[t, j, y].astype(F32)
        return total.astype(BF)

    cores, ys, xs, zs_ = {2: c2, 3: c3}, (y0, y1), (x0, x1), (z0, z1, z2, z3)
    outs = (o0, o1, o2, o3)
    far = [sorted(range(nz), key=lambda d: (-abs(d - z), d)) for z in range(nz)]
    order_e = [at.pick([far[z][k] for z in range(nz)]) for k in range(nz)]
    halves = [[d for d in row if d >= nz // 2] + [d for d in row if d < nz // 2] for row in far]
    order_d = [at.pick([halves[z][k] for z in range(nz)]) for k in range(nz)]
    e_waits = []

    def expert_part(a, d, c):
        return ge.at[pl.ds(bases[a] + (d * 2 + c) * block_units, block_units)]

    def start_expert(a, k):
        one = remote(expert_part(a, order_e[k], 1 - at.c), cores[a].at[k], core_send.at[a, k, 0],
                     core_recv.at[a, k, 0], c=1 - at.c)
        one.start()
        e_waits.append(one.wait_send)

    def core_expert(a, k):
        arrive(cores[a].at[k], core_recv.at[a, k, 0])
        add_into(cores[a].at[k], expert_part(a, order_e[k], at.c))

    def free_experts():
        for wait in e_waits:
            wait()
        pl.semaphore_signal(free_sem, inc=1, device_id=at.device(c=1 - at.c), device_id_type=MESH)

    def dense_part(a, d, x, c):
        return big.at[pl.ds(bases[a] + ((d * nx + x) * 2 + c) * ny * units[a], ny * units[a])]

    def dense_core(a, k, x, y=None, u=None):
        first = bases[a] // 2 + (k * nx + x) * ny * units[a]
        if y is None:
            return ge.at[pl.ds(first, ny * units[a])]
        if u is None:
            return ge.at[pl.ds(first + y * units[a], units[a])]
        return ge.at[pl.ds(first + y * units[a] + u, 1)]

    def xs_in_order():
        return [(x, True) for x in at.other_x()] + [(at.x, False)]

    def start_dense(k, a):
        for x in range(nx):
            send(dense_part(a, order_d[k], x, 1 - at.c), dense_core(a, k, x), core_send.at[a, k, x],
                     core_recv.at[a, k, x], c=1 - at.c)

    def first_dense(k, a):
        if a == 0:
            for x, _ in xs_in_order():
                arrive(dense_core(0, k, x), core_recv.at[0, k, x])
                add_into(dense_core(0, k, x), dense_part(0, order_d[k], x, at.c))
                for u in range(units[0]):
                    for j, y in enumerate(at.other_y()):
                        send(dense_core(0, k, x, y, u), ys[0].at[k, ny - 2 - j, x, pl.ds(u, 1)],
                             y_send.at[k, j, x, u], y_recv.at[k, ny - 2 - j, x, u], y=y)
            return
        for x, away in xs_in_order():
            arrive(dense_core(1, k, x), core_recv.at[1, k, x])
            add_into(dense_core(1, k, x), dense_part(1, order_d[k], x, at.c))
            if away:
                j = lax.rem(x - at.x + nx, nx) - 1
                send(dense_core(1, k, x), xs[1].at[k, nx - 2 - j], x_send.at[k, j, units[0]],
                     x_recv.at[k, nx - 2 - j, units[0]], x=x)

    def second_dense(k, a):
        if a == 0:
            for x, away in xs_in_order():
                for u in range(units[0]):
                    total = ys[0].at[k, 0, x, pl.ds(u, 1)]
                    for j in range(ny - 1):
                        piece = ys[0].at[k, j, x, pl.ds(u, 1)]
                        arrive(piece, y_recv.at[k, j, x, u])
                        add_into(total, piece if j else dense_core(0, k, x, at.y, u))
                    if away:
                        j = lax.rem(x - at.x + nx, nx) - 1
                        send(total, xs[0].at[k, nx - 2 - j, pl.ds(u, 1)], x_send.at[k, j, u], x_recv.at[k, nx - 2 - j, u], x=x)
            return
        for j in range(nx - 1):
            arrive(xs[1].at[k, j], x_recv.at[k, j, units[0]])
            add_into(xs[1].at[k, 0], xs[1].at[k, j] if j else dense_core(1, k, at.x))
        for j, y in enumerate(at.other_y()):
            send(xs[1].at[k, 0, pl.ds(y * units[1], units[1])], ys[1].at[k, ny - 2 - j],
                 y_send.at[k, j, nx, 0], y_recv.at[k, ny - 2 - j, nx, 0], y=y)

    def piece_of(k, p):
        return xs[0].at[k, 0, pl.ds(p, 1)] if p < units[0] else ys[1].at[k, 0]

    def inbox_of(slot, p):
        return zs_[0].at[slot, pl.ds(p, 1)] if p < units[0] else zs_[1].at[slot]

    def line_dense(k, a):
        d = order_d[k]
        for p in range(units[0]) if a == 0 else [units[0]]:
            total = piece_of(k, p)
            if p < units[0]:
                for j in range(nx - 1):
                    piece = xs[0].at[k, j, pl.ds(p, 1)]
                    arrive(piece, x_recv.at[k, j, p])
                    add(total, piece if j else ys[0].at[k, 0, at.x, pl.ds(p, 1)])
            else:
                for j in range(ny - 1):
                    arrive(ys[1].at[k, j], y_recv.at[k, j, nx, 0])
                    add(total, ys[1].at[k, j] if j else xs[1].at[k, 0, pl.ds(at.y * units[1], units[1])])
            for side in range(2):

                @pl.when((at.z > 0) & (d > at.z) if side == 0 else (at.z < nz - 1) & (d < at.z))
                def _(total=total, p=p):
                    arrive(inbox_of(d, p), zd_recv.at[d, p])
                    add(total, inbox_of(d, p))

            def hop(to, total=total, p=p):
                slot = d if to > 0 else jnp.where(d == at.z - 1, nz, d)
                return remote(total, inbox_of(slot, p), zd_send.at[k, p], zd_recv.at[slot, p], z=at.z + to)

            start_when(d < at.z, functools.partial(hop, -1))
            start_when(d > at.z, functools.partial(hop, 1))

            continue_waits(waits, hop, d, at)

    def finish_dense():
        for k in (nz // 2 - 1, nz - 1):

            @pl.when(order_d[k] == at.z)
            def _(k=k):
                for p in range(units[0] + 1):
                    total = piece_of(k, p)
                    for side, here in enumerate((at.z > 0, at.z < nz - 1)):
                        slot = at.z if side == 0 else nz

                        @pl.when(here)
                        def _(total=total, slot=slot, p=p):
                            arrive(inbox_of(slot, p), zd_recv.at[slot, p])
                            add_into(total, inbox_of(slot, p))

                write_out(0, xs[0].at[k, 0])
                write_out(1, ys[1].at[k, 0])

    def write_out(a, total):
        if a != e_in:
            if acts_now[0]:
                outs[a][...] = total[...].astype(F32).reshape(outs[a].shape)
            return
        for j, x in enumerate(at.other_x()):
            send(total.at[pl.ds(x * panels, panels)], ex_in.at[nx - 2 - j], ex_send.at[j], ex_recv.at[nx - 2 - j], x=x)

    def finish_expert_in():
        for j in range(nx - 1):
            arrive(ex_in.at[j], ex_recv.at[j])
        total = cores[e_in].at[nz - 1]
        for x in range(nx):
            for u in range(panels):
                value = None
                for j, other in enumerate(at.other_x()):
                    value = ex_in[j, u] if value is None else jnp.where(other == x, ex_in[j, u], value)
                mine = total[pl.ds(at.x * panels + u, 1)][0]
                value = jnp.where(at.x == x, mine.astype(F32), value.astype(F32))
                for i in range(width // columns):
                    z = u * (width // columns) + i
                    outs[e_in][:, (z * nx + x) * columns : (z * nx + x + 1) * columns] = value[:, i * columns : (i + 1) * columns]

    def line(kind, k):
        for a in kind:
            d = order_e[k]
            total = cores[a].at[k]
            for side in range(2):
                feeds = (at.z > 0) & (d >= at.z) if side == 0 else (at.z < nz - 1) & (d <= at.z)
                slot = d if side == 0 else jnp.where(d == at.z, nz, d)

                @pl.when(feeds)
                def _(a=a, slot=slot, total=total):
                    arrive(zs_[a].at[slot], z_recv.at[a, slot])
                    add(total, zs_[a].at[slot])

            def hop(to, a=a, total=total, d=d):
                slot = d if to > 0 else jnp.where(d == at.z - 1, nz, d)
                return remote(total, zs_[a].at[slot], z_send.at[a, k], z_recv.at[a, slot], z=at.z + to)

            start_when(d < at.z, functools.partial(hop, -1))
            start_when(d > at.z, functools.partial(hop, 1))

            if k == nz - 1:
                write_out(a, total)
            continue_waits(waits, hop, d, at)

    def start_act(i):
        for p in range(packs):
            for x in range(nx):
                send(act_rows((kc, k_)[i], p, x, 1 - at.c), act_core.at[i, p, x], sum_send.at[i, p, x],
                     sum_recv.at[i, p, x], c=1 - at.c)

    def core_act(i):
        for p in range(packs):
            for x in range(nx):
                arrive(act_core.at[i, p, x], sum_recv.at[i, p, x])
                add_into(act_core.at[i, p, x], act_rows((kc, k_)[i], p, x, at.c))
        for j, x in enumerate(at.other_x()):
            send(act_core.at[i, :, x], act_x.at[i, nx - 2 - j], sum_send.at[i, packs, j], sum_recv.at[i, packs, nx - 2 - j], x=x)

    def x_act(i):
        for j in range(nx - 1):
            arrive(act_x.at[i, j], sum_recv.at[i, packs, j])
        for p in range(packs):
            out = act_core[i, p, at.x].astype(F32)
            for j in range(nx - 1):
                out = out + act_x[i, j, p].astype(F32)
            if i == 0:
                grad_mem[pl.ds(p * tok, tok), :] = out
            else:
                gn[pl.ds(p * tok, tok), :] += out

    pair_sums = ((wide_sum, wide_in), (table_sum, table_in))
    stages = [("c", [1 - at.c]), ("y", at.other_y()), ("x", at.other_x())]

    def start_small(t):
        axis, peers = stages[t]
        base = [0, 1, ny][t]
        for i, (total, inbox) in enumerate(pair_sums):
            for j, peer in enumerate(peers):
                back = base + len(peers) - 1 - j
                send(total.at[t], inbox.at[back], small_send.at[i, base + j], small_recv.at[i, back], **{axis: peer})

    def end_small(t):
        axis, peers = stages[t]
        base = [0, 1, ny][t]
        for i, (total, inbox) in enumerate(pair_sums):
            out = total[t]
            for j in range(len(peers)):
                arrive(inbox.at[base + j], small_recv.at[i, base + j])
                out = out + inbox[base + j]
            total[t + 1] = out

    tail = ny + nx - 1

    def start_line():
        for i, (total, inbox) in enumerate(pair_sums):
            for j in range(1, nz):
                z = lax.rem(at.z + j, nz)
                send(total.at[3], inbox.at[tail + at.z], small_send.at[i, tail + j], small_recv.at[i, tail + at.z], z=z)

    def end_line():
        for i, (total, inbox) in enumerate(pair_sums):
            for j in range(1, nz):
                z = lax.rem(at.z + j, nz)
                arrive(inbox.at[tail + z], small_recv.at[i, tail + z])
            out = None
            for z in range(nz):
                term = jnp.where(at.z == z, total[3], inbox[tail + z])
                out = term if out is None else out + term
            if i == 0:
                sum_gains[...] = out[: sum_gains.shape[0]]
                sum_router[...] = out[sum_gains.shape[0] : sum_gains.shape[0] + experts]
            else:
                sum_table[...] = out[: sum_table.shape[0], : sum_table.shape[1]]

    dense_events(0)
    start_prep()
    at_planes(False, lambda: dense_events(1), False)
    at_planes(False, lambda: dense_events(2), False)
    at_planes(False, lambda: dense_events(3), False)
    side_x(0)
    at_planes(True, lambda: dense_events(1), True)
    expert_events(0, (e_out,))
    side_y(0)
    side_x(1)
    at_planes(True, lambda: dense_events(2), True)
    at_planes(True, lambda: dense_events(3), True)
    expert_events(0, (e_in,))
    send_acts()
    at_planes(False, lambda: expert_events(1, (e_out,)), False)
    side_y(1)
    prepare_bias(rel, table, bias, at.s, tok, group)
    prepare_masks(lengths, same, causal, at.s, tok, group)
    hot, dispatch = route_slots(route, experts, each // packs)
    load_g.wait()
    top = g_ref[...].astype(F32).reshape(packs * tok, width)
    side_x(2)
    side_x(3)
    at_planes(True, lambda: expert_events(1, (e_out,)), True)
    side_y(2)
    at_planes(False, lambda: expert_events(1, (e_in,)), False)
    side_y(3)
    slots_out[1] = by_slot(dispatch, g_ref[...].reshape(packs * tok, width))
    send_slots(1)
    at_planes(True, lambda: expert_events(1, (e_in,)), True)
    at_planes(False, lambda: expert_events(2, (e_out,)), False)
    at_planes(False, lambda: expert_events(3, (e_out,)), False)
    act_events()
    corner_events(0)
    at_planes(True, lambda: expert_events(2, (e_out,)), True)
    corner_events(1)
    first_norm()
    at_planes(False, lambda: expert_events(2, (e_in,)), False)
    corner_events(2)
    at_planes(False, lambda: expert_events(3, (e_in,)), False)
    for a in dense:
        for z in zs[: nz // 2]:
            for x in range(nx):
                for y in range(ny):
                    arrive(spot(a, z, x, 1 - at.c, y), spread_recv.at[a, z, x, y])
    corner_events(3)
    keys_and_values(at.z < nz // 2)
    for a in dense:
        for z in zs[nz // 2 :]:
            for x in range(nx):
                for y in range(ny):
                    arrive(spot(a, z, x, 1 - at.c, y), spread_recv.at[a, z, x, y])
    keys_and_values(at.z >= nz // 2)
    for j, y in enumerate(at.other_y()):
        here = slots_in.at[1, at.x, y]
        arrive(here, slot_recv.at[y_sem(1, j)])
        for i, x in enumerate(at.other_x()):
            slot_copy(False, here, here, x_sem(1, i, y), x_sem(1, nx - 2 - i, y), x=x)
    project(n1, w, 0, q)
    attend_pairs(q, k_, v, bias, causal, pr_self, mixed)
    add_product(h1, mixed, w, 6)
    rms_rows(h1, gains[1:2], n2, packs * tok)
    project(n2, w, 3, qc)
    attend_pairs(qc, kc, vc, None, same, pr_cross, cross_mixed)
    h2[...] = h1[...]
    add_product(h2, cross_mixed, w, 7)
    rms_rows(h2, gains[2:3], n3, packs * tok)
    slots_out[0] = by_slot(dispatch, n3[...])
    send_slots(0)
    at_planes(True, lambda: expert_events(3, (e_out,)), True)
    for j, y in enumerate(at.other_y()):
        here = slots_in.at[0, at.x, y]
        arrive(here, slot_recv.at[y_sem(0, j)])
        for i, x in enumerate(at.other_x()):
            slot_copy(False, here, here, x_sem(0, i, y), x_sem(0, nx - 2 - i, y), x=x)
    at_planes(True, lambda: expert_events(2, (e_in,)), True)
    at_planes(True, lambda: expert_events(3, (e_in,)), True)
    for a in experts_:
        for z in range(nz):
            arrive(pack_of(a, z, 1 - at.c), spread_recv.at[a, z, 0, 0])
    for t in range(2):
        for i, x in enumerate(at.other_x()):
            for y in range(ny):
                arrive(slots_in.at[t, x, y], slot_recv.at[x_sem(t, i, y)])
    here = slots_in[0].reshape(nx * count, width)
    g_here = slots_in[1].reshape(nx * count, width).astype(F32)
    mine, chances = chances_of(here, router_t, at.y)
    gate_here = jnp.sum(chances * mine, axis=1, keepdims=True)
    grad_here[...] = (gate_here * g_here).astype(BF)
    for u in range(panels):
        in_panel = jnp.concatenate([big[place + u] for place in places], axis=0)
        out_panel = big[pl.ds(bases[e_out] + u * row_units, row_units)].reshape(width, width)
        inner = jnp.dot(here, in_panel, preferred_element_type=F32)
        hidden, slope = gelu_both(inner)
        hid[u] = hidden.astype(BF)
        grad_hidden = lax.dot_general(grad_here[...], out_panel, (((1,), (1,)), ((), ())), preferred_element_type=F32)
        gin_[u] = (grad_hidden * slope).astype(BF)
        result = jnp.dot(hid[u], out_panel, preferred_element_type=F32).reshape(nx, ny, each, width)
        grad_slots = lax.dot_general(gin_[u], in_panel, (((1,), (1,)), ((), ())), preferred_element_type=F32)
        grad_slots = grad_slots.reshape(nx, ny, each, width)
        if u:
            slots_acc[0] += result
            slots_acc[1] += grad_slots
        else:
            slots_acc[0] = result
            slots_acc[1] = grad_slots
    grad_gate = jnp.sum(g_here * slots_acc[0].reshape(nx * count, width), axis=1, keepdims=True)
    grad_logits = grad_gate * chances * (mine - gate_here)
    extra_grad = 0.0
    for e in range(experts):
        extra_grad = extra_grad + grad_logits[:, e : e + 1] * router_t[e : e + 1, :].astype(F32)
    slots_acc[1] += extra_grad.reshape(nx, ny, each, width)
    for wait in waits:
        wait()
    waits.clear()
    for y in [*at.other_y(), at.y]:
        for j, x in enumerate(at.other_x()):
            ret_out[1, j, y] = slots_acc[1, x, y].astype(BF)
            slot_copy(True, ret_out.at[1, j, y], ret_in.at[1, nx - 2 - j, y], ret_sem(1, j, y), ret_sem(1, nx - 2 - j, y), x=x)
    for u in range(panels):
        grad = lax.dot_general(here, gin_[u], (((0,), (0,)), ((), ())), preferred_element_type=F32).astype(BF)
        for i, place in enumerate(places):
            ge[place + u] = grad[i * unit : (i + 1) * unit]
    for k in range(nz):
        start_expert(e_in, k)
    router_grad = lax.dot_general(
        grad_logits, here.astype(F32), (((0,), (0,)), ((), ())), precision=HIGHEST, preferred_element_type=F32
    )
    for u in range(panels):
        grad = lax.dot_general(hid[u], grad_here[...], (((0,), (0,)), ((), ())), preferred_element_type=F32).astype(BF)
        ge[pl.ds(bases[e_out] + u * row_units, row_units)] = grad.reshape(row_units, unit, width)
    for k in range(nz):
        start_expert(e_out, k)
    for y in [*at.other_y(), at.y]:
        for j, x in enumerate(at.other_x()):
            ret_out[0, j, y] = slots_acc[0, x, y].astype(BF)
            slot_copy(True, ret_out.at[0, j, y], ret_in.at[0, nx - 2 - j, y], ret_sem(0, j, y), ret_sem(0, nx - 2 - j, y), x=x)
    core_expert(e_in, 0)
    at_planes(True, lambda: line((e_in,), 0), False)
    for wait in slot_waits:
        wait()
    for j, y in enumerate(at.other_y()):
        slots_out[1, y] = summed(1, y)
        slot_copy(True, slots_out.at[1, y], back_in.at[1, at.y], y_sem(3, j), y_sem(3, ny - 2 - j), y=y)
    core_expert(e_out, 0)
    core_expert(e_in, 1)
    core_expert(e_out, 1)
    back_in[1, at.y] = summed(1, at.y)
    core_expert(e_in, 3)
    core_expert(e_out, 2)
    core_expert(e_out, 3)
    at_planes(True, lambda: line((e_out,), 0), False)
    core_expert(e_in, 2)
    free_experts()
    for j, y in enumerate(at.other_y()):
        arrive(back_in.at[1, y], slot_recv.at[y_sem(3, j)])
    diagonal[...] = jnp.zeros_like(diagonal)
    for i, (_, inbox) in enumerate(pair_sums):
        inbox[pl.ds(tail + at.z, 1)] = jnp.zeros_like(inbox[pl.ds(0, 1)])
    wide_sum[0] = jnp.zeros_like(wide_sum[0])
    wide_sum[0, pl.ds(3, experts), :] = router_grad
    gn[...] = jnp.dot(dispatch, back_in[1].reshape(count, width), preferred_element_type=F32)
    grad_x[...] = top
    norm_back_rows(h2, gains[2:3], gn, grad_x, gain_row)
    wide_sum[0, 2:3, :] = gain_row[...]
    gb[...] = grad_x[...].astype(BF)
    product_t(gb, w, 7, ga)
    attend_pairs_back(qc, kc, vc, pr_cross, ga, gq, gk, gv, None)
    outer_product(n2, gq, big, 3)
    outer_product(mo, gk, big, 4)
    outer_product(mo, gv, big, 5)
    pl.semaphore_wait(free_sem, 1)
    start_dense(1, 0)
    for j, y in enumerate(at.other_y()):
        slots_out[0, y] = summed(0, y)
        slot_copy(True, slots_out.at[0, y], back_in.at[0, at.y], y_sem(2, j), y_sem(2, ny - 2 - j), y=y)
    at_planes(True, lambda: line((e_in,), 1), False)
    product_t(gq, w, 3, gn)
    norm_back_rows(h1, gains[1:2], gn, grad_x, gain_row)
    wide_sum[0, 1:2, :] = gain_row[...]
    back_in[0, at.y] = summed(0, at.y)
    outer_product(cross_mixed, gb, big, 7)
    start_dense(0, 1)
    first_dense(1, 0)
    start_dense(1, 1)
    gb[...] = grad_x[...].astype(BF)
    product_t(gb, w, 6, ga)
    outer_product(mixed, gb, big, 6)
    at_planes(True, lambda: line((e_out,), 1), False)
    first_dense(0, 1)
    start_dense(3, 1)
    at_planes(False, lambda: line((e_in,), 0), True)
    start_dense(0, 0)
    at_planes(False, lambda: line((e_out,), 0), True)
    start_dense(2, 1)
    two_products_t(gk, 4, gv, 5, w, kc)
    first_dense(1, 1)
    at_planes(True, lambda: line((e_out,), 2), False)
    first_dense(3, 1)
    attend_pairs_back(q, k_, v, pr_self, ga, gq, gk, gv, diagonal)
    second_dense(0, 1)
    first_dense(2, 1)
    first_dense(0, 0)
    start_act(0)
    at_planes(False, lambda: line((e_in,), 1), True)
    two_products_t(gk, 1, gv, 2, w, k_)
    at_planes(True, lambda: line((e_in,), 2), False)
    start_act(1)
    outer_product(n1, gq, big, 0)
    outer_product(n1_all, gk, big, 1)
    outer_product(n1_all, gv, big, 2)
    start_dense(2, 0)
    core_act(1)
    table_sum[0] = table_grad(rel, diagonal, at.s, tok, group)
    start_dense(3, 0)
    product_t(gq, w, 0, gn)
    for j, y in enumerate(at.other_y()):
        arrive(back_in.at[0, y], slot_recv.at[y_sem(2, j)])
    _, routing = chances_of(n3[...], router_t, at.y)
    gate = jnp.sum(routing * hot, axis=1, keepdims=True)
    combined = jnp.dot(dispatch, back_in[0].reshape(count, width), preferred_element_type=F32)
    rows_out = (h2[...] + gate * combined).astype(BF)
    for p in range(packs):
        out_rows[p] = rows_out[p * tok : (p + 1) * tok]
    at_planes(False, lambda: line((e_out,), 1), True)
    second_dense(3, 1)
    first_dense(2, 0)
    second_dense(2, 1)
    second_dense(0, 0)
    at_planes(False, lambda: line((e_in,), 2), True)
    x_act(1)
    h1[...] = x_keep[...].astype(F32)
    norm_back_rows(h1, gains[0:1], gn, grad_x, gain_row)
    wide_sum[0, 0:1, :] = gain_row[...]
    at_planes(True, lambda: line_dense(0, 1), False)
    core_act(0)
    second_dense(1, 0)
    at_planes(True, lambda: line_dense(0, 0), False)
    start_small(0)
    end_small(0)
    start_small(1)
    first_dense(3, 0)
    at_planes(False, lambda: line_dense(3, 1), False)
    at_planes(True, lambda: line_dense(3, 1), True)
    at_planes(False, lambda: line_dense(0, 0), True)
    second_dense(2, 0)
    at_planes(False, lambda: line_dense(0, 1), True)
    at_planes(True, lambda: line_dense(1, 0), False)
    at_planes(True, lambda: line((e_in,), 3), False)
    x_act(0)
    end_small(1)
    start_small(2)
    second_dense(1, 1)
    at_planes(False, lambda: line((e_in,), 3), True)
    at_planes(True, lambda: line_dense(2, 0), False)
    at_planes(False, lambda: line((e_out,), 2), True)
    at_planes(False, lambda: line_dense(1, 0), True)
    at_planes(True, lambda: line_dense(2, 1), False)
    at_planes(False, lambda: line_dense(2, 0), True)
    second_dense(3, 0)
    at_planes(False, lambda: line_dense(2, 1), True)
    at_planes(True, lambda: line_dense(3, 0), False)
    at_planes(True, lambda: line_dense(1, 1), False)
    end_small(2)
    start_line()
    at_planes(False, lambda: line_dense(1, 1), True)
    at_planes(False, lambda: line((e_out,), 3), False)
    at_planes(False, lambda: line_dense(3, 0), True)
    finish_expert_in()
    end_line()
    finish_dense()
    at_planes(True, lambda: line((e_out,), 3), True)
    for wait in waits:
        wait()


def shapes_of(layer_input, routes, attn_in, attn_out, expert_in, expert_out):
    nz, ns, ny = (lax.axis_size(a) for a in ("dp", "seq", "expert"))
    packs, tok, width = layer_input.shape[0], layer_input.shape[3], layer_input.shape[4]
    return nz, ns, ny, packs, tok, width


def fits_kernel(layer_input, routes, attn_in, attn_out, expert_in, expert_out):
    nz, ns, ny, packs, tok, width = shapes_of(layer_input, routes, attn_in, attn_out, expert_in, expert_out)
    unit, hidden = expert_in.shape[1:]
    capacity = (5 * tok + 4 * ny - 1) // (4 * ny)
    nx = ns // 2
    return (
        unit % 16 == 0
        and tok % 16 == 0
        and packs * capacity % 16 == 0
        and attn_in.shape[0] % unit == 0
        and attn_out.shape[0] % unit == 0
        and expert_out.shape[1] % (unit * nx) == 0
        and width % (2 * unit) == 0
        and hidden % (nx * width) == 0
        and width % (hidden // (nz * nx)) == 0
        and hidden // (nz * nx) % 128 == 0
        and expert_out.shape[1] * nz * ns == hidden
        and expert_out.shape[1] * width == hidden * unit
        and expert_in.shape[0] == 1
    )


def deliver_body(*refs):
    count = (len(refs) - 2) // 3
    came, gone = refs[-2:]
    copies = []
    for i in range(count):
        place = refs[2 * count + i]
        copies.append((
            pltpu.make_async_copy(refs[i], place, came.at[i]),
            pltpu.make_async_copy(place, refs[count + i], gone.at[i]),
        ))
    for first, _ in copies:
        first.start()
    for first, second in copies:
        first.wait()
        second.start()
    for _, second in copies:
        second.wait()


def deliver(arrays):
    any_ = pl.BlockSpec(memory_space=pl.ANY)
    count = len(arrays)
    return pl.pallas_call(
        deliver_body,
        out_shape=[jax.ShapeDtypeStruct(a.shape, a.dtype) for a in arrays],
        in_specs=[any_] * count,
        out_specs=[any_] * count,
        scratch_shapes=[
            *[pltpu.VMEM(a.shape, a.dtype) for a in arrays],
            pltpu.SemaphoreType.DMA((count,)),
            pltpu.SemaphoreType.DMA((count,)),
        ],
        name="deliver",
    )(*arrays)


def layer_kernel(layer_input, memory, cotangent, routes, doc_lengths, rel_buckets, gains, bias_table, router,
                 attn_in, attn_out, expert_in, expert_out):
    nz, ns, ny, packs, tok, width = shapes_of(layer_input, routes, attn_in, attn_out, expert_in, expert_out)
    nx = ns // 2
    group, pairs = ns * tok, width // 128
    unit = expert_in.shape[1]
    hidden = expert_in.shape[2]
    panels = hidden // width // nx
    pack_units = nx * panels
    experts, buckets = router.shape[1], bias_table.shape[0]
    each = packs * ((5 * tok + 4 * experts - 1) // (4 * experts))
    tall = nz * ns
    units = (attn_in.shape[0] // unit, attn_out.shape[0] // unit)
    total = tall * ny * (units[0] + units[1])
    grads = max(4 * nz * pack_units, total // 2)
    extra = -(-(3 + experts) // 8) * 8
    small = ny + nx - 1 + nz
    mine, every = packs * tok, packs * group
    any_ = pl.BlockSpec(memory_space=pl.ANY)
    vmem = pl.BlockSpec(memory_space=pltpu.VMEM)
    smem = pl.BlockSpec(memory_space=pltpu.SMEM)
    dma = pltpu.SemaphoreType.DMA
    low = lambda *shape: pltpu.VMEM(shape, BF)
    wide = lambda *shape: pltpu.VMEM(shape, F32)
    shape = lambda *dims: jax.ShapeDtypeStruct(dims, F32)
    results = pl.pallas_call(
        layer_body,
        out_shape=[
            jax.ShapeDtypeStruct((packs, tok, width), BF),
            shape(*attn_in.shape),
            shape(*attn_out.shape),
            shape(*expert_in.shape[1:]),
            shape(*expert_out.shape[1:]),
            shape(mine, width),
            shape(mine, width),
            shape(3, width),
            shape(experts, width),
            shape(2 * pairs, buckets),
        ],
        in_specs=[smem, *[vmem] * 5, *[any_] * 7],
        out_specs=[vmem] * 10,
        scratch_shapes=[
            low(total, unit, width),
            low(total, unit, width),
            low(grads, unit, width),
            low(nx, panels, unit, width),
            *[low(nz, pack_units, unit, width)] * 2,
            low(nz, ny - 1, nx, units[0], unit, width),
            low(nz, ny - 1, units[1], unit, width),
            low(nz, nx - 1, units[0], unit, width),
            low(nz, nx - 1, ny * units[1], unit, width),
            low(nx - 1, panels, unit, width),
            *[low(nz + 1, u, unit, width) for u in (*units, pack_units, pack_units)],
            *[low(every, width)] * 8,
            *[low(mine, width)] * 10,
            *[low(packs, pairs, 2 * tok, group)] * 2,
            *[wide(mine, width)] * 3,
            wide(pairs, 2 * tok, group),
            wide(packs, tok, group),
            wide(packs, tok, group),
            wide(16, group + 128),
            wide(1, width),
            low(2, packs, nx, tok, width),
            low(2, nx - 1, packs, tok, width),
            wide(4, extra, width),
            wide(4, 16, 128),
            wide(small, extra, width),
            wide(small, 16, 128),
            low(2, ny, each, width),
            low(2, nx, ny, each, width),
            wide(2, nx, ny, each, width),
            low(2, nx - 1, ny, each, width),
            low(2, nx - 1, ny, each, width),
            low(2, ny, each, width),
            low(nx * ny * each, width),
            low(panels, nx * ny * each, width),
            low(panels, nx * ny * each, width),
            dma((2, packs, 2 * nx)),
            dma((2, packs, nx, 2)),
            dma((nx - 1,)),
            dma((nx,)),
            dma((4, nz, 2)),
            dma((2, nz, nx - 1 + ny - 1 + max((ny - 1) * nx, (nx - 1) * ny))),
            dma((4, nz, nx, ny)),
            dma((4, nz, nx, ny)),
            dma((4, nz, nx, ny)),
            dma((6, packs)),
            dma((4, nz, nx)),
            dma((4, nz, nx)),
            dma((nz, ny - 1, nx + 1, units[0])),
            dma((nz, ny - 1, nx + 1, units[0])),
            dma((nz, nx - 1, units[0] + 1)),
            dma((nz, nx - 1, units[0] + 1)),
            dma((nx - 1,)),
            dma((nx - 1,)),
            dma((4, nz)),
            dma((4, nz + 1)),
            dma((nz, units[0] + 1)),
            dma((nz + 1, units[0] + 1)),
            dma((2, packs + 1, nx)),
            dma((2, packs + 1, nx)),
            dma((2, small)),
            dma((2, small)),
            dma((4 * (ny - 1) + 4 * (nx - 1) * ny,)),
            dma((4 * (ny - 1) + 4 * (nx - 1) * ny,)),
            pltpu.SemaphoreType.REGULAR,
            low(packs, tok, width),
            low(unit, hidden),
            low(mine, width),
            dma((2,)),
        ],
        compiler_params=pltpu.CompilerParams(
            collective_id=0, has_side_effects=True, vmem_limit_bytes=64 * 2**20
        ),
        name="layer",
    )(
        doc_lengths[:, 0, 0],
        rel_buckets.reshape(1, -1),
        gains,
        bias_table.T,
        router.T,
        routes.reshape(packs, 1, tok),
        layer_input[:, 0, 0],
        memory[:, 0, 0],
        cotangent[:, 0, 0],
        attn_in.reshape(units[0], unit, width),
        attn_out.reshape(units[1], unit, width),
        expert_in[0],
        expert_out.reshape(pack_units, unit, width),
    )
    out_rows, g0, g1, g2, g3, grad_x, grad_mem, gains_sum, router_sum, table_sum = deliver(results)
    spread = (packs, 1, 1, tok, width)
    return (
        out_rows.reshape(spread),
        grad_x.reshape(spread),
        grad_mem.reshape(spread),
        gains_sum,
        table_sum.T,
        router_sum.T,
        g0,
        g1,
        g2[None],
        g3[None],
    )


def norm_apply(value, gain):
    return value * lax.rsqrt(jnp.mean(value * value, axis=-1, keepdims=True) + EPS) * gain


def norm_back(value, gain, grad):
    r = lax.rsqrt(jnp.mean(value * value, axis=-1, keepdims=True) + EPS)
    scaled = grad * gain
    back = r * scaled - value * (r * r * r) * jnp.mean(scaled * value, axis=-1, keepdims=True)
    return back, jnp.sum(grad * value * r, axis=0)


def gelu_tanh(value):
    return jax.nn.gelu(value, approximate=True)


def times(left, right):
    return jnp.dot(left, right, preferred_element_type=F32)


def times_right(left, right):
    return jnp.einsum("te,de->td", left, right, preferred_element_type=F32)


def times_left(left, right):
    return jnp.einsum("td,te->de", left, right, preferred_element_type=F32)


def split(a, packs):
    return a.reshape(packs, -1, HEADS, HEAD)


def attend(query, keys, values, allowed, bias, packs):
    scores = jnp.einsum("pqhd,pkhd->phqk", split(query, packs), split(keys, packs), preferred_element_type=F32)
    masked = jnp.where(allowed[:, None], scores * HEAD**-0.5 + bias, NEG)
    raised = jnp.exp(masked - jnp.max(masked, axis=3, keepdims=True))
    chances = raised / jnp.sum(raised, axis=3, keepdims=True)
    mixed = jnp.einsum("phqk,pkhd->pqhd", chances.astype(BF), split(values, packs), preferred_element_type=F32)
    return mixed.reshape(query.shape).astype(BF), chances


def attend_back(query, keys, values, chances, grad, packs):
    scale = HEAD**-0.5
    g4 = split(grad, packs)
    grad_chances = jnp.einsum("pqhd,pkhd->phqk", g4, split(values, packs), preferred_element_type=F32)
    spread_ = jnp.sum(chances * grad_chances, axis=3, keepdims=True)
    grad_scores = (chances * (grad_chances - spread_)).astype(BF)
    grad_query = jnp.einsum("phqk,pkhd->pqhd", grad_scores, split(keys, packs), preferred_element_type=F32) * scale
    grad_keys = jnp.einsum("phqk,pqhd->pkhd", grad_scores, split(query, packs), preferred_element_type=F32) * scale
    grad_values = jnp.einsum("phqk,pqhd->pkhd", chances.astype(BF), g4, preferred_element_type=F32)
    return (
        grad_query.reshape(query.shape).astype(BF),
        grad_keys.reshape(keys.shape).astype(BF),
        grad_values.reshape(keys.shape).astype(BF),
        grad_scores,
    )


def per_device(layer_input, memory, cotangent, routes, doc_lengths, rel_buckets, gains, bias_table, router,
               attn_in, attn_out, expert_in, expert_out):
    packs, rows, width = layer_input.shape[0], layer_input.shape[3], layer_input.shape[4]
    seqs = lax.axis_size("seq")
    group = rows * seqs
    experts = router.shape[1]
    capacity = (5 * rows + 4 * experts - 1) // (4 * experts)
    buckets = bias_table.shape[0]
    rank = lax.axis_index("seq")

    x_in, m_in, e_in, e_out = layer_input[:, 0, 0], memory[:, 0, 0], expert_in[0], expert_out[0]
    if fits_kernel(layer_input, routes, attn_in, attn_out, expert_in, expert_out):
        return layer_kernel(layer_input, memory, cotangent, routes, doc_lengths, rel_buckets, gains, bias_table, router,
                            attn_in, attn_out, expert_in, expert_out)
    x_rows = x_in.reshape(packs * rows, width).astype(F32)
    everywhere, peers = ("dp", "seq", "expert"), ("dp", "seq")
    x_all, m_all = (lax.all_gather(a, "seq", axis=1, tiled=True) for a in (x_in, m_in))
    w_in, w_out = (lax.all_gather(a, everywhere, axis=0, tiled=True) for a in (attn_in, attn_out))
    e_in, e_out = (lax.all_gather(a, peers, axis=0, tiled=True) for a in (e_in, e_out))
    w_in = w_in.reshape(6, width, width)
    w_out = w_out.reshape(2, width, width)
    x_all = x_all.reshape(packs * group, width)
    m_all = m_all.reshape(packs * group, width)
    wide = group + rows
    query_pos = rank * rows + jnp.arange(rows, dtype=jnp.int32)
    key_pos = jnp.arange(group, dtype=jnp.int32)
    ends = jnp.cumsum(doc_lengths[:, 0, 0], axis=1)
    query_doc = jnp.sum((query_pos[None, :, None] >= ends[:, None, :]).astype(jnp.int32), axis=2)
    key_doc = jnp.sum((key_pos[None, :, None] >= ends[:, None, :]).astype(jnp.int32), axis=2)
    same = query_doc[:, :, None] == key_doc[:, None, :]
    causal = same & (key_pos[None, None, :] <= query_pos[None, :, None])
    bucket_hot = (rel_buckets[:, None] == jnp.arange(buckets, dtype=jnp.int32)).astype(F32)
    line_at = jnp.arange(group + rows, dtype=jnp.int32) - (group - 1) + rank * rows
    line_hot = (jnp.take(rel_buckets, jnp.clip(line_at, 0, group - 1))[None, :] == jnp.arange(buckets)[:, None]).astype(F32)
    line = jnp.einsum("bh,bj->hj", bias_table, line_hot, precision=HIGHEST)
    line = line[:, ::-1]
    wide = group + rows
    tiled = jnp.broadcast_to(line[:, None, :], (HEADS, rows, wide)).reshape(HEADS, rows * wide)
    skew = tiled[:, rows : rows + rows * (wide - 1)].reshape(HEADS, rows, wide - 1)[:, :, :group]

    normed1_all = norm_apply(x_all.astype(F32), gains[0]).astype(BF)
    normed1 = norm_apply(x_rows, gains[0]).astype(BF)
    query = times(normed1, w_in[0]).astype(BF)
    keys = times(normed1_all, w_in[1]).astype(BF)
    values = times(normed1_all, w_in[2]).astype(BF)
    mem_keys = times(m_all, w_in[4]).astype(BF)
    mem_values = times(m_all, w_in[5]).astype(BF)
    mixed, chances_self = attend(query, keys, values, causal, skew[None], packs)
    hidden1 = x_rows + times(mixed, w_out[0])
    normed2 = norm_apply(hidden1, gains[1]).astype(BF)
    cross_query = times(normed2, w_in[3]).astype(BF)
    cross_mixed, chances_cross = attend(cross_query, mem_keys, mem_values, same, 0.0, packs)
    hidden2 = hidden1 + times(cross_mixed, w_out[1])
    normed3 = norm_apply(hidden2, gains[2]).astype(BF)

    routing = jax.nn.softmax(times(normed3, router), axis=1)
    route = routes[:, 0, 0, :, 0]
    route_hot = (route[:, :, None] == jnp.arange(experts, dtype=jnp.int32)).astype(jnp.int32)
    slot = jnp.sum((jnp.cumsum(route_hot, axis=1) - route_hot) * route_hot, axis=2)
    hot = route_hot.reshape(packs * rows, experts).astype(F32)
    gate = jnp.sum(routing * hot, axis=1)
    target = jnp.where(slot < capacity, (route * packs + jnp.arange(packs)[:, None]) * capacity + slot, -1).reshape(-1)
    dispatch = (target[:, None] == jnp.arange(experts * packs * capacity, dtype=jnp.int32)).astype(BF)

    def swap(a):
        shape = (experts, packs * capacity, width)
        return lax.all_to_all(a.reshape(shape), "expert", split_axis=0, concat_axis=0, tiled=True).reshape(-1, width)

    received = swap(times_left(dispatch, normed3).astype(BF))
    inner = times(received, e_in)
    hidden, pull = jax.vjp(gelu_tanh, inner)
    hidden = hidden.astype(BF)
    result = times(hidden, e_out).astype(BF)
    combined = times(dispatch, swap(result))
    out_rows = (hidden2 + gate[:, None] * combined).astype(BF)
    grad_top = cotangent.reshape(packs * rows, width).astype(F32)
    grad_gate = jnp.sum(grad_top * combined, axis=1)
    grad_result = swap(times_left(dispatch, (gate[:, None] * grad_top).astype(BF)).astype(BF))
    grad_hidden = times_right(grad_result, e_out)
    grad_eout = times_left(hidden, grad_result).astype(BF)
    grad_inner = pull(grad_hidden)[0].astype(BF)
    grad_ein = times_left(received, grad_inner).astype(BF)
    grad_send = swap(times_right(grad_inner, e_in).astype(BF))
    grad_logits = grad_gate[:, None] * routing * (hot - gate[:, None])
    grad_router = jnp.einsum("td,te->de", normed3.astype(F32), grad_logits, precision=HIGHEST)
    grad_normed3 = times(dispatch, grad_send) + jnp.einsum(
        "te,de->td", grad_logits, router.astype(F32), precision=HIGHEST
    )
    back3, gain3 = norm_back(hidden2, gains[2], grad_normed3)
    grad_h2 = grad_top + back3
    grad_h2_low = grad_h2.astype(BF)
    grad_wco = times_left(cross_mixed, grad_h2_low)
    grad_cross = times_right(grad_h2_low, w_out[1]).astype(BF)
    grad_cq, grad_ck, grad_cv, _ = attend_back(cross_query, mem_keys, mem_values, chances_cross, grad_cross, packs)
    back2, gain2 = norm_back(hidden1, gains[1], times_right(grad_cq, w_in[3]))
    grad_h1 = grad_h2 + back2
    grad_h1_low = grad_h1.astype(BF)
    grad_wso = times_left(mixed, grad_h1_low)
    grad_mixed = times_right(grad_h1_low, w_out[0]).astype(BF)
    grad_q, grad_k, grad_v, grad_scores = attend_back(query, keys, values, chances_self, grad_mixed, packs)

    total = jnp.sum(grad_scores.astype(F32), axis=0)[:, ::-1]
    padded = jnp.pad(total, ((0, 0), (0, 0), (0, wide - group))).reshape(HEADS, rows * wide)
    diagonal = padded[:, : rows * (wide - 1)].reshape(HEADS, rows, wide - 1).sum(axis=1)
    at = jnp.clip(rank * rows + (rows - 1) - jnp.arange(wide - 1, dtype=jnp.int32), 0, group - 1)
    diagonal_hot = (jnp.take(rel_buckets, at)[:, None] == jnp.arange(buckets)).astype(F32)
    grad_table = jnp.einsum("jb,hj->bh", diagonal_hot, diagonal, precision=HIGHEST)

    def to_owner(a):
        return lax.psum_scatter(a.reshape(packs, group, width), "seq", scatter_dimension=1, tiled=True)

    grad_memory = to_owner((times_right(grad_ck, w_in[4]) + times_right(grad_cv, w_in[5])).astype(BF))
    part1 = to_owner((times_right(grad_k, w_in[1]) + times_right(grad_v, w_in[2])).astype(BF))
    grad_normed1 = times_right(grad_q, w_in[0]) + part1.reshape(packs * rows, width).astype(F32)
    back1, gain1 = norm_back(x_rows, gains[0], grad_normed1)
    grad_x = grad_h1 + back1
    grad_in = jnp.concatenate(
        [
            times_left(normed1, grad_q),
            times_left(normed1_all, grad_k),
            times_left(normed1_all, grad_v),
            times_left(normed2, grad_cq),
            times_left(m_all, grad_ck),
            times_left(m_all, grad_cv),
        ]
    ).astype(BF)
    grad_out = jnp.concatenate([grad_wso, grad_wco]).astype(BF)
    shards = [
        lax.psum_scatter(a, over, scatter_dimension=0, tiled=True).astype(F32)
        for a, over in ((grad_in, everywhere), (grad_out, everywhere), (grad_ein, peers), (grad_eout, peers))
    ]
    small = lax.psum((jnp.stack([gain1, gain2, gain3]), grad_table, grad_router), ("dp", "seq", "expert"))
    shape = (packs, 1, 1, rows, width)
    return (
        out_rows.reshape(shape),
        grad_x.reshape(shape),
        grad_memory.astype(F32).reshape(shape),
        *small,
        shards[0],
        shards[1],
        shards[2][None],
        shards[3][None],
    )


def solution(mesh):
    tokens = P(None, "dp", "expert", "seq", None)
    dense = P(("dp", "seq", "expert"), None)
    expert = P("expert", ("dp", "seq"), None)
    return jax.shard_map(
        per_device,
        mesh=mesh,
        in_specs=(tokens, tokens, tokens, tokens, P(None, "dp", "expert", None), P(), P(), P(), P(),
                  dense, dense, expert, expert),
        out_specs=(tokens, tokens, tokens, P(), P(), P(), dense, dense, expert, expert),
        check_vma=False,
    )
```
